32 devices in a mesh: wide: 8 (over z, y), narrow: 4 (over x, core).
Axes of the slice: x: 2, y: 2, z: 4, core: 2. Of those that a mesh axis runs over, the one named last changes fastest.
Arguments:
- features: bfloat16 [8192, 2048], P(('wide', 'narrow')), may hold values from -6 to 6
- projection: bfloat16 [2048, 32], replicated, may hold values from -0.125 to 0.125
- targets: float32 [8192], P(('wide', 'narrow')), may hold values from -9 to 9
Outputs:
- solution: float32 [8192], P(('wide', 'narrow'))
- residual: float32 [8192], P(('wide', 'narrow'))
The draws below stay inside these ranges and needn't reach their ends.
All inputs are finite; a program needn't handle non-finite values.
Results may differ from the reference program's by a relative error of at most 0.0003.
Values sent between devices are 32-bit elements; how exact they have to be, the bound alone decides.
No kernel may reach another device: no remote copies, remote signals or barrier semaphores. Data moves between devices by JAX's collectives and lax.ppermute only.
A program may use at most 64 MiB of HBM per device.

```python
import math
import jax
import jax.numpy as jnp
from jax import lax

FEAT = 2048
PROJ = 32
ITERS = 2
SOURCES = 8192


def draw_targets(key, part):
    key = jax.random.fold_in(key, 7)
    position = jnp.arange(SOURCES, dtype=jnp.float32) / SOURCES
    base = jnp.clip(jax.random.normal(key, (SOURCES,), jnp.float32), -5.0, 5.0)
    growth = jnp.exp(0.5 * jnp.log(3.0) * position)
    return base * growth


def block_scale(rng, shape, split, smallest, largest):
    level = 1.0
    for dim, shards_of in split:
        heights = jax.random.uniform(jax.random.fold_in(jax.random.fold_in(rng, 6), dim), (shards_of,), jnp.float32, smallest / len(split), largest / len(split))
        level = level * jnp.repeat(jnp.exp(heights), shape[dim] // shards_of).reshape((-1,) + (1,) * (len(shape) - 1 - dim))
    return level


def scatter_about(rng, dims, spread, bound, shards=(), kind=jnp.bfloat16):
    level = block_scale(rng, dims, shards, -0.22, 0.18) if shards else 1.0
    entries = jax.random.normal(rng, dims, jnp.float32) * spread * level
    return jnp.minimum(jnp.maximum(entries, -bound), bound).astype(kind)


def setup_inputs(seed: int = 0) -> dict:
    streams_of = jax.random.split(jax.random.key(seed), 4)
    features = scatter_about(streams_of[0], (SOURCES, FEAT), 1.0, 6.0, ((0, 32),))
    projection = scatter_about(streams_of[1], (FEAT, PROJ), FEAT ** -0.5, 0.125)
    targets = draw_targets(jax.random.fold_in(streams_of[3], 71), 0)
    return dict(features=features, projection=projection, targets=targets)


noise_var = 0.5
highest = lax.Precision.HIGHEST


def kernel_block(left, left_square, right, right_square):
    cross = jnp.dot(left, right.T, precision=highest)
    distance = left_square[:, None] + right_square[None, :] - 2.0 * cross
    return jnp.exp(distance * (-2.0 / left.shape[1]))


def apply_operator(latent, squares, vector):
    total = latent.shape[0]
    width = math.gcd(total, 1024)
    blocks = latent.reshape(total // width, width, latent.shape[1])
    block_squares = squares.reshape(total // width, width)

    def one_block(pair):
        tile = kernel_block(pair[0], pair[1], latent, squares)
        return jnp.dot(tile, vector, precision=highest)

    products = lax.map(one_block, (blocks, block_squares)).reshape(total)
    return products + noise_var * vector


def reference(features, projection, targets):
    latent = jnp.dot(features, projection, preferred_element_type=jnp.float32)
    squares = jnp.sum(latent * latent, axis=1)
    solution = jnp.zeros_like(targets)
    residual = targets
    direction = targets
    norm_now = jnp.sum(residual * residual)
    for step in range(ITERS):
        image = apply_operator(latent, squares, direction)
        alpha = norm_now / jnp.sum(direction * image)
        solution = solution + alpha * direction
        residual = residual - alpha * image
        norm_next = jnp.sum(residual * residual)
        direction = residual + (norm_next / norm_now) * direction
        norm_now = norm_next
    return solution, residual
```

```python
import functools
import math

import jax
import jax.numpy as jnp
from jax import lax
from jax.experimental import pallas as pl
from jax.experimental.pallas import tpu as pltpu
from jax.sharding import PartitionSpec as P

noise_var = 0.5
LANES = 128
VMEM_BYTES = 48 * 2**20
highest = lax.Precision.HIGHEST
f32 = jnp.float32
bf16 = jnp.bfloat16


def split3(values):
    high = values.astype(bf16)
    rest = values - high.astype(f32)
    mid = rest.astype(bf16)
    low = (rest - mid.astype(f32)).astype(bf16)
    return high, mid, low


def exponent_rows(first, second):
    width = (first if not isinstance(first, float) else second).shape[1]
    row = lax.broadcasted_iota(jnp.int32, (16, width), 0)
    out = jnp.zeros((16, width), f32)
    for base, value in ((0, first), (3, second)):
        parts = (1.0, 1.0, 1.0) if isinstance(value, float) else [p.astype(f32) for p in split3(value)]
        for k, part in enumerate(parts):
            out = jnp.where(row == base + k, part, out)
    return out.astype(bf16)


def right_operand(latent, scale):
    square = jnp.sum(latent * latent, axis=0, keepdims=True) * scale
    h, m, l = split3(latent)
    return jnp.concatenate([h, m, l, h, m, h, exponent_rows(square, 1.0)], axis=0)


def left_operand(latent, scale):
    square = jnp.sum(latent * latent, axis=0, keepdims=True) * scale
    h, m, l = split3(latent * (-2.0 * scale))
    stacked = jnp.concatenate([h, h, h, m, m, l, exponent_rows(1.0, square)], axis=0)
    return stacked.astype(f32).T.astype(bf16)


def kernel_times(left, proj, scale, shards, shard_latent, shard_vector):
    rows = left.shape[0]

    def one_shard(s, acc):
        right = right_operand(shard_latent(s), scale)
        exponent = jnp.dot(left, right, preferred_element_type=f32)
        tile = jnp.exp2(exponent)
        for half in range(rows // LANES):
            acc = acc + tile[:, half * LANES:(half + 1) * LANES] * shard_vector(s, half)
        return acc

    acc = lax.fori_loop(0, shards, one_shard, jnp.zeros((rows, LANES), f32), unroll=4)
    ones = jnp.ones((8, LANES), f32)
    summed = lax.dot_general(ones, acc, (((1,), (1,)), ((), ())),
                             precision=highest, preferred_element_type=f32)
    return summed[0:1, :]


def project_kernel(features, projection_t, targets, out):
    proj = projection_t.shape[0]
    out[0:proj, :] = lax.dot_general(
        projection_t[...], features[...], (((1,), (1,)), ((), ())), preferred_element_type=f32)
    out[proj:proj + 8, :] = jnp.broadcast_to(targets[...], (8, targets.shape[1]))


def first_kernel(proj, scale, gathered, own, image, all_targets):
    shards, _, rows = gathered.shape
    halves = rows // LANES
    left = left_operand(own[0:proj, :], scale)

    def spread(s, _):
        for half in range(halves):
            all_targets[pl.ds(s * halves + half, 1), :] = gathered[
                s, proj:proj + 1, half * LANES:(half + 1) * LANES]
        return 0

    lax.fori_loop(0, shards, spread, 0, unroll=8)
    product = kernel_times(
        left, proj, scale, shards,
        lambda s: gathered[s, 0:proj, :],
        lambda s, half: gathered[s, proj:proj + 1, half * LANES:(half + 1) * LANES])
    total = product + noise_var * own[proj:proj + 1, :]
    for half in range(halves):
        image[half:half + 1, :] = total[:, half * LANES:(half + 1) * LANES]


def total_sum(values):
    return jnp.sum(jnp.sum(values, axis=0, keepdims=True), axis=1, keepdims=True)


def second_kernel(proj, scale, gathered, own, all_targets, all_image, own_image,
                  image, partial, step_scalars, direction):
    shards, _, rows = gathered.shape
    halves = rows // LANES
    targets, first = all_targets[...], all_image[...]
    norm = total_sum(targets * targets)
    alpha = norm / total_sum(targets * first)
    residual = targets - alpha * first
    norm_next = total_sum(residual * residual)
    beta = norm_next / norm
    direction[...] = residual + beta * targets
    left = left_operand(own[0:proj, :], scale)
    product = kernel_times(
        left, proj, scale, shards,
        lambda s: gathered[s, 0:proj, :],
        lambda s, half: direction[pl.ds(s * halves + half, 1), :])
    lane = lax.broadcasted_iota(jnp.int32, (1, LANES), 1)
    step_scalars[...] = jnp.where(lane == 0, alpha, jnp.where(lane == 1, norm_next, beta))
    part = jnp.zeros((1, LANES), f32)
    for half in range(halves):
        cut = slice(half * LANES, (half + 1) * LANES)
        start = own[proj:proj + 1, cut]
        own_direction = start - alpha * own_image[half:half + 1, :] + beta * start
        own_product = product[:, cut] + noise_var * own_direction
        image[half:half + 1, :] = own_product
        part = part + own_direction * own_product
    partial[...] = part


def last_kernel(partials, step_scalars, targets, first, second, solution_out, residual_out):
    alpha = step_scalars[0:1, 0:1]
    norm = step_scalars[0:1, 1:2]
    beta = step_scalars[0:1, 2:3]
    curve = total_sum(partials[...])
    alpha_next = norm / curve
    start = targets[...]
    residual = start - alpha * first[...]
    direction = residual + beta * start
    solution_out[...] = alpha * start + alpha_next * direction
    residual_out[...] = residual - alpha_next * second[...]


def call(kernel, out_shape, *args, scratch=()):
    return pl.pallas_call(
        kernel,
        out_shape=out_shape,
        scratch_shapes=list(scratch),
        compiler_params=pltpu.CompilerParams(vmem_limit_bytes=VMEM_BYTES),
    )(*args)


def on_device(axes, devices, features, projection, targets):
    rows, proj = features.shape[0], projection.shape[1]
    halves = rows // LANES
    scale = -2.0 / proj * math.log2(math.e)

    def shape(*dims):
        return jax.ShapeDtypeStruct(dims, f32)

    def gather(x):
        return lax.all_gather(x, axes, axis=0, tiled=False)

    own = call(project_kernel, shape(proj + 8, rows), features, projection.T, targets.reshape(1, rows))
    gathered = gather(own)
    first, all_targets = call(
        functools.partial(first_kernel, proj, scale),
        (shape(halves, LANES), shape(devices * halves, LANES)), gathered, own)
    all_first = gather(first).reshape(devices * halves, LANES)
    second, partial, step_scalars = call(
        functools.partial(second_kernel, proj, scale),
        (shape(halves, LANES), shape(1, LANES), shape(1, LANES)),
        gathered, own, all_targets, all_first, first,
        scratch=[pltpu.VMEM((devices * halves, LANES), f32)])
    partials = gather(partial).reshape(devices, LANES)
    answer, residual = call(
        last_kernel, (shape(halves, LANES), shape(halves, LANES)),
        partials, step_scalars, targets.reshape(halves, LANES), first, second)
    return answer.reshape(rows), residual.reshape(rows)


def solution(mesh):
    axes = ("wide", "narrow")
    devices = mesh.shape["wide"] * mesh.shape["narrow"]
    in_specs = (P(axes, None), P(), P(axes))
    return jax.shard_map(
        functools.partial(on_device, axes, devices), mesh=mesh,
        in_specs=in_specs, out_specs=(P(axes), P(axes)), check_vma=False,
    )
```

```python
import functools
import math

import jax
import jax.numpy as jnp
from jax import lax
from jax.experimental import pallas as pl
from jax.experimental.pallas import tpu as pltpu
from jax.sharding import PartitionSpec as P

noise_var = 0.5
LANES = 128
VMEM_BYTES = 48 * 2**20
DIRECT = 8
WIDE, NARROW = "wide", "narrow"
highest = lax.Precision.HIGHEST
f32 = jnp.float32
bf16 = jnp.bfloat16


def split3(values):
    high = values.astype(bf16)
    rest = values - high.astype(f32)
    mid = rest.astype(bf16)
    low = (rest - mid.astype(f32)).astype(bf16)
    return high, mid, low


def exponent_rows(first, second):
    width = (first if not isinstance(first, float) else second).shape[1]
    row = lax.broadcasted_iota(jnp.int32, (16, width), 0)
    out = jnp.zeros((16, width), f32)
    for base, value in ((0, first), (3, second)):
        parts = (1.0, 1.0, 1.0) if isinstance(value, float) else [p.astype(f32) for p in split3(value)]
        for k, part in enumerate(parts):
            out = jnp.where(row == base + k, part, out)
    return out.astype(bf16)


def right_operand(latent, scale):
    square = jnp.sum(latent * latent, axis=0, keepdims=True) * scale
    h, m, l = split3(latent)
    return jnp.concatenate([h, m, l, h, m, h, exponent_rows(square, 1.0)], axis=0)


def left_operand(latent, scale):
    square = jnp.sum(latent * latent, axis=0, keepdims=True) * scale
    h, m, l = split3(latent * (-2.0 * scale))
    stacked = jnp.concatenate([h, h, h, m, m, l, exponent_rows(1.0, square)], axis=0)
    return stacked.astype(f32).T.astype(bf16)


def sources(axis, blocks):
    size = sum(b.shape[0] for b in blocks)
    if len(blocks) == 1:
        return [(blocks[0], i, i) for i in range(size)]
    me = lax.axis_index(axis)
    return [(b, 0, lax.rem(me + (size - k), size)) for k, b in enumerate(blocks)]


def total_sum(values):
    return jnp.sum(jnp.sum(values, axis=0, keepdims=True), axis=1, keepdims=True)


def block_product(left, right, read_vector, write_rows):
    groups, rows, _ = left.shape
    columns = right.shape[0]
    halves = rows // LANES
    ones = jnp.ones((8, LANES), f32)

    def one_group(g, _):
        left_group = left[g]

        def one_column(c, acc):
            exponent = jnp.dot(left_group, right[c], preferred_element_type=f32)
            tile = jnp.exp2(exponent)
            for half in range(halves):
                acc = acc + tile[:, half * LANES:(half + 1) * LANES] * read_vector(c, half)
            return acc

        acc = lax.fori_loop(0, columns, one_column, jnp.zeros((rows, LANES), f32), unroll=8)
        summed = lax.dot_general(ones, acc, (((1,), (1,)), ((), ())),
                                 precision=highest, preferred_element_type=f32)
        write_rows(g, summed[0:1, :])
        return 0

    lax.fori_loop(0, groups, one_group, 0)


def row_writer(out, halves):
    def write(g, rows):
        for half in range(halves):
            out[pl.ds(g * halves + half, 1), :] = rows[:, half * LANES:(half + 1) * LANES]
    return write


def project_kernel(features, projection_t, targets, out):
    proj = projection_t.shape[0]
    out[0, 0:proj, :] = lax.dot_general(
        projection_t[...], features[...], (((1,), (1,)), ((), ())), preferred_element_type=f32)
    out[0, proj:proj + 8, :] = jnp.broadcast_to(targets[...], (8, targets.shape[1]))


def first_kernel(proj, scale, narrow_count, *refs):
    narrow_blocks, wide_blocks = refs[:narrow_count], refs[narrow_count:-5]
    left, right, partial, own_rows, column_vector = refs[-5:]
    rows = left.shape[1]
    halves = rows // LANES
    for block, i, source in sources(NARROW, narrow_blocks):
        left[source] = left_operand(block[i, 0:proj, :], scale)
        for half in range(halves):
            own_rows[pl.ds(source * halves + half, 1), :] = block[
                i, proj:proj + 1, half * LANES:(half + 1) * LANES]
    for block, i, source in sources(WIDE, wide_blocks):
        right[source] = right_operand(block[i, 0:proj, :], scale)
        for half in range(halves):
            column_vector[pl.ds(source * halves + half, 1), :] = block[
                i, proj:proj + 1, half * LANES:(half + 1) * LANES]
    block_product(
        left, right, lambda c, half: column_vector[pl.ds(c * halves + half, 1), :],
        row_writer(partial.at[0], halves))


def image_kernel(*refs):
    blocks, own_rows, out, held = refs[:-3], refs[-3], refs[-2], refs[-1]
    lines = own_rows.shape[0]
    for block, i, source in sources(NARROW, blocks):
        held[source] = block[i]
    total = noise_var * own_rows[...]
    for i in range(held.shape[0]):
        total = total + held[i]
    out[0, 0:lines, :] = total
    out[0, lines:, :] = own_rows[...]


def second_kernel(*refs):
    blocks, left, right = refs[:-7], refs[-7], refs[-6]
    out, step_scalars, direction, images, targets = refs[-5:]
    groups, rows, _ = left.shape
    halves = rows // LANES
    lines = groups * halves
    for block, i, source in sources(WIDE, blocks):
        place = pl.ds(pl.multiple_of(source * lines, lines), lines)
        images[place, :] = block[i, 0:lines, :]
        targets[place, :] = block[i, lines:, :]
    start, first = targets[...], images[...]
    norm = total_sum(start * start)
    alpha = norm / total_sum(start * first)
    residual = start - alpha * first
    norm_next = total_sum(residual * residual)
    beta = norm_next / norm
    whole = residual + beta * start
    direction[...] = whole
    mine = lax.axis_index(NARROW)
    block_product(
        left, right,
        lambda c, half: direction[pl.ds(c * lines + mine * halves + half, 1), :],
        row_writer(out.at[0], halves))
    place = pl.ds(pl.multiple_of(lax.axis_index(WIDE) * lines, lines), lines)
    share = jnp.sum(direction[place, :] * out[0, 0:lines, :], axis=0, keepdims=True)
    out[0, lines:, :] = jnp.broadcast_to(share, (8, LANES))
    lane = lax.broadcasted_iota(jnp.int32, (1, LANES), 1)
    noise = noise_var * total_sum(whole * whole)
    step_scalars[...] = jnp.where(lane == 0, alpha, jnp.where(
        lane == 1, norm_next, jnp.where(lane == 2, beta, noise)))


def share_kernel(*refs):
    blocks, out, rows_out, held = refs[:-3], refs[-3], refs[-2], refs[-1]
    groups = held.shape[0]
    lines = held.shape[1] - 8
    halves = lines // groups
    for block, i, source in sources(NARROW, blocks):
        held[source] = block[i]
    mine = lax.axis_index(NARROW) * halves
    total = jnp.zeros((1, LANES), f32)
    for i in range(groups):
        total = total + held[i, lines:lines + 1, :]
    out[0] = total
    for half in range(halves):
        line = jnp.zeros((1, LANES), f32)
        for i in range(groups):
            line = line + held[i, pl.ds(mine + half, 1), :]
        rows_out[half:half + 1, :] = line


def last_kernel(*refs):
    blocks = refs[:-7]
    step_scalars, start_ref, first_ref, second_ref, solution_out, residual_out, held = refs[-7:]
    alpha = step_scalars[0:1, 0:1]
    norm = step_scalars[0:1, 1:2]
    beta = step_scalars[0:1, 2:3]
    noise = step_scalars[0:1, 3:4]
    for block, i, source in sources(WIDE, blocks):
        held[pl.ds(source, 1), :] = block[i]
    alpha_next = norm / (total_sum(held[...]) + noise)
    start = start_ref[...]
    halves = start.shape[0]
    mine = lax.axis_index(NARROW) * halves
    for half in range(halves):
        begin = start[half:half + 1, :]
        residual = begin - alpha * first_ref[0, pl.ds(mine + half, 1), :]
        direction = residual + beta * begin
        image = second_ref[half:half + 1, :] + noise_var * direction
        solution_out[half:half + 1, :] = alpha * begin + alpha_next * direction
        residual_out[half:half + 1, :] = residual - alpha_next * image


def call(kernel, out_shape, *args, scratch=()):
    return pl.pallas_call(
        kernel,
        out_shape=out_shape,
        scratch_shapes=list(scratch),
        compiler_params=pltpu.CompilerParams(vmem_limit_bytes=VMEM_BYTES),
    )(*args)


def exchange(x, axis, size):
    if size > DIRECT:
        return [lax.all_gather(x, axis, axis=0, tiled=True)]
    return [x] + [
        lax.ppermute(x, axis, [(i, (i + k) % size) for i in range(size)])
        for k in range(1, size)]


def on_device(wide, narrow, features, projection, targets):
    rows, proj = features.shape[0], projection.shape[1]
    halves = rows // LANES
    lines = narrow * halves
    scale = -2.0 / proj * math.log2(math.e)
    depth = 6 * proj + 16

    def shape(*dims, dtype=f32):
        return jax.ShapeDtypeStruct(dims, dtype)

    def scratch(*dims):
        return pltpu.VMEM(dims, f32)

    own = call(project_kernel, shape(1, proj + 8, rows),
               features, projection.T, targets.reshape(1, rows))
    narrow_blocks = exchange(own, NARROW, narrow)
    wide_blocks = exchange(own, WIDE, wide)
    left, right, partial, own_rows = call(
        functools.partial(first_kernel, proj, scale, len(narrow_blocks)),
        (shape(narrow, rows, depth, dtype=bf16), shape(wide, depth, rows, dtype=bf16),
         shape(1, lines, LANES), shape(lines, LANES)),
        *narrow_blocks, *wide_blocks, scratch=[scratch(wide * halves, LANES)])
    image = call(
        image_kernel, shape(1, 2 * lines, LANES),
        *exchange(partial, NARROW, narrow), own_rows,
        scratch=[scratch(narrow, lines, LANES)])
    out, step_scalars = call(
        second_kernel, (shape(1, lines + 8, LANES), shape(1, LANES)),
        *exchange(image, WIDE, wide), left, right,
        scratch=[scratch(wide * lines, LANES)] * 3)
    share, second = call(
        share_kernel, (shape(1, 1, LANES), shape(halves, LANES)),
        *exchange(out, NARROW, narrow), scratch=[scratch(narrow, lines + 8, LANES)])
    answer, residual = call(
        last_kernel, (shape(halves, LANES), shape(halves, LANES)),
        *exchange(share, WIDE, wide), step_scalars, targets.reshape(halves, LANES), image, second,
        scratch=[scratch(wide, LANES)])
    return answer.reshape(rows), residual.reshape(rows)


def solution(mesh):
    axes = (WIDE, NARROW)
    in_specs = (P(axes, None), P(), P(axes))
    return jax.shard_map(
        functools.partial(on_device, mesh.shape[WIDE], mesh.shape[NARROW]), mesh=mesh,
        in_specs=in_specs, out_specs=(P(axes), P(axes)), check_vma=False,
    )
```

```python
import functools
import math

import jax
import jax.numpy as jnp
from jax import lax
from jax.experimental import pallas as pl
from jax.experimental.pallas import tpu as pltpu
from jax.sharding import PartitionSpec as P

noise_var = 0.5
LANES = 128
VMEM_BYTES = 48 * 2**20
WIDE, NARROW = "wide", "narrow"
highest = lax.Precision.HIGHEST
f32 = jnp.float32
bf16 = jnp.bfloat16


def split3(values):
    high = values.astype(bf16)
    rest = values - high.astype(f32)
    mid = rest.astype(bf16)
    low = (rest - mid.astype(f32)).astype(bf16)
    return high, mid, low


def exponent_rows(first, second):
    width = (first if not isinstance(first, float) else second).shape[1]
    row = lax.broadcasted_iota(jnp.int32, (16, width), 0)
    out = jnp.zeros((16, width), f32)
    for base, value in ((0, first), (3, second)):
        parts = (1.0, 1.0, 1.0) if isinstance(value, float) else [p.astype(f32) for p in split3(value)]
        for k, part in enumerate(parts):
            out = jnp.where(row == base + k, part, out)
    return out.astype(bf16)


def right_operand(latent, scale):
    square = jnp.sum(latent * latent, axis=0, keepdims=True) * scale
    h, m, l = split3(latent)
    return jnp.concatenate([h, m, l, h, m, h, exponent_rows(square, 1.0)], axis=0)


def left_operand(latent, scale):
    square = jnp.sum(latent * latent, axis=0, keepdims=True) * scale
    h, m, l = split3(latent * (-2.0 * scale))
    stacked = jnp.concatenate([h, h, h, m, m, l, exponent_rows(1.0, square)], axis=0)
    return stacked.astype(f32).T.astype(bf16)


def sources(axis, blocks):
    size = sum(b.shape[0] for b in blocks)
    if len(blocks) == 1:
        return [(blocks[0], i, i) for i in range(size)]
    me = lax.axis_index(axis)
    return [(b, 0, lax.rem(me + (size - k), size)) for k, b in enumerate(blocks)]


def total_sum(values):
    return jnp.sum(jnp.sum(values, axis=0, keepdims=True), axis=1, keepdims=True)


def block_product(left, right, read_vector, write_rows):
    groups, rows, _ = left.shape
    columns = right.shape[0]
    halves = rows // LANES
    ones = jnp.ones((8, LANES), f32)

    def one_group(g, _):
        left_group = left[g]

        def one_column(c, acc):
            exponent = jnp.dot(left_group, right[c], preferred_element_type=f32)
            tile = jnp.exp2(exponent)
            for half in range(halves):
                acc = acc + tile[:, half * LANES:(half + 1) * LANES] * read_vector(c, half)
            return acc

        acc = lax.fori_loop(0, columns, one_column, jnp.zeros((rows, LANES), f32), unroll=8)
        summed = lax.dot_general(ones, acc, (((1,), (1,)), ((), ())),
                                 precision=highest, preferred_element_type=f32)
        write_rows(g, summed[0:1, :])
        return 0

    lax.fori_loop(0, groups, one_group, 0)


def row_writer(out, halves):
    def write(g, rows):
        for half in range(halves):
            out[pl.ds(g * halves + half, 1), :] = rows[:, half * LANES:(half + 1) * LANES]
    return write


def project_kernel(features, projection_t, targets, out):
    copies, proj = out.shape[0], projection_t.shape[0]
    latent = lax.dot_general(
        projection_t[...], features[...], (((1,), (1,)), ((), ())), preferred_element_type=f32)
    tail = jnp.broadcast_to(targets[...], (8, targets.shape[1]))
    for i in range(copies):
        out[i, 0:proj, :] = latent
        out[i, proj:proj + 8, :] = tail


def first_kernel(proj, scale, narrow_count, *refs):
    narrow_blocks, wide_blocks = refs[:narrow_count], refs[narrow_count:-6]
    left, right, out, own_rows, column_vector, partial = refs[-6:]
    rows = left.shape[1]
    halves = rows // LANES
    lines = partial.shape[0]
    for block, i, source in sources(NARROW, narrow_blocks):
        left[source] = left_operand(block[i, 0:proj, :], scale)
        for half in range(halves):
            own_rows[pl.ds(source * halves + half, 1), :] = block[
                i, proj:proj + 1, half * LANES:(half + 1) * LANES]
    for block, i, source in sources(WIDE, wide_blocks):
        right[source] = right_operand(block[i, 0:proj, :], scale)
        for half in range(halves):
            column_vector[pl.ds(source * halves + half, 1), :] = block[
                i, proj:proj + 1, half * LANES:(half + 1) * LANES]
    block_product(
        left, right, lambda c, half: column_vector[pl.ds(c * halves + half, 1), :],
        row_writer(partial, halves))
    mine = lax.axis_index(NARROW) * halves
    pieces = [partial[line:line + 1, :] for line in range(lines)]
    pieces += [own_rows[pl.ds(mine + half, 1), :] for half in range(halves)]
    block = jnp.concatenate(pieces, axis=1)

    def copy(i, _):
        out[i] = block
        return 0

    lax.fori_loop(0, out.shape[0], copy, 0, unroll=8)


def second_kernel(arrived, left, right, out, step_scalars, direction, images, targets, partial):
    groups, rows, _ = left.shape
    halves = rows // LANES
    lines = groups * halves
    wide = right.shape[0]

    def unpack(w, _):
        total = arrived[w * groups]
        for g in range(1, groups):
            total = total + arrived[w * groups + g]
        for g in range(groups):
            block = arrived[w * groups + g]
            for half in range(halves):
                line = g * halves + half
                start = block[:, (lines + half) * LANES:(lines + half + 1) * LANES]
                place = pl.ds(w * lines + line, 1)
                targets[place, :] = start
                images[place, :] = total[:, line * LANES:(line + 1) * LANES] + noise_var * start
        return 0

    lax.fori_loop(0, wide, unpack, 0, unroll=8)
    start, first = targets[...], images[...]
    norm = total_sum(start * start)
    alpha = norm / total_sum(start * first)
    residual = start - alpha * first
    norm_next = total_sum(residual * residual)
    beta = norm_next / norm
    whole = residual + beta * start
    direction[...] = whole
    mine = lax.axis_index(NARROW)
    block_product(
        left, right,
        lambda c, half: direction[pl.ds(c * lines + mine * halves + half, 1), :],
        row_writer(partial, halves))
    group = lax.axis_index(WIDE) * lines
    share = jnp.sum(direction[pl.ds(pl.multiple_of(group, lines), lines), :] * partial[...],
                    axis=0, keepdims=True)
    blocks = [
        jnp.concatenate([partial[g * halves + half:g * halves + half + 1, :]
                         for half in range(halves)] + [share], axis=1)
        for g in range(groups)]

    def copy(w, _):
        for g in range(groups):
            out[w * groups + g] = blocks[g]
        return 0

    lax.fori_loop(0, wide, copy, 0, unroll=8)
    lane = lax.broadcasted_iota(jnp.int32, (1, LANES), 1)
    noise = noise_var * total_sum(whole * whole)
    step_scalars[0:1, :] = jnp.where(lane == 0, alpha, jnp.where(
        lane == 1, norm_next, jnp.where(lane == 2, beta, noise)))
    for half in range(halves):
        step_scalars[1 + half:2 + half, :] = images[pl.ds(group + mine * halves + half, 1), :]


def last_kernel(groups, arrived, step_scalars, start_ref, solution_out, residual_out):
    alpha = step_scalars[0:1, 0:1]
    norm = step_scalars[0:1, 1:2]
    beta = step_scalars[0:1, 2:3]
    noise = step_scalars[0:1, 3:4]
    halves = start_ref.shape[0]

    def add(i, total):
        return total + arrived[i, :, halves * LANES:(halves + 1) * LANES]

    share = lax.fori_loop(0, arrived.shape[0], add, jnp.zeros((1, LANES), f32), unroll=8)
    alpha_next = norm / (total_sum(share) + noise)
    group = lax.axis_index(WIDE) * groups
    product = arrived[group]
    for g in range(1, groups):
        product = product + arrived[group + g]
    for half in range(halves):
        begin = start_ref[half:half + 1, :]
        residual = begin - alpha * step_scalars[1 + half:2 + half, :]
        direction = residual + beta * begin
        image = product[:, half * LANES:(half + 1) * LANES] + noise_var * direction
        solution_out[half:half + 1, :] = alpha * begin + alpha_next * direction
        residual_out[half:half + 1, :] = residual - alpha_next * image


def call(kernel, out_shape, *args, scratch=()):
    return pl.pallas_call(
        kernel,
        out_shape=out_shape,
        scratch_shapes=list(scratch),
        compiler_params=pltpu.CompilerParams(vmem_limit_bytes=VMEM_BYTES),
    )(*args)


def to_all(blocks, axes):
    return lax.all_to_all(blocks, axes, split_axis=0, concat_axis=0, tiled=True)


def passed_round(x, axis, size):
    return [x] + [
        lax.ppermute(x, axis, [(i, (i + k) % size) for i in range(size)])
        for k in range(1, size)]


def on_device(wide, narrow, features, projection, targets):
    rows, proj = features.shape[0], projection.shape[1]
    halves = rows // LANES
    lines = narrow * halves
    devices = wide * narrow
    scale = -2.0 / proj * math.log2(math.e)
    depth = 6 * proj + 16
    axes = (WIDE, NARROW)

    def shape(*dims, dtype=f32):
        return jax.ShapeDtypeStruct(dims, dtype)

    def scratch(*dims):
        return pltpu.VMEM(dims, f32)

    own = call(project_kernel, shape(wide, proj + 8, rows),
               features, projection.T, targets.reshape(1, rows))
    narrow_blocks = passed_round(own[0:1], NARROW, narrow)
    wide_blocks = to_all(own, WIDE)
    left, right, out, _ = call(
        functools.partial(first_kernel, proj, scale, len(narrow_blocks)),
        (shape(narrow, rows, depth, dtype=bf16), shape(wide, depth, rows, dtype=bf16),
         shape(devices, 1, (lines + halves) * LANES), shape(lines, LANES)),
        *narrow_blocks, wide_blocks,
        scratch=[scratch(wide * halves, LANES), scratch(lines, LANES)])
    out, step_scalars = call(
        second_kernel, (shape(devices, 1, (halves + 1) * LANES), shape(1 + halves, LANES)),
        to_all(out, axes), left, right,
        scratch=[scratch(wide * lines, LANES)] * 3 + [scratch(lines, LANES)])
    answer, residual = call(
        functools.partial(last_kernel, narrow), (shape(halves, LANES), shape(halves, LANES)),
        to_all(out, axes), step_scalars, targets.reshape(halves, LANES))
    return answer.reshape(rows), residual.reshape(rows)


def solution(mesh):
    axes = (WIDE, NARROW)
    in_specs = (P(axes, None), P(), P(axes))
    return jax.shard_map(
        functools.partial(on_device, mesh.shape[WIDE], mesh.shape[NARROW]), mesh=mesh,
        in_specs=in_specs, out_specs=(P(axes), P(axes)), check_vma=False,
    )
```

```python
import functools
import math

import jax
import jax.numpy as jnp
from jax import lax
from jax.experimental import pallas as pl
from jax.experimental.pallas import tpu as pltpu
from jax.sharding import PartitionSpec as P

noise_var = 0.5
LANES = 128
CHUNKS = 4
DIRECT = 8
KEEP_BYTES = 8 * 2**20
VMEM_BYTES = 32 * 2**20
WHOLE_VMEM_BYTES = 60 * 2**20
WIDE, NARROW = "wide", "narrow"
highest = lax.Precision.HIGHEST
f32 = jnp.float32
bf16 = jnp.bfloat16


def split3(values):
    high = values.astype(bf16)
    rest = values - high.astype(f32)
    mid = rest.astype(bf16)
    low = (rest - mid.astype(f32)).astype(bf16)
    return high, mid, low


def exponent_rows(first, second):
    width = (first if not isinstance(first, float) else second).shape[1]
    row = lax.broadcasted_iota(jnp.int32, (16, width), 0)
    out = jnp.zeros((16, width), f32)
    for base, value in ((0, first), (3, second)):
        parts = (1.0, 1.0, 1.0) if isinstance(value, float) else [p.astype(f32) for p in split3(value)]
        for k, part in enumerate(parts):
            out = jnp.where(row == base + k, part, out)
    return out.astype(bf16)


def right_operand(latent, scale):
    square = jnp.sum(latent * latent, axis=0, keepdims=True) * scale
    h, m, l = split3(latent)
    return jnp.concatenate([h, m, l, h, m, h, exponent_rows(square, 1.0)], axis=0)


def left_operand(latent, scale):
    square = jnp.sum(latent * latent, axis=0, keepdims=True) * scale
    h, m, l = split3(latent * (-2.0 * scale))
    stacked = jnp.concatenate([h, h, h, m, m, l, exponent_rows(1.0, square)], axis=0)
    return stacked.astype(f32).T.astype(bf16)


def place():
    w, n = lax.axis_index(WIDE), lax.axis_index(NARROW)
    return w // 2, w % 2, n // 2, n % 2


def device_at(z, y, x, core, narrow):
    return ((z * 2 + y) * (narrow // 2) + x) * 2 + core


def row_sources(blocks, narrow):
    if len(blocks) == 1:
        return [(blocks[0], i, i) for i in range(narrow)]
    z, y, x, core = place()
    me = y * (narrow // 2) + x
    return [(b, 0, jnp.bitwise_xor(me, k)) for k, b in enumerate(blocks)]


def column_sources(blocks, wide):
    if len(blocks) == 1:
        return [(blocks[0], i, i) for i in range(wide)]
    z, y, x, core = place()
    depth = wide // 2
    return [(b, 0, jnp.bitwise_xor(z, k % depth) * 2 + jnp.bitwise_xor(core, k // depth))
            for k, b in enumerate(blocks)]


def total_sum(values):
    return jnp.sum(jnp.sum(values, axis=0, keepdims=True), axis=1, keepdims=True)


def lane_sums(values):
    ones = jnp.ones((8, values.shape[1]), f32)
    return lax.dot_general(ones, values, (((1,), (1,)), ((), ())),
                           precision=highest, preferred_element_type=f32)[0:1, :]


def make_rows(left, right, kept, read_vector, write_rows):
    groups, rows, _ = left.shape
    columns = right.shape[0]
    halves = rows // LANES

    def one_group(g, _):
        left_group = left[g]

        def one_column(c, acc):
            exponent = jnp.dot(left_group, right[c], preferred_element_type=f32)
            tile = jnp.exp2(exponent)
            if kept is not None:
                kept[g, c] = tile
            for half in range(halves):
                acc = acc + tile[:, half * LANES:(half + 1) * LANES] * read_vector(c, half)
            return acc

        acc = lax.fori_loop(0, columns, one_column, jnp.zeros((rows, LANES), f32), unroll=8)
        write_rows(g, lane_sums(acc))
        return 0

    lax.fori_loop(0, groups, one_group, 0)


def use_rows(kept, read_vector, write_rows):
    groups, columns, rows, _ = kept.shape
    halves = rows // LANES

    def one_group(g, _):
        def one_column(c, acc):
            for half in range(halves):
                acc = acc + kept[g, c, :, half * LANES:(half + 1) * LANES] * read_vector(c, half)
            return acc

        acc = lax.fori_loop(0, columns, one_column, jnp.zeros((rows, LANES), f32), unroll=8)
        write_rows(g, lane_sums(acc))
        return 0

    lax.fori_loop(0, groups, one_group, 0)


def row_writer(out, halves):
    def write(g, rows):
        for half in range(halves):
            out[pl.ds(g * halves + half, 1), :] = rows[:, half * LANES:(half + 1) * LANES]
    return write


def project_kernel(features, projection_t, targets, out, feature_buf, projection_buf, target_buf, sems):
    proj = projection_t.shape[0]
    chunks, _, width = feature_buf.shape
    copies = [pltpu.make_async_copy(projection_t, projection_buf, sems.at[0])]
    copies += [
        pltpu.make_async_copy(features.at[:, pl.ds(i * width, width)], feature_buf.at[i], sems.at[i + 1])
        for i in range(chunks)]
    copies += [pltpu.make_async_copy(targets, target_buf, sems.at[chunks + 1])]
    for copy in copies:
        copy.start()
    copies[0].wait()
    latent = jnp.zeros((proj, features.shape[0]), f32)
    for i in range(chunks):
        copies[i + 1].wait()
        latent = latent + lax.dot_general(
            projection_buf[:, i * width:(i + 1) * width], feature_buf[i],
            (((1,), (1,)), ((), ())), preferred_element_type=f32)
    copies[-1].wait()
    out[0, 0:proj, :] = latent
    out[0, proj:proj + 8, :] = jnp.broadcast_to(target_buf[...], (8, out.shape[2]))


def first_kernel(proj, scale, wide, narrow, keep, row_count, column_count, *refs):
    row_blocks, column_blocks = refs[:row_count], refs[row_count:row_count + column_count]
    refs = refs[row_count + column_count:]
    if keep:
        kept, out, left, right, own_rows, column_vector, partial = refs
    else:
        kept = None
        left, right, out, own_rows, column_vector, partial = refs
    rows = left.shape[1]
    halves = rows // LANES
    lines = partial.shape[0]
    for block, i, source in row_sources(row_blocks, narrow):
        left[source] = left_operand(block[i, 0:proj, :], scale)
        for half in range(halves):
            own_rows[pl.ds(source * halves + half, 1), :] = block[
                i, proj:proj + 1, half * LANES:(half + 1) * LANES]
    for block, i, source in column_sources(column_blocks, wide):
        right[source] = right_operand(block[i, 0:proj, :], scale)
        for half in range(halves):
            column_vector[pl.ds(source * halves + half, 1), :] = block[
                i, proj:proj + 1, half * LANES:(half + 1) * LANES]
    make_rows(
        left, right, kept, lambda c, half: column_vector[pl.ds(c * halves + half, 1), :],
        row_writer(partial, halves))
    z, y, x, core = place()
    mine = (y * (narrow // 2) + x) * halves
    pieces = [partial[line:line + 1, :] for line in range(lines)]
    pieces += [own_rows[pl.ds(mine + half, 1), :] for half in range(halves)]
    block = jnp.concatenate(pieces, axis=1)

    def copy(i, _):
        out[i] = block
        return 0

    lax.fori_loop(0, out.shape[0], copy, 0, unroll=8)


def second_kernel(wide, narrow, keep, *refs):
    arrived, out, step_scalars, direction, images, targets, partial = refs[:1] + refs[-6:]
    lines = partial.shape[0]
    halves = lines // narrow
    across = narrow // 2
    group = [(y, x) for y in range(2) for x in range(across)]

    def unpack(z, _):
        for core in range(2):
            members = [device_at(z, y, x, core, narrow) for y, x in group]
            total = arrived[members[0]]
            for member in members[1:]:
                total = total + arrived[member]
            for r, member in enumerate(members):
                for half in range(halves):
                    start = arrived[member, :, (lines + half) * LANES:(lines + half + 1) * LANES]
                    line = r * halves + half
                    spot = pl.ds(member * halves + half, 1)
                    targets[spot, :] = start
                    images[spot, :] = total[:, line * LANES:(line + 1) * LANES] + noise_var * start
        return 0

    lax.fori_loop(0, wide // 2, unpack, 0, unroll=4)
    start, first = targets[...], images[...]
    norm = total_sum(start * start)
    alpha = norm / total_sum(start * first)
    residual = start - alpha * first
    norm_next = total_sum(residual * residual)
    beta = norm_next / norm
    whole = residual + beta * start
    direction[...] = whole
    z, y, x, core = place()

    def read_vector(c, half):
        return direction[pl.ds(device_at(c // 2, y, x, c % 2, narrow) * halves + half, 1), :]

    if keep:
        use_rows(refs[1], read_vector, row_writer(partial, halves))
    else:
        make_rows(refs[1], refs[2], None, read_vector, row_writer(partial, halves))
    share = jnp.zeros((1, LANES), f32)
    for r, (row_y, row_x) in enumerate(group):
        for half in range(halves):
            spot = pl.ds(device_at(z, row_y, row_x, core, narrow) * halves + half, 1)
            line = r * halves + half
            share = share + direction[spot, :] * partial[line:line + 1, :]
    blocks = [
        jnp.concatenate([partial[r * halves + half:r * halves + half + 1, :]
                         for half in range(halves)] + [share], axis=1)
        for r in range(narrow)]

    def copy(to_z, _):
        for r, (to_y, to_x) in enumerate(group):
            for to_core in range(2):
                out[device_at(to_z, to_y, to_x, to_core, narrow)] = blocks[r]
        return 0

    lax.fori_loop(0, wide // 2, copy, 0, unroll=4)
    lane = lax.broadcasted_iota(jnp.int32, (1, LANES), 1)
    noise = noise_var * total_sum(whole * whole)
    step_scalars[0:1, :] = jnp.where(lane == 0, alpha, jnp.where(
        lane == 1, norm_next, jnp.where(lane == 2, beta, noise)))
    for half in range(halves):
        spot = pl.ds(device_at(z, y, x, core, narrow) * halves + half, 1)
        step_scalars[1 + half:2 + half, :] = images[spot, :]


def last_kernel(narrow, arrived, step_scalars, start_ref, solution_out, residual_out):
    alpha = step_scalars[0:1, 0:1]
    norm = step_scalars[0:1, 1:2]
    beta = step_scalars[0:1, 2:3]
    noise = step_scalars[0:1, 3:4]
    halves = start_ref.shape[0]

    def add(i, total):
        return total + arrived[i, :, halves * LANES:(halves + 1) * LANES]

    share = lax.fori_loop(0, arrived.shape[0], add, jnp.zeros((1, LANES), f32), unroll=8)
    alpha_next = norm / (total_sum(share) + noise)
    z, _, _, core = place()
    product = jnp.zeros((1, (halves + 1) * LANES), f32)
    for y in range(2):
        for x in range(narrow // 2):
            product = product + arrived[device_at(z, y, x, core, narrow)]
    for half in range(halves):
        begin = start_ref[half:half + 1, :]
        residual = begin - alpha * step_scalars[1 + half:2 + half, :]
        direction = residual + beta * begin
        image = product[:, half * LANES:(half + 1) * LANES] + noise_var * direction
        solution_out[half:half + 1, :] = alpha * begin + alpha_next * direction
        residual_out[half:half + 1, :] = residual - alpha_next * image


def call(kernel, out_shape, *args, scratch=(), vmem=VMEM_BYTES, **options):
    return pl.pallas_call(
        kernel,
        out_shape=out_shape,
        scratch_shapes=list(scratch),
        compiler_params=pltpu.CompilerParams(vmem_limit_bytes=vmem),
        **options,
    )(*args)


def to_all(blocks, axes):
    return lax.all_to_all(blocks, axes, split_axis=0, concat_axis=0, tiled=True)


def first_round(own, wide, narrow):
    axes = (WIDE, NARROW)
    depth, across = wide // 2, narrow // 2
    if depth > DIRECT or depth & (depth - 1) or across & (across - 1):
        every = lax.all_gather(own, axes, axis=0, tiled=True)
        every = every.reshape(depth, 2, across, 2, *own.shape[1:])
        z, y, x, core = place()
        rows = lax.dynamic_index_in_dim(every, z, 0, keepdims=False)
        rows = lax.dynamic_index_in_dim(rows, core, 2, keepdims=False)
        columns = lax.dynamic_index_in_dim(every, y, 1, keepdims=False)
        columns = lax.dynamic_index_in_dim(columns, x, 1, keepdims=False)
        return [rows.reshape(narrow, *own.shape[1:])], [columns.reshape(wide, *own.shape[1:])]

    def swap(value, z_flip, row_flip, core_flip):
        pairs = []
        for z in range(depth):
            for r in range(narrow):
                for core in range(2):
                    other = r ^ row_flip
                    pairs.append((
                        device_at(z, r // across, r % across, core, narrow),
                        device_at(z ^ z_flip, other // across, other % across, core ^ core_flip, narrow)))
        return lax.ppermute(value, axes, pairs)

    columns = [own] + [swap(own, k, 0, 0) for k in range(1, depth)]
    rows = [own] + [swap(own, 0, k, 0) for k in range(1, narrow)]
    columns += [swap(column, 0, 0, 1) for column in columns]
    return rows, columns


def on_device(wide, narrow, features, projection, targets):
    rows, proj = features.shape[0], projection.shape[1]
    halves = rows // LANES
    lines = narrow * halves
    devices = wide * narrow
    scale = -2.0 / proj * math.log2(math.e)
    depth = 6 * proj + 16
    keep = 4 * devices * rows * rows <= KEEP_BYTES
    axes = (WIDE, NARROW)

    def shape(*dims, dtype=f32):
        return jax.ShapeDtypeStruct(dims, dtype)

    def scratch(*dims, dtype=f32):
        return pltpu.VMEM(dims, dtype)

    feat = features.shape[1]
    own = call(
        project_kernel, shape(1, proj + 8, rows), features, projection.T, targets.reshape(1, rows),
        in_specs=[pl.BlockSpec(memory_space=pl.ANY)] * 3, vmem=WHOLE_VMEM_BYTES,
        scratch=[scratch(CHUNKS, rows, feat // CHUNKS, dtype=bf16), scratch(proj, feat, dtype=bf16),
                 scratch(1, rows), pltpu.SemaphoreType.DMA((CHUNKS + 2,))])
    row_blocks, column_blocks = first_round(own, wide, narrow)
    left = (narrow, rows, depth)
    right = (wide, depth, rows)
    block_out = shape(devices, 1, (lines + halves) * LANES)
    work = [scratch(lines, LANES), scratch(wide * halves, LANES), scratch(lines, LANES)]
    first = functools.partial(
        first_kernel, proj, scale, wide, narrow, keep, len(row_blocks), len(column_blocks))
    if keep:
        *block, out = call(
            first, (shape(narrow, wide, rows, rows), block_out), *row_blocks, *column_blocks,
            scratch=[scratch(*left, dtype=bf16), scratch(*right, dtype=bf16)] + work)
    else:
        *block, out = call(
            first, (shape(*left, dtype=bf16), shape(*right, dtype=bf16), block_out),
            *row_blocks, *column_blocks, scratch=work)
    out, step_scalars = call(
        functools.partial(second_kernel, wide, narrow, keep),
        (shape(devices, 1, (halves + 1) * LANES), shape(1 + halves, LANES)),
        to_all(out, axes), *block,
        scratch=[scratch(devices * halves, LANES)] * 3 + [scratch(lines, LANES)])
    answer, residual = call(
        functools.partial(last_kernel, narrow), (shape(halves, LANES), shape(halves, LANES)),
        to_all(out, axes), step_scalars, targets.reshape(halves, LANES))
    return answer.reshape(rows), residual.reshape(rows)


def solution(mesh):
    axes = (WIDE, NARROW)
    in_specs = (P(axes, None), P(), P(axes))
    return jax.shard_map(
        functools.partial(on_device, mesh.shape[WIDE], mesh.shape[NARROW]), mesh=mesh,
        in_specs=in_specs, out_specs=(P(axes), P(axes)), check_vma=False,
    )
```

```python
import functools
import math

import jax
import jax.numpy as jnp
from jax import lax
from jax.experimental import pallas as pl
from jax.experimental.pallas import tpu as pltpu
from jax.sharding import PartitionSpec as P

noise_var = 0.5
LANES = 128
CHUNKS = 4
DIRECT = 8
KEEP_BYTES = 8 * 2**20
VMEM_BYTES = 32 * 2**20
WHOLE_VMEM_BYTES = (53 * 1024 + 870) * 2**10
WIDE, NARROW = "wide", "narrow"
highest = lax.Precision.HIGHEST
f32 = jnp.float32
bf16 = jnp.bfloat16


def split3(values):
    high = values.astype(bf16)
    rest = values - high.astype(f32)
    mid = rest.astype(bf16)
    low = (rest - mid.astype(f32)).astype(bf16)
    return high, mid, low


def exponent_rows(first, second):
    width = (first if not isinstance(first, float) else second).shape[1]
    row = lax.broadcasted_iota(jnp.int32, (16, width), 0)
    out = jnp.zeros((16, width), f32)
    for base, value in ((0, first), (3, second)):
        parts = (1.0, 1.0, 1.0) if isinstance(value, float) else [p.astype(f32) for p in split3(value)]
        for k, part in enumerate(parts):
            out = jnp.where(row == base + k, part, out)
    return out.astype(bf16)


def right_operand(latent, scale):
    square = jnp.sum(latent * latent, axis=0, keepdims=True) * scale
    h, m, l = split3(latent)
    return jnp.concatenate([h, m, l, h, m, h, exponent_rows(square, 1.0)], axis=0)


def left_operand(latent, scale):
    square = jnp.sum(latent * latent, axis=0, keepdims=True) * scale
    h, m, l = split3(latent * (-2.0 * scale))
    stacked = jnp.concatenate([h, h, h, m, m, l, exponent_rows(1.0, square)], axis=0)
    return stacked.astype(f32).T.astype(bf16)


def place():
    w, n = lax.axis_index(WIDE), lax.axis_index(NARROW)
    return w // 2, w % 2, n // 2, n % 2


def device_at(z, y, x, core, narrow):
    return ((z * 2 + y) * (narrow // 2) + x) * 2 + core


def row_sources(blocks, narrow):
    if len(blocks) == 1:
        return [(blocks[0], i, i) for i in range(narrow)]
    z, y, x, core = place()
    me = y * (narrow // 2) + x
    return [(b, 0, jnp.bitwise_xor(me, k)) for k, b in enumerate(blocks)]


def column_sources(blocks, wide):
    if len(blocks) == 1:
        return [(blocks[0], i, i) for i in range(wide)]
    z, y, x, core = place()
    depth = wide // 2
    return [(b, 0, jnp.bitwise_xor(z, k % depth) * 2 + jnp.bitwise_xor(core, k // depth))
            for k, b in enumerate(blocks)]


def total_sum(values):
    return jnp.sum(jnp.sum(values, axis=0, keepdims=True), axis=1, keepdims=True)


def lane_sums(values):
    parts = jnp.concatenate(split3(values), axis=1)
    ones = jnp.ones((16, parts.shape[1]), bf16)
    return lax.dot_general(ones, parts, (((1,), (1,)), ((), ())),
                           preferred_element_type=f32)[0:1, :]


def make_rows(left, right, kept, read_vector, sums):
    groups, rows, _ = left.shape
    columns = right.shape[0]
    halves = rows // LANES

    def one_group(g, _):
        left_group = left[g]

        def one_column(c, acc):
            exponent = jnp.dot(left_group, right[c], preferred_element_type=f32)
            tile = jnp.exp2(exponent)
            if kept is not None:
                kept[g, c] = tile
            for half in range(halves):
                acc = acc + tile[:, half * LANES:(half + 1) * LANES] * read_vector(c, half)
            return acc

        sums[g] = lax.fori_loop(0, columns, one_column, jnp.zeros((rows, LANES), f32), unroll=8)
        return 0

    lax.fori_loop(0, groups, one_group, 0)


def use_rows(kept, read_vector, sums):
    groups, columns, rows, _ = kept.shape
    halves = rows // LANES

    def one_group(g, _):
        def one_column(c, acc):
            for half in range(halves):
                acc = acc + kept[g, c, :, half * LANES:(half + 1) * LANES] * read_vector(c, half)
            return acc

        sums[g] = lax.fori_loop(0, columns, one_column, jnp.zeros((rows, LANES), f32), unroll=8)
        return 0

    lax.fori_loop(0, groups, one_group, 0)


def write_rows(sums, out):
    groups, rows, _ = sums.shape
    total = lane_sums(sums[...].reshape(groups * rows, LANES))
    for line in range(out.shape[0]):
        out[line:line + 1, :] = total[:, line * LANES:(line + 1) * LANES]


def project_kernel(features, projection_t, targets, out, feature_buf, projection_buf, target_buf, sems):
    proj = projection_t.shape[0]
    chunks, _, width = feature_buf.shape
    copies = [pltpu.make_async_copy(projection_t, projection_buf, sems.at[0])]
    copies += [
        pltpu.make_async_copy(features.at[:, pl.ds(i * width, width)], feature_buf.at[i], sems.at[i + 1])
        for i in range(chunks)]
    copies += [pltpu.make_async_copy(targets, target_buf, sems.at[chunks + 1])]
    for copy in copies:
        copy.start()
    copies[0].wait()
    latent = jnp.zeros((proj, features.shape[0]), f32)
    for i in range(chunks):
        copies[i + 1].wait()
        latent = latent + lax.dot_general(
            projection_buf[:, i * width:(i + 1) * width], feature_buf[i],
            (((1,), (1,)), ((), ())), preferred_element_type=f32)
    copies[-1].wait()
    out[0, 0:proj, :] = latent
    out[0, proj:proj + 8, :] = jnp.broadcast_to(target_buf[...], (8, out.shape[2]))


def first_kernel(proj, scale, wide, narrow, keep, row_count, column_count, *refs):
    row_blocks, column_blocks = refs[:row_count], refs[row_count:row_count + column_count]
    refs = refs[row_count + column_count:]
    if keep:
        kept, out, left, right, own_rows, column_vector, partial, sums, own, sem = refs
    else:
        kept = None
        left, right, out, own_rows, column_vector, partial, sums, own, sem = refs
    rows = left.shape[1]
    halves = rows // LANES
    lines = partial.shape[0]

    def prepare_row(block, i, source):
        left[source] = left_operand(block[i, 0:proj, :], scale)
        for half in range(halves):
            own_rows[pl.ds(source * halves + half, 1), :] = block[
                i, proj:proj + 1, half * LANES:(half + 1) * LANES]

    def prepare_column(block, i, source):
        right[source] = right_operand(block[i, 0:proj, :], scale)
        for half in range(halves):
            column_vector[pl.ds(source * halves + half, 1), :] = block[
                i, proj:proj + 1, half * LANES:(half + 1) * LANES]

    if row_count > 1:
        copy_own = pltpu.make_async_copy(row_blocks[0], own, sem)
        copy_own.start()
        row_blocks, column_blocks = (own, *row_blocks[1:]), (own, *column_blocks)
    row_list, column_list = row_sources(row_blocks, narrow), column_sources(column_blocks, wide)
    for item in column_list[1:]:
        prepare_column(*item)
    for item in row_list[1:]:
        prepare_row(*item)
    if row_count > 1:
        copy_own.wait()
    prepare_column(*column_list[0])
    prepare_row(*row_list[0])
    make_rows(left, right, kept, lambda c, half: column_vector[pl.ds(c * halves + half, 1), :], sums)
    write_rows(sums, partial)
    z, y, x, core = place()
    mine = (y * (narrow // 2) + x) * halves
    pieces = [partial[line:line + 1, :] for line in range(lines)]
    pieces += [own_rows[pl.ds(mine + half, 1), :] for half in range(halves)]
    block = jnp.concatenate(pieces, axis=1)

    def copy(i, _):
        out[i] = block
        return 0

    lax.fori_loop(0, out.shape[0], copy, 0, unroll=8)


def second_kernel(wide, narrow, keep, *refs):
    arrived, out, step_scalars, direction, images, targets, partial, sums = refs[:1] + refs[-7:]
    lines = partial.shape[0]
    halves = lines // narrow
    across = narrow // 2
    group = [(y, x) for y in range(2) for x in range(across)]

    def unpack(z, _):
        for core in range(2):
            members = [device_at(z, y, x, core, narrow) for y, x in group]
            total = arrived[members[0]]
            for member in members[1:]:
                total = total + arrived[member]
            for r, member in enumerate(members):
                for half in range(halves):
                    start = arrived[member, :, (lines + half) * LANES:(lines + half + 1) * LANES]
                    line = r * halves + half
                    spot = pl.ds(member * halves + half, 1)
                    targets[spot, :] = start
                    images[spot, :] = total[:, line * LANES:(line + 1) * LANES] + noise_var * start
        return 0

    lax.fori_loop(0, wide // 2, unpack, 0, unroll=4)
    start, first = targets[...], images[...]
    norm = total_sum(start * start)
    alpha = norm / total_sum(start * first)
    residual = start - alpha * first
    norm_next = total_sum(residual * residual)
    beta = norm_next / norm
    whole = residual + beta * start
    direction[...] = whole
    z, y, x, core = place()

    def read_vector(c, half):
        return direction[pl.ds(device_at(c // 2, y, x, c % 2, narrow) * halves + half, 1), :]

    if keep:
        use_rows(refs[1], read_vector, sums)
    else:
        make_rows(refs[1], refs[2], None, read_vector, sums)
    write_rows(sums, partial)
    share = jnp.zeros((1, LANES), f32)
    for r, (row_y, row_x) in enumerate(group):
        for half in range(halves):
            spot = pl.ds(device_at(z, row_y, row_x, core, narrow) * halves + half, 1)
            line = r * halves + half
            share = share + direction[spot, :] * partial[line:line + 1, :]
    blocks = [
        jnp.concatenate([partial[r * halves + half:r * halves + half + 1, :]
                         for half in range(halves)] + [share], axis=1)
        for r in range(narrow)]

    def copy(to_z, _):
        for r, (to_y, to_x) in enumerate(group):
            for to_core in range(2):
                out[device_at(to_z, to_y, to_x, to_core, narrow)] = blocks[r]
        return 0

    lax.fori_loop(0, wide // 2, copy, 0, unroll=4)
    lane = lax.broadcasted_iota(jnp.int32, (1, LANES), 1)
    noise = noise_var * total_sum(whole * whole)
    step_scalars[0:1, :] = jnp.where(lane == 0, alpha, jnp.where(
        lane == 1, norm_next, jnp.where(lane == 2, beta, noise)))
    for half in range(halves):
        spot = pl.ds(device_at(z, y, x, core, narrow) * halves + half, 1)
        step_scalars[1 + half:2 + half, :] = images[spot, :]


def last_kernel(narrow, arrived, step_scalars, start_ref, solution_out, residual_out):
    alpha = step_scalars[0:1, 0:1]
    norm = step_scalars[0:1, 1:2]
    beta = step_scalars[0:1, 2:3]
    noise = step_scalars[0:1, 3:4]
    halves = start_ref.shape[0]

    def add(i, total):
        return total + arrived[i, :, halves * LANES:(halves + 1) * LANES]

    share = lax.fori_loop(0, arrived.shape[0], add, jnp.zeros((1, LANES), f32), unroll=8)
    alpha_next = norm / (total_sum(share) + noise)
    z, _, _, core = place()
    product = jnp.zeros((1, (halves + 1) * LANES), f32)
    for y in range(2):
        for x in range(narrow // 2):
            product = product + arrived[device_at(z, y, x, core, narrow)]
    for half in range(halves):
        begin = start_ref[half:half + 1, :]
        residual = begin - alpha * step_scalars[1 + half:2 + half, :]
        direction = residual + beta * begin
        image = product[:, half * LANES:(half + 1) * LANES] + noise_var * direction
        solution_out[half:half + 1, :] = alpha * begin + alpha_next * direction
        residual_out[half:half + 1, :] = residual - alpha_next * image


def call(kernel, out_shape, *args, scratch=(), vmem=VMEM_BYTES, **options):
    return pl.pallas_call(
        kernel,
        out_shape=out_shape,
        scratch_shapes=list(scratch),
        compiler_params=pltpu.CompilerParams(vmem_limit_bytes=vmem),
        **{name: value for name, value in options.items() if value is not None},
    )(*args)


def to_all(blocks, axes):
    return lax.all_to_all(blocks, axes, split_axis=0, concat_axis=0, tiled=True)


def first_round(own, wide, narrow):
    axes = (WIDE, NARROW)
    depth, across = wide // 2, narrow // 2
    if depth > DIRECT or depth & (depth - 1) or across & (across - 1):
        every = lax.all_gather(own, axes, axis=0, tiled=True)
        every = every.reshape(depth, 2, across, 2, *own.shape[1:])
        z, y, x, core = place()
        rows = lax.dynamic_index_in_dim(every, z, 0, keepdims=False)
        rows = lax.dynamic_index_in_dim(rows, core, 2, keepdims=False)
        columns = lax.dynamic_index_in_dim(every, y, 1, keepdims=False)
        columns = lax.dynamic_index_in_dim(columns, x, 1, keepdims=False)
        return [rows.reshape(narrow, *own.shape[1:])], [columns.reshape(wide, *own.shape[1:])]

    def swap(value, z_flip, row_flip, core_flip):
        pairs = []
        for z in range(depth):
            for r in range(narrow):
                for core in range(2):
                    other = r ^ row_flip
                    pairs.append((
                        device_at(z, r // across, r % across, core, narrow),
                        device_at(z ^ z_flip, other // across, other % across, core ^ core_flip, narrow)))
        return lax.ppermute(value, axes, pairs)

    rows = [swap(own, 0, k, 0) for k in range(1, narrow)]
    columns = [swap(own, k, 0, 0) for k in range(1, depth)]
    columns += [swap(column, 0, 0, 1) for column in [own] + columns]
    return [own] + rows, columns


def on_device(wide, narrow, features, projection, targets):
    rows, proj = features.shape[0], projection.shape[1]
    halves = rows // LANES
    lines = narrow * halves
    devices = wide * narrow
    scale = -2.0 / proj * math.log2(math.e)
    depth = 6 * proj + 16
    keep = 4 * devices * rows * rows <= KEEP_BYTES
    axes = (WIDE, NARROW)

    def shape(*dims, dtype=f32):
        return jax.ShapeDtypeStruct(dims, dtype)

    def scratch(*dims, dtype=f32):
        return pltpu.VMEM(dims, dtype)

    feat = features.shape[1]
    own = call(
        project_kernel, shape(1, proj + 8, rows), features, projection.T, targets.reshape(1, rows),
        in_specs=[pl.BlockSpec(memory_space=pl.ANY)] * 3, vmem=WHOLE_VMEM_BYTES,
        scratch=[scratch(CHUNKS, rows, feat // CHUNKS, dtype=bf16), scratch(proj, feat, dtype=bf16),
                 scratch(1, rows), pltpu.SemaphoreType.DMA((CHUNKS + 2,))])
    row_blocks, column_blocks = first_round(own, wide, narrow)
    left = (narrow, rows, depth)
    right = (wide, depth, rows)
    block_out = shape(devices, 1, (lines + halves) * LANES)
    sums = scratch(narrow, rows, LANES)
    work = [scratch(lines, LANES), scratch(wide * halves, LANES), scratch(lines, LANES), sums,
            scratch(1, proj + 8, rows), pltpu.SemaphoreType.DMA]
    specs = None
    if len(row_blocks) > 1:
        specs = [pl.BlockSpec(memory_space=pl.ANY)]
        specs += [pl.BlockSpec(memory_space=pltpu.VMEM)] * (len(row_blocks) + len(column_blocks) - 1)
    first = functools.partial(
        first_kernel, proj, scale, wide, narrow, keep, len(row_blocks), len(column_blocks))
    if keep:
        *block, out = call(
            first, (shape(narrow, wide, rows, rows), block_out), *row_blocks, *column_blocks,
            scratch=[scratch(*left, dtype=bf16), scratch(*right, dtype=bf16)] + work, in_specs=specs)
    else:
        *block, out = call(
            first, (shape(*left, dtype=bf16), shape(*right, dtype=bf16), block_out),
            *row_blocks, *column_blocks, scratch=work, in_specs=specs)
    out, step_scalars = call(
        functools.partial(second_kernel, wide, narrow, keep),
        (shape(devices, 1, (halves + 1) * LANES), shape(1 + halves, LANES)),
        to_all(out, axes), *block,
        scratch=[scratch(devices * halves, LANES)] * 3 + [scratch(lines, LANES), sums])
    answer, residual = call(
        functools.partial(last_kernel, narrow), (shape(halves, LANES), shape(halves, LANES)),
        to_all(out, axes), step_scalars, targets.reshape(halves, LANES))
    return answer.reshape(rows), residual.reshape(rows)


def solution(mesh):
    axes = (WIDE, NARROW)
    in_specs = (P(axes, None), P(), P(axes))
    return jax.shard_map(
        functools.partial(on_device, mesh.shape[WIDE], mesh.shape[NARROW]), mesh=mesh,
        in_specs=in_specs, out_specs=(P(axes), P(axes)), check_vma=False,
    )
```

```python
import functools
import math

import jax
import jax.numpy as jnp
from jax import lax
from jax.experimental import pallas as pl
from jax.experimental.pallas import tpu as pltpu
from jax.sharding import PartitionSpec as P

noise_var = 0.5
LANES = 128
CHUNKS = 4
DIRECT = 8
KEEP_BYTES = 8 * 2**20
VMEM_BYTES = 32 * 2**20
WHOLE_VMEM_BYTES = (53 * 1024 + 870) * 2**10
Z, Y, X, CORE = "z", "y", "x", "core"
ALL = (Z, Y, X, CORE)
highest = lax.Precision.HIGHEST
f32 = jnp.float32
bf16 = jnp.bfloat16


def split3(values):
    high = values.astype(bf16)
    rest = values - high.astype(f32)
    mid = rest.astype(bf16)
    low = (rest - mid.astype(f32)).astype(bf16)
    return high, mid, low


def exponent_rows(first, second):
    width = (first if not isinstance(first, float) else second).shape[1]
    row = lax.broadcasted_iota(jnp.int32, (16, width), 0)
    out = jnp.zeros((16, width), f32)
    for base, value in ((0, first), (3, second)):
        parts = (1.0, 1.0, 1.0) if isinstance(value, float) else [p.astype(f32) for p in split3(value)]
        for k, part in enumerate(parts):
            out = jnp.where(row == base + k, part, out)
    return out.astype(bf16)


def right_operand(latent, scale):
    square = jnp.sum(latent * latent, axis=0, keepdims=True) * scale
    h, m, l = split3(latent)
    return jnp.concatenate([h, m, l, h, m, h, exponent_rows(square, 1.0)], axis=0)


def left_operand(latent, scale):
    square = jnp.sum(latent * latent, axis=0, keepdims=True) * scale
    h, m, l = split3(latent * (-2.0 * scale))
    stacked = jnp.concatenate([h, h, h, m, m, l, exponent_rows(1.0, square)], axis=0)
    return stacked.astype(f32).T.astype(bf16)


def place():
    return tuple(lax.axis_index(name) for name in ALL)


def device_at(z, y, x, core, narrow):
    return ((z * 2 + y) * (narrow // 2) + x) * 2 + core


def row_sources(blocks, narrow):
    if len(blocks) == 1:
        return [(blocks[0], i, i) for i in range(narrow)]
    z, y, x, core = place()
    me = y * (narrow // 2) + x
    return [(b, 0, jnp.bitwise_xor(me, k)) for k, b in enumerate(blocks)]


def column_sources(blocks, wide):
    if len(blocks) == 1:
        return [(blocks[0], i, i) for i in range(wide)]
    z, y, x, core = place()
    depth = wide // 2
    spots = [(b, 0) for b in blocks[:-1]] + [(blocks[-1], i) for i in range(depth)]
    return [(b, i, jnp.bitwise_xor(z, k % depth) * 2 + jnp.bitwise_xor(core, k // depth))
            for k, (b, i) in enumerate(spots)]


def total_sum(values):
    return jnp.sum(jnp.sum(values, axis=0, keepdims=True), axis=1, keepdims=True)


def lane_sums(values):
    parts = jnp.concatenate(split3(values), axis=1)
    ones = jnp.ones((16, parts.shape[1]), bf16)
    return lax.dot_general(ones, parts, (((1,), (1,)), ((), ())),
                           preferred_element_type=f32)[0:1, :]


def make_rows(left, right, kept, read_vector, sums):
    groups, rows, _ = left.shape
    columns = right.shape[0]
    halves = rows // LANES

    def one_group(g, _):
        left_group = left[g]

        def one_column(c, acc):
            exponent = jnp.dot(left_group, right[c], preferred_element_type=f32)
            tile = jnp.exp2(exponent)
            if kept is not None:
                kept[g, c] = tile
            for half in range(halves):
                acc = acc + tile[:, half * LANES:(half + 1) * LANES] * read_vector(c, half)
            return acc

        sums[g] = lax.fori_loop(0, columns, one_column, jnp.zeros((rows, LANES), f32), unroll=8)
        return 0

    lax.fori_loop(0, groups, one_group, 0)


def use_rows(kept, read_vector, sums):
    groups, columns, rows, _ = kept.shape
    halves = rows // LANES

    def one_group(g, _):
        def one_column(c, acc):
            for half in range(halves):
                acc = acc + kept[g, c, :, half * LANES:(half + 1) * LANES] * read_vector(c, half)
            return acc

        sums[g] = lax.fori_loop(0, columns, one_column, jnp.zeros((rows, LANES), f32), unroll=8)
        return 0

    lax.fori_loop(0, groups, one_group, 0)


def write_rows(sums, out):
    groups, rows, _ = sums.shape
    total = lane_sums(sums[...].reshape(groups * rows, LANES))
    for line in range(out.shape[0]):
        out[line:line + 1, :] = total[:, line * LANES:(line + 1) * LANES]


def project_kernel(features, projection_t, targets, out, feature_buf, projection_buf, target_buf, sems):
    proj = projection_t.shape[0]
    chunks, _, width = feature_buf.shape
    copies = [pltpu.make_async_copy(projection_t, projection_buf, sems.at[0])]
    copies += [
        pltpu.make_async_copy(features.at[:, pl.ds(i * width, width)], feature_buf.at[i], sems.at[i + 1])
        for i in range(chunks)]
    copies += [pltpu.make_async_copy(targets, target_buf, sems.at[chunks + 1])]
    for copy in copies:
        copy.start()
    copies[0].wait()
    latent = jnp.zeros((proj, features.shape[0]), f32)
    for i in range(chunks):
        copies[i + 1].wait()
        latent = latent + lax.dot_general(
            projection_buf[:, i * width:(i + 1) * width], feature_buf[i],
            (((1,), (1,)), ((), ())), preferred_element_type=f32)
    copies[-1].wait()
    out[0, 0:proj, :] = latent
    out[0, proj:proj + 8, :] = jnp.broadcast_to(target_buf[...], (8, out.shape[2]))


def first_kernel(proj, scale, wide, narrow, keep, row_count, column_count, *refs):
    row_blocks, column_blocks = refs[:row_count], refs[row_count:row_count + column_count]
    refs = refs[row_count + column_count:]
    if keep:
        kept, out, left, right, own_rows, column_vector, partial, sums, own, sem = refs
    else:
        kept = None
        left, right, out, own_rows, column_vector, partial, sums, own, sem = refs
    rows = left.shape[1]
    halves = rows // LANES
    lines = partial.shape[0]

    def prepare_row(block, i, source):
        left[source] = left_operand(block[i, 0:proj, :], scale)
        for half in range(halves):
            own_rows[pl.ds(source * halves + half, 1), :] = block[
                i, proj:proj + 1, half * LANES:(half + 1) * LANES]

    def prepare_column(block, i, source):
        right[source] = right_operand(block[i, 0:proj, :], scale)
        for half in range(halves):
            column_vector[pl.ds(source * halves + half, 1), :] = block[
                i, proj:proj + 1, half * LANES:(half + 1) * LANES]

    if row_count > 1:
        copy_own = pltpu.make_async_copy(row_blocks[0], own, sem)
        copy_own.start()
        row_blocks, column_blocks = (own, *row_blocks[1:]), (own, *column_blocks)
    row_list, column_list = row_sources(row_blocks, narrow), column_sources(column_blocks, wide)
    for item in column_list[1:]:
        prepare_column(*item)
    for item in row_list[1:]:
        prepare_row(*item)
    if row_count > 1:
        copy_own.wait()
    prepare_column(*column_list[0])
    prepare_row(*row_list[0])
    make_rows(left, right, kept, lambda c, half: column_vector[pl.ds(c * halves + half, 1), :], sums)
    write_rows(sums, partial)
    z, y, x, core = place()
    mine = (y * (narrow // 2) + x) * halves
    pieces = [partial[line:line + 1, :] for line in range(lines)]
    pieces += [own_rows[pl.ds(mine + half, 1), :] for half in range(halves)]
    block = jnp.concatenate(pieces, axis=1)

    def copy(i, _):
        out[i] = block
        return 0

    lax.fori_loop(0, out.shape[0], copy, 0, unroll=8)


def second_kernel(wide, narrow, keep, *refs):
    arrived, share_out, rows_out, step_scalars, direction, images, targets, partial, sums = (
        refs[:1] + refs[-8:])
    lines = partial.shape[0]
    halves = lines // narrow
    across = narrow // 2
    group = [(y, x) for y in range(2) for x in range(across)]

    def unpack(z, _):
        for core in range(2):
            members = [device_at(z, y, x, core, narrow) for y, x in group]
            total = arrived[members[0]]
            for member in members[1:]:
                total = total + arrived[member]
            for r, member in enumerate(members):
                for half in range(halves):
                    start = arrived[member, :, (lines + half) * LANES:(lines + half + 1) * LANES]
                    line = r * halves + half
                    spot = pl.ds(member * halves + half, 1)
                    targets[spot, :] = start
                    images[spot, :] = total[:, line * LANES:(line + 1) * LANES] + noise_var * start
        return 0

    lax.fori_loop(0, wide // 2, unpack, 0, unroll=4)
    start, first = targets[...], images[...]
    norm = total_sum(start * start)
    alpha = norm / total_sum(start * first)
    residual = start - alpha * first
    norm_next = total_sum(residual * residual)
    beta = norm_next / norm
    whole = residual + beta * start
    direction[...] = whole
    z, y, x, core = place()

    def read_vector(c, half):
        return direction[pl.ds(device_at(c // 2, y, x, c % 2, narrow) * halves + half, 1), :]

    if keep:
        use_rows(refs[1], read_vector, sums)
    else:
        make_rows(refs[1], refs[2], None, read_vector, sums)
    write_rows(sums, partial)
    share = jnp.zeros((1, LANES), f32)
    for r, (row_y, row_x) in enumerate(group):
        for half in range(halves):
            spot = pl.ds(device_at(z, row_y, row_x, core, narrow) * halves + half, 1)
            line = r * halves + half
            share = share + direction[spot, :] * partial[line:line + 1, :]
    share_out[0] = share
    rows_out[...] = partial[...]
    lane = lax.broadcasted_iota(jnp.int32, (1, LANES), 1)
    noise = noise_var * total_sum(whole * whole)
    step_scalars[0:1, :] = jnp.where(lane == 0, alpha, jnp.where(
        lane == 1, norm_next, jnp.where(lane == 2, beta, noise)))
    for half in range(halves):
        spot = pl.ds(device_at(z, y, x, core, narrow) * halves + half, 1)
        step_scalars[1 + half:2 + half, :] = images[spot, :]


def block_kernel(share, other_share, rows, out):
    halves = out.shape[2] // LANES - 1
    groups = rows.shape[0] // halves
    both = share[0] + other_share[0]
    blocks = [
        jnp.concatenate([rows[r * halves + half:r * halves + half + 1, :]
                         for half in range(halves)] + [both], axis=1)
        for r in range(groups)]

    def copy(z, _):
        for r in range(groups):
            out[z * groups + r] = blocks[r]
        return 0

    lax.fori_loop(0, out.shape[0] // groups, copy, 0, unroll=4)


def last_kernel(groups, arrived, step_scalars, start_ref, solution_out, residual_out):
    alpha = step_scalars[0:1, 0:1]
    norm = step_scalars[0:1, 1:2]
    beta = step_scalars[0:1, 2:3]
    noise = step_scalars[0:1, 3:4]
    halves = start_ref.shape[0]

    def add(i, total):
        return total + arrived[i, :, halves * LANES:(halves + 1) * LANES]

    share = lax.fori_loop(0, arrived.shape[0], add, jnp.zeros((1, LANES), f32), unroll=8)
    alpha_next = norm / (total_sum(share) + noise)
    group = lax.axis_index(Z) * groups
    product = arrived[group]
    for r in range(1, groups):
        product = product + arrived[group + r]
    for half in range(halves):
        begin = start_ref[half:half + 1, :]
        residual = begin - alpha * step_scalars[1 + half:2 + half, :]
        direction = residual + beta * begin
        image = product[:, half * LANES:(half + 1) * LANES] + noise_var * direction
        solution_out[half:half + 1, :] = alpha * begin + alpha_next * direction
        residual_out[half:half + 1, :] = residual - alpha_next * image


def join_kernel(*refs):
    out = refs[-1]
    for i in range(out.shape[0]):
        out[i] = refs[i][0]


def call(kernel, out_shape, *args, scratch=(), vmem=VMEM_BYTES, **options):
    return pl.pallas_call(
        kernel,
        out_shape=out_shape,
        scratch_shapes=list(scratch),
        compiler_params=pltpu.CompilerParams(vmem_limit_bytes=vmem),
        **{name: value for name, value in options.items() if value is not None},
    )(*args)


def to_all(blocks, axes):
    return lax.all_to_all(blocks, axes, split_axis=0, concat_axis=0, tiled=True)


def swap_cores(value):
    return lax.ppermute(value, CORE, [(0, 1), (1, 0)])


def first_round(own, wide, narrow):
    depth, across = wide // 2, narrow // 2
    if depth > DIRECT or depth & (depth - 1) or across & (across - 1):
        every = lax.all_gather(own, ALL, axis=0, tiled=True)
        every = every.reshape(depth, 2, across, 2, *own.shape[1:])
        z, y, x, core = place()
        rows = lax.dynamic_index_in_dim(every, z, 0, keepdims=False)
        rows = lax.dynamic_index_in_dim(rows, core, 2, keepdims=False)
        columns = lax.dynamic_index_in_dim(every, y, 1, keepdims=False)
        columns = lax.dynamic_index_in_dim(columns, x, 1, keepdims=False)
        return [rows.reshape(narrow, *own.shape[1:])], [columns.reshape(wide, *own.shape[1:])]

    def passed(axes, size, flip):
        return lax.ppermute(own, axes, [(i, i ^ flip) for i in range(size)])

    rows = [passed((Y, X), narrow, k) for k in range(1, narrow)]
    columns = [passed(Z, depth, k) for k in range(1, depth)]
    before = rows[:2]
    specs = [pl.BlockSpec(memory_space=pltpu.VMEM)] * depth
    specs += [pl.BlockSpec(memory_space=pl.ANY)] * len(before)
    joined = call(join_kernel, jax.ShapeDtypeStruct((depth, *own.shape[1:]), f32),
                  own, *columns, *before, in_specs=specs)
    return [own] + rows, columns + [swap_cores(joined)]


def on_device(wide, narrow, features, projection, targets):
    rows, proj = features.shape[0], projection.shape[1]
    halves = rows // LANES
    lines = narrow * halves
    devices = wide * narrow
    scale = -2.0 / proj * math.log2(math.e)
    depth = 6 * proj + 16
    keep = 4 * devices * rows * rows <= KEEP_BYTES

    def shape(*dims, dtype=f32):
        return jax.ShapeDtypeStruct(dims, dtype)

    def scratch(*dims, dtype=f32):
        return pltpu.VMEM(dims, dtype)

    feat = features.shape[1]
    own = call(
        project_kernel, shape(1, proj + 8, rows), features, projection.T, targets.reshape(1, rows),
        in_specs=[pl.BlockSpec(memory_space=pl.ANY)] * 3, vmem=WHOLE_VMEM_BYTES,
        scratch=[scratch(CHUNKS, rows, feat // CHUNKS, dtype=bf16), scratch(proj, feat, dtype=bf16),
                 scratch(1, rows), pltpu.SemaphoreType.DMA((CHUNKS + 2,))])
    row_blocks, column_blocks = first_round(own, wide, narrow)
    left = (narrow, rows, depth)
    right = (wide, depth, rows)
    block_out = shape(devices, 1, (lines + halves) * LANES)
    sums = scratch(narrow, rows, LANES)
    work = [scratch(lines, LANES), scratch(wide * halves, LANES), scratch(lines, LANES), sums,
            scratch(1, proj + 8, rows), pltpu.SemaphoreType.DMA]
    specs = None
    if len(row_blocks) > 1:
        specs = [pl.BlockSpec(memory_space=pl.ANY)]
        specs += [pl.BlockSpec(memory_space=pltpu.VMEM)] * (len(row_blocks) + len(column_blocks) - 1)
    first = functools.partial(
        first_kernel, proj, scale, wide, narrow, keep, len(row_blocks), len(column_blocks))
    if keep:
        *block, out = call(
            first, (shape(narrow, wide, rows, rows), block_out), *row_blocks, *column_blocks,
            scratch=[scratch(*left, dtype=bf16), scratch(*right, dtype=bf16)] + work, in_specs=specs)
    else:
        *block, out = call(
            first, (shape(*left, dtype=bf16), shape(*right, dtype=bf16), block_out),
            *row_blocks, *column_blocks, scratch=work, in_specs=specs)
    share, product, step_scalars = call(
        functools.partial(second_kernel, wide, narrow, keep),
        (shape(1, 1, LANES), shape(lines, LANES), shape(1 + halves, LANES)),
        to_all(out, ALL), *block,
        scratch=[scratch(devices * halves, LANES)] * 3 + [scratch(lines, LANES), sums])
    out = call(
        block_kernel, shape(devices // 2, 1, (halves + 1) * LANES), share, swap_cores(share), product)
    answer, residual = call(
        functools.partial(last_kernel, narrow), (shape(halves, LANES), shape(halves, LANES)),
        to_all(out, ALL[:-1]), step_scalars, targets.reshape(halves, LANES))
    return answer.reshape(rows), residual.reshape(rows)


def solution(mesh):
    wide, narrow = mesh.shape["wide"], mesh.shape["narrow"]
    split = jax.sharding.Mesh(mesh.devices.reshape(wide // 2, 2, narrow // 2, 2), ALL)
    in_specs = (P(ALL, None), P(), P(ALL))
    return jax.shard_map(
        functools.partial(on_device, wide, narrow), mesh=split,
        in_specs=in_specs, out_specs=(P(ALL), P(ALL)), check_vma=False,
    )
```

```python
import functools
import math

import jax
import jax.numpy as jnp
from jax import lax
from jax.experimental import pallas as pl
from jax.experimental.pallas import tpu as pltpu
from jax.sharding import PartitionSpec as P

noise_var = 0.5
LANES = 128
CHUNKS = 4
DIRECT = 8
KEEP_BYTES = 8 * 2**20
VMEM_BYTES = 32 * 2**20
WHOLE_VMEM_BYTES = (53 * 1024 + 870) * 2**10
Z, Y, X, CORE = "z", "y", "x", "core"
ALL = (Z, Y, X, CORE)
highest = lax.Precision.HIGHEST
f32 = jnp.float32
bf16 = jnp.bfloat16


def split3(values):
    high = values.astype(bf16)
    rest = values - high.astype(f32)
    mid = rest.astype(bf16)
    low = (rest - mid.astype(f32)).astype(bf16)
    return high, mid, low


def exponent_rows(first, second):
    width = (first if not isinstance(first, float) else second).shape[1]
    row = lax.broadcasted_iota(jnp.int32, (16, width), 0)
    out = jnp.zeros((16, width), f32)
    for base, value in ((0, first), (3, second)):
        parts = (1.0, 1.0, 1.0) if isinstance(value, float) else [p.astype(f32) for p in split3(value)]
        for k, part in enumerate(parts):
            out = jnp.where(row == base + k, part, out)
    return out.astype(bf16)


def right_operand(latent, scale):
    square = jnp.sum(latent * latent, axis=0, keepdims=True) * scale
    h, m, l = split3(latent)
    return jnp.concatenate([h, m, l, h, m, h, exponent_rows(square, 1.0)], axis=0)


def left_operand(latent, scale):
    square = jnp.sum(latent * latent, axis=0, keepdims=True) * scale
    h, m, l = split3(latent * (-2.0 * scale))
    stacked = jnp.concatenate([h, h, h, m, m, l, exponent_rows(1.0, square)], axis=0)
    return stacked.astype(f32).T.astype(bf16)


def place():
    return tuple(lax.axis_index(name) for name in ALL)


def device_at(z, y, x, core, narrow):
    return ((z * 2 + y) * (narrow // 2) + x) * 2 + core


def row_sources(blocks, narrow):
    if len(blocks) == 1:
        return [(blocks[0], i, i) for i in range(narrow)]
    z, y, x, core = place()
    me = y * (narrow // 2) + x
    return [(b, 0, jnp.bitwise_xor(me, k)) for k, b in enumerate(blocks)]


def column_sources(blocks, wide):
    if len(blocks) == 1:
        return [(blocks[0], i, i) for i in range(wide)]
    z, y, x, core = place()
    depth = wide // 2
    return [(b, 0, jnp.bitwise_xor(z, k % depth) * 2 + jnp.bitwise_xor(core, k // depth))
            for k, b in enumerate(blocks)]


def total_sum(values):
    return jnp.sum(jnp.sum(values, axis=0, keepdims=True), axis=1, keepdims=True)


def lane_sums(values):
    parts = jnp.concatenate(split3(values), axis=1)
    ones = jnp.ones((16, parts.shape[1]), bf16)
    return lax.dot_general(ones, parts, (((1,), (1,)), ((), ())),
                           preferred_element_type=f32)[0:1, :]


def make_rows(left, right, kept, read_vector, sums):
    groups, rows, _ = left.shape
    columns = right.shape[0]
    halves = rows // LANES

    def one_group(g, _):
        left_group = left[g]

        def one_column(c, acc):
            exponent = jnp.dot(left_group, right[c], preferred_element_type=f32)
            tile = jnp.exp2(exponent)
            if kept is not None:
                kept[g, c] = tile
            for half in range(halves):
                acc = acc + tile[:, half * LANES:(half + 1) * LANES] * read_vector(c, half)
            return acc

        sums[g] = lax.fori_loop(0, columns, one_column, jnp.zeros((rows, LANES), f32), unroll=8)
        return 0

    lax.fori_loop(0, groups, one_group, 0)


def use_rows(kept, read_vector, sums):
    groups, columns, rows, _ = kept.shape
    halves = rows // LANES

    def one_group(g, _):
        def one_column(c, acc):
            for half in range(halves):
                acc = acc + kept[g, c, :, half * LANES:(half + 1) * LANES] * read_vector(c, half)
            return acc

        sums[g] = lax.fori_loop(0, columns, one_column, jnp.zeros((rows, LANES), f32), unroll=8)
        return 0

    lax.fori_loop(0, groups, one_group, 0)


def write_rows(sums, out):
    groups, rows, _ = sums.shape
    total = lane_sums(sums[...].reshape(groups * rows, LANES))
    for line in range(out.shape[0]):
        out[line:line + 1, :] = total[:, line * LANES:(line + 1) * LANES]


def project_kernel(features, projection_t, targets, out, feature_buf, projection_buf, target_buf, sems):
    proj = projection_t.shape[0]
    chunks, _, width = feature_buf.shape
    copies = [pltpu.make_async_copy(projection_t, projection_buf, sems.at[0])]
    copies += [
        pltpu.make_async_copy(features.at[:, pl.ds(i * width, width)], feature_buf.at[i], sems.at[i + 1])
        for i in range(chunks)]
    copies += [pltpu.make_async_copy(targets, target_buf, sems.at[chunks + 1])]
    for copy in copies:
        copy.start()
    copies[0].wait()
    latent = jnp.zeros((proj, features.shape[0]), f32)
    for i in range(chunks):
        copies[i + 1].wait()
        latent = latent + lax.dot_general(
            projection_buf[:, i * width:(i + 1) * width], feature_buf[i],
            (((1,), (1,)), ((), ())), preferred_element_type=f32)
    copies[-1].wait()
    out[0, 0:proj, :] = latent
    out[0, proj:proj + 8, :] = jnp.broadcast_to(target_buf[...], (8, out.shape[2]))


def first_kernel(proj, scale, wide, narrow, keep, row_count, column_count, *refs):
    row_blocks, column_blocks = refs[:row_count], refs[row_count:row_count + column_count]
    refs = refs[row_count + column_count:]
    if keep:
        kept, out, left, right, own_rows, column_vector, partial, sums, own, sem = refs
    else:
        kept = None
        left, right, out, own_rows, column_vector, partial, sums, own, sem = refs
    rows = left.shape[1]
    halves = rows // LANES
    lines = partial.shape[0]

    def prepare_row(block, i, source):
        left[source] = left_operand(block[i, 0:proj, :], scale)
        for half in range(halves):
            own_rows[pl.ds(source * halves + half, 1), :] = block[
                i, proj:proj + 1, half * LANES:(half + 1) * LANES]

    def prepare_column(block, i, source):
        right[source] = right_operand(block[i, 0:proj, :], scale)
        for half in range(halves):
            column_vector[pl.ds(source * halves + half, 1), :] = block[
                i, proj:proj + 1, half * LANES:(half + 1) * LANES]

    if row_count > 1:
        copy_own = pltpu.make_async_copy(row_blocks[0], own, sem)
        copy_own.start()
        row_blocks, column_blocks = (own, *row_blocks[1:]), (own, *column_blocks)
    row_list, column_list = row_sources(row_blocks, narrow), column_sources(column_blocks, wide)
    for item in column_list[1:]:
        prepare_column(*item)
    for item in row_list[1:]:
        prepare_row(*item)
    if row_count > 1:
        copy_own.wait()
    prepare_column(*column_list[0])
    prepare_row(*row_list[0])
    make_rows(left, right, kept, lambda c, half: column_vector[pl.ds(c * halves + half, 1), :], sums)
    write_rows(sums, partial)
    out[0, 0:lines, :] = partial[...]
    out[0, lines:, :] = own_rows[...]


def image_kernel(narrow, *refs):
    blocks, out, held = refs[:-2], refs[-2], refs[-1]
    lines = out.shape[1] // 2
    for block, i, source in row_sources(blocks, narrow):
        held[source] = block[i, 0:lines, :]
    start = blocks[0][0, lines:, :]
    total = noise_var * start
    for r in range(narrow):
        total = total + held[r]
    out[0, 0:lines, :] = total
    out[0, lines:, :] = start


def second_kernel(wide, narrow, keep, column_count, *refs):
    blocks, refs = refs[:column_count], refs[column_count:]
    out, step_scalars, direction, images, targets, partial, sums = refs[-7:]
    lines = partial.shape[0]
    halves = lines // narrow
    group = [(y, x) for y in range(2) for x in range(narrow // 2)]
    for block, i, source in column_sources(blocks, wide):
        for r, (row_y, row_x) in enumerate(group):
            for half in range(halves):
                line = r * halves + half
                spot = pl.ds(device_at(source // 2, row_y, row_x, source % 2, narrow) * halves + half, 1)
                images[spot, :] = block[i, line:line + 1, :]
                targets[spot, :] = block[i, lines + line:lines + line + 1, :]
    start, first = targets[...], images[...]
    norm = total_sum(start * start)
    alpha = norm / total_sum(start * first)
    residual = start - alpha * first
    norm_next = total_sum(residual * residual)
    beta = norm_next / norm
    whole = residual + beta * start
    direction[...] = whole
    z, y, x, core = place()

    def read_vector(c, half):
        return direction[pl.ds(device_at(c // 2, y, x, c % 2, narrow) * halves + half, 1), :]

    if keep:
        use_rows(refs[0], read_vector, sums)
    else:
        make_rows(refs[0], refs[1], None, read_vector, sums)
    write_rows(sums, partial)
    share = jnp.zeros((1, LANES), f32)
    for r, (row_y, row_x) in enumerate(group):
        for half in range(halves):
            spot = pl.ds(device_at(z, row_y, row_x, core, narrow) * halves + half, 1)
            line = r * halves + half
            share = share + direction[spot, :] * partial[line:line + 1, :]
    blocks = [
        jnp.concatenate([partial[r * halves + half:r * halves + half + 1, :]
                         for half in range(halves)] + [share], axis=1)
        for r in range(narrow)]

    def copy(to_z, _):
        for r, (to_y, to_x) in enumerate(group):
            for to_core in range(2):
                out[device_at(to_z, to_y, to_x, to_core, narrow)] = blocks[r]
        return 0

    lax.fori_loop(0, wide // 2, copy, 0, unroll=4)
    lane = lax.broadcasted_iota(jnp.int32, (1, LANES), 1)
    noise = noise_var * total_sum(whole * whole)
    step_scalars[0:1, :] = jnp.where(lane == 0, alpha, jnp.where(
        lane == 1, norm_next, jnp.where(lane == 2, beta, noise)))
    for half in range(halves):
        spot = pl.ds(device_at(z, y, x, core, narrow) * halves + half, 1)
        step_scalars[1 + half:2 + half, :] = images[spot, :]


def last_kernel(narrow, arrived, step_scalars, start_ref, solution_out, residual_out):
    alpha = step_scalars[0:1, 0:1]
    norm = step_scalars[0:1, 1:2]
    beta = step_scalars[0:1, 2:3]
    noise = step_scalars[0:1, 3:4]
    halves = start_ref.shape[0]

    def add(i, total):
        return total + arrived[i, :, halves * LANES:(halves + 1) * LANES]

    share = lax.fori_loop(0, arrived.shape[0], add, jnp.zeros((1, LANES), f32), unroll=8)
    alpha_next = norm / (total_sum(share) + noise)
    z, _, _, core = place()
    product = jnp.zeros((1, (halves + 1) * LANES), f32)
    for y in range(2):
        for x in range(narrow // 2):
            product = product + arrived[device_at(z, y, x, core, narrow)]
    for half in range(halves):
        begin = start_ref[half:half + 1, :]
        residual = begin - alpha * step_scalars[1 + half:2 + half, :]
        direction = residual + beta * begin
        image = product[:, half * LANES:(half + 1) * LANES] + noise_var * direction
        solution_out[half:half + 1, :] = alpha * begin + alpha_next * direction
        residual_out[half:half + 1, :] = residual - alpha_next * image


def call(kernel, out_shape, *args, scratch=(), vmem=VMEM_BYTES, **options):
    return pl.pallas_call(
        kernel,
        out_shape=out_shape,
        scratch_shapes=list(scratch),
        compiler_params=pltpu.CompilerParams(vmem_limit_bytes=vmem),
        **{name: value for name, value in options.items() if value is not None},
    )(*args)


def to_all(blocks, axes):
    return lax.all_to_all(blocks, axes, split_axis=0, concat_axis=0, tiled=True)


def direct(wide, narrow):
    depth, across = wide // 2, narrow // 2
    return depth <= DIRECT and not depth & (depth - 1) and not across & (across - 1)


def every_block(own, wide, narrow):
    every = lax.all_gather(own, ALL, axis=0, tiled=True)
    every = every.reshape(wide // 2, 2, narrow // 2, 2, *own.shape[1:])
    z, y, x, core = place()
    rows = lax.dynamic_index_in_dim(every, z, 0, keepdims=False)
    rows = lax.dynamic_index_in_dim(rows, core, 2, keepdims=False)
    columns = lax.dynamic_index_in_dim(every, y, 1, keepdims=False)
    columns = lax.dynamic_index_in_dim(columns, x, 1, keepdims=False)
    return [rows.reshape(narrow, *own.shape[1:])], [columns.reshape(wide, *own.shape[1:])]


def passed(value, axes, size):
    return [lax.ppermute(value, axes, [(i, i ^ flip) for i in range(size)]) for flip in range(1, size)]


def row_group(own, narrow):
    return [own] + passed(own, (Y, X), narrow)


def column_group(own, wide):
    blocks = [own] + passed(own, Z, wide // 2)
    return blocks + [passed(block, CORE, 2)[0] for block in blocks]


def on_device(wide, narrow, features, projection, targets):
    rows, proj = features.shape[0], projection.shape[1]
    halves = rows // LANES
    lines = narrow * halves
    devices = wide * narrow
    scale = -2.0 / proj * math.log2(math.e)
    depth = 6 * proj + 16
    keep = 4 * devices * rows * rows <= KEEP_BYTES

    def shape(*dims, dtype=f32):
        return jax.ShapeDtypeStruct(dims, dtype)

    def scratch(*dims, dtype=f32):
        return pltpu.VMEM(dims, dtype)

    feat = features.shape[1]
    own = call(
        project_kernel, shape(1, proj + 8, rows), features, projection.T, targets.reshape(1, rows),
        in_specs=[pl.BlockSpec(memory_space=pl.ANY)] * 3, vmem=WHOLE_VMEM_BYTES,
        scratch=[scratch(CHUNKS, rows, feat // CHUNKS, dtype=bf16), scratch(proj, feat, dtype=bf16),
                 scratch(1, rows), pltpu.SemaphoreType.DMA((CHUNKS + 2,))])
    by_permutes = direct(wide, narrow)
    if by_permutes:
        row_blocks, column_blocks = row_group(own, narrow), column_group(own, wide)[1:]
    else:
        row_blocks, column_blocks = every_block(own, wide, narrow)
    left = (narrow, rows, depth)
    right = (wide, depth, rows)
    block_out = shape(1, 2 * lines, LANES)
    sums = scratch(narrow, rows, LANES)
    work = [scratch(lines, LANES), scratch(wide * halves, LANES), scratch(lines, LANES), sums,
            scratch(1, proj + 8, rows), pltpu.SemaphoreType.DMA]
    specs = None
    if len(row_blocks) > 1:
        specs = [pl.BlockSpec(memory_space=pl.ANY)]
        specs += [pl.BlockSpec(memory_space=pltpu.VMEM)] * (len(row_blocks) + len(column_blocks) - 1)
    first = functools.partial(
        first_kernel, proj, scale, wide, narrow, keep, len(row_blocks), len(column_blocks))
    if keep:
        *block, out = call(
            first, (shape(narrow, wide, rows, rows), block_out), *row_blocks, *column_blocks,
            scratch=[scratch(*left, dtype=bf16), scratch(*right, dtype=bf16)] + work, in_specs=specs)
    else:
        *block, out = call(
            first, (shape(*left, dtype=bf16), shape(*right, dtype=bf16), block_out),
            *row_blocks, *column_blocks, scratch=work, in_specs=specs)
    row_blocks = row_group(out, narrow) if by_permutes else every_block(out, wide, narrow)[0]
    image = call(functools.partial(image_kernel, narrow), block_out, *row_blocks,
                 scratch=[scratch(narrow, lines, LANES)])
    column_blocks = column_group(image, wide) if by_permutes else every_block(image, wide, narrow)[1]
    out, step_scalars = call(
        functools.partial(second_kernel, wide, narrow, keep, len(column_blocks)),
        (shape(devices, 1, (halves + 1) * LANES), shape(1 + halves, LANES)),
        *column_blocks, *block,
        scratch=[scratch(devices * halves, LANES)] * 3 + [scratch(lines, LANES), sums])
    answer, residual = call(
        functools.partial(last_kernel, narrow), (shape(halves, LANES), shape(halves, LANES)),
        to_all(out, ALL), step_scalars, targets.reshape(halves, LANES))
    return answer.reshape(rows), residual.reshape(rows)


def solution(mesh):
    wide, narrow = mesh.shape["wide"], mesh.shape["narrow"]
    split = jax.sharding.Mesh(mesh.devices.reshape(wide // 2, 2, narrow // 2, 2), ALL)
    in_specs = (P(ALL, None), P(), P(ALL))
    return jax.shard_map(
        functools.partial(on_device, wide, narrow), mesh=split,
        in_specs=in_specs, out_specs=(P(ALL), P(ALL)), check_vma=False,
    )
```

```python
import functools
import math

import jax
import jax.numpy as jnp
from jax import lax
from jax.experimental import pallas as pl
from jax.experimental.pallas import tpu as pltpu
from jax.sharding import PartitionSpec as P

noise_var = 0.5
LANES = 128
CHUNKS = 4
DIRECT = 8
KEEP_BYTES = 8 * 2**20
VMEM_BYTES = 32 * 2**20
WHOLE_VMEM_BYTES = (53 * 1024 + 870) * 2**10
Z, Y, X, CORE = "z", "y", "x", "core"
ALL = (Z, Y, X, CORE)
highest = lax.Precision.HIGHEST
f32 = jnp.float32
bf16 = jnp.bfloat16


def split3(values):
    high = values.astype(bf16)
    rest = values - high.astype(f32)
    mid = rest.astype(bf16)
    low = (rest - mid.astype(f32)).astype(bf16)
    return high, mid, low


def exponent_rows(first, second):
    width = (first if not isinstance(first, float) else second).shape[1]
    row = lax.broadcasted_iota(jnp.int32, (16, width), 0)
    out = jnp.zeros((16, width), f32)
    for base, value in ((0, first), (3, second)):
        parts = (1.0, 1.0, 1.0) if isinstance(value, float) else [p.astype(f32) for p in split3(value)]
        for k, part in enumerate(parts):
            out = jnp.where(row == base + k, part, out)
    return out.astype(bf16)


def right_operand(latent, scale):
    square = jnp.sum(latent * latent, axis=0, keepdims=True) * scale
    h, m, l = split3(latent)
    return jnp.concatenate([h, m, l, h, m, h, exponent_rows(square, 1.0)], axis=0)


def left_operand(latent, scale):
    square = jnp.sum(latent * latent, axis=0, keepdims=True) * scale
    h, m, l = split3(latent * (-2.0 * scale))
    stacked = jnp.concatenate([h, h, h, m, m, l, exponent_rows(1.0, square)], axis=0)
    return stacked.astype(f32).T.astype(bf16)


def place():
    return tuple(lax.axis_index(name) for name in ALL)


def device_at(z, y, x, core, narrow):
    return ((z * 2 + y) * (narrow // 2) + x) * 2 + core


def row_sources(blocks, narrow, flips):
    if flips is None:
        return [(blocks[0], i, i) for i in range(narrow)]
    z, y, x, core = place()
    me = y * (narrow // 2) + x
    spots = [(b, i) for b in blocks for i in range(b.shape[0])]
    return [(b, i, jnp.bitwise_xor(me, flip)) for (b, i), flip in zip(spots, flips)]


def column_sources(blocks, wide, flips):
    if flips is None:
        return [(blocks[0], i, i) for i in range(wide)]
    z, y, x, core = place()
    spots = [(b, i) for b in blocks for i in range(b.shape[0])]
    return [(b, i, jnp.bitwise_xor(z, z_flip) * 2 + jnp.bitwise_xor(core, core_flip))
            for (b, i), (z_flip, core_flip) in zip(spots, flips)]


def total_sum(values):
    return jnp.sum(jnp.sum(values, axis=0, keepdims=True), axis=1, keepdims=True)


def lane_sums(values):
    parts = jnp.concatenate(split3(values), axis=1)
    ones = jnp.ones((16, parts.shape[1]), bf16)
    return lax.dot_general(ones, parts, (((1,), (1,)), ((), ())),
                           preferred_element_type=f32)[0:1, :]


def make_rows(left, right, kept, read_vector, sums):
    groups, rows, _ = left.shape
    columns = right.shape[0]
    halves = rows // LANES

    def one_group(g, _):
        left_group = left[g]

        def one_column(c, acc):
            exponent = jnp.dot(left_group, right[c], preferred_element_type=f32)
            tile = jnp.exp2(exponent)
            if kept is not None:
                kept[g, c] = tile
            for half in range(halves):
                acc = acc + tile[:, half * LANES:(half + 1) * LANES] * read_vector(c, half)
            return acc

        sums[g] = lax.fori_loop(0, columns, one_column, jnp.zeros((rows, LANES), f32), unroll=8)
        return 0

    lax.fori_loop(0, groups, one_group, 0)


def use_rows(kept, read_vector, sums):
    groups, columns, rows, _ = kept.shape
    halves = rows // LANES

    def one_group(g, _):
        def one_column(c, acc):
            for half in range(halves):
                acc = acc + kept[g, c, :, half * LANES:(half + 1) * LANES] * read_vector(c, half)
            return acc

        sums[g] = lax.fori_loop(0, columns, one_column, jnp.zeros((rows, LANES), f32), unroll=8)
        return 0

    lax.fori_loop(0, groups, one_group, 0)


def write_rows(sums, out):
    groups, rows, _ = sums.shape
    total = lane_sums(sums[...].reshape(groups * rows, LANES))
    for line in range(out.shape[0]):
        out[line:line + 1, :] = total[:, line * LANES:(line + 1) * LANES]


def project_kernel(features, projection_t, targets, out, feature_buf, projection_buf, target_buf, sems):
    proj = projection_t.shape[0]
    chunks, _, width = feature_buf.shape
    copies = [pltpu.make_async_copy(projection_t, projection_buf, sems.at[0])]
    copies += [
        pltpu.make_async_copy(features.at[:, pl.ds(i * width, width)], feature_buf.at[i], sems.at[i + 1])
        for i in range(chunks)]
    copies += [pltpu.make_async_copy(targets, target_buf, sems.at[chunks + 1])]
    for copy in copies:
        copy.start()
    copies[0].wait()
    latent = jnp.zeros((proj, features.shape[0]), f32)
    for i in range(chunks):
        copies[i + 1].wait()
        latent = latent + lax.dot_general(
            projection_buf[:, i * width:(i + 1) * width], feature_buf[i],
            (((1,), (1,)), ((), ())), preferred_element_type=f32)
    copies[-1].wait()
    out[0, 0:proj, :] = latent
    out[0, proj:proj + 8, :] = jnp.broadcast_to(target_buf[...], (8, out.shape[2]))


def first_kernel(proj, scale, wide, narrow, keep, flips, row_count, column_count, *refs):
    row_blocks, column_blocks = refs[:row_count], refs[row_count:row_count + column_count]
    refs = refs[row_count + column_count:]
    if keep:
        kept, out, left, right, own_rows, column_vector, partial, sums = refs
    else:
        kept = None
        left, right, out, own_rows, column_vector, partial, sums = refs
    rows = left.shape[1]
    halves = rows // LANES
    lines = partial.shape[0]

    def prepare_row(block, i, source):
        left[source] = left_operand(block[i, 0:proj, :], scale)
        for half in range(halves):
            own_rows[pl.ds(source * halves + half, 1), :] = block[
                i, proj:proj + 1, half * LANES:(half + 1) * LANES]

    def prepare_column(block, i, source):
        right[source] = right_operand(block[i, 0:proj, :], scale)
        for half in range(halves):
            column_vector[pl.ds(source * halves + half, 1), :] = block[
                i, proj:proj + 1, half * LANES:(half + 1) * LANES]

    for item in column_sources(column_blocks, wide, flips[1]):
        prepare_column(*item)
    for item in row_sources(row_blocks, narrow, flips[0]):
        prepare_row(*item)
    make_rows(left, right, kept, lambda c, half: column_vector[pl.ds(c * halves + half, 1), :], sums)
    write_rows(sums, partial)
    z, y, x, core = place()
    mine = (y * (narrow // 2) + x) * halves
    pieces = [partial[line:line + 1, :] for line in range(lines)]
    pieces += [own_rows[pl.ds(mine + half, 1), :] for half in range(halves)]
    block = jnp.concatenate(pieces, axis=1)

    def copy(i, _):
        out[i] = block
        return 0

    lax.fori_loop(0, out.shape[0], copy, 0, unroll=8)


def second_kernel(wide, narrow, keep, *refs):
    arrived, out, step_scalars, direction, images, targets, partial, sums = refs[:1] + refs[-7:]
    lines = partial.shape[0]
    halves = lines // narrow
    across = narrow // 2
    group = [(y, x) for y in range(2) for x in range(across)]

    def unpack(z, _):
        for core in range(2):
            members = [device_at(z, y, x, core, narrow) for y, x in group]
            total = arrived[members[0]]
            for member in members[1:]:
                total = total + arrived[member]
            for r, member in enumerate(members):
                for half in range(halves):
                    start = arrived[member, :, (lines + half) * LANES:(lines + half + 1) * LANES]
                    line = r * halves + half
                    spot = pl.ds(member * halves + half, 1)
                    targets[spot, :] = start
                    images[spot, :] = total[:, line * LANES:(line + 1) * LANES] + noise_var * start
        return 0

    lax.fori_loop(0, wide // 2, unpack, 0, unroll=4)
    start, first = targets[...], images[...]
    norm = total_sum(start * start)
    alpha = norm / total_sum(start * first)
    residual = start - alpha * first
    norm_next = total_sum(residual * residual)
    beta = norm_next / norm
    whole = residual + beta * start
    direction[...] = whole
    z, y, x, core = place()

    def read_vector(c, half):
        return direction[pl.ds(device_at(c // 2, y, x, c % 2, narrow) * halves + half, 1), :]

    if keep:
        use_rows(refs[1], read_vector, sums)
    else:
        make_rows(refs[1], refs[2], None, read_vector, sums)
    write_rows(sums, partial)
    share = jnp.zeros((1, LANES), f32)
    for r, (row_y, row_x) in enumerate(group):
        for half in range(halves):
            spot = pl.ds(device_at(z, row_y, row_x, core, narrow) * halves + half, 1)
            line = r * halves + half
            share = share + direction[spot, :] * partial[line:line + 1, :]
    blocks = [
        jnp.concatenate([partial[r * halves + half:r * halves + half + 1, :]
                         for half in range(halves)] + [share], axis=1)
        for r in range(narrow)]

    def copy(to_z, _):
        for r, (to_y, to_x) in enumerate(group):
            for to_core in range(2):
                out[device_at(to_z, to_y, to_x, to_core, narrow)] = blocks[r]
        return 0

    lax.fori_loop(0, wide // 2, copy, 0, unroll=4)
    lane = lax.broadcasted_iota(jnp.int32, (1, LANES), 1)
    noise = noise_var * total_sum(whole * whole)
    step_scalars[0:1, :] = jnp.where(lane == 0, alpha, jnp.where(
        lane == 1, norm_next, jnp.where(lane == 2, beta, noise)))
    for half in range(halves):
        spot = pl.ds(device_at(z, y, x, core, narrow) * halves + half, 1)
        step_scalars[1 + half:2 + half, :] = images[spot, :]


def last_kernel(narrow, arrived, step_scalars, start_ref, solution_out, residual_out):
    alpha = step_scalars[0:1, 0:1]
    norm = step_scalars[0:1, 1:2]
    beta = step_scalars[0:1, 2:3]
    noise = step_scalars[0:1, 3:4]
    halves = start_ref.shape[0]

    def add(i, total):
        return total + arrived[i, :, halves * LANES:(halves + 1) * LANES]

    share = lax.fori_loop(0, arrived.shape[0], add, jnp.zeros((1, LANES), f32), unroll=8)
    alpha_next = norm / (total_sum(share) + noise)
    z, _, _, core = place()
    product = jnp.zeros((1, (halves + 1) * LANES), f32)
    for y in range(2):
        for x in range(narrow // 2):
            product = product + arrived[device_at(z, y, x, core, narrow)]
    for half in range(halves):
        begin = start_ref[half:half + 1, :]
        residual = begin - alpha * step_scalars[1 + half:2 + half, :]
        direction = residual + beta * begin
        image = product[:, half * LANES:(half + 1) * LANES] + noise_var * direction
        solution_out[half:half + 1, :] = alpha * begin + alpha_next * direction
        residual_out[half:half + 1, :] = residual - alpha_next * image


def call(kernel, out_shape, *args, scratch=(), vmem=VMEM_BYTES, **options):
    return pl.pallas_call(
        kernel,
        out_shape=out_shape,
        scratch_shapes=list(scratch),
        compiler_params=pltpu.CompilerParams(vmem_limit_bytes=vmem),
        **options,
    )(*args)


def to_all(blocks, axes):
    return lax.all_to_all(blocks, axes, split_axis=0, concat_axis=0, tiled=True)


def join_kernel(*refs):
    i = 0
    for block in refs[:-1]:
        for j in range(block.shape[0]):
            refs[-1][i] = block[j]
            i += 1


def join(*blocks):
    total = sum(b.shape[0] for b in blocks)
    return call(join_kernel, jax.ShapeDtypeStruct((total, *blocks[0].shape[1:]), f32), *blocks)


def first_round(own, wide, narrow):
    depth, across = wide // 2, narrow // 2
    if depth & (depth - 1) or across & (across - 1) or depth > DIRECT:
        every = lax.all_gather(own, ALL, axis=0, tiled=True)
        every = every.reshape(depth, 2, across, 2, *own.shape[1:])
        z, y, x, core = place()
        rows = lax.dynamic_index_in_dim(every, z, 0, keepdims=False)
        rows = lax.dynamic_index_in_dim(rows, core, 2, keepdims=False)
        columns = lax.dynamic_index_in_dim(every, y, 1, keepdims=False)
        columns = lax.dynamic_index_in_dim(columns, x, 1, keepdims=False)
        return ([rows.reshape(narrow, *own.shape[1:])], [columns.reshape(wide, *own.shape[1:])],
                (None, None))

    def swap(value, axis, size, flip):
        return lax.ppermute(value, axis, [(i, i ^ flip) for i in range(size)])

    rows, row_flips = own, [0]
    for k in range(across.bit_length() - 1):
        rows = join(rows, swap(rows, X, across, 1 << k))
        row_flips += [f ^ (1 << k) for f in row_flips]
    columns = [own] + [swap(own, Z, depth, flip) for flip in range(1, depth)]
    columns += [swap(block, CORE, 2, 1) for block in columns]
    rows = [rows, swap(rows, Y, 2, 1)]
    row_flips += [f ^ across for f in row_flips]
    return rows, columns, (row_flips, [(f, c) for c in range(2) for f in range(depth)])


def on_device(wide, narrow, features, projection, targets):
    rows, proj = features.shape[0], projection.shape[1]
    halves = rows // LANES
    lines = narrow * halves
    devices = wide * narrow
    scale = -2.0 / proj * math.log2(math.e)
    depth = 6 * proj + 16
    keep = 4 * devices * rows * rows <= KEEP_BYTES

    def shape(*dims, dtype=f32):
        return jax.ShapeDtypeStruct(dims, dtype)

    def scratch(*dims, dtype=f32):
        return pltpu.VMEM(dims, dtype)

    feat = features.shape[1]
    own = call(
        project_kernel, shape(1, proj + 8, rows), features, projection.T, targets.reshape(1, rows),
        in_specs=[pl.BlockSpec(memory_space=pl.ANY)] * 3, vmem=WHOLE_VMEM_BYTES,
        scratch=[scratch(CHUNKS, rows, feat // CHUNKS, dtype=bf16), scratch(proj, feat, dtype=bf16),
                 scratch(1, rows), pltpu.SemaphoreType.DMA((CHUNKS + 2,))])
    row_blocks, column_blocks, flips = first_round(own, wide, narrow)
    left = (narrow, rows, depth)
    right = (wide, depth, rows)
    block_out = shape(devices, 1, (lines + halves) * LANES)
    sums = scratch(narrow, rows, LANES)
    work = [scratch(lines, LANES), scratch(wide * halves, LANES), scratch(lines, LANES), sums]
    first = functools.partial(
        first_kernel, proj, scale, wide, narrow, keep, flips, len(row_blocks), len(column_blocks))
    if keep:
        *block, out = call(
            first, (shape(narrow, wide, rows, rows), block_out), *row_blocks, *column_blocks,
            scratch=[scratch(*left, dtype=bf16), scratch(*right, dtype=bf16)] + work)
    else:
        *block, out = call(
            first, (shape(*left, dtype=bf16), shape(*right, dtype=bf16), block_out),
            *row_blocks, *column_blocks, scratch=work)
    out, step_scalars = call(
        functools.partial(second_kernel, wide, narrow, keep),
        (shape(devices, 1, (halves + 1) * LANES), shape(1 + halves, LANES)),
        to_all(out, ALL), *block,
        scratch=[scratch(devices * halves, LANES)] * 3 + [scratch(lines, LANES), sums])
    answer, residual = call(
        functools.partial(last_kernel, narrow), (shape(halves, LANES), shape(halves, LANES)),
        to_all(out, ALL), step_scalars, targets.reshape(halves, LANES))
    return answer.reshape(rows), residual.reshape(rows)


def solution(mesh):
    wide, narrow = mesh.shape["wide"], mesh.shape["narrow"]
    split = jax.sharding.Mesh(mesh.devices.reshape(wide // 2, 2, narrow // 2, 2), ALL)
    in_specs = (P(ALL, None), P(), P(ALL))
    return jax.shard_map(
        functools.partial(on_device, wide, narrow), mesh=split,
        in_specs=in_specs, out_specs=(P(ALL), P(ALL)), check_vma=False,
    )
```

```python
import functools
import math

import jax
import jax.numpy as jnp
from jax import lax
from jax.experimental import pallas as pl
from jax.experimental.pallas import tpu as pltpu
from jax.sharding import PartitionSpec as P

noise_var = 0.5
LANES = 128
CHUNKS = 8
DIRECT = 8
KEEP_BYTES = 8 * 2**20
VMEM_BYTES = 32 * 2**20
WHOLE_VMEM_BYTES = (53 * 1024 + 870) * 2**10
Z, Y, X, CORE = "z", "y", "x", "core"
ALL = (Z, Y, X, CORE)
highest = lax.Precision.HIGHEST
f32 = jnp.float32
bf16 = jnp.bfloat16


def split3(values):
    high = values.astype(bf16)
    rest = values - high.astype(f32)
    mid = rest.astype(bf16)
    low = (rest - mid.astype(f32)).astype(bf16)
    return high, mid, low


def exponent_rows(first, second):
    width = (first if not isinstance(first, float) else second).shape[1]
    row = lax.broadcasted_iota(jnp.int32, (16, width), 0)
    out = jnp.zeros((16, width), f32)
    for base, value in ((0, first), (3, second)):
        parts = (1.0, 1.0, 1.0) if isinstance(value, float) else [p.astype(f32) for p in split3(value)]
        for k, part in enumerate(parts):
            out = jnp.where(row == base + k, part, out)
    return out.astype(bf16)


def right_operand(latent, scale):
    square = jnp.sum(latent * latent, axis=0, keepdims=True) * scale
    h, m, l = split3(latent)
    return jnp.concatenate([h, m, l, h, m, h, exponent_rows(square, 1.0)], axis=0)


def left_operand(latent, scale):
    square = jnp.sum(latent * latent, axis=0, keepdims=True) * scale
    h, m, l = split3(latent * (-2.0 * scale))
    stacked = jnp.concatenate([h, h, h, m, m, l, exponent_rows(1.0, square)], axis=0)
    return stacked.T


def place():
    return tuple(lax.axis_index(name) for name in ALL)


def device_at(z, y, x, core, narrow):
    return ((z * 2 + y) * (narrow // 2) + x) * 2 + core


def row_sources(blocks, narrow, flips):
    if flips is None:
        return [(blocks[0], i, i) for i in range(narrow)]
    z, y, x, core = place()
    me = y * (narrow // 2) + x
    spots = [(b, i) for b in blocks for i in range(b.shape[0])]
    return [(b, i, jnp.bitwise_xor(me, flip)) for (b, i), flip in zip(spots, flips)]


def column_sources(blocks, wide, flips):
    if flips is None:
        return [(blocks[0], i, i) for i in range(wide)]
    z, y, x, core = place()
    spots = [(b, i) for b in blocks for i in range(b.shape[0])]
    return [(b, i, jnp.bitwise_xor(z, z_flip) * 2 + jnp.bitwise_xor(core, core_flip))
            for (b, i), (z_flip, core_flip) in zip(spots, flips)]


def total_sum(values):
    return jnp.sum(jnp.sum(values, axis=0, keepdims=True), axis=1, keepdims=True)


def lane_sums(values):
    parts = jnp.concatenate(split3(values), axis=1)
    ones = jnp.ones((16, parts.shape[1]), bf16)
    return lax.dot_general(ones, parts, (((1,), (1,)), ((), ())),
                           preferred_element_type=f32)[0:1, :]


def make_rows(left, right, kept, read_vector, sums):
    groups, rows, _ = left.shape
    columns = right.shape[0]
    halves = rows // LANES

    def one_group(g, _):
        left_group = left[g]

        def one_column(c, acc):
            exponent = jnp.dot(left_group, right[c], preferred_element_type=f32)
            tile = jnp.exp2(exponent)
            if kept is not None:
                kept[g, c] = tile
            for half in range(halves):
                acc = acc + tile[:, half * LANES:(half + 1) * LANES] * read_vector(c, half)
            return acc

        sums[g] = lax.fori_loop(0, columns, one_column, jnp.zeros((rows, LANES), f32), unroll=8)
        return 0

    lax.fori_loop(0, groups, one_group, 0)


def use_rows(kept, read_vector, sums):
    groups, columns, rows, _ = kept.shape
    halves = rows // LANES

    def one_group(g, _):
        def one_column(c, acc):
            for half in range(halves):
                acc = acc + kept[g, c, :, half * LANES:(half + 1) * LANES] * read_vector(c, half)
            return acc

        sums[g] = lax.fori_loop(0, columns, one_column, jnp.zeros((rows, LANES), f32), unroll=8)
        return 0

    lax.fori_loop(0, groups, one_group, 0)


def write_rows(sums, out):
    groups, rows, _ = sums.shape
    total = lane_sums(sums[...].reshape(groups * rows, LANES))
    for line in range(out.shape[0]):
        out[line:line + 1, :] = total[:, line * LANES:(line + 1) * LANES]


def project_kernel(features, projection_t, targets, out, feature_buf, projection_buf, target_buf, sems):
    proj = projection_t.shape[0]
    chunks, _, width = feature_buf.shape
    copies = [pltpu.make_async_copy(projection_t, projection_buf, sems.at[0])]
    copies += [
        pltpu.make_async_copy(features.at[:, pl.ds(i * width, width)], feature_buf.at[i], sems.at[i + 1])
        for i in range(chunks)]
    copies += [pltpu.make_async_copy(targets, target_buf, sems.at[chunks + 1])]
    for copy in copies:
        copy.start()
    copies[0].wait()
    latent = jnp.zeros((proj, features.shape[0]), f32)
    for i in range(chunks):
        copies[i + 1].wait()
        latent = latent + lax.dot_general(
            projection_buf[:, i * width:(i + 1) * width], feature_buf[i],
            (((1,), (1,)), ((), ())), preferred_element_type=f32)
    out[0, 0:proj, :] = latent
    copies[-1].wait()
    out[0, proj:proj + 8, :] = jnp.broadcast_to(target_buf[...], (8, out.shape[2]))


def first_kernel(proj, scale, wide, narrow, keep, flips, row_count, column_count, *refs):
    row_blocks, column_blocks = refs[:row_count], refs[row_count:row_count + column_count]
    refs = refs[row_count + column_count:]
    if keep:
        kept, out, left, right, own_rows, column_vector, partial, sums = refs
    else:
        kept = None
        left, right, out, own_rows, column_vector, partial, sums = refs
    rows = left.shape[1]
    halves = rows // LANES
    lines = partial.shape[0]

    def prepare_row(block, i, source):
        left[source] = left_operand(block[i, 0:proj, :], scale)
        for half in range(halves):
            own_rows[pl.ds(source * halves + half, 1), :] = block[
                i, proj:proj + 1, half * LANES:(half + 1) * LANES]

    def prepare_column(block, i, source):
        right[source] = right_operand(block[i, 0:proj, :], scale)
        for half in range(halves):
            column_vector[pl.ds(source * halves + half, 1), :] = block[
                i, proj:proj + 1, half * LANES:(half + 1) * LANES]

    for item in column_sources(column_blocks, wide, flips[1]):
        prepare_column(*item)
    for item in row_sources(row_blocks, narrow, flips[0]):
        prepare_row(*item)
    make_rows(left, right, kept, lambda c, half: column_vector[pl.ds(c * halves + half, 1), :], sums)
    write_rows(sums, partial)
    z, y, x, core = place()
    mine = (y * (narrow // 2) + x) * halves
    pieces = [partial[line:line + 1, :] for line in range(lines)]
    pieces += [own_rows[pl.ds(mine + half, 1), :] for half in range(halves)]
    block = jnp.concatenate(pieces, axis=1)

    def copy(i, _):
        out[i] = block
        return 0

    lax.fori_loop(0, out.shape[0], copy, 0, unroll=8)


def second_kernel(wide, narrow, keep, *refs):
    arrived, out, step_scalars, direction, images, targets, partial, sums = refs[:1] + refs[-7:]
    lines = partial.shape[0]
    halves = lines // narrow
    across = narrow // 2
    group = [(y, x) for y in range(2) for x in range(across)]

    def unpack(z, _):
        for core in range(2):
            members = [device_at(z, y, x, core, narrow) for y, x in group]
            total = arrived[members[0]]
            for member in members[1:]:
                total = total + arrived[member]
            for r, member in enumerate(members):
                for half in range(halves):
                    start = arrived[member, :, (lines + half) * LANES:(lines + half + 1) * LANES]
                    line = r * halves + half
                    spot = pl.ds(member * halves + half, 1)
                    targets[spot, :] = start
                    images[spot, :] = total[:, line * LANES:(line + 1) * LANES] + noise_var * start
        return 0

    lax.fori_loop(0, wide // 2, unpack, 0, unroll=4)
    start, first = targets[...], images[...]
    norm = total_sum(start * start)
    alpha = norm / total_sum(start * first)
    residual = start - alpha * first
    norm_next = total_sum(residual * residual)
    beta = norm_next / norm
    whole = residual + beta * start
    direction[...] = whole
    z, y, x, core = place()

    def read_vector(c, half):
        return direction[pl.ds(device_at(c // 2, y, x, c % 2, narrow) * halves + half, 1), :]

    if keep:
        use_rows(refs[1], read_vector, sums)
    else:
        make_rows(refs[1], refs[2], None, read_vector, sums)
    write_rows(sums, partial)
    share = jnp.zeros((1, LANES), f32)
    for r, (row_y, row_x) in enumerate(group):
        for half in range(halves):
            spot = pl.ds(device_at(z, row_y, row_x, core, narrow) * halves + half, 1)
            line = r * halves + half
            share = share + direction[spot, :] * partial[line:line + 1, :]
    blocks = [
        jnp.concatenate([partial[r * halves + half:r * halves + half + 1, :]
                         for half in range(halves)] + [share], axis=1)
        for r in range(narrow)]

    def copy(to_z, _):
        for r, (to_y, to_x) in enumerate(group):
            for to_core in range(2):
                out[device_at(to_z, to_y, to_x, to_core, narrow)] = blocks[r]
        return 0

    lax.fori_loop(0, wide // 2, copy, 0, unroll=4)
    lane = lax.broadcasted_iota(jnp.int32, (1, LANES), 1)
    noise = noise_var * total_sum(whole * whole)
    step_scalars[0:1, :] = jnp.where(lane == 0, alpha, jnp.where(
        lane == 1, norm_next, jnp.where(lane == 2, beta, noise)))
    for half in range(halves):
        spot = pl.ds(device_at(z, y, x, core, narrow) * halves + half, 1)
        step_scalars[1 + half:2 + half, :] = images[spot, :]
        step_scalars[1 + halves + half:2 + halves + half, :] = targets[spot, :]


def last_kernel(narrow, arrived, step_scalars, solution_out, residual_out, answer, sems):
    alpha = step_scalars[0:1, 0:1]
    norm = step_scalars[0:1, 1:2]
    beta = step_scalars[0:1, 2:3]
    noise = step_scalars[0:1, 3:4]
    halves = answer.shape[1]

    def add(i, total):
        return total + arrived[i, :, halves * LANES:(halves + 1) * LANES]

    share = lax.fori_loop(0, arrived.shape[0], add, jnp.zeros((1, LANES), f32), unroll=8)
    alpha_next = norm / (total_sum(share) + noise)
    z, _, _, core = place()
    product = jnp.zeros((1, (halves + 1) * LANES), f32)
    for y in range(2):
        for x in range(narrow // 2):
            product = product + arrived[device_at(z, y, x, core, narrow)]
    for half in range(halves):
        begin = step_scalars[1 + halves + half:2 + halves + half, :]
        residual = begin - alpha * step_scalars[1 + half:2 + half, :]
        direction = residual + beta * begin
        image = product[:, half * LANES:(half + 1) * LANES] + noise_var * direction
        answer[0, half:half + 1, :] = alpha * begin + alpha_next * direction
        answer[1, half:half + 1, :] = residual - alpha_next * image
    copies = [pltpu.make_async_copy(answer.at[i], out, sems.at[i])
              for i, out in enumerate((solution_out, residual_out))]
    for copy in copies:
        copy.start()
    for copy in copies:
        copy.wait()


def call(kernel, out_shape, *args, scratch=(), vmem=VMEM_BYTES, **options):
    return pl.pallas_call(
        kernel,
        out_shape=out_shape,
        scratch_shapes=list(scratch),
        compiler_params=pltpu.CompilerParams(vmem_limit_bytes=vmem),
        **options,
    )(*args)


def to_all(blocks, axes):
    return lax.all_to_all(blocks, axes, split_axis=0, concat_axis=0, tiled=True)


def join_kernel(*refs):
    i = 0
    for block in refs[:-1]:
        for j in range(block.shape[0]):
            refs[-1][i] = block[j]
            i += 1


def join(*blocks):
    total = sum(b.shape[0] for b in blocks)
    return call(join_kernel, jax.ShapeDtypeStruct((total, *blocks[0].shape[1:]), f32), *blocks)


def first_round(own, wide, narrow):
    depth, across = wide // 2, narrow // 2
    if depth & (depth - 1) or across & (across - 1) or depth > DIRECT:
        every = lax.all_gather(own, ALL, axis=0, tiled=True)
        every = every.reshape(depth, 2, across, 2, *own.shape[1:])
        z, y, x, core = place()
        rows = lax.dynamic_index_in_dim(every, z, 0, keepdims=False)
        rows = lax.dynamic_index_in_dim(rows, core, 2, keepdims=False)
        columns = lax.dynamic_index_in_dim(every, y, 1, keepdims=False)
        columns = lax.dynamic_index_in_dim(columns, x, 1, keepdims=False)
        return ([rows.reshape(narrow, *own.shape[1:])], [columns.reshape(wide, *own.shape[1:])],
                (None, None))

    def swap(value, axis, size, flip):
        return lax.ppermute(value, axis, [(i, i ^ flip) for i in range(size)])

    rows, row_flips = own, [0]
    for k in range(across.bit_length() - 1):
        rows = join(rows, swap(rows, X, across, 1 << k))
        row_flips += [f ^ (1 << k) for f in row_flips]
    columns = [own] + [swap(own, Z, depth, flip) for flip in range(1, depth)]
    columns += [swap(block, CORE, 2, 1) for block in columns]
    rows = [rows, swap(rows, Y, 2, 1)]
    row_flips += [f ^ across for f in row_flips]
    return rows, columns, (row_flips, [(f, c) for c in range(2) for f in range(depth)])


def on_device(wide, narrow, features, projection, targets):
    rows, proj = features.shape[0], projection.shape[1]
    halves = rows // LANES
    lines = narrow * halves
    devices = wide * narrow
    scale = -2.0 / proj * math.log2(math.e)
    depth = 6 * proj + 16
    keep = 4 * devices * rows * rows <= KEEP_BYTES

    def shape(*dims, dtype=f32):
        return jax.ShapeDtypeStruct(dims, dtype)

    def scratch(*dims, dtype=f32):
        return pltpu.VMEM(dims, dtype)

    feat = features.shape[1]
    own = call(
        project_kernel, shape(1, proj + 8, rows), features, projection.T, targets.reshape(1, rows),
        in_specs=[pl.BlockSpec(memory_space=pl.ANY)] * 3, vmem=WHOLE_VMEM_BYTES,
        scratch=[scratch(CHUNKS, rows, feat // CHUNKS, dtype=bf16), scratch(proj, feat, dtype=bf16),
                 scratch(1, rows), pltpu.SemaphoreType.DMA((CHUNKS + 2,))])
    row_blocks, column_blocks, flips = first_round(own, wide, narrow)
    left = (narrow, rows, depth)
    right = (wide, depth, rows)
    block_out = shape(devices, 1, (lines + halves) * LANES)
    sums = scratch(narrow, rows, LANES)
    work = [scratch(lines, LANES), scratch(wide * halves, LANES), scratch(lines, LANES), sums]
    first = functools.partial(
        first_kernel, proj, scale, wide, narrow, keep, flips, len(row_blocks), len(column_blocks))
    if keep:
        *block, out = call(
            first, (shape(narrow, wide, rows, rows), block_out), *row_blocks, *column_blocks,
            scratch=[scratch(*left, dtype=bf16), scratch(*right, dtype=bf16)] + work)
    else:
        *block, out = call(
            first, (shape(*left, dtype=bf16), shape(*right, dtype=bf16), block_out),
            *row_blocks, *column_blocks, scratch=work)
    out, step_scalars = call(
        functools.partial(second_kernel, wide, narrow, keep),
        (shape(devices, 1, (halves + 1) * LANES), shape(1 + 2 * halves, LANES)),
        to_all(out, ALL), *block,
        scratch=[scratch(devices * halves, LANES)] * 3 + [scratch(lines, LANES), sums])
    answer, residual = call(
        functools.partial(last_kernel, narrow), (shape(halves, LANES), shape(halves, LANES)),
        to_all(out, ALL), step_scalars,
        out_specs=(pl.BlockSpec(memory_space=pl.ANY),) * 2,
        scratch=[scratch(2, halves, LANES), pltpu.SemaphoreType.DMA((2,))])
    return answer.reshape(rows), residual.reshape(rows)


def solution(mesh):
    wide, narrow = mesh.shape["wide"], mesh.shape["narrow"]
    split = jax.sharding.Mesh(mesh.devices.reshape(wide // 2, 2, narrow // 2, 2), ALL)
    in_specs = (P(ALL, None), P(), P(ALL))
    return jax.shard_map(
        functools.partial(on_device, wide, narrow), mesh=split,
        in_specs=in_specs, out_specs=(P(ALL), P(ALL)), check_vma=False,
    )
```

```python
import functools
import math

import jax
import jax.numpy as jnp
from jax import lax
from jax.experimental import pallas as pl
from jax.experimental.pallas import tpu as pltpu
from jax.sharding import PartitionSpec as P

noise_var = 0.5
LANES = 128
CHUNKS = 8
DIRECT = 8
KEEP_BYTES = 8 * 2**20
VMEM_BYTES = 32 * 2**20
WHOLE_VMEM_BYTES = (53 * 1024 + 870) * 2**10
Z, Y, X, CORE = "z", "y", "x", "core"
ALL = (Z, Y, X, CORE)
highest = lax.Precision.HIGHEST
f32 = jnp.float32
bf16 = jnp.bfloat16


def split3(values):
    high = values.astype(bf16)
    rest = values - high.astype(f32)
    mid = rest.astype(bf16)
    low = (rest - mid.astype(f32)).astype(bf16)
    return high, mid, low


def exponent_rows(first, second):
    width = (first if not isinstance(first, float) else second).shape[1]
    row = lax.broadcasted_iota(jnp.int32, (16, width), 0)
    out = jnp.zeros((16, width), f32)
    for base, value in ((0, first), (3, second)):
        parts = (1.0, 1.0, 1.0) if isinstance(value, float) else [p.astype(f32) for p in split3(value)]
        for k, part in enumerate(parts):
            out = jnp.where(row == base + k, part, out)
    return out.astype(bf16)


def right_operand(latent, scale):
    square = jnp.sum(latent * latent, axis=0, keepdims=True) * scale
    h, m, l = split3(latent)
    return jnp.concatenate([h, m, l, h, m, h, exponent_rows(square, 1.0)], axis=0)


def left_operand(latent, scale):
    square = jnp.sum(latent * latent, axis=0, keepdims=True) * scale
    h, m, l = split3(latent * (-2.0 * scale))
    stacked = jnp.concatenate([h, h, h, m, m, l, exponent_rows(1.0, square)], axis=0)
    return stacked.T


def place():
    return tuple(lax.axis_index(name) for name in ALL)


def device_at(z, y, x, core, narrow):
    return ((z * 2 + y) * (narrow // 2) + x) * 2 + core


def part_base(part, parts, narrow):
    return 0 if parts == 1 else jnp.bitwise_xor(lax.axis_index(Y), part) * (narrow // 2)


def row_sources(blocks, flips):
    spots = [(b, i) for b in blocks for i in range(b.shape[0])]
    if flips is None:
        return [(b, i, i) for b, i in spots]
    x = lax.axis_index(X)
    return [(b, i, jnp.bitwise_xor(x, flip)) for (b, i), flip in zip(spots, flips)]


def column_sources(blocks, wide, flips):
    if flips is None:
        return [(blocks[0], i, i) for i in range(wide)]
    z, y, x, core = place()
    spots = [(b, i) for b in blocks for i in range(b.shape[0])]
    return [(b, i, jnp.bitwise_xor(z, z_flip) * 2 + jnp.bitwise_xor(core, core_flip))
            for (b, i), (z_flip, core_flip) in zip(spots, flips)]


def total_sum(values):
    return jnp.sum(jnp.sum(values, axis=0, keepdims=True), axis=1, keepdims=True)


def lane_sums(values):
    parts = jnp.concatenate(split3(values), axis=1)
    ones = jnp.ones((16, parts.shape[1]), bf16)
    return lax.dot_general(ones, parts, (((1,), (1,)), ((), ())),
                           preferred_element_type=f32)[0:1, :]


def make_rows(left, right, kept, read_vector, sums):
    groups, rows, _ = left.shape
    columns = right.shape[0]
    halves = rows // LANES

    def one_group(g, _):
        left_group = left[g]

        def one_column(c, acc):
            exponent = jnp.dot(left_group, right[c], preferred_element_type=f32)
            tile = jnp.exp2(exponent)
            if kept is not None:
                kept[g, c] = tile
            for half in range(halves):
                acc = acc + tile[:, half * LANES:(half + 1) * LANES] * read_vector(c, half)
            return acc

        sums[g] = lax.fori_loop(0, columns, one_column, jnp.zeros((rows, LANES), f32), unroll=8)
        return 0

    lax.fori_loop(0, groups, one_group, 0)


def use_rows(kept, read_vector, sums):
    groups, columns, rows, _ = kept.shape
    halves = rows // LANES

    def one_group(g, _):
        def one_column(c, acc):
            for half in range(halves):
                acc = acc + kept[g, c, :, half * LANES:(half + 1) * LANES] * read_vector(c, half)
            return acc

        sums[g] = lax.fori_loop(0, columns, one_column, jnp.zeros((rows, LANES), f32), unroll=8)
        return 0

    lax.fori_loop(0, groups, one_group, 0)


def write_rows(sums, out, bases):
    groups, rows, _ = sums.shape
    halves = rows // LANES
    total = lane_sums(sums[...].reshape(groups * rows, LANES))
    for g in range(groups):
        base = bases[g * len(bases) // groups]
        for half in range(halves):
            line = (base + g % (groups // len(bases))) * halves + half
            start = (g * halves + half) * LANES
            out[pl.ds(line, 1), :] = total[:, start:start + LANES]


def project_kernel(features, projection_t, targets, out, feature_buf, projection_buf, target_buf, sems):
    proj = projection_t.shape[0]
    chunks, _, width = feature_buf.shape
    copies = [pltpu.make_async_copy(projection_t, projection_buf, sems.at[0])]
    copies += [
        pltpu.make_async_copy(features.at[:, pl.ds(i * width, width)], feature_buf.at[i], sems.at[i + 1])
        for i in range(chunks)]
    copies += [pltpu.make_async_copy(targets, target_buf, sems.at[chunks + 1])]
    for copy in copies:
        copy.start()
    copies[0].wait()
    latent = jnp.zeros((proj, features.shape[0]), f32)
    for i in range(chunks):
        copies[i + 1].wait()
        latent = latent + lax.dot_general(
            projection_buf[:, i * width:(i + 1) * width], feature_buf[i],
            (((1,), (1,)), ((), ())), preferred_element_type=f32)
    out[0, 0:proj, :] = latent
    copies[-1].wait()
    out[0, proj:proj + 8, :] = jnp.broadcast_to(target_buf[...], (8, out.shape[2]))


def first_kernel(proj, scale, wide, keep, flips, row_count, column_count, *refs):
    row_blocks, column_blocks = refs[:row_count], refs[row_count:row_count + column_count]
    refs = refs[row_count + column_count:]
    right, column_vector = refs[:2]
    kept, left = (refs[2], refs[-2]) if keep else (None, refs[2])
    partial, starts, sums = refs[3], refs[4] if column_count else None, refs[-1]
    rows = left.shape[1]
    halves = rows // LANES
    for block, i, source in column_sources(column_blocks, wide, flips[1]) if column_count else ():
        right[source] = right_operand(block[i, 0:proj, :], scale)
        for half in range(halves):
            column_vector[pl.ds(source * halves + half, 1), :] = block[
                i, proj:proj + 1, half * LANES:(half + 1) * LANES]
    for block, i, source in row_sources(row_blocks, flips[0]):
        left[source] = left_operand(block[i, 0:proj, :], scale)
        for half in range(halves) if column_count else ():
            starts[pl.ds(source * halves + half, 1), :] = block[
                i, proj:proj + 1, half * LANES:(half + 1) * LANES]
    make_rows(left, right, kept, lambda c, half: column_vector[pl.ds(c * halves + half, 1), :], sums)
    write_rows(sums, partial, [0])


def message_kernel(parts, narrow, halves, *refs):
    partials, start, out, held = refs[:parts], refs[parts], refs[-2], refs[-1]
    for part, lines in enumerate(partials):
        base = part_base(part, parts, narrow) * halves
        for line in range(lines.shape[0]):
            held[pl.ds(base + line, 1), :] = lines[line:line + 1, :]
    mine = lax.axis_index(X) * halves
    if parts == 1:
        mine = mine + lax.axis_index(Y) * (narrow // 2) * halves
    pieces = [held[line:line + 1, :] for line in range(held.shape[0])]
    pieces += [start[pl.ds(mine + half, 1), :] for half in range(halves)]
    block = jnp.concatenate(pieces, axis=1)

    def copy(i, _):
        out[i] = block
        return 0

    lax.fori_loop(0, out.shape[0], copy, 0, unroll=8)


def second_kernel(wide, narrow, keep, parts, *refs):
    arrived, out, step_scalars, direction, images, targets, partial, sums = refs[:1] + refs[-7:]
    lines = partial.shape[0]
    halves = lines // narrow
    across = narrow // 2
    group = [(y, x) for y in range(2) for x in range(across)]

    def unpack(z, _):
        for core in range(2):
            members = [device_at(z, y, x, core, narrow) for y, x in group]
            total = arrived[members[0]]
            for member in members[1:]:
                total = total + arrived[member]
            for r, member in enumerate(members):
                for half in range(halves):
                    start = arrived[member, :, (lines + half) * LANES:(lines + half + 1) * LANES]
                    line = r * halves + half
                    spot = pl.ds(member * halves + half, 1)
                    targets[spot, :] = start
                    images[spot, :] = total[:, line * LANES:(line + 1) * LANES] + noise_var * start
        return 0

    lax.fori_loop(0, wide // 2, unpack, 0, unroll=4)
    start, first = targets[...], images[...]
    norm = total_sum(start * start)
    alpha = norm / total_sum(start * first)
    residual = start - alpha * first
    norm_next = total_sum(residual * residual)
    beta = norm_next / norm
    whole = residual + beta * start
    direction[...] = whole
    z, y, x, core = place()

    def read_vector(c, half):
        return direction[pl.ds(device_at(c // 2, y, x, c % 2, narrow) * halves + half, 1), :]

    groups = narrow // parts
    for part in range(parts):
        part_sums = sums.at[part * groups:(part + 1) * groups]
        if keep:
            use_rows(refs[1 + part], read_vector, part_sums)
        else:
            make_rows(refs[2 + part], refs[1], None, read_vector, part_sums)
    write_rows(sums, partial, [part_base(part, parts, narrow) for part in range(parts)])
    share = jnp.zeros((1, LANES), f32)
    for r, (row_y, row_x) in enumerate(group):
        for half in range(halves):
            spot = pl.ds(device_at(z, row_y, row_x, core, narrow) * halves + half, 1)
            line = r * halves + half
            share = share + direction[spot, :] * partial[line:line + 1, :]
    blocks = [
        jnp.concatenate([partial[r * halves + half:r * halves + half + 1, :]
                         for half in range(halves)] + [share], axis=1)
        for r in range(narrow)]

    def copy(to_z, _):
        for r, (to_y, to_x) in enumerate(group):
            for to_core in range(2):
                out[device_at(to_z, to_y, to_x, to_core, narrow)] = blocks[r]
        return 0

    lax.fori_loop(0, wide // 2, copy, 0, unroll=4)
    lane = lax.broadcasted_iota(jnp.int32, (1, LANES), 1)
    noise = noise_var * total_sum(whole * whole)
    step_scalars[0:1, :] = jnp.where(lane == 0, alpha, jnp.where(
        lane == 1, norm_next, jnp.where(lane == 2, beta, noise)))
    for half in range(halves):
        spot = pl.ds(device_at(z, y, x, core, narrow) * halves + half, 1)
        step_scalars[1 + half:2 + half, :] = images[spot, :]
        step_scalars[1 + halves + half:2 + halves + half, :] = targets[spot, :]


def last_kernel(narrow, arrived, step_scalars, solution_out, residual_out, answer, sems):
    alpha = step_scalars[0:1, 0:1]
    norm = step_scalars[0:1, 1:2]
    beta = step_scalars[0:1, 2:3]
    noise = step_scalars[0:1, 3:4]
    halves = answer.shape[1]

    def add(i, total):
        return total + arrived[i, :, halves * LANES:(halves + 1) * LANES]

    share = lax.fori_loop(0, arrived.shape[0], add, jnp.zeros((1, LANES), f32), unroll=8)
    alpha_next = norm / (total_sum(share) + noise)
    z, _, _, core = place()
    product = jnp.zeros((1, (halves + 1) * LANES), f32)
    for y in range(2):
        for x in range(narrow // 2):
            product = product + arrived[device_at(z, y, x, core, narrow)]
    for half in range(halves):
        begin = step_scalars[1 + halves + half:2 + halves + half, :]
        residual = begin - alpha * step_scalars[1 + half:2 + half, :]
        direction = residual + beta * begin
        image = product[:, half * LANES:(half + 1) * LANES] + noise_var * direction
        answer[0, half:half + 1, :] = alpha * begin + alpha_next * direction
        answer[1, half:half + 1, :] = residual - alpha_next * image
    copies = [pltpu.make_async_copy(answer.at[i], out, sems.at[i])
              for i, out in enumerate((solution_out, residual_out))]
    for copy in copies:
        copy.start()
    for copy in copies:
        copy.wait()


def call(kernel, out_shape, *args, scratch=(), vmem=VMEM_BYTES, **options):
    return pl.pallas_call(
        kernel,
        out_shape=out_shape,
        scratch_shapes=list(scratch),
        compiler_params=pltpu.CompilerParams(vmem_limit_bytes=vmem),
        **options,
    )(*args)


def to_all(blocks, axes):
    return lax.all_to_all(blocks, axes, split_axis=0, concat_axis=0, tiled=True)


def join_kernel(*refs):
    i = 0
    for block in refs[:-1]:
        for j in range(block.shape[0]):
            refs[-1][i] = block[j]
            i += 1


def join(*blocks):
    total = sum(b.shape[0] for b in blocks)
    return call(join_kernel, jax.ShapeDtypeStruct((total, *blocks[0].shape[1:]), f32), *blocks)


def first_round(own, wide, narrow):
    depth, across = wide // 2, narrow // 2
    if depth & (depth - 1) or across & (across - 1) or depth > DIRECT:
        every = lax.all_gather(own, ALL, axis=0, tiled=True)
        every = every.reshape(depth, 2, across, 2, *own.shape[1:])
        z, y, x, core = place()
        rows = lax.dynamic_index_in_dim(every, z, 0, keepdims=False)
        rows = lax.dynamic_index_in_dim(rows, core, 2, keepdims=False)
        columns = lax.dynamic_index_in_dim(every, y, 1, keepdims=False)
        columns = lax.dynamic_index_in_dim(columns, x, 1, keepdims=False)
        return ([[rows.reshape(narrow, *own.shape[1:])]], [columns.reshape(wide, *own.shape[1:])],
                (None, None))

    def swap(value, axis, size, flip):
        return lax.ppermute(value, axis, [(i, i ^ flip) for i in range(size)])

    rows, row_flips = own, [0]
    for k in range(across.bit_length() - 1):
        rows = join(rows, swap(rows, X, across, 1 << k))
        row_flips += [f ^ (1 << k) for f in row_flips]
    z_flips = [0, 1, *range(depth - 1, 1, -1)][:depth]
    columns = [own] + [swap(own, Z, depth, flip) for flip in z_flips[1:]]
    columns += [swap(block, CORE, 2, 1) for block in columns]
    parts = [[rows], [swap(rows, Y, 2, 1)]]
    return parts, columns, (row_flips, [(f, c) for c in range(2) for f in z_flips])


def on_device(wide, narrow, features, projection, targets):
    rows, proj = features.shape[0], projection.shape[1]
    halves = rows // LANES
    lines = narrow * halves
    devices = wide * narrow
    scale = -2.0 / proj * math.log2(math.e)
    depth = 6 * proj + 16
    keep = 4 * devices * rows * rows <= KEEP_BYTES

    def shape(*dims, dtype=f32):
        return jax.ShapeDtypeStruct(dims, dtype)

    def scratch(*dims, dtype=f32):
        return pltpu.VMEM(dims, dtype)

    feat = features.shape[1]
    own = call(
        project_kernel, shape(1, proj + 8, rows), features, projection.T, targets.reshape(1, rows),
        in_specs=[pl.BlockSpec(memory_space=pl.ANY)] * 3, vmem=WHOLE_VMEM_BYTES,
        scratch=[scratch(CHUNKS, rows, feat // CHUNKS, dtype=bf16), scratch(proj, feat, dtype=bf16),
                 scratch(1, rows), pltpu.SemaphoreType.DMA((CHUNKS + 2,))])
    row_parts, column_blocks, flips = first_round(own, wide, narrow)
    parts = len(row_parts)
    groups = narrow // parts
    left = shape(groups, rows, depth, dtype=bf16)
    right = shape(wide, depth, rows, dtype=bf16)
    vector = shape(wide * halves, LANES)
    kept = shape(groups, wide, rows, rows) if keep else left
    group_lines = shape(groups * halves, LANES)
    sums = scratch(groups, rows, LANES)
    work = [scratch(*left.shape, dtype=bf16), sums] if keep else [sums]
    blocks, partials = [], []
    for part, row_blocks in enumerate(row_parts):
        fresh = part == 0
        first = functools.partial(
            first_kernel, proj, scale, wide, keep, flips, len(row_blocks),
            len(column_blocks) if fresh else 0)
        tiles = groups * wide * rows * rows
        made = call(
            first, (right, vector, kept, group_lines, group_lines) if fresh else (kept, group_lines),
            *row_blocks, *(column_blocks if fresh else columns_made), scratch=work,
            cost_estimate=pl.CostEstimate(
                flops=2 * tiles * depth, bytes_accessed=4 * tiles, transcendentals=tiles))
        if fresh:
            *columns_made, block, partial, own_start = made
        else:
            block, partial = made
        blocks.append(block)
        partials.append(partial)
    out = call(
        functools.partial(message_kernel, parts, narrow, halves),
        shape(devices, 1, (lines + halves) * LANES), *partials, own_start,
        scratch=[scratch(lines, LANES)])
    block = blocks if keep else [columns_made[0], *blocks]
    sums = scratch(narrow, rows, LANES)
    out, step_scalars = call(
        functools.partial(second_kernel, wide, narrow, keep, parts),
        (shape(devices, 1, (halves + 1) * LANES), shape(1 + 2 * halves, LANES)),
        to_all(out, ALL), *block,
        scratch=[scratch(devices * halves, LANES)] * 3 + [scratch(lines, LANES), sums])
    answer, residual = call(
        functools.partial(last_kernel, narrow), (shape(halves, LANES), shape(halves, LANES)),
        to_all(out, ALL), step_scalars,
        out_specs=(pl.BlockSpec(memory_space=pl.ANY),) * 2,
        scratch=[scratch(2, halves, LANES), pltpu.SemaphoreType.DMA((2,))])
    return answer.reshape(rows), residual.reshape(rows)


def solution(mesh):
    wide, narrow = mesh.shape["wide"], mesh.shape["narrow"]
    split = jax.sharding.Mesh(mesh.devices.reshape(wide // 2, 2, narrow // 2, 2), ALL)
    in_specs = (P(ALL, None), P(), P(ALL))
    return jax.shard_map(
        functools.partial(on_device, wide, narrow), mesh=split,
        in_specs=in_specs, out_specs=(P(ALL), P(ALL)), check_vma=False,
    )
```

```python
import functools
import math

import jax
import jax.numpy as jnp
from jax import lax
from jax.experimental import pallas as pl
from jax.experimental.pallas import tpu as pltpu
from jax.sharding import PartitionSpec as P

noise_var = 0.5
LANES = 128
CHUNKS = 8
DIRECT = 8
KEEP_BYTES = 8 * 2**20
VMEM_BYTES = 32 * 2**20
WHOLE_VMEM_BYTES = (53 * 1024 + 870) * 2**10
HIGH, LOW, Y, X, CORE = "high", "low", "y", "x", "core"
ALL = (HIGH, LOW, Y, X, CORE)
highest = lax.Precision.HIGHEST
f32 = jnp.float32
bf16 = jnp.bfloat16


def split3(values):
    high = values.astype(bf16)
    rest = values - high.astype(f32)
    mid = rest.astype(bf16)
    low = (rest - mid.astype(f32)).astype(bf16)
    return high, mid, low


def exponent_rows(first, second):
    width = (first if not isinstance(first, float) else second).shape[1]
    row = lax.broadcasted_iota(jnp.int32, (16, width), 0)
    out = jnp.zeros((16, width), f32)
    for base, value in ((0, first), (3, second)):
        parts = (1.0, 1.0, 1.0) if isinstance(value, float) else [p.astype(f32) for p in split3(value)]
        for k, part in enumerate(parts):
            out = jnp.where(row == base + k, part, out)
    return out.astype(bf16)


def right_operand(latent, scale):
    square = jnp.sum(latent * latent, axis=0, keepdims=True) * scale
    h, m, l = split3(latent)
    return jnp.concatenate([h, m, l, h, m, h, exponent_rows(square, 1.0)], axis=0)


def left_operand(latent, scale):
    square = jnp.sum(latent * latent, axis=0, keepdims=True) * scale
    h, m, l = split3(latent * (-2.0 * scale))
    stacked = jnp.concatenate([h, h, h, m, m, l, exponent_rows(1.0, square)], axis=0)
    return stacked.T


def place():
    return tuple(lax.axis_index(name) for name in ALL)


def device_at(high, low, y, x, core, wide, narrow):
    return (((high * (wide // 4) + low) * 2 + y) * (narrow // 2) + x) * 2 + core


def part_base(part, parts):
    return 0 if parts == 1 else jnp.bitwise_xor(lax.axis_index(X), part) * 2


def row_sources(blocks, flips):
    spots = [(b, i) for b in blocks for i in range(b.shape[0])]
    if flips is None:
        return [(b, i, i) for b, i in spots]
    high = lax.axis_index(HIGH)
    return [(b, i, jnp.bitwise_xor(high, flip)) for (b, i), flip in zip(spots, flips)]


def column_sources(blocks, flips):
    spots = [(b, i) for b in blocks for i in range(b.shape[0])]
    if flips is None:
        return [(b, i, i) for b, i in spots]
    _, low, y, _, core = place()
    return [(b, i, (jnp.bitwise_xor(low, f) * 2 + jnp.bitwise_xor(y, g)) * 2 + jnp.bitwise_xor(core, h))
            for (b, i), (f, g, h) in zip(spots, flips)]


def total_sum(values):
    return jnp.sum(jnp.sum(values, axis=0, keepdims=True), axis=1, keepdims=True)


def lane_sums(values):
    parts = jnp.concatenate(split3(values), axis=1)
    ones = jnp.ones((16, parts.shape[1]), bf16)
    return lax.dot_general(ones, parts, (((1,), (1,)), ((), ())),
                           preferred_element_type=f32)[0:1, :]


def make_rows(left, right, kept, read_vector, sums):
    groups, rows, _ = left.shape
    columns = right.shape[0]
    halves = rows // LANES

    def one_group(g, _):
        left_group = left[g]

        def one_column(c, acc):
            exponent = jnp.dot(left_group, right[c], preferred_element_type=f32)
            tile = jnp.exp2(exponent)
            if kept is not None:
                kept[g, c] = tile
            for half in range(halves):
                acc = acc + tile[:, half * LANES:(half + 1) * LANES] * read_vector(c, half)
            return acc

        sums[g] = lax.fori_loop(0, columns, one_column, jnp.zeros((rows, LANES), f32), unroll=8)
        return 0

    lax.fori_loop(0, groups, one_group, 0)


def use_rows(kept, read_vector, sums):
    groups, columns, rows, _ = kept.shape
    halves = rows // LANES

    def one_group(g, _):
        def one_column(c, acc):
            for half in range(halves):
                acc = acc + kept[g, c, :, half * LANES:(half + 1) * LANES] * read_vector(c, half)
            return acc

        sums[g] = lax.fori_loop(0, columns, one_column, jnp.zeros((rows, LANES), f32), unroll=8)
        return 0

    lax.fori_loop(0, groups, one_group, 0)


def write_rows(sums, out, bases):
    groups, rows, _ = sums.shape
    halves = rows // LANES
    total = lane_sums(sums[...].reshape(groups * rows, LANES))
    for g in range(groups):
        base = bases[g * len(bases) // groups]
        for half in range(halves):
            line = (base + g % (groups // len(bases))) * halves + half
            start = (g * halves + half) * LANES
            out[pl.ds(line, 1), :] = total[:, start:start + LANES]


def project_kernel(features, projection_t, targets, out, feature_buf, projection_buf, target_buf, sems):
    proj = projection_t.shape[0]
    chunks, _, width = feature_buf.shape
    copies = [pltpu.make_async_copy(projection_t, projection_buf, sems.at[0])]
    copies += [
        pltpu.make_async_copy(features.at[:, pl.ds(i * width, width)], feature_buf.at[i], sems.at[i + 1])
        for i in range(chunks)]
    copies += [pltpu.make_async_copy(targets, target_buf, sems.at[chunks + 1])]
    for copy in copies:
        copy.start()
    copies[0].wait()
    latent = jnp.zeros((proj, features.shape[0]), f32)
    for i in range(chunks):
        copies[i + 1].wait()
        latent = latent + lax.dot_general(
            projection_buf[:, i * width:(i + 1) * width], feature_buf[i],
            (((1,), (1,)), ((), ())), preferred_element_type=f32)
    out[0, 0:proj, :] = latent
    copies[-1].wait()
    out[0, proj:proj + 8, :] = jnp.broadcast_to(target_buf[...], (8, out.shape[2]))


def first_kernel(proj, scale, wide, keep, flips, row_count, column_count, *refs):
    row_blocks, column_blocks = refs[:row_count], refs[row_count:row_count + column_count]
    refs = refs[row_count + column_count:]
    right, column_vector = refs[:2]
    kept, left = (refs[2], refs[-2]) if keep else (None, refs[2])
    partial, starts, sums = refs[3], refs[4] if column_count else None, refs[-1]
    rows = left.shape[1]
    halves = rows // LANES
    for block, i, source in column_sources(column_blocks, flips[1]) if column_count else ():
        right[source] = right_operand(block[i, 0:proj, :], scale)
        for half in range(halves):
            column_vector[pl.ds(source * halves + half, 1), :] = block[
                i, proj:proj + 1, half * LANES:(half + 1) * LANES]
    for block, i, source in row_sources(row_blocks, flips[0]):
        left[source] = left_operand(block[i, 0:proj, :], scale)
        for half in range(halves) if column_count else ():
            starts[pl.ds(source * halves + half, 1), :] = block[
                i, proj:proj + 1, half * LANES:(half + 1) * LANES]
    make_rows(left, right, kept, lambda c, half: column_vector[pl.ds(c * halves + half, 1), :], sums)
    write_rows(sums, partial, [0])


def message_kernel(parts, halves, *refs):
    partials, start, out, held = refs[:parts], refs[parts], refs[-2], refs[-1]
    for part, lines in enumerate(partials):
        base = part_base(part, parts) * halves
        for line in range(lines.shape[0]):
            held[pl.ds(base + line, 1), :] = lines[line:line + 1, :]
    mine = lax.axis_index(HIGH) * halves
    if parts == 1:
        mine = mine + lax.axis_index(X) * 2 * halves
    pieces = [held[line:line + 1, :] for line in range(held.shape[0])]
    pieces += [start[pl.ds(mine + half, 1), :] for half in range(halves)]
    block = jnp.concatenate(pieces, axis=1)

    def copy(i, _):
        out[i] = block
        return 0

    lax.fori_loop(0, out.shape[0], copy, 0, unroll=8)


def second_kernel(wide, narrow, keep, parts, *refs):
    arrived, out, step_scalars, direction, images, targets, partial, sums = refs[:1] + refs[-7:]
    lines = partial.shape[0]
    halves = lines // narrow
    across = narrow // 2
    group = [(high, x) for x in range(narrow // 2) for high in range(2)]

    def unpack(low, _):
        for y, core in ((0, 0), (0, 1), (1, 0), (1, 1)):
            members = [device_at(high, low, y, x, core, wide, narrow) for high, x in group]
            total = arrived[members[0]]
            for member in members[1:]:
                total = total + arrived[member]
            for r, member in enumerate(members):
                for half in range(halves):
                    start = arrived[member, :, (lines + half) * LANES:(lines + half + 1) * LANES]
                    line = r * halves + half
                    spot = pl.ds(member * halves + half, 1)
                    targets[spot, :] = start
                    images[spot, :] = total[:, line * LANES:(line + 1) * LANES] + noise_var * start
        return 0

    lax.fori_loop(0, wide // 4, unpack, 0, unroll=2)
    start, first = targets[...], images[...]
    norm = total_sum(start * start)
    alpha = norm / total_sum(start * first)
    residual = start - alpha * first
    norm_next = total_sum(residual * residual)
    beta = norm_next / norm
    whole = residual + beta * start
    direction[...] = whole
    high, low, y, x, core = place()

    def read_vector(c, half):
        source = device_at(high, c // 4, c // 2 % 2, x, c % 2, wide, narrow)
        return direction[pl.ds(source * halves + half, 1), :]

    groups = narrow // parts
    for part in range(parts):
        part_sums = sums.at[part * groups:(part + 1) * groups]
        if keep:
            use_rows(refs[1 + part], read_vector, part_sums)
        else:
            make_rows(refs[2 + part], refs[1], None, read_vector, part_sums)
    write_rows(sums, partial, [part_base(part, parts) for part in range(parts)])
    share = jnp.zeros((1, LANES), f32)
    for r, (row_high, row_x) in enumerate(group):
        for half in range(halves):
            spot = pl.ds(device_at(row_high, low, y, row_x, core, wide, narrow) * halves + half, 1)
            line = r * halves + half
            share = share + direction[spot, :] * partial[line:line + 1, :]
    blocks = [
        jnp.concatenate([partial[r * halves + half:r * halves + half + 1, :]
                         for half in range(halves)] + [share], axis=1)
        for r in range(narrow)]

    def copy(to_low, _):
        for r, (to_high, to_x) in enumerate(group):
            for to_y, to_core in ((0, 0), (0, 1), (1, 0), (1, 1)):
                out[device_at(to_high, to_low, to_y, to_x, to_core, wide, narrow)] = blocks[r]
        return 0

    lax.fori_loop(0, wide // 4, copy, 0, unroll=2)
    lane = lax.broadcasted_iota(jnp.int32, (1, LANES), 1)
    noise = noise_var * total_sum(whole * whole)
    step_scalars[0:1, :] = jnp.where(lane == 0, alpha, jnp.where(
        lane == 1, norm_next, jnp.where(lane == 2, beta, noise)))
    for half in range(halves):
        spot = pl.ds(device_at(high, low, y, x, core, wide, narrow) * halves + half, 1)
        step_scalars[1 + half:2 + half, :] = images[spot, :]
        step_scalars[1 + halves + half:2 + halves + half, :] = targets[spot, :]


def last_kernel(wide, narrow, arrived, step_scalars, solution_out, residual_out, answer, sems):
    alpha = step_scalars[0:1, 0:1]
    norm = step_scalars[0:1, 1:2]
    beta = step_scalars[0:1, 2:3]
    noise = step_scalars[0:1, 3:4]
    halves = answer.shape[1]

    def add(i, total):
        return total + arrived[i, :, halves * LANES:(halves + 1) * LANES]

    share = lax.fori_loop(0, arrived.shape[0], add, jnp.zeros((1, LANES), f32), unroll=8)
    alpha_next = norm / (total_sum(share) + noise)
    _, low, y, _, core = place()
    product = jnp.zeros((1, (halves + 1) * LANES), f32)
    for high in range(2):
        for x in range(narrow // 2):
            product = product + arrived[device_at(high, low, y, x, core, wide, narrow)]
    for half in range(halves):
        begin = step_scalars[1 + halves + half:2 + halves + half, :]
        residual = begin - alpha * step_scalars[1 + half:2 + half, :]
        direction = residual + beta * begin
        image = product[:, half * LANES:(half + 1) * LANES] + noise_var * direction
        answer[0, half:half + 1, :] = alpha * begin + alpha_next * direction
        answer[1, half:half + 1, :] = residual - alpha_next * image
    copies = [pltpu.make_async_copy(answer.at[i], out, sems.at[i])
              for i, out in enumerate((solution_out, residual_out))]
    for copy in copies:
        copy.start()
    for copy in copies:
        copy.wait()


def call(kernel, out_shape, *args, scratch=(), vmem=VMEM_BYTES, **options):
    return pl.pallas_call(
        kernel,
        out_shape=out_shape,
        scratch_shapes=list(scratch),
        compiler_params=pltpu.CompilerParams(vmem_limit_bytes=vmem),
        **options,
    )(*args)


def to_all(blocks, axes):
    return lax.all_to_all(blocks, axes, split_axis=0, concat_axis=0, tiled=True)


def join_kernel(*refs):
    i = 0
    for block in refs[:-1]:
        for j in range(block.shape[0]):
            refs[-1][i] = block[j]
            i += 1


def join(*blocks):
    total = sum(b.shape[0] for b in blocks)
    return call(join_kernel, jax.ShapeDtypeStruct((total, *blocks[0].shape[1:]), f32), *blocks)


def first_round(own, wide, narrow):
    lows, across = wide // 4, narrow // 2
    if lows & (lows - 1) or across != 2 or lows > DIRECT:
        every = lax.all_gather(own, ALL, axis=0, tiled=True)
        every = every.reshape(2, lows, 2, across, 2, *own.shape[1:])
        high, low, y, x, core = place()
        rows = every
        for place_in, axis in ((low, 1), (y, 1), (core, 2)):
            rows = lax.dynamic_index_in_dim(rows, place_in, axis, keepdims=False)
        columns = lax.dynamic_index_in_dim(every, high, 0, keepdims=False)
        columns = lax.dynamic_index_in_dim(columns, x, 2, keepdims=False)
        rows = jnp.swapaxes(rows, 0, 1).reshape(narrow, *own.shape[1:])
        return [[rows]], [columns.reshape(wide, *own.shape[1:])], (None, None)

    def swap(value, axis, size=2, flip=1):
        return lax.ppermute(value, axis, [(i, i ^ flip) for i in range(size)])

    rows = join(own, swap(own, HIGH))
    columns = [own] + [swap(own, (LOW, Y), 2 * lows, flip) for flip in range(1, 2 * lows)]
    columns += [swap(block, CORE) for block in columns]
    parts = [[rows], [swap(rows, X)]]
    flips = [(flip // 2, flip % 2, core) for core in range(2) for flip in range(2 * lows)]
    return parts, columns, ([0, 1], flips)


def on_device(wide, narrow, features, projection, targets):
    rows, proj = features.shape[0], projection.shape[1]
    halves = rows // LANES
    lines = narrow * halves
    devices = wide * narrow
    scale = -2.0 / proj * math.log2(math.e)
    depth = 6 * proj + 16
    keep = 4 * devices * rows * rows <= KEEP_BYTES

    def shape(*dims, dtype=f32):
        return jax.ShapeDtypeStruct(dims, dtype)

    def scratch(*dims, dtype=f32):
        return pltpu.VMEM(dims, dtype)

    feat = features.shape[1]
    own = call(
        project_kernel, shape(1, proj + 8, rows), features, projection.T, targets.reshape(1, rows),
        in_specs=[pl.BlockSpec(memory_space=pl.ANY)] * 3, vmem=WHOLE_VMEM_BYTES,
        scratch=[scratch(CHUNKS, rows, feat // CHUNKS, dtype=bf16), scratch(proj, feat, dtype=bf16),
                 scratch(1, rows), pltpu.SemaphoreType.DMA((CHUNKS + 2,))])
    row_parts, column_blocks, flips = first_round(own, wide, narrow)
    parts = len(row_parts)
    groups = narrow // parts
    left = shape(groups, rows, depth, dtype=bf16)
    right = shape(wide, depth, rows, dtype=bf16)
    vector = shape(wide * halves, LANES)
    kept = shape(groups, wide, rows, rows) if keep else left
    group_lines = shape(groups * halves, LANES)
    sums = scratch(groups, rows, LANES)
    work = [scratch(*left.shape, dtype=bf16), sums] if keep else [sums]
    blocks, partials = [], []
    for part, row_blocks in enumerate(row_parts):
        fresh = part == 0
        first = functools.partial(
            first_kernel, proj, scale, wide, keep, flips, len(row_blocks),
            len(column_blocks) if fresh else 0)
        tiles = groups * wide * rows * rows
        made = call(
            first, (right, vector, kept, group_lines, group_lines) if fresh else (kept, group_lines),
            *row_blocks, *(column_blocks if fresh else columns_made), scratch=work,
            cost_estimate=pl.CostEstimate(
                flops=2 * tiles * depth, bytes_accessed=4 * tiles, transcendentals=tiles))
        if fresh:
            *columns_made, block, partial, own_start = made
        else:
            block, partial = made
        blocks.append(block)
        partials.append(partial)
    out = call(
        functools.partial(message_kernel, parts, halves),
        shape(devices, 1, (lines + halves) * LANES), *partials, own_start,
        scratch=[scratch(lines, LANES)])
    block = blocks if keep else [columns_made[0], *blocks]
    sums = scratch(narrow, rows, LANES)
    out, step_scalars = call(
        functools.partial(second_kernel, wide, narrow, keep, parts),
        (shape(devices, 1, (halves + 1) * LANES), shape(1 + 2 * halves, LANES)),
        to_all(out, ALL), *block,
        scratch=[scratch(devices * halves, LANES)] * 3 + [scratch(lines, LANES), sums])
    answer, residual = call(
        functools.partial(last_kernel, wide, narrow), (shape(halves, LANES), shape(halves, LANES)),
        to_all(out, ALL), step_scalars,
        out_specs=(pl.BlockSpec(memory_space=pl.ANY),) * 2,
        scratch=[scratch(2, halves, LANES), pltpu.SemaphoreType.DMA((2,))])
    return answer.reshape(rows), residual.reshape(rows)


def solution(mesh):
    wide, narrow = mesh.shape["wide"], mesh.shape["narrow"]
    split = jax.sharding.Mesh(mesh.devices.reshape(2, wide // 4, 2, narrow // 2, 2), ALL)
    in_specs = (P(ALL, None), P(), P(ALL))
    return jax.shard_map(
        functools.partial(on_device, wide, narrow), mesh=split,
        in_specs=in_specs, out_specs=(P(ALL), P(ALL)), check_vma=False,
    )
```

```python
import functools
import math

import jax
import jax.numpy as jnp
from jax import lax
from jax.experimental import pallas as pl
from jax.experimental.pallas import tpu as pltpu
from jax.sharding import PartitionSpec as P

noise_var = 0.5
LANES = 128
CHUNKS = 8
DIRECT = 8
KEEP_BYTES = 8 * 2**20
VMEM_BYTES = 32 * 2**20
WHOLE_VMEM_BYTES = (53 * 1024 + 870) * 2**10
HIGH, LOW, Y, X, CORE = "high", "low", "y", "x", "core"
ALL = (HIGH, LOW, Y, X, CORE)
highest = lax.Precision.HIGHEST
f32 = jnp.float32
bf16 = jnp.bfloat16


def split3(values):
    high = values.astype(bf16)
    rest = values - high.astype(f32)
    mid = rest.astype(bf16)
    low = (rest - mid.astype(f32)).astype(bf16)
    return high, mid, low


def exponent_rows(first, second):
    width = (first if not isinstance(first, float) else second).shape[1]
    row = lax.broadcasted_iota(jnp.int32, (16, width), 0)
    out = jnp.zeros((16, width), f32)
    for base, value in ((0, first), (3, second)):
        parts = (1.0, 1.0, 1.0) if isinstance(value, float) else [p.astype(f32) for p in split3(value)]
        for k, part in enumerate(parts):
            out = jnp.where(row == base + k, part, out)
    return out.astype(bf16)


def right_operand(latent, scale):
    square = jnp.sum(latent * latent, axis=0, keepdims=True) * scale
    h, m, l = split3(latent)
    return jnp.concatenate([h, m, l, h, m, h, exponent_rows(square, 1.0)], axis=0)


def left_operand(latent, scale):
    square = jnp.sum(latent * latent, axis=0, keepdims=True) * scale
    h, m, l = split3(latent * (-2.0 * scale))
    stacked = jnp.concatenate([h, h, h, m, m, l, exponent_rows(1.0, square)], axis=0)
    return stacked.T


def place():
    return tuple(lax.axis_index(name) for name in ALL)


def device_at(high, low, y, x, core, wide, narrow):
    return (((high * (wide // 4) + low) * 2 + y) * (narrow // 2) + x) * 2 + core


def part_base(part, parts):
    return 0 if parts == 1 else jnp.bitwise_xor(lax.axis_index(X), part) * 2


def row_sources(blocks, flips):
    spots = [(b, i) for b in blocks for i in range(b.shape[0])]
    if flips is None:
        return [(b, i, i) for b, i in spots]
    high = lax.axis_index(HIGH)
    return [(b, i, jnp.bitwise_xor(high, flip)) for (b, i), flip in zip(spots, flips)]


def column_sources(blocks, flips):
    spots = [(b, i) for b in blocks for i in range(b.shape[0])]
    if flips is None:
        return [(b, i, i) for b, i in spots]
    _, low, y, _, core = place()
    return [(b, i, (jnp.bitwise_xor(low, f) * 2 + jnp.bitwise_xor(y, g)) * 2 + jnp.bitwise_xor(core, h))
            for (b, i), (f, g, h) in zip(spots, flips)]


def total_sum(values):
    return jnp.sum(jnp.sum(values, axis=0, keepdims=True), axis=1, keepdims=True)


def lane_sums(values):
    parts = jnp.concatenate(split3(values), axis=1)
    ones = jnp.ones((16, parts.shape[1]), bf16)
    return lax.dot_general(ones, parts, (((1,), (1,)), ((), ())),
                           preferred_element_type=f32)[0:1, :]


def make_rows(left, right, kept, read_vector, sums):
    groups, rows, _ = left.shape
    columns = right.shape[0]
    halves = rows // LANES

    def one_group(g, _):
        left_group = left[g]

        def one_column(c, acc):
            exponent = jnp.dot(left_group, right[c], preferred_element_type=f32)
            tile = jnp.exp2(exponent)
            if kept is not None:
                kept[g, c] = tile
            for half in range(halves):
                acc = acc + tile[:, half * LANES:(half + 1) * LANES] * read_vector(c, half)
            return acc

        sums[g] = lax.fori_loop(0, columns, one_column, jnp.zeros((rows, LANES), f32), unroll=8)
        return 0

    lax.fori_loop(0, groups, one_group, 0, unroll=groups <= 2)


def use_rows(kept, read_vector, sums):
    groups, columns, rows, _ = kept.shape
    halves = rows // LANES

    def one_group(g, _):
        def one_column(c, acc):
            for half in range(halves):
                acc = acc + kept[g, c, :, half * LANES:(half + 1) * LANES] * read_vector(c, half)
            return acc

        sums[g] = lax.fori_loop(0, columns, one_column, jnp.zeros((rows, LANES), f32), unroll=8)
        return 0

    lax.fori_loop(0, groups, one_group, 0, unroll=groups <= 2)


def write_rows(sums, out, bases):
    groups, rows, _ = sums.shape
    halves = rows // LANES
    total = lane_sums(sums[...].reshape(groups * rows, LANES))
    for g in range(groups):
        base = bases[g * len(bases) // groups]
        for half in range(halves):
            line = (base + g % (groups // len(bases))) * halves + half
            start = (g * halves + half) * LANES
            out[pl.ds(line, 1), :] = total[:, start:start + LANES]


def project_kernel(features, projection_t, targets, out, feature_buf, projection_buf, target_buf, sems):
    proj = projection_t.shape[0]
    chunks, _, width = feature_buf.shape
    copies = [pltpu.make_async_copy(projection_t, projection_buf, sems.at[0])]
    copies += [
        pltpu.make_async_copy(features.at[:, pl.ds(i * width, width)], feature_buf.at[i], sems.at[i + 1])
        for i in range(chunks)]
    copies += [pltpu.make_async_copy(targets, target_buf, sems.at[chunks + 1])]
    for copy in copies:
        copy.start()
    copies[0].wait()
    latent = jnp.zeros((features.shape[0], proj), f32)
    for i in range(chunks):
        copies[i + 1].wait()
        latent = latent + lax.dot_general(
            feature_buf[i], projection_buf[:, i * width:(i + 1) * width],
            (((1,), (1,)), ((), ())), preferred_element_type=f32)
    out[0, 0:proj, :] = latent.T
    copies[-1].wait()
    out[0, proj:proj + 8, :] = jnp.broadcast_to(target_buf[...], (8, out.shape[2]))


def first_kernel(proj, scale, wide, keep, flips, row_count, column_count, *refs):
    row_blocks, column_blocks = refs[:row_count], refs[row_count:row_count + column_count]
    refs = refs[row_count + column_count:]
    right, column_vector = refs[:2]
    kept, left = (refs[2], refs[-2]) if keep else (None, refs[2])
    partial, starts, sums = refs[3], refs[4] if column_count else None, refs[-1]
    rows = left.shape[1]
    halves = rows // LANES
    for block, i, source in column_sources(column_blocks, flips[1]) if column_count else ():
        right[source] = right_operand(block[i, 0:proj, :], scale)
        for half in range(halves):
            column_vector[pl.ds(source * halves + half, 1), :] = block[
                i, proj:proj + 1, half * LANES:(half + 1) * LANES]
    for block, i, source in row_sources(row_blocks, flips[0]):
        left[source] = left_operand(block[i, 0:proj, :], scale)
        for half in range(halves) if column_count else ():
            starts[pl.ds(source * halves + half, 1), :] = block[
                i, proj:proj + 1, half * LANES:(half + 1) * LANES]
    make_rows(left, right, kept, lambda c, half: column_vector[pl.ds(c * halves + half, 1), :], sums)
    write_rows(sums, partial, [0])


def message_kernel(parts, halves, *refs):
    partials, start, out, held = refs[:parts], refs[parts], refs[-2], refs[-1]
    for part, lines in enumerate(partials):
        base = part_base(part, parts) * halves
        for line in range(lines.shape[0]):
            held[pl.ds(base + line, 1), :] = lines[line:line + 1, :]
    mine = lax.axis_index(HIGH) * halves
    if parts == 1:
        mine = mine + lax.axis_index(X) * 2 * halves
    pieces = [held[line:line + 1, :] for line in range(held.shape[0])]
    pieces += [start[pl.ds(mine + half, 1), :] for half in range(halves)]
    block = jnp.concatenate(pieces, axis=1)

    def copy(i, _):
        out[i] = block
        return 0

    lax.fori_loop(0, out.shape[0], copy, 0, unroll=8)


def second_kernel(wide, narrow, keep, parts, *refs):
    arrived, out, step_scalars, direction, images, targets, partial, sums = refs[:1] + refs[-7:]
    lines = partial.shape[0]
    halves = lines // narrow
    across = narrow // 2
    group = [(high, x) for x in range(narrow // 2) for high in range(2)]

    def unpack(low, _):
        for y, core in ((0, 0), (0, 1), (1, 0), (1, 1)):
            members = [device_at(high, low, y, x, core, wide, narrow) for high, x in group]
            total = arrived[members[0]]
            for member in members[1:]:
                total = total + arrived[member]
            for r, member in enumerate(members):
                for half in range(halves):
                    start = arrived[member, :, (lines + half) * LANES:(lines + half + 1) * LANES]
                    line = r * halves + half
                    spot = pl.ds(member * halves + half, 1)
                    targets[spot, :] = start
                    images[spot, :] = total[:, line * LANES:(line + 1) * LANES] + noise_var * start
        return 0

    lax.fori_loop(0, wide // 4, unpack, 0, unroll=2)
    start, first = targets[...], images[...]
    norm = total_sum(start * start)
    alpha = norm / total_sum(start * first)
    residual = start - alpha * first
    norm_next = total_sum(residual * residual)
    beta = norm_next / norm
    whole = residual + beta * start
    direction[...] = whole
    high, low, y, x, core = place()

    def read_vector(c, half):
        source = device_at(high, c // 4, c // 2 % 2, x, c % 2, wide, narrow)
        return direction[pl.ds(source * halves + half, 1), :]

    groups = narrow // parts
    for part in range(parts):
        part_sums = sums.at[part * groups:(part + 1) * groups]
        if keep:
            use_rows(refs[1 + part], read_vector, part_sums)
        else:
            make_rows(refs[2 + part], refs[1], None, read_vector, part_sums)
    write_rows(sums, partial, [part_base(part, parts) for part in range(parts)])
    share = jnp.zeros((1, LANES), f32)
    for r, (row_high, row_x) in enumerate(group):
        for half in range(halves):
            spot = pl.ds(device_at(row_high, low, y, row_x, core, wide, narrow) * halves + half, 1)
            line = r * halves + half
            share = share + direction[spot, :] * partial[line:line + 1, :]
    blocks = [
        jnp.concatenate([partial[r * halves + half:r * halves + half + 1, :]
                         for half in range(halves)] + [share], axis=1)
        for r in range(narrow)]

    def copy(to_low, _):
        for r, (to_high, to_x) in enumerate(group):
            for to_y, to_core in ((0, 0), (0, 1), (1, 0), (1, 1)):
                out[device_at(to_high, to_low, to_y, to_x, to_core, wide, narrow)] = blocks[r]
        return 0

    lax.fori_loop(0, wide // 4, copy, 0, unroll=2)
    lane = lax.broadcasted_iota(jnp.int32, (1, LANES), 1)
    noise = noise_var * total_sum(whole * whole)
    step_scalars[0:1, :] = jnp.where(lane == 0, alpha, jnp.where(
        lane == 1, norm_next, jnp.where(lane == 2, beta, noise)))
    for half in range(halves):
        spot = pl.ds(device_at(high, low, y, x, core, wide, narrow) * halves + half, 1)
        step_scalars[1 + half:2 + half, :] = images[spot, :]
        step_scalars[1 + halves + half:2 + halves + half, :] = targets[spot, :]


def last_kernel(wide, narrow, arrived, step_scalars, solution_out, residual_out, answer, sems):
    alpha = step_scalars[0:1, 0:1]
    norm = step_scalars[0:1, 1:2]
    beta = step_scalars[0:1, 2:3]
    noise = step_scalars[0:1, 3:4]
    halves = answer.shape[1]

    def add(i, total):
        return total + arrived[i, :, halves * LANES:(halves + 1) * LANES]

    share = lax.fori_loop(0, arrived.shape[0], add, jnp.zeros((1, LANES), f32), unroll=8)
    alpha_next = norm / (total_sum(share) + noise)
    _, low, y, _, core = place()
    product = jnp.zeros((1, (halves + 1) * LANES), f32)
    for high in range(2):
        for x in range(narrow // 2):
            product = product + arrived[device_at(high, low, y, x, core, wide, narrow)]
    for half in range(halves):
        begin = step_scalars[1 + halves + half:2 + halves + half, :]
        residual = begin - alpha * step_scalars[1 + half:2 + half, :]
        direction = residual + beta * begin
        image = product[:, half * LANES:(half + 1) * LANES] + noise_var * direction
        answer[0, half:half + 1, :] = alpha * begin + alpha_next * direction
        answer[1, half:half + 1, :] = residual - alpha_next * image
    copies = [pltpu.make_async_copy(answer.at[i], out, sems.at[i])
              for i, out in enumerate((solution_out, residual_out))]
    for copy in copies:
        copy.start()
    for copy in copies:
        copy.wait()


def call(kernel, out_shape, *args, scratch=(), vmem=VMEM_BYTES, **options):
    return pl.pallas_call(
        kernel,
        out_shape=out_shape,
        scratch_shapes=list(scratch),
        compiler_params=pltpu.CompilerParams(vmem_limit_bytes=vmem),
        **options,
    )(*args)


def to_all(blocks, axes):
    return lax.all_to_all(blocks, axes, split_axis=0, concat_axis=0, tiled=True)


def join_kernel(*refs):
    i = 0
    for block in refs[:-1]:
        for j in range(block.shape[0]):
            refs[-1][i] = block[j]
            i += 1


def join(*blocks):
    total = sum(b.shape[0] for b in blocks)
    return call(join_kernel, jax.ShapeDtypeStruct((total, *blocks[0].shape[1:]), f32), *blocks)


def first_round(own, wide, narrow):
    lows, across = wide // 4, narrow // 2
    if lows & (lows - 1) or across != 2 or lows > DIRECT:
        every = lax.all_gather(own, ALL, axis=0, tiled=True)
        every = every.reshape(2, lows, 2, across, 2, *own.shape[1:])
        high, low, y, x, core = place()
        rows = every
        for place_in, axis in ((low, 1), (y, 1), (core, 2)):
            rows = lax.dynamic_index_in_dim(rows, place_in, axis, keepdims=False)
        columns = lax.dynamic_index_in_dim(every, high, 0, keepdims=False)
        columns = lax.dynamic_index_in_dim(columns, x, 2, keepdims=False)
        rows = jnp.swapaxes(rows, 0, 1).reshape(narrow, *own.shape[1:])
        return [[rows]], [columns.reshape(wide, *own.shape[1:])], (None, None)

    def swap(value, axis, size=2, flip=1):
        return lax.ppermute(value, axis, [(i, i ^ flip) for i in range(size)])

    rows = join(own, swap(own, HIGH))
    columns = [own] + [swap(own, (LOW, Y), 2 * lows, flip) for flip in range(1, 2 * lows)]
    columns += [swap(block, CORE) for block in columns]
    parts = [[rows], [swap(rows, X)]]
    flips = [(flip // 2, flip % 2, core) for core in range(2) for flip in range(2 * lows)]
    return parts, columns, ([0, 1], flips)


def on_device(wide, narrow, features, projection, targets):
    rows, proj = features.shape[0], projection.shape[1]
    halves = rows // LANES
    lines = narrow * halves
    devices = wide * narrow
    scale = -2.0 / proj * math.log2(math.e)
    depth = 6 * proj + 16
    keep = 4 * devices * rows * rows <= KEEP_BYTES

    def shape(*dims, dtype=f32):
        return jax.ShapeDtypeStruct(dims, dtype)

    def scratch(*dims, dtype=f32):
        return pltpu.VMEM(dims, dtype)

    feat = features.shape[1]
    own = call(
        project_kernel, shape(1, proj + 8, rows), features, projection.T, targets.reshape(1, rows),
        in_specs=[pl.BlockSpec(memory_space=pl.ANY)] * 3, vmem=WHOLE_VMEM_BYTES,
        scratch=[scratch(CHUNKS, rows, feat // CHUNKS, dtype=bf16), scratch(proj, feat, dtype=bf16),
                 scratch(1, rows), pltpu.SemaphoreType.DMA((CHUNKS + 2,))])
    row_parts, column_blocks, flips = first_round(own, wide, narrow)
    parts = len(row_parts)
    groups = narrow // parts
    left = shape(groups, rows, depth, dtype=bf16)
    right = shape(wide, depth, rows, dtype=bf16)
    vector = shape(wide * halves, LANES)
    kept = shape(groups, wide, rows, rows) if keep else left
    group_lines = shape(groups * halves, LANES)
    sums = scratch(groups, rows, LANES)
    work = [scratch(*left.shape, dtype=bf16), sums] if keep else [sums]
    blocks, partials = [], []
    for part, row_blocks in enumerate(row_parts):
        fresh = part == 0
        first = functools.partial(
            first_kernel, proj, scale, wide, keep, flips, len(row_blocks),
            len(column_blocks) if fresh else 0)
        tiles = groups * wide * rows * rows
        made = call(
            first, (right, vector, kept, group_lines, group_lines) if fresh else (kept, group_lines),
            *row_blocks, *(column_blocks if fresh else columns_made), scratch=work,
            cost_estimate=pl.CostEstimate(
                flops=2 * tiles * depth, bytes_accessed=4 * tiles, transcendentals=tiles))
        if fresh:
            *columns_made, block, partial, own_start = made
        else:
            block, partial = made
        blocks.append(block)
        partials.append(partial)
    out = call(
        functools.partial(message_kernel, parts, halves),
        shape(devices, 1, (lines + halves) * LANES), *partials, own_start,
        scratch=[scratch(lines, LANES)])
    block = blocks if keep else [columns_made[0], *blocks]
    sums = scratch(narrow, rows, LANES)
    out, step_scalars = call(
        functools.partial(second_kernel, wide, narrow, keep, parts),
        (shape(devices, 1, (halves + 1) * LANES), shape(1 + 2 * halves, LANES)),
        to_all(out, ALL), *block,
        scratch=[scratch(devices * halves, LANES)] * 3 + [scratch(lines, LANES), sums])
    answer, residual = call(
        functools.partial(last_kernel, wide, narrow), (shape(halves, LANES), shape(halves, LANES)),
        to_all(out, ALL), step_scalars,
        out_specs=(pl.BlockSpec(memory_space=pl.ANY),) * 2,
        scratch=[scratch(2, halves, LANES), pltpu.SemaphoreType.DMA((2,))])
    return answer.reshape(rows), residual.reshape(rows)


def solution(mesh):
    wide, narrow = mesh.shape["wide"], mesh.shape["narrow"]
    split = jax.sharding.Mesh(mesh.devices.reshape(2, wide // 4, 2, narrow // 2, 2), ALL)
    in_specs = (P(ALL, None), P(), P(ALL))
    return jax.shard_map(
        functools.partial(on_device, wide, narrow), mesh=split,
        in_specs=in_specs, out_specs=(P(ALL), P(ALL)), check_vma=False,
    )
```

```python
import functools
import math

import jax
import jax.numpy as jnp
import numpy as np
from jax import lax
from jax.experimental import pallas as pl
from jax.experimental.pallas import tpu as pltpu
from jax.sharding import PartitionSpec as P

noise_var = 0.5
LANES = 128
CHUNKS = 8
DIRECT = 8
KEEP_BYTES = 8 * 2**20
VMEM_BYTES = 32 * 2**20
WHOLE_VMEM_BYTES = (53 * 1024 + 870) * 2**10
ALL = "all"
HIGH, LOW, Y, X, CORE = range(5)
highest = lax.Precision.HIGHEST
f32 = jnp.float32
bf16 = jnp.bfloat16


def split3(values):
    high = values.astype(bf16)
    rest = values - high.astype(f32)
    mid = rest.astype(bf16)
    low = (rest - mid.astype(f32)).astype(bf16)
    return high, mid, low


def exponent_rows(first, second):
    width = (first if not isinstance(first, float) else second).shape[1]
    row = lax.broadcasted_iota(jnp.int32, (16, width), 0)
    out = jnp.zeros((16, width), f32)
    for base, value in ((0, first), (3, second)):
        parts = (1.0, 1.0, 1.0) if isinstance(value, float) else [p.astype(f32) for p in split3(value)]
        for k, part in enumerate(parts):
            out = jnp.where(row == base + k, part, out)
    return out.astype(bf16)


def right_operand(latent, scale):
    square = jnp.sum(latent * latent, axis=0, keepdims=True) * scale
    h, m, l = split3(latent)
    return jnp.concatenate([h, m, l, h, m, h, exponent_rows(square, 1.0)], axis=0)


def left_operand(latent, scale):
    square = jnp.sum(latent * latent, axis=0, keepdims=True) * scale
    h, m, l = split3(latent * (-2.0 * scale))
    stacked = jnp.concatenate([h, h, h, m, m, l, exponent_rows(1.0, square)], axis=0)
    return stacked.T


def axis_sizes(wide, narrow):
    return 2, wide // 4, 2, narrow // 2, 2


def place(wide, narrow):
    rest, out = lax.axis_index(ALL), []
    for size in reversed(axis_sizes(wide, narrow)):
        out.append(rest % size)
        rest = rest // size
    return tuple(reversed(out))


def device_at(high, low, y, x, core, wide, narrow):
    return (((high * (wide // 4) + low) * 2 + y) * (narrow // 2) + x) * 2 + core


def slot(device, wide, narrow):
    return wide * narrow - 1 - device


def part_base(part, parts, wide, narrow):
    return 0 if parts == 1 else jnp.bitwise_xor(place(wide, narrow)[X], part) * 2


def row_sources(blocks, flips, wide, narrow):
    spots = [(b, i) for b in blocks for i in range(b.shape[0])]
    if flips is None:
        return [(b, i, i) for b, i in spots]
    high = place(wide, narrow)[HIGH]
    return [(b, i, jnp.bitwise_xor(high, flip)) for (b, i), flip in zip(spots, flips)]


def column_sources(blocks, flips, wide, narrow):
    spots = [(b, i) for b in blocks for i in range(b.shape[0])]
    if flips is None:
        return [(b, i, i) for b, i in spots]
    _, low, y, _, core = place(wide, narrow)
    return [(b, i, (jnp.bitwise_xor(low, f) * 2 + jnp.bitwise_xor(y, g)) * 2 + jnp.bitwise_xor(core, h))
            for (b, i), (f, g, h) in zip(spots, flips)]


def total_sum(values):
    return jnp.sum(jnp.sum(values, axis=0, keepdims=True), axis=1, keepdims=True)


def lane_sums(values):
    parts = jnp.concatenate(split3(values), axis=1)
    ones = jnp.ones((16, parts.shape[1]), bf16)
    return lax.dot_general(ones, parts, (((1,), (1,)), ((), ())),
                           preferred_element_type=f32)[0:1, :]


def make_rows(left, right, kept, read_vector, sums):
    groups, rows, _ = left.shape
    columns = right.shape[0]
    halves = rows // LANES

    def one_group(g, _):
        left_group = left[g]

        def one_column(c, acc):
            exponent = jnp.dot(left_group, right[c], preferred_element_type=f32)
            tile = jnp.exp2(exponent)
            if kept is not None:
                kept[g, c] = tile
            for half in range(halves):
                acc = acc + tile[:, half * LANES:(half + 1) * LANES] * read_vector(c, half)
            return acc

        sums[g] = lax.fori_loop(0, columns, one_column, jnp.zeros((rows, LANES), f32), unroll=8)
        return 0

    lax.fori_loop(0, groups, one_group, 0, unroll=groups <= 2)


def use_rows(kept, read_vector, sums):
    groups, columns, rows, _ = kept.shape
    halves = rows // LANES

    def one_group(g, _):
        def one_column(c, acc):
            for half in range(halves):
                acc = acc + kept[g, c, :, half * LANES:(half + 1) * LANES] * read_vector(c, half)
            return acc

        sums[g] = lax.fori_loop(0, columns, one_column, jnp.zeros((rows, LANES), f32), unroll=8)
        return 0

    lax.fori_loop(0, groups, one_group, 0, unroll=groups <= 2)


def write_rows(sums, out, bases):
    groups, rows, _ = sums.shape
    halves = rows // LANES
    total = lane_sums(sums[...].reshape(groups * rows, LANES))
    for g in range(groups):
        base = bases[g * len(bases) // groups]
        for half in range(halves):
            line = (base + g % (groups // len(bases))) * halves + half
            start = (g * halves + half) * LANES
            out[pl.ds(line, 1), :] = total[:, start:start + LANES]


def project_kernel(features, projection_t, targets, out, feature_buf, projection_buf, target_buf, sems):
    proj = projection_t.shape[0]
    chunks, _, width = feature_buf.shape
    copies = [pltpu.make_async_copy(projection_t, projection_buf, sems.at[0])]
    copies += [
        pltpu.make_async_copy(features.at[:, pl.ds(i * width, width)], feature_buf.at[i], sems.at[i + 1])
        for i in range(chunks)]
    copies += [pltpu.make_async_copy(targets, target_buf, sems.at[chunks + 1])]
    for copy in copies:
        copy.start()
    copies[0].wait()
    latent = jnp.zeros((proj, features.shape[0]), f32)
    for i in range(chunks):
        copies[i + 1].wait()
        latent = latent + lax.dot_general(
            projection_buf[:, i * width:(i + 1) * width], feature_buf[i],
            (((1,), (1,)), ((), ())), preferred_element_type=f32)
    out[0, 0:proj, :] = latent
    copies[-1].wait()
    out[0, proj:proj + 8, :] = jnp.broadcast_to(target_buf[...], (8, out.shape[2]))


def first_kernel(proj, scale, wide, narrow, keep, flips, row_count, column_count, *refs):
    row_blocks, column_blocks = refs[:row_count], refs[row_count:row_count + column_count]
    refs = refs[row_count + column_count:]
    right, column_vector = refs[:2]
    kept, left = (refs[2], refs[-2]) if keep else (None, refs[2])
    partial, starts, sums = refs[3], refs[4] if column_count else None, refs[-1]
    rows = left.shape[1]
    halves = rows // LANES
    for block, i, source in column_sources(column_blocks, flips[1], wide, narrow) if column_count else ():
        right[source] = right_operand(block[i, 0:proj, :], scale)
        for half in range(halves):
            column_vector[pl.ds(source * halves + half, 1), :] = block[
                i, proj:proj + 1, half * LANES:(half + 1) * LANES]
    for block, i, source in row_sources(row_blocks, flips[0], wide, narrow):
        left[source] = left_operand(block[i, 0:proj, :], scale)
        for half in range(halves) if column_count else ():
            starts[pl.ds(source * halves + half, 1), :] = block[
                i, proj:proj + 1, half * LANES:(half + 1) * LANES]
    make_rows(left, right, kept, lambda c, half: column_vector[pl.ds(c * halves + half, 1), :], sums)
    write_rows(sums, partial, [0])


def message_kernel(parts, wide, narrow, halves, *refs):
    partials, start, out, held = refs[:parts], refs[parts], refs[-2], refs[-1]
    for part, lines in enumerate(partials):
        base = part_base(part, parts, wide, narrow) * halves
        for line in range(lines.shape[0]):
            held[pl.ds(base + line, 1), :] = lines[line:line + 1, :]
    here = place(wide, narrow)
    mine = here[HIGH] * halves
    if parts == 1:
        mine = mine + here[X] * 2 * halves
    pieces = [held[line:line + 1, :] for line in range(held.shape[0])]
    pieces += [start[pl.ds(mine + half, 1), :] for half in range(halves)]
    block = jnp.concatenate(pieces, axis=1)

    def copy(i, _):
        out[i] = block
        return 0

    lax.fori_loop(0, out.shape[0], copy, 0, unroll=8)


def second_kernel(wide, narrow, keep, parts, *refs):
    arrived, out, step_scalars, direction, images, targets, partial, sums = refs[:1] + refs[-7:]
    lines = partial.shape[0]
    halves = lines // narrow
    across = narrow // 2
    group = [(high, x) for x in range(narrow // 2) for high in range(2)]

    def unpack(low, _):
        for y, core in ((0, 0), (0, 1), (1, 0), (1, 1)):
            members = [device_at(high, low, y, x, core, wide, narrow) for high, x in group]
            slots = [slot(member, wide, narrow) for member in members]
            total = arrived[slots[0]]
            for spot in slots[1:]:
                total = total + arrived[spot]
            for r, member in enumerate(members):
                for half in range(halves):
                    start = arrived[slots[r], :, (lines + half) * LANES:(lines + half + 1) * LANES]
                    line = r * halves + half
                    spot = pl.ds(member * halves + half, 1)
                    targets[spot, :] = start
                    images[spot, :] = total[:, line * LANES:(line + 1) * LANES] + noise_var * start
        return 0

    lax.fori_loop(0, wide // 4, unpack, 0, unroll=2)
    start, first = targets[...], images[...]
    norm = total_sum(start * start)
    alpha = norm / total_sum(start * first)
    residual = start - alpha * first
    norm_next = total_sum(residual * residual)
    beta = norm_next / norm
    whole = residual + beta * start
    direction[...] = whole
    high, low, y, x, core = place(wide, narrow)

    def read_vector(c, half):
        source = device_at(high, c // 4, c // 2 % 2, x, c % 2, wide, narrow)
        return direction[pl.ds(source * halves + half, 1), :]

    groups = narrow // parts
    for part in range(parts):
        part_sums = sums.at[part * groups:(part + 1) * groups]
        if keep:
            use_rows(refs[1 + part], read_vector, part_sums)
        else:
            make_rows(refs[2 + part], refs[1], None, read_vector, part_sums)
    write_rows(sums, partial, [part_base(part, parts, wide, narrow) for part in range(parts)])
    share = jnp.zeros((1, LANES), f32)
    for r, (row_high, row_x) in enumerate(group):
        for half in range(halves):
            spot = pl.ds(device_at(row_high, low, y, row_x, core, wide, narrow) * halves + half, 1)
            line = r * halves + half
            share = share + direction[spot, :] * partial[line:line + 1, :]
    blocks = [
        jnp.concatenate([partial[r * halves + half:r * halves + half + 1, :]
                         for half in range(halves)] + [share], axis=1)
        for r in range(narrow)]

    def copy(to_low, _):
        for r, (to_high, to_x) in enumerate(group):
            for to_y, to_core in ((0, 0), (0, 1), (1, 0), (1, 1)):
                to = device_at(to_high, to_low, to_y, to_x, to_core, wide, narrow)
                out[slot(to, wide, narrow)] = blocks[r]
        return 0

    lax.fori_loop(0, wide // 4, copy, 0, unroll=2)
    lane = lax.broadcasted_iota(jnp.int32, (1, LANES), 1)
    noise = noise_var * total_sum(whole * whole)
    step_scalars[0:1, :] = jnp.where(lane == 0, alpha, jnp.where(
        lane == 1, norm_next, jnp.where(lane == 2, beta, noise)))
    for half in range(halves):
        spot = pl.ds(device_at(high, low, y, x, core, wide, narrow) * halves + half, 1)
        step_scalars[1 + half:2 + half, :] = images[spot, :]
        step_scalars[1 + halves + half:2 + halves + half, :] = targets[spot, :]


def last_kernel(wide, narrow, arrived, step_scalars, solution_out, residual_out, answer, sems):
    alpha = step_scalars[0:1, 0:1]
    norm = step_scalars[0:1, 1:2]
    beta = step_scalars[0:1, 2:3]
    noise = step_scalars[0:1, 3:4]
    halves = answer.shape[1]

    def add(i, total):
        return total + arrived[i, :, halves * LANES:(halves + 1) * LANES]

    share = lax.fori_loop(0, arrived.shape[0], add, jnp.zeros((1, LANES), f32), unroll=8)
    alpha_next = norm / (total_sum(share) + noise)
    _, low, y, _, core = place(wide, narrow)
    product = jnp.zeros((1, (halves + 1) * LANES), f32)
    for high in range(2):
        for x in range(narrow // 2):
            member = device_at(high, low, y, x, core, wide, narrow)
            product = product + arrived[slot(member, wide, narrow)]
    for half in range(halves):
        begin = step_scalars[1 + halves + half:2 + halves + half, :]
        residual = begin - alpha * step_scalars[1 + half:2 + half, :]
        direction = residual + beta * begin
        image = product[:, half * LANES:(half + 1) * LANES] + noise_var * direction
        answer[0, half:half + 1, :] = alpha * begin + alpha_next * direction
        answer[1, half:half + 1, :] = residual - alpha_next * image
    copies = [pltpu.make_async_copy(answer.at[i], out, sems.at[i])
              for i, out in enumerate((solution_out, residual_out))]
    for copy in copies:
        copy.start()
    for copy in copies:
        copy.wait()


def call(kernel, out_shape, *args, scratch=(), vmem=VMEM_BYTES, **options):
    return pl.pallas_call(
        kernel,
        out_shape=out_shape,
        scratch_shapes=list(scratch),
        compiler_params=pltpu.CompilerParams(vmem_limit_bytes=vmem),
        **options,
    )(*args)


def to_all(blocks):
    group = list(range(blocks.shape[0] - 1, -1, -1))
    return lax.all_to_all(blocks, ALL, split_axis=0, concat_axis=0, axis_index_groups=[group], tiled=True)


def join_kernel(*refs):
    i = 0
    for block in refs[:-1]:
        for j in range(block.shape[0]):
            refs[-1][i] = block[j]
            i += 1


def join(*blocks):
    total = sum(b.shape[0] for b in blocks)
    return call(join_kernel, jax.ShapeDtypeStruct((total, *blocks[0].shape[1:]), f32), *blocks)


def first_round(own, wide, narrow):
    lows, across = wide // 4, narrow // 2
    if lows & (lows - 1) or across != 2 or lows > DIRECT:
        every = lax.all_gather(own, ALL, axis=0, tiled=True)
        every = every.reshape(2, lows, 2, across, 2, *own.shape[1:])
        high, low, y, x, core = place(wide, narrow)
        rows = every
        for place_in, axis in ((low, 1), (y, 1), (core, 2)):
            rows = lax.dynamic_index_in_dim(rows, place_in, axis, keepdims=False)
        columns = lax.dynamic_index_in_dim(every, high, 0, keepdims=False)
        columns = lax.dynamic_index_in_dim(columns, x, 2, keepdims=False)
        rows = jnp.swapaxes(rows, 0, 1).reshape(narrow, *own.shape[1:])
        return [[rows]], [columns.reshape(wide, *own.shape[1:])], (None, None)

    sizes = axis_sizes(wide, narrow)

    def swap(value, **flips):
        pairs = []
        for i in range(wide * narrow):
            spot = list(np.unravel_index(i, sizes))
            for name, flip in flips.items():
                axis = dict(high=HIGH, low=LOW, y=Y, x=X, core=CORE)[name]
                spot[axis] = int(spot[axis]) ^ flip
            pairs.append((i, int(np.ravel_multi_index(spot, sizes))))
        return lax.ppermute(value, ALL, pairs)

    rows = join(own, swap(own, high=1))
    columns = [own] + [swap(own, low=flip // 2, y=flip % 2) for flip in range(1, 2 * lows)]
    columns += [swap(block, core=1) for block in columns]
    parts = [[rows], [swap(rows, x=1)]]
    flips = [(flip // 2, flip % 2, core) for core in range(2) for flip in range(2 * lows)]
    return parts, columns, ([0, 1], flips)


def on_device(wide, narrow, features, projection, targets):
    rows, proj = features.shape[0], projection.shape[1]
    halves = rows // LANES
    lines = narrow * halves
    devices = wide * narrow
    scale = -2.0 / proj * math.log2(math.e)
    depth = 6 * proj + 16
    keep = 4 * devices * rows * rows <= KEEP_BYTES

    def shape(*dims, dtype=f32):
        return jax.ShapeDtypeStruct(dims, dtype)

    def scratch(*dims, dtype=f32):
        return pltpu.VMEM(dims, dtype)

    feat = features.shape[1]
    own = call(
        project_kernel, shape(1, proj + 8, rows), features, projection.T, targets.reshape(1, rows),
        in_specs=[pl.BlockSpec(memory_space=pl.ANY)] * 3, vmem=WHOLE_VMEM_BYTES,
        scratch=[scratch(CHUNKS, rows, feat // CHUNKS, dtype=bf16), scratch(proj, feat, dtype=bf16),
                 scratch(1, rows), pltpu.SemaphoreType.DMA((CHUNKS + 2,))])
    row_parts, column_blocks, flips = first_round(own, wide, narrow)
    parts = len(row_parts)
    groups = narrow // parts
    left = shape(groups, rows, depth, dtype=bf16)
    right = shape(wide, depth, rows, dtype=bf16)
    vector = shape(wide * halves, LANES)
    kept = shape(groups, wide, rows, rows) if keep else left
    group_lines = shape(groups * halves, LANES)
    sums = scratch(groups, rows, LANES)
    work = [scratch(*left.shape, dtype=bf16), sums] if keep else [sums]
    blocks, partials = [], []
    for part, row_blocks in enumerate(row_parts):
        fresh = part == 0
        first = functools.partial(
            first_kernel, proj, scale, wide, narrow, keep, flips, len(row_blocks),
            len(column_blocks) if fresh else 0)
        tiles = groups * wide * rows * rows
        made = call(
            first, (right, vector, kept, group_lines, group_lines) if fresh else (kept, group_lines),
            *row_blocks, *(column_blocks if fresh else columns_made), scratch=work,
            cost_estimate=pl.CostEstimate(
                flops=2 * tiles * depth, bytes_accessed=4 * tiles, transcendentals=tiles))
        if fresh:
            *columns_made, block, partial, own_start = made
        else:
            block, partial = made
        blocks.append(block)
        partials.append(partial)
    out = call(
        functools.partial(message_kernel, parts, wide, narrow, halves),
        shape(devices, 1, (lines + halves) * LANES), *partials, own_start,
        scratch=[scratch(lines, LANES)])
    block = blocks if keep else [columns_made[0], *blocks]
    sums = scratch(narrow, rows, LANES)
    out, step_scalars = call(
        functools.partial(second_kernel, wide, narrow, keep, parts),
        (shape(devices, 1, (halves + 1) * LANES), shape(1 + 2 * halves, LANES)),
        to_all(out), *block,
        scratch=[scratch(devices * halves, LANES)] * 3 + [scratch(lines, LANES), sums])
    answer, residual = call(
        functools.partial(last_kernel, wide, narrow), (shape(halves, LANES), shape(halves, LANES)),
        to_all(out), step_scalars,
        out_specs=(pl.BlockSpec(memory_space=pl.ANY),) * 2,
        scratch=[scratch(2, halves, LANES), pltpu.SemaphoreType.DMA((2,))])
    return answer.reshape(rows), residual.reshape(rows)


def solution(mesh):
    wide, narrow = mesh.shape["wide"], mesh.shape["narrow"]
    line = jax.sharding.Mesh(mesh.devices.reshape(wide * narrow), (ALL,))
    in_specs = (P(ALL, None), P(), P(ALL))
    return jax.shard_map(
        functools.partial(on_device, wide, narrow), mesh=line,
        in_specs=in_specs, out_specs=(P(ALL), P(ALL)), check_vma=False,
    )
```

```python
import functools
import math

import jax
import jax.numpy as jnp
import numpy as np
from jax import lax
from jax.experimental import pallas as pl
from jax.experimental.pallas import tpu as pltpu
from jax.sharding import PartitionSpec as P

noise_var = 0.5
LANES = 128
CHUNKS = 2
DIRECT = 8
KEEP_BYTES = 8 * 2**20
VMEM_BYTES = 32 * 2**20
WHOLE_VMEM_BYTES = (53 * 1024 + 870) * 2**10
ALL = "all"
HIGH, LOW, Y, X, CORE = range(5)
highest = lax.Precision.HIGHEST
f32 = jnp.float32
bf16 = jnp.bfloat16


def split3(values):
    high = values.astype(bf16)
    rest = values - high.astype(f32)
    mid = rest.astype(bf16)
    low = (rest - mid.astype(f32)).astype(bf16)
    return high, mid, low


def exponent_rows(first, second):
    width = (first if not isinstance(first, float) else second).shape[1]
    row = lax.broadcasted_iota(jnp.int32, (16, width), 0)
    out = jnp.zeros((16, width), f32)
    for base, value in ((0, first), (3, second)):
        parts = (1.0, 1.0, 1.0) if isinstance(value, float) else [p.astype(f32) for p in split3(value)]
        for k, part in enumerate(parts):
            out = jnp.where(row == base + k, part, out)
    return out.astype(bf16)


def right_operand(latent, scale):
    square = jnp.sum(latent * latent, axis=0, keepdims=True) * scale
    h, m, l = split3(latent)
    return jnp.concatenate([h, m, l, h, m, h, exponent_rows(square, 1.0)], axis=0)


def left_operand(latent, scale):
    square = jnp.sum(latent * latent, axis=0, keepdims=True) * scale
    h, m, l = split3(latent * (-2.0 * scale))
    stacked = jnp.concatenate([h, h, h, m, m, l, exponent_rows(1.0, square)], axis=0)
    return stacked.T


def axis_sizes(wide, narrow):
    return 2, wide // 4, 2, narrow // 2, 2


def place(wide, narrow):
    rest, out = lax.axis_index(ALL), []
    for size in reversed(axis_sizes(wide, narrow)):
        out.append(rest % size)
        rest = rest // size
    return tuple(reversed(out))


def device_at(high, low, y, x, core, wide, narrow):
    return (((high * (wide // 4) + low) * 2 + y) * (narrow // 2) + x) * 2 + core


def slot(device, wide, narrow):
    return wide * narrow - 1 - device


def part_base(part, parts, wide, narrow):
    return 0 if parts == 1 else jnp.bitwise_xor(place(wide, narrow)[X], part) * 2


def row_sources(blocks, flips, wide, narrow):
    spots = [(b, i) for b in blocks for i in range(b.shape[0])]
    if flips is None:
        return [(b, i, i) for b, i in spots]
    high = place(wide, narrow)[HIGH]
    return [(b, i, jnp.bitwise_xor(high, flip)) for (b, i), flip in zip(spots, flips)]


def column_sources(blocks, flips, wide, narrow):
    spots = [(b, i) for b in blocks for i in range(b.shape[0])]
    if flips is None:
        return [(b, i, i) for b, i in spots]
    _, low, y, _, core = place(wide, narrow)
    return [(b, i, (jnp.bitwise_xor(low, f) * 2 + jnp.bitwise_xor(y, g)) * 2 + jnp.bitwise_xor(core, h))
            for (b, i), (f, g, h) in zip(spots, flips)]


def total_sum(values):
    return jnp.sum(jnp.sum(values, axis=0, keepdims=True), axis=1, keepdims=True)


def lane_sums(values):
    parts = jnp.concatenate(split3(values), axis=1)
    ones = jnp.ones((16, parts.shape[1]), bf16)
    return lax.dot_general(ones, parts, (((1,), (1,)), ((), ())),
                           preferred_element_type=f32)[0:1, :]


def make_rows(left, right, kept, read_vector, sums):
    groups, rows, _ = left.shape
    columns = right.shape[0]
    halves = rows // LANES

    def one_group(g, _):
        left_group = left[g]

        def one_column(c, acc):
            exponent = jnp.dot(left_group, right[c], preferred_element_type=f32)
            tile = jnp.exp2(exponent)
            if kept is not None:
                kept[g, c] = tile
            for half in range(halves):
                acc = acc + tile[:, half * LANES:(half + 1) * LANES] * read_vector(c, half)
            return acc

        sums[g] = lax.fori_loop(0, columns, one_column, jnp.zeros((rows, LANES), f32), unroll=8)
        return 0

    lax.fori_loop(0, groups, one_group, 0, unroll=groups <= 2)


def use_rows(kept, read_vector, sums):
    groups, columns, rows, _ = kept.shape
    halves = rows // LANES

    def one_group(g, _):
        def one_column(c, acc):
            for half in range(halves):
                acc = acc + kept[g, c, :, half * LANES:(half + 1) * LANES] * read_vector(c, half)
            return acc

        sums[g] = lax.fori_loop(0, columns, one_column, jnp.zeros((rows, LANES), f32), unroll=8)
        return 0

    lax.fori_loop(0, groups, one_group, 0, unroll=groups <= 2)


def write_rows(sums, out, bases):
    groups, rows, _ = sums.shape
    halves = rows // LANES
    total = lane_sums(sums[...].reshape(groups * rows, LANES))
    for g in range(groups):
        base = bases[g * len(bases) // groups]
        for half in range(halves):
            line = (base + g % (groups // len(bases))) * halves + half
            start = (g * halves + half) * LANES
            out[pl.ds(line, 1), :] = total[:, start:start + LANES]


def project_kernel(features, projection_t, targets, out, feature_buf, projection_buf, target_buf, sems):
    proj = projection_t.shape[0]
    chunks, height, _ = feature_buf.shape
    copies = [
        pltpu.make_async_copy(features.at[pl.ds(i * height, height)], feature_buf.at[i], sems.at[i])
        for i in range(chunks)]
    copies.insert(1, pltpu.make_async_copy(projection_t, projection_buf, sems.at[chunks]))
    copies.append(pltpu.make_async_copy(targets, target_buf, sems.at[chunks + 1]))
    for copy in copies:
        copy.start()
    copies.pop(1).wait()
    for i in range(chunks):
        copies[i].wait()
        out[0, 0:proj, i * height:(i + 1) * height] = lax.dot_general(
            projection_buf[...], feature_buf[i], (((1,), (1,)), ((), ())), preferred_element_type=f32)
    copies[-1].wait()
    out[0, proj:proj + 8, :] = jnp.broadcast_to(target_buf[...], (8, out.shape[2]))


def first_kernel(proj, scale, wide, narrow, keep, flips, row_count, column_count, *refs):
    row_blocks, column_blocks = refs[:row_count], refs[row_count:row_count + column_count]
    refs = refs[row_count + column_count:]
    right, column_vector = refs[:2]
    kept, left = (refs[2], refs[-2]) if keep else (None, refs[2])
    partial, starts, sums = refs[3], refs[4] if column_count else None, refs[-1]
    rows = left.shape[1]
    halves = rows // LANES
    for block, i, source in column_sources(column_blocks, flips[1], wide, narrow) if column_count else ():
        right[source] = right_operand(block[i, 0:proj, :], scale)
        for half in range(halves):
            column_vector[pl.ds(source * halves + half, 1), :] = block[
                i, proj:proj + 1, half * LANES:(half + 1) * LANES]
    for block, i, source in row_sources(row_blocks, flips[0], wide, narrow):
        left[source] = left_operand(block[i, 0:proj, :], scale)
        for half in range(halves) if column_count else ():
            starts[pl.ds(source * halves + half, 1), :] = block[
                i, proj:proj + 1, half * LANES:(half + 1) * LANES]
    make_rows(left, right, kept, lambda c, half: column_vector[pl.ds(c * halves + half, 1), :], sums)
    write_rows(sums, partial, [0])


def message_kernel(parts, wide, narrow, halves, *refs):
    partials, start, out, held = refs[:parts], refs[parts], refs[-2], refs[-1]
    for part, lines in enumerate(partials):
        base = part_base(part, parts, wide, narrow) * halves
        for line in range(lines.shape[0]):
            held[pl.ds(base + line, 1), :] = lines[line:line + 1, :]
    here = place(wide, narrow)
    mine = here[HIGH] * halves
    if parts == 1:
        mine = mine + here[X] * 2 * halves
    pieces = [held[line:line + 1, :] for line in range(held.shape[0])]
    pieces += [start[pl.ds(mine + half, 1), :] for half in range(halves)]
    block = jnp.concatenate(pieces, axis=1)

    def copy(i, _):
        out[i] = block
        return 0

    lax.fori_loop(0, out.shape[0], copy, 0, unroll=8)


def second_kernel(wide, narrow, keep, parts, *refs):
    arrived, out, step_scalars, direction, images, targets, partial, sums = refs[:1] + refs[-7:]
    lines = partial.shape[0]
    halves = lines // narrow
    across = narrow // 2
    group = [(high, x) for x in range(narrow // 2) for high in range(2)]

    def unpack(low, _):
        for y, core in ((0, 0), (0, 1), (1, 0), (1, 1)):
            members = [device_at(high, low, y, x, core, wide, narrow) for high, x in group]
            slots = [slot(member, wide, narrow) for member in members]
            total = arrived[slots[0]]
            for spot in slots[1:]:
                total = total + arrived[spot]
            for r, member in enumerate(members):
                for half in range(halves):
                    start = arrived[slots[r], :, (lines + half) * LANES:(lines + half + 1) * LANES]
                    line = r * halves + half
                    spot = pl.ds(member * halves + half, 1)
                    targets[spot, :] = start
                    images[spot, :] = total[:, line * LANES:(line + 1) * LANES] + noise_var * start
        return 0

    lax.fori_loop(0, wide // 4, unpack, 0, unroll=2)
    start, first = targets[...], images[...]
    norm = total_sum(start * start)
    alpha = norm / total_sum(start * first)
    residual = start - alpha * first
    norm_next = total_sum(residual * residual)
    beta = norm_next / norm
    whole = residual + beta * start
    direction[...] = whole
    high, low, y, x, core = place(wide, narrow)

    def read_vector(c, half):
        source = device_at(high, c // 4, c // 2 % 2, x, c % 2, wide, narrow)
        return direction[pl.ds(source * halves + half, 1), :]

    groups = narrow // parts
    for part in range(parts):
        part_sums = sums.at[part * groups:(part + 1) * groups]
        if keep:
            use_rows(refs[1 + part], read_vector, part_sums)
        else:
            make_rows(refs[2 + part], refs[1], None, read_vector, part_sums)
    write_rows(sums, partial, [part_base(part, parts, wide, narrow) for part in range(parts)])
    share = jnp.zeros((1, LANES), f32)
    for r, (row_high, row_x) in enumerate(group):
        for half in range(halves):
            spot = pl.ds(device_at(row_high, low, y, row_x, core, wide, narrow) * halves + half, 1)
            line = r * halves + half
            share = share + direction[spot, :] * partial[line:line + 1, :]
    blocks = [
        jnp.concatenate([partial[r * halves + half:r * halves + half + 1, :]
                         for half in range(halves)] + [share], axis=1)
        for r in range(narrow)]

    def copy(to_low, _):
        for r, (to_high, to_x) in enumerate(group):
            for to_y, to_core in ((0, 0), (0, 1), (1, 0), (1, 1)):
                to = device_at(to_high, to_low, to_y, to_x, to_core, wide, narrow)
                out[slot(to, wide, narrow)] = blocks[r]
        return 0

    lax.fori_loop(0, wide // 4, copy, 0, unroll=2)
    lane = lax.broadcasted_iota(jnp.int32, (1, LANES), 1)
    noise = noise_var * total_sum(whole * whole)
    step_scalars[0:1, :] = jnp.where(lane == 0, alpha, jnp.where(
        lane == 1, norm_next, jnp.where(lane == 2, beta, noise)))
    for half in range(halves):
        spot = pl.ds(device_at(high, low, y, x, core, wide, narrow) * halves + half, 1)
        step_scalars[1 + half:2 + half, :] = images[spot, :]
        step_scalars[1 + halves + half:2 + halves + half, :] = targets[spot, :]


def last_kernel(wide, narrow, arrived, step_scalars, solution_out, residual_out, answer, sems):
    alpha = step_scalars[0:1, 0:1]
    norm = step_scalars[0:1, 1:2]
    beta = step_scalars[0:1, 2:3]
    noise = step_scalars[0:1, 3:4]
    halves = answer.shape[1]

    def add(i, total):
        return total + arrived[i, :, halves * LANES:(halves + 1) * LANES]

    share = lax.fori_loop(0, arrived.shape[0], add, jnp.zeros((1, LANES), f32), unroll=8)
    alpha_next = norm / (total_sum(share) + noise)
    _, low, y, _, core = place(wide, narrow)
    product = jnp.zeros((1, (halves + 1) * LANES), f32)
    for high in range(2):
        for x in range(narrow // 2):
            member = device_at(high, low, y, x, core, wide, narrow)
            product = product + arrived[slot(member, wide, narrow)]
    for half in range(halves):
        begin = step_scalars[1 + halves + half:2 + halves + half, :]
        residual = begin - alpha * step_scalars[1 + half:2 + half, :]
        direction = residual + beta * begin
        image = product[:, half * LANES:(half + 1) * LANES] + noise_var * direction
        answer[0, half:half + 1, :] = alpha * begin + alpha_next * direction
        answer[1, half:half + 1, :] = residual - alpha_next * image
    copies = [pltpu.make_async_copy(answer.at[i], out, sems.at[i])
              for i, out in enumerate((solution_out, residual_out))]
    for copy in copies:
        copy.start()
    for copy in copies:
        copy.wait()


def call(kernel, out_shape, *args, scratch=(), vmem=VMEM_BYTES, **options):
    return pl.pallas_call(
        kernel,
        out_shape=out_shape,
        scratch_shapes=list(scratch),
        compiler_params=pltpu.CompilerParams(vmem_limit_bytes=vmem),
        **options,
    )(*args)


def to_all(blocks):
    group = list(range(blocks.shape[0] - 1, -1, -1))
    return lax.all_to_all(blocks, ALL, split_axis=0, concat_axis=0, axis_index_groups=[group], tiled=True)


def join_kernel(*refs):
    i = 0
    for block in refs[:-1]:
        for j in range(block.shape[0]):
            refs[-1][i] = block[j]
            i += 1


def join(*blocks):
    total = sum(b.shape[0] for b in blocks)
    return call(join_kernel, jax.ShapeDtypeStruct((total, *blocks[0].shape[1:]), f32), *blocks)


def first_round(own, wide, narrow):
    lows, across = wide // 4, narrow // 2
    if lows & (lows - 1) or across != 2 or lows > DIRECT:
        every = lax.all_gather(own, ALL, axis=0, tiled=True)
        every = every.reshape(2, lows, 2, across, 2, *own.shape[1:])
        high, low, y, x, core = place(wide, narrow)
        rows = every
        for place_in, axis in ((low, 1), (y, 1), (core, 2)):
            rows = lax.dynamic_index_in_dim(rows, place_in, axis, keepdims=False)
        columns = lax.dynamic_index_in_dim(every, high, 0, keepdims=False)
        columns = lax.dynamic_index_in_dim(columns, x, 2, keepdims=False)
        rows = jnp.swapaxes(rows, 0, 1).reshape(narrow, *own.shape[1:])
        return [[rows]], [columns.reshape(wide, *own.shape[1:])], (None, None)

    sizes = axis_sizes(wide, narrow)

    def swap(value, **flips):
        pairs = []
        for i in range(wide * narrow):
            spot = list(np.unravel_index(i, sizes))
            for name, flip in flips.items():
                axis = dict(high=HIGH, low=LOW, y=Y, x=X, core=CORE)[name]
                spot[axis] = int(spot[axis]) ^ flip
            pairs.append((i, int(np.ravel_multi_index(spot, sizes))))
        return lax.ppermute(value, ALL, pairs)

    rows = join(own, swap(own, high=1))
    columns = [own] + [swap(own, low=flip // 2, y=flip % 2) for flip in range(1, 2 * lows)]
    columns += [swap(block, core=1) for block in columns]
    parts = [[rows], [swap(rows, x=1)]]
    flips = [(flip // 2, flip % 2, core) for core in range(2) for flip in range(2 * lows)]
    return parts, columns, ([0, 1], flips)


def on_device(wide, narrow, features, projection, targets):
    rows, proj = features.shape[0], projection.shape[1]
    halves = rows // LANES
    lines = narrow * halves
    devices = wide * narrow
    scale = -2.0 / proj * math.log2(math.e)
    depth = 6 * proj + 16
    keep = 4 * devices * rows * rows <= KEEP_BYTES

    def shape(*dims, dtype=f32):
        return jax.ShapeDtypeStruct(dims, dtype)

    def scratch(*dims, dtype=f32):
        return pltpu.VMEM(dims, dtype)

    feat = features.shape[1]
    own = call(
        project_kernel, shape(1, proj + 8, rows), features, projection.T, targets.reshape(1, rows),
        in_specs=[pl.BlockSpec(memory_space=pl.ANY)] * 3, vmem=WHOLE_VMEM_BYTES,
        scratch=[scratch(CHUNKS, rows // CHUNKS, feat, dtype=bf16), scratch(proj, feat, dtype=bf16),
                 scratch(1, rows), pltpu.SemaphoreType.DMA((CHUNKS + 2,))])
    row_parts, column_blocks, flips = first_round(own, wide, narrow)
    parts = len(row_parts)
    groups = narrow // parts
    left = shape(groups, rows, depth, dtype=bf16)
    right = shape(wide, depth, rows, dtype=bf16)
    vector = shape(wide * halves, LANES)
    kept = shape(groups, wide, rows, rows) if keep else left
    group_lines = shape(groups * halves, LANES)
    sums = scratch(groups, rows, LANES)
    work = [scratch(*left.shape, dtype=bf16), sums] if keep else [sums]
    blocks, partials = [], []
    for part, row_blocks in enumerate(row_parts):
        fresh = part == 0
        first = functools.partial(
            first_kernel, proj, scale, wide, narrow, keep, flips, len(row_blocks),
            len(column_blocks) if fresh else 0)
        tiles = groups * wide * rows * rows
        made = call(
            first, (right, vector, kept, group_lines, group_lines) if fresh else (kept, group_lines),
            *row_blocks, *(column_blocks if fresh else columns_made), scratch=work,
            cost_estimate=pl.CostEstimate(
                flops=2 * tiles * depth, bytes_accessed=4 * tiles, transcendentals=tiles))
        if fresh:
            *columns_made, block, partial, own_start = made
        else:
            block, partial = made
        blocks.append(block)
        partials.append(partial)
    out = call(
        functools.partial(message_kernel, parts, wide, narrow, halves),
        shape(devices, 1, (lines + halves) * LANES), *partials, own_start,
        scratch=[scratch(lines, LANES)])
    block = blocks if keep else [columns_made[0], *blocks]
    sums = scratch(narrow, rows, LANES)
    out, step_scalars = call(
        functools.partial(second_kernel, wide, narrow, keep, parts),
        (shape(devices, 1, (halves + 1) * LANES), shape(1 + 2 * halves, LANES)),
        to_all(out), *block,
        scratch=[scratch(devices * halves, LANES)] * 3 + [scratch(lines, LANES), sums])
    answer, residual = call(
        functools.partial(last_kernel, wide, narrow), (shape(halves, LANES), shape(halves, LANES)),
        to_all(out), step_scalars,
        out_specs=(pl.BlockSpec(memory_space=pl.ANY),) * 2,
        scratch=[scratch(2, halves, LANES), pltpu.SemaphoreType.DMA((2,))])
    return answer.reshape(rows), residual.reshape(rows)


def solution(mesh):
    wide, narrow = mesh.shape["wide"], mesh.shape["narrow"]
    line = jax.sharding.Mesh(mesh.devices.reshape(wide * narrow), (ALL,))
    in_specs = (P(ALL, None), P(), P(ALL))
    return jax.shard_map(
        functools.partial(on_device, wide, narrow), mesh=line,
        in_specs=in_specs, out_specs=(P(ALL), P(ALL)), check_vma=False,
    )
```

```python
import functools

import jax
import jax.numpy as jnp
import numpy as np
from jax import lax
from jax.experimental import pallas as pl
from jax.experimental.pallas import tpu as pltpu
from jax.sharding import PartitionSpec as P

noise_var = 0.5
LANES = 128
CHUNKS = 2
DIRECT = 8
KEEP_BYTES = 8 * 2**20
VMEM_BYTES = 32 * 2**20
WHOLE_VMEM_BYTES = (53 * 1024 + 870) * 2**10
ALL = "all"
HIGH, LOW, Y, X, CORE = range(5)
highest = lax.Precision.HIGHEST
f32 = jnp.float32
bf16 = jnp.bfloat16


def split3(values):
    high = values.astype(bf16)
    rest = values - high.astype(f32)
    mid = rest.astype(bf16)
    low = (rest - mid.astype(f32)).astype(bf16)
    return high, mid, low


def exponent_rows(first, second):
    width = (first if not isinstance(first, float) else second).shape[1]
    row = lax.broadcasted_iota(jnp.int32, (16, width), 0)
    out = jnp.zeros((16, width), f32)
    for base, value in ((0, first), (3, second)):
        parts = (1.0, 1.0, 1.0) if isinstance(value, float) else [p.astype(f32) for p in split3(value)]
        for k, part in enumerate(parts):
            out = jnp.where(row == base + k, part, out)
    return out.astype(bf16)


def right_operand(latent, scale):
    square = jnp.sum(latent * latent, axis=0, keepdims=True) * scale
    h, m, l = split3(latent)
    return jnp.concatenate([h, m, l, h, m, h, exponent_rows(square, 1.0)], axis=0)


def left_operand(latent, scale):
    square = jnp.sum(latent * latent, axis=0, keepdims=True) * scale
    h, m, l = split3(latent * (-2.0 * scale))
    stacked = jnp.concatenate([h, h, h, m, m, l, exponent_rows(1.0, square)], axis=0)
    return stacked.T


def axis_sizes(wide, narrow):
    return 2, wide // 4, 2, narrow // 2, 2


def place(wide, narrow):
    rest, out = lax.axis_index(ALL), []
    for size in reversed(axis_sizes(wide, narrow)):
        out.append(rest % size)
        rest = rest // size
    return tuple(reversed(out))


def device_at(high, low, y, x, core, wide, narrow):
    return (((high * (wide // 4) + low) * 2 + y) * (narrow // 2) + x) * 2 + core


def slot(device, wide, narrow):
    return wide * narrow - 1 - device


def part_base(part, parts, wide, narrow):
    return 0 if parts == 1 else jnp.bitwise_xor(place(wide, narrow)[X], part) * 2


def row_sources(blocks, flips, wide, narrow):
    spots = [(b, i) for b in blocks for i in range(b.shape[0])]
    if flips is None:
        return [(b, i, i) for b, i in spots]
    high = place(wide, narrow)[HIGH]
    return [(b, i, jnp.bitwise_xor(high, flip)) for (b, i), flip in zip(spots, flips)]


def column_sources(blocks, flips, wide, narrow):
    spots = [(b, i) for b in blocks for i in range(b.shape[0])]
    if flips is None:
        return [(b, i, i) for b, i in spots]
    _, low, y, _, core = place(wide, narrow)
    return [(b, i, (jnp.bitwise_xor(low, f) * 2 + jnp.bitwise_xor(y, g)) * 2 + jnp.bitwise_xor(core, h))
            for (b, i), (f, g, h) in zip(spots, flips)]


def total_sum(values):
    return jnp.sum(jnp.sum(values, axis=0, keepdims=True), axis=1, keepdims=True)


def lane_sums(values):
    parts = jnp.concatenate(split3(values), axis=1)
    ones = jnp.ones((16, parts.shape[1]), bf16)
    return lax.dot_general(ones, parts, (((1,), (1,)), ((), ())),
                           preferred_element_type=f32)[0:1, :]


def make_rows(left, right, kept, read_vector, sums):
    groups, rows, _ = left.shape
    columns = right.shape[0]
    halves = rows // LANES

    def one_group(g, _):
        left_group = left[g]

        def one_column(c, acc):
            exponent = jnp.dot(left_group, right[c], preferred_element_type=f32)
            tile = jnp.exp(exponent)
            if kept is not None:
                kept[g, c] = tile
            for half in range(halves):
                acc = acc + tile[:, half * LANES:(half + 1) * LANES] * read_vector(c, half)
            return acc

        sums[g] = lax.fori_loop(0, columns, one_column, jnp.zeros((rows, LANES), f32), unroll=8)
        return 0

    lax.fori_loop(0, groups, one_group, 0, unroll=groups <= 2)


def use_rows(kept, read_vector, sums):
    groups, columns, rows, _ = kept.shape
    halves = rows // LANES

    def one_group(g, _):
        def one_column(c, acc):
            for half in range(halves):
                acc = acc + kept[g, c, :, half * LANES:(half + 1) * LANES] * read_vector(c, half)
            return acc

        sums[g] = lax.fori_loop(0, columns, one_column, jnp.zeros((rows, LANES), f32), unroll=8)
        return 0

    lax.fori_loop(0, groups, one_group, 0, unroll=groups <= 2)


def write_rows(sums, out, bases):
    groups, rows, _ = sums.shape
    halves = rows // LANES
    total = lane_sums(sums[...].reshape(groups * rows, LANES))
    for g in range(groups):
        base = bases[g * len(bases) // groups]
        for half in range(halves):
            line = (base + g % (groups // len(bases))) * halves + half
            start = (g * halves + half) * LANES
            out[pl.ds(line, 1), :] = total[:, start:start + LANES]


def project_kernel(features, projection_t, targets, out, feature_buf, projection_buf, target_buf, sems):
    proj = projection_t.shape[0]
    chunks, height, _ = feature_buf.shape
    copies = [
        pltpu.make_async_copy(features.at[pl.ds(i * height, height)], feature_buf.at[i], sems.at[i])
        for i in range(chunks)]
    copies.insert(1, pltpu.make_async_copy(projection_t, projection_buf, sems.at[chunks]))
    copies.append(pltpu.make_async_copy(targets, target_buf, sems.at[chunks + 1]))
    for copy in copies:
        copy.start()
    copies.pop(1).wait()
    for i in range(chunks):
        copies[i].wait()
        out[0, 0:proj, i * height:(i + 1) * height] = lax.dot_general(
            projection_buf[...], feature_buf[i], (((1,), (1,)), ((), ())), preferred_element_type=f32)
    copies[-1].wait()
    out[0, proj:proj + 8, :] = jnp.broadcast_to(target_buf[...], (8, out.shape[2]))


def first_kernel(proj, scale, wide, narrow, keep, flips, row_count, column_count, *refs):
    row_blocks, column_blocks = refs[:row_count], refs[row_count:row_count + column_count]
    refs = refs[row_count + column_count:]
    right, column_vector = refs[:2]
    kept, left = (refs[2], refs[-2]) if keep else (None, refs[2])
    partial, starts, sums = refs[3], refs[4] if column_count else None, refs[-1]
    rows = left.shape[1]
    halves = rows // LANES
    for block, i, source in column_sources(column_blocks, flips[1], wide, narrow) if column_count else ():
        right[source] = right_operand(block[i, 0:proj, :], scale)
        for half in range(halves):
            column_vector[pl.ds(source * halves + half, 1), :] = block[
                i, proj:proj + 1, half * LANES:(half + 1) * LANES]
    for block, i, source in row_sources(row_blocks, flips[0], wide, narrow):
        left[source] = left_operand(block[i, 0:proj, :], scale)
        for half in range(halves) if column_count else ():
            starts[pl.ds(source * halves + half, 1), :] = block[
                i, proj:proj + 1, half * LANES:(half + 1) * LANES]
    make_rows(left, right, kept, lambda c, half: column_vector[pl.ds(c * halves + half, 1), :], sums)
    write_rows(sums, partial, [0])


def message_kernel(parts, wide, narrow, halves, *refs):
    partials, start, out, held = refs[:parts], refs[parts], refs[-2], refs[-1]
    for part, lines in enumerate(partials):
        base = part_base(part, parts, wide, narrow) * halves
        for line in range(lines.shape[0]):
            held[pl.ds(base + line, 1), :] = lines[line:line + 1, :]
    here = place(wide, narrow)
    mine = here[HIGH] * halves
    if parts == 1:
        mine = mine + here[X] * 2 * halves
    pieces = [held[line:line + 1, :] for line in range(held.shape[0])]
    pieces += [start[pl.ds(mine + half, 1), :] for half in range(halves)]
    block = jnp.concatenate(pieces, axis=1)

    def copy(i, _):
        out[i] = block
        return 0

    lax.fori_loop(0, out.shape[0], copy, 0, unroll=8)


def second_kernel(wide, narrow, keep, parts, *refs):
    arrived, out, step_scalars, direction, images, targets, partial, sums = refs[:1] + refs[-7:]
    lines = partial.shape[0]
    halves = lines // narrow
    across = narrow // 2
    group = [(high, x) for x in range(narrow // 2) for high in range(2)]

    def unpack(low, _):
        for y, core in ((0, 0), (0, 1), (1, 0), (1, 1)):
            members = [device_at(high, low, y, x, core, wide, narrow) for high, x in group]
            slots = [slot(member, wide, narrow) for member in members]
            total = arrived[slots[0], :, 0:lines * LANES]
            for spot in slots[1:]:
                total = total + arrived[spot, :, 0:lines * LANES]
            for r, member in enumerate(members):
                for half in range(halves):
                    start = arrived[slots[r], :, (lines + half) * LANES:(lines + half + 1) * LANES]
                    line = r * halves + half
                    spot = pl.ds(member * halves + half, 1)
                    targets[spot, :] = start
                    images[spot, :] = total[:, line * LANES:(line + 1) * LANES] + noise_var * start
        return 0

    lax.fori_loop(0, wide // 4, unpack, 0, unroll=2)
    start, first = targets[...], images[...]
    norm = total_sum(start * start)
    alpha = norm / total_sum(start * first)
    residual = start - alpha * first
    norm_next = total_sum(residual * residual)
    beta = norm_next / norm
    whole = residual + beta * start
    direction[...] = whole
    high, low, y, x, core = place(wide, narrow)

    def read_vector(c, half):
        source = device_at(high, c // 4, c // 2 % 2, x, c % 2, wide, narrow)
        return direction[pl.ds(source * halves + half, 1), :]

    groups = narrow // parts
    for part in range(parts):
        part_sums = sums.at[part * groups:(part + 1) * groups]
        if keep:
            use_rows(refs[1 + part], read_vector, part_sums)
        else:
            make_rows(refs[2 + part], refs[1], None, read_vector, part_sums)
    write_rows(sums, partial, [part_base(part, parts, wide, narrow) for part in range(parts)])
    share = jnp.zeros((1, LANES), f32)
    for r, (row_high, row_x) in enumerate(group):
        for half in range(halves):
            spot = pl.ds(device_at(row_high, low, y, row_x, core, wide, narrow) * halves + half, 1)
            line = r * halves + half
            share = share + direction[spot, :] * partial[line:line + 1, :]
    blocks = [
        jnp.concatenate([partial[r * halves + half:r * halves + half + 1, :]
                         for half in range(halves)] + [share], axis=1)
        for r in range(narrow)]

    def copy(to_low, _):
        for r, (to_high, to_x) in enumerate(group):
            for to_y, to_core in ((0, 0), (0, 1), (1, 0), (1, 1)):
                to = device_at(to_high, to_low, to_y, to_x, to_core, wide, narrow)
                out[slot(to, wide, narrow)] = blocks[r]
        return 0

    lax.fori_loop(0, wide // 4, copy, 0, unroll=2)
    lane = lax.broadcasted_iota(jnp.int32, (1, LANES), 1)
    noise = noise_var * total_sum(whole * whole)
    step_scalars[0:1, :] = jnp.where(lane == 0, alpha, jnp.where(
        lane == 1, norm_next, jnp.where(lane == 2, beta, noise)))
    for half in range(halves):
        spot = pl.ds(device_at(high, low, y, x, core, wide, narrow) * halves + half, 1)
        step_scalars[1 + half:2 + half, :] = images[spot, :]
        step_scalars[1 + halves + half:2 + halves + half, :] = targets[spot, :]


def last_kernel(wide, narrow, arrived, step_scalars, solution_out, residual_out, answer, sems):
    alpha = step_scalars[0:1, 0:1]
    norm = step_scalars[0:1, 1:2]
    beta = step_scalars[0:1, 2:3]
    noise = step_scalars[0:1, 3:4]
    halves = answer.shape[1]

    def add(i, total):
        return total + arrived[i, :, halves * LANES:(halves + 1) * LANES]

    share = lax.fori_loop(0, arrived.shape[0], add, jnp.zeros((1, LANES), f32), unroll=32)
    alpha_next = norm / (total_sum(share) + noise)
    _, low, y, _, core = place(wide, narrow)
    product = jnp.zeros((1, (halves + 1) * LANES), f32)
    for high in range(2):
        for x in range(narrow // 2):
            member = device_at(high, low, y, x, core, wide, narrow)
            product = product + arrived[slot(member, wide, narrow)]
    for half in range(halves):
        begin = step_scalars[1 + halves + half:2 + halves + half, :]
        residual = begin - alpha * step_scalars[1 + half:2 + half, :]
        direction = residual + beta * begin
        image = product[:, half * LANES:(half + 1) * LANES] + noise_var * direction
        answer[0, half:half + 1, :] = alpha * begin + alpha_next * direction
        answer[1, half:half + 1, :] = residual - alpha_next * image
    copies = [pltpu.make_async_copy(answer.at[i], out, sems.at[i])
              for i, out in enumerate((solution_out, residual_out))]
    for copy in copies:
        copy.start()
    for copy in copies:
        copy.wait()


def call(kernel, out_shape, *args, scratch=(), vmem=VMEM_BYTES, **options):
    return pl.pallas_call(
        kernel,
        out_shape=out_shape,
        scratch_shapes=list(scratch),
        compiler_params=pltpu.CompilerParams(vmem_limit_bytes=vmem),
        **options,
    )(*args)


def to_all(blocks):
    group = list(range(blocks.shape[0] - 1, -1, -1))
    return lax.all_to_all(blocks, ALL, split_axis=0, concat_axis=0, axis_index_groups=[group], tiled=True)


def join_kernel(*refs):
    i = 0
    for block in refs[:-1]:
        for j in range(block.shape[0]):
            refs[-1][i] = block[j]
            i += 1


def join(*blocks):
    total = sum(b.shape[0] for b in blocks)
    return call(join_kernel, jax.ShapeDtypeStruct((total, *blocks[0].shape[1:]), f32), *blocks)


def first_round(own, wide, narrow):
    lows, across = wide // 4, narrow // 2
    if lows & (lows - 1) or across != 2 or lows > DIRECT:
        every = lax.all_gather(own, ALL, axis=0, tiled=True)
        every = every.reshape(2, lows, 2, across, 2, *own.shape[1:])
        high, low, y, x, core = place(wide, narrow)
        rows = every
        for place_in, axis in ((low, 1), (y, 1), (core, 2)):
            rows = lax.dynamic_index_in_dim(rows, place_in, axis, keepdims=False)
        columns = lax.dynamic_index_in_dim(every, high, 0, keepdims=False)
        columns = lax.dynamic_index_in_dim(columns, x, 2, keepdims=False)
        rows = jnp.swapaxes(rows, 0, 1).reshape(narrow, *own.shape[1:])
        return [[rows]], [columns.reshape(wide, *own.shape[1:])], (None, None)

    sizes = axis_sizes(wide, narrow)

    def swap(value, **flips):
        pairs = []
        for i in range(wide * narrow):
            spot = list(np.unravel_index(i, sizes))
            for name, flip in flips.items():
                axis = dict(high=HIGH, low=LOW, y=Y, x=X, core=CORE)[name]
                spot[axis] = int(spot[axis]) ^ flip
            pairs.append((i, int(np.ravel_multi_index(spot, sizes))))
        return lax.ppermute(value, ALL, pairs)

    rows = join(own, swap(own, high=1))
    columns = [own] + [swap(own, low=flip // 2, y=flip % 2) for flip in range(1, 2 * lows)]
    columns += [swap(block, core=1) for block in columns]
    parts = [[rows], [swap(rows, x=1)]]
    flips = [(flip // 2, flip % 2, core) for core in range(2) for flip in range(2 * lows)]
    return parts, columns, ([0, 1], flips)


def on_device(wide, narrow, features, projection, targets):
    rows, proj = features.shape[0], projection.shape[1]
    halves = rows // LANES
    lines = narrow * halves
    devices = wide * narrow
    scale = -2.0 / proj
    depth = 6 * proj + 16
    keep = 4 * devices * rows * rows <= KEEP_BYTES

    def shape(*dims, dtype=f32):
        return jax.ShapeDtypeStruct(dims, dtype)

    def scratch(*dims, dtype=f32):
        return pltpu.VMEM(dims, dtype)

    feat = features.shape[1]
    own = call(
        project_kernel, shape(1, proj + 8, rows), features, projection.T, targets.reshape(1, rows),
        in_specs=[pl.BlockSpec(memory_space=pl.ANY)] * 3, vmem=WHOLE_VMEM_BYTES,
        scratch=[scratch(CHUNKS, rows // CHUNKS, feat, dtype=bf16), scratch(proj, feat, dtype=bf16),
                 scratch(1, rows), pltpu.SemaphoreType.DMA((CHUNKS + 2,))])
    row_parts, column_blocks, flips = first_round(own, wide, narrow)
    parts = len(row_parts)
    groups = narrow // parts
    left = shape(groups, rows, depth, dtype=bf16)
    right = shape(wide, depth, rows, dtype=bf16)
    vector = shape(wide * halves, LANES)
    kept = shape(groups, wide, rows, rows) if keep else left
    group_lines = shape(groups * halves, LANES)
    sums = scratch(groups, rows, LANES)
    work = [scratch(*left.shape, dtype=bf16), sums] if keep else [sums]
    blocks, partials = [], []
    for part, row_blocks in enumerate(row_parts):
        fresh = part == 0
        first = functools.partial(
            first_kernel, proj, scale, wide, narrow, keep, flips, len(row_blocks),
            len(column_blocks) if fresh else 0)
        tiles = groups * wide * rows * rows
        made = call(
            first, (right, vector, kept, group_lines, group_lines) if fresh else (kept, group_lines),
            *row_blocks, *(column_blocks if fresh else columns_made), scratch=work,
            cost_estimate=pl.CostEstimate(
                flops=2 * tiles * depth, bytes_accessed=4 * tiles, transcendentals=tiles))
        if fresh:
            *columns_made, block, partial, own_start = made
        else:
            block, partial = made
        blocks.append(block)
        partials.append(partial)
    out = call(
        functools.partial(message_kernel, parts, wide, narrow, halves),
        shape(devices, 1, (lines + halves) * LANES), *partials, own_start,
        scratch=[scratch(lines, LANES)])
    block = blocks if keep else [columns_made[0], *blocks]
    sums = scratch(narrow, rows, LANES)
    out, step_scalars = call(
        functools.partial(second_kernel, wide, narrow, keep, parts),
        (shape(devices, 1, (halves + 1) * LANES), shape(1 + 2 * halves, LANES)),
        to_all(out), *block,
        scratch=[scratch(devices * halves, LANES)] * 3 + [scratch(lines, LANES), sums])
    answer, residual = call(
        functools.partial(last_kernel, wide, narrow), (shape(halves, LANES), shape(halves, LANES)),
        to_all(out), step_scalars,
        out_specs=(pl.BlockSpec(memory_space=pl.ANY),) * 2,
        scratch=[scratch(2, halves, LANES), pltpu.SemaphoreType.DMA((2,))])
    return answer.reshape(rows), residual.reshape(rows)


def solution(mesh):
    wide, narrow = mesh.shape["wide"], mesh.shape["narrow"]
    line = jax.sharding.Mesh(mesh.devices.reshape(wide * narrow), (ALL,))
    in_specs = (P(ALL, None), P(), P(ALL))
    return jax.shard_map(
        functools.partial(on_device, wide, narrow), mesh=line,
        in_specs=in_specs, out_specs=(P(ALL), P(ALL)), check_vma=False,
    )
```

```python
import functools
import math

import jax
import jax.numpy as jnp
import numpy as np
from jax import lax
from jax.experimental import pallas as pl
from jax.experimental.pallas import tpu as pltpu
from jax.sharding import PartitionSpec as P

noise_var = 0.5
LANES = 128
CHUNKS = 2
EARLY = 10**9
KEEP_BYTES = 8 * 2**20
VMEM_BYTES = 32 * 2**20
WHOLE_VMEM_BYTES = (53 * 1024 + 870) * 2**10
ALL = "all"
HIGH, LOW, Y, X, CORE = range(5)
highest = lax.Precision.HIGHEST
f32 = jnp.float32
bf16 = jnp.bfloat16


def split3(values):
    high = values.astype(bf16)
    rest = values - high.astype(f32)
    mid = rest.astype(bf16)
    low = (rest - mid.astype(f32)).astype(bf16)
    return high, mid, low


def exponent_rows(first, second):
    width = (first if not isinstance(first, float) else second).shape[1]
    row = lax.broadcasted_iota(jnp.int32, (16, width), 0)
    out = jnp.zeros((16, width), f32)
    for base, value in ((0, first), (3, second)):
        parts = (1.0, 1.0, 1.0) if isinstance(value, float) else [p.astype(f32) for p in split3(value)]
        for k, part in enumerate(parts):
            out = jnp.where(row == base + k, part, out)
    return out.astype(bf16)


def right_operand(latent, scale):
    square = jnp.sum(latent * latent, axis=0, keepdims=True) * scale
    h, m, l = split3(latent)
    return jnp.concatenate([h, m, l, h, m, h, exponent_rows(square, 1.0)], axis=0)


def left_operand(latent, scale):
    square = jnp.sum(latent * latent, axis=0, keepdims=True) * scale
    h, m, l = split3(latent * (-2.0 * scale))
    stacked = jnp.concatenate([h, h, h, m, m, l, exponent_rows(1.0, square)], axis=0)
    return stacked.T


def axis_sizes(wide, narrow):
    return 2, wide // 4, 2, narrow // 2, 2


def place(wide, narrow):
    rest, out = lax.axis_index(ALL), []
    for size in reversed(axis_sizes(wide, narrow)):
        out.append(rest % size)
        rest = rest // size
    return tuple(reversed(out))


def device_at(high, low, y, x, core, wide, narrow):
    return (((high * (wide // 4) + low) * 2 + y) * (narrow // 2) + x) * 2 + core


def slot(device, wide, narrow):
    return wide * narrow - 1 - device


def part_base(part, parts, wide, narrow):
    return 0 if parts == 1 else jnp.bitwise_xor(place(wide, narrow)[X], part) * 2


def row_sources(blocks, flips, wide, narrow):
    spots = [(b, i) for b in blocks for i in range(b.shape[0])]
    if flips is None:
        return [(b, i, i) for b, i in spots]
    high = place(wide, narrow)[HIGH]
    return [(b, i, jnp.bitwise_xor(high, flip)) for (b, i), flip in zip(spots, flips)]


def column_sources(blocks, flips, wide, narrow):
    spots = [(b, i) for b in blocks for i in range(b.shape[0])]
    if flips is None:
        return [(b, i, i) for b, i in spots]
    _, low, y, _, core = place(wide, narrow)

    def flipped(value, flip):
        constant, by_core = flip
        return jnp.bitwise_xor(value, jnp.bitwise_xor(constant, by_core * core))

    return [(b, i, (flipped(low, f) * 2 + flipped(y, g)) * 2 + jnp.bitwise_xor(core, h))
            for (b, i), (f, g, h) in zip(spots, flips)]


def total_sum(values):
    return jnp.sum(jnp.sum(values, axis=0, keepdims=True), axis=1, keepdims=True)


def lane_sums(values):
    parts = jnp.concatenate(split3(values), axis=1)
    ones = jnp.ones((16, parts.shape[1]), bf16)
    return lax.dot_general(ones, parts, (((1,), (1,)), ((), ())),
                           preferred_element_type=f32)[0:1, :]


def make_rows(left, right, kept, read_vector, sums):
    groups, rows, _ = left.shape
    columns = right.shape[0]
    halves = rows // LANES

    def one_group(g, _):
        left_group = left[g]

        def one_column(c, acc):
            exponent = jnp.dot(left_group, right[c], preferred_element_type=f32)
            tile = jnp.exp2(exponent)
            if kept is not None:
                kept[g, c] = tile
            for half in range(halves):
                acc = acc + tile[:, half * LANES:(half + 1) * LANES] * read_vector(c, half)
            return acc

        sums[g] = lax.fori_loop(0, columns, one_column, jnp.zeros((rows, LANES), f32), unroll=8)
        return 0

    lax.fori_loop(0, groups, one_group, 0, unroll=groups <= 2)


def use_rows(kept, read_vector, sums):
    groups, columns, rows, _ = kept.shape
    halves = rows // LANES

    def one_group(g, _):
        def one_column(c, acc):
            for half in range(halves):
                acc = acc + kept[g, c, :, half * LANES:(half + 1) * LANES] * read_vector(c, half)
            return acc

        sums[g] = lax.fori_loop(0, columns, one_column, jnp.zeros((rows, LANES), f32), unroll=8)
        return 0

    lax.fori_loop(0, groups, one_group, 0, unroll=groups <= 2)


def write_rows(sums, out, bases):
    groups, rows, _ = sums.shape
    halves = rows // LANES
    total = lane_sums(sums[...].reshape(groups * rows, LANES))
    for g in range(groups):
        base = bases[g * len(bases) // groups]
        for half in range(halves):
            line = (base + g % (groups // len(bases))) * halves + half
            start = (g * halves + half) * LANES
            out[pl.ds(line, 1), :] = total[:, start:start + LANES]


def project_kernel(features, projection_t, targets, out, feature_buf, projection_buf, target_buf, sems):
    proj = projection_t.shape[0]
    chunks, height, _ = feature_buf.shape
    copies = [
        pltpu.make_async_copy(features.at[pl.ds(i * height, height)], feature_buf.at[i], sems.at[i])
        for i in range(chunks)]
    copies.insert(1, pltpu.make_async_copy(projection_t, projection_buf, sems.at[chunks]))
    copies.append(pltpu.make_async_copy(targets, target_buf, sems.at[chunks + 1]))
    for copy in copies:
        copy.start()
    copies.pop(1).wait()
    for i in range(chunks):
        copies[i].wait()
        out[0, 0:proj, i * height:(i + 1) * height] = lax.dot_general(
            projection_buf[...], feature_buf[i], (((1,), (1,)), ((), ())), preferred_element_type=f32)
    copies[-1].wait()
    out[0, proj:proj + 8, :] = jnp.broadcast_to(target_buf[...], (8, out.shape[2]))


def first_kernel(proj, scale, wide, narrow, keep, flips, row_count, column_count, *refs):
    row_blocks, column_blocks = refs[:row_count], refs[row_count:row_count + column_count]
    refs = refs[row_count + column_count:]
    right, column_vector = refs[:2]
    kept, left = (refs[2], refs[-2]) if keep else (None, refs[2])
    partial, starts, sums = refs[3], refs[4] if column_count else None, refs[-1]
    rows = left.shape[1]
    halves = rows // LANES
    for block, i, source in column_sources(column_blocks, flips[1], wide, narrow) if column_count else ():
        right[source] = right_operand(block[i, 0:proj, :], scale)
        for half in range(halves):
            column_vector[pl.ds(source * halves + half, 1), :] = block[
                i, proj:proj + 1, half * LANES:(half + 1) * LANES]
    for block, i, source in row_sources(row_blocks, flips[0], wide, narrow):
        left[source] = left_operand(block[i, 0:proj, :], scale)
        for half in range(halves) if column_count else ():
            starts[pl.ds(source * halves + half, 1), :] = block[
                i, proj:proj + 1, half * LANES:(half + 1) * LANES]
    make_rows(left, right, kept, lambda c, half: column_vector[pl.ds(c * halves + half, 1), :], sums)
    write_rows(sums, partial, [0])


def message_kernel(parts, wide, narrow, halves, *refs):
    partials, start, out, held = refs[:parts], refs[parts], refs[-2], refs[-1]
    for part, lines in enumerate(partials):
        base = part_base(part, parts, wide, narrow) * halves
        for line in range(lines.shape[0]):
            held[pl.ds(base + line, 1), :] = lines[line:line + 1, :]
    here = place(wide, narrow)
    mine = here[HIGH] * halves
    if parts == 1:
        mine = mine + here[X] * 2 * halves
    pieces = [held[line:line + 1, :] for line in range(held.shape[0])]
    pieces += [start[pl.ds(mine + half, 1), :] for half in range(halves)]
    block = jnp.concatenate(pieces, axis=1)

    def copy(i, _):
        out[i] = block
        return 0

    lax.fori_loop(0, out.shape[0], copy, 0, unroll=8)


def second_kernel(wide, narrow, keep, parts, *refs):
    arrived, out, step_scalars, direction, images, targets, partial, sums = refs[:1] + refs[-7:]
    lines = partial.shape[0]
    halves = lines // narrow
    across = narrow // 2
    group = [(high, x) for x in range(narrow // 2) for high in range(2)]

    def unpack(low, _):
        for y, core in ((0, 0), (0, 1), (1, 0), (1, 1)):
            members = [device_at(high, low, y, x, core, wide, narrow) for high, x in group]
            slots = [slot(member, wide, narrow) for member in members]
            total = arrived[slots[0], :, 0:lines * LANES]
            for spot in slots[1:]:
                total = total + arrived[spot, :, 0:lines * LANES]
            for r, member in enumerate(members):
                for half in range(halves):
                    start = arrived[slots[r], :, (lines + half) * LANES:(lines + half + 1) * LANES]
                    line = r * halves + half
                    spot = pl.ds(member * halves + half, 1)
                    targets[spot, :] = start
                    images[spot, :] = total[:, line * LANES:(line + 1) * LANES] + noise_var * start
        return 0

    lax.fori_loop(0, wide // 4, unpack, 0, unroll=2)
    start, first = targets[...], images[...]
    norm = total_sum(start * start)
    alpha = norm / total_sum(start * first)
    residual = start - alpha * first
    norm_next = total_sum(residual * residual)
    beta = norm_next / norm
    whole = residual + beta * start
    direction[...] = whole
    high, low, y, x, core = place(wide, narrow)

    def read_vector(c, half):
        source = device_at(high, c // 4, c // 2 % 2, x, c % 2, wide, narrow)
        return direction[pl.ds(source * halves + half, 1), :]

    groups = narrow // parts
    for part in range(parts):
        part_sums = sums.at[part * groups:(part + 1) * groups]
        if keep:
            use_rows(refs[1 + part], read_vector, part_sums)
        else:
            make_rows(refs[2 + part], refs[1], None, read_vector, part_sums)
    write_rows(sums, partial, [part_base(part, parts, wide, narrow) for part in range(parts)])
    share = jnp.zeros((1, LANES), f32)
    for r, (row_high, row_x) in enumerate(group):
        for half in range(halves):
            spot = pl.ds(device_at(row_high, low, y, row_x, core, wide, narrow) * halves + half, 1)
            line = r * halves + half
            share = share + direction[spot, :] * partial[line:line + 1, :]
    blocks = [
        jnp.concatenate([partial[r * halves + half:r * halves + half + 1, :]
                         for half in range(halves)] + [share], axis=1)
        for r in range(narrow)]

    def copy(to_low, _):
        for r, (to_high, to_x) in enumerate(group):
            for to_y, to_core in ((0, 0), (0, 1), (1, 0), (1, 1)):
                to = device_at(to_high, to_low, to_y, to_x, to_core, wide, narrow)
                out[slot(to, wide, narrow)] = blocks[r]
        return 0

    lax.fori_loop(0, wide // 4, copy, 0, unroll=2)
    lane = lax.broadcasted_iota(jnp.int32, (1, LANES), 1)
    noise = noise_var * total_sum(whole * whole)
    step_scalars[0:1, :] = jnp.where(lane == 0, alpha, jnp.where(
        lane == 1, norm_next, jnp.where(lane == 2, beta, noise)))
    for half in range(halves):
        spot = pl.ds(device_at(high, low, y, x, core, wide, narrow) * halves + half, 1)
        step_scalars[1 + half:2 + half, :] = images[spot, :]
        step_scalars[1 + halves + half:2 + halves + half, :] = targets[spot, :]


def last_kernel(wide, narrow, arrived, step_scalars, solution_out, residual_out, answer, sems):
    alpha = step_scalars[0:1, 0:1]
    norm = step_scalars[0:1, 1:2]
    beta = step_scalars[0:1, 2:3]
    noise = step_scalars[0:1, 3:4]
    halves = answer.shape[1]

    def add(i, total):
        return total + arrived[i, :, halves * LANES:(halves + 1) * LANES]

    share = lax.fori_loop(0, arrived.shape[0], add, jnp.zeros((1, LANES), f32), unroll=32)
    alpha_next = norm / (total_sum(share) + noise)
    _, low, y, _, core = place(wide, narrow)
    product = jnp.zeros((1, (halves + 1) * LANES), f32)
    for high in range(2):
        for x in range(narrow // 2):
            member = device_at(high, low, y, x, core, wide, narrow)
            product = product + arrived[slot(member, wide, narrow)]
    for half in range(halves):
        begin = step_scalars[1 + halves + half:2 + halves + half, :]
        residual = begin - alpha * step_scalars[1 + half:2 + half, :]
        direction = residual + beta * begin
        image = product[:, half * LANES:(half + 1) * LANES] + noise_var * direction
        answer[0, half:half + 1, :] = alpha * begin + alpha_next * direction
        answer[1, half:half + 1, :] = residual - alpha_next * image
    copies = [pltpu.make_async_copy(answer.at[i], out, sems.at[i])
              for i, out in enumerate((solution_out, residual_out))]
    for copy in copies:
        copy.start()
    for copy in copies:
        copy.wait()


def call(kernel, out_shape, *args, scratch=(), vmem=VMEM_BYTES, **options):
    return pl.pallas_call(
        kernel,
        out_shape=out_shape,
        scratch_shapes=list(scratch),
        compiler_params=pltpu.CompilerParams(vmem_limit_bytes=vmem),
        **options,
    )(*args)


def to_all(blocks):
    group = list(range(blocks.shape[0] - 1, -1, -1))
    return lax.all_to_all(blocks, ALL, split_axis=0, concat_axis=0, axis_index_groups=[group], tiled=True)


def join_kernel(*refs):
    i = 0
    for block in refs[:-1]:
        for j in range(block.shape[0]):
            refs[-1][i] = block[j]
            i += 1


def pick_kernel(i, block, out):
    out[0] = block[i]


def pick(blocks, i):
    return call(functools.partial(pick_kernel, i), jax.ShapeDtypeStruct((1, *blocks.shape[1:]), f32), blocks)


def join(*blocks, flops=0):
    total = sum(b.shape[0] for b in blocks)
    return call(join_kernel, jax.ShapeDtypeStruct((total, *blocks[0].shape[1:]), f32), *blocks,
                cost_estimate=pl.CostEstimate(flops=flops, bytes_accessed=0, transcendentals=0))


def first_round(own, wide, narrow):
    lows, across = wide // 4, narrow // 2
    if lows != 2 or across != 2:
        every = lax.all_gather(own, ALL, axis=0, tiled=True)
        every = every.reshape(2, lows, 2, across, 2, *own.shape[1:])
        high, low, y, x, core = place(wide, narrow)
        rows = every
        for place_in, axis in ((low, 1), (y, 1), (core, 2)):
            rows = lax.dynamic_index_in_dim(rows, place_in, axis, keepdims=False)
        columns = lax.dynamic_index_in_dim(every, high, 0, keepdims=False)
        columns = lax.dynamic_index_in_dim(columns, x, 2, keepdims=False)
        rows = jnp.swapaxes(rows, 0, 1).reshape(narrow, *own.shape[1:])
        return [[rows]], [columns.reshape(wide, *own.shape[1:])], (None, None)

    sizes = axis_sizes(wide, narrow)

    def swap(value, *flips):
        pairs = []
        for i in range(wide * narrow):
            spot = [int(p) for p in np.unravel_index(i, sizes)]
            for axis in flips[spot[CORE] % len(flips)]:
                spot[axis] ^= 1
            pairs.append((i, int(np.ravel_multi_index(spot, sizes))))
        return lax.ppermute(value, ALL, pairs)

    rows = join(own, swap(own, [HIGH]), flops=EARLY)
    parts = [[rows], [swap(rows, [X])]]
    pair = join(own, swap(own, [CORE]))
    near = swap(pair, [LOW], [Y])
    across_both = swap(own, [LOW, Y])
    columns = [pair, near, swap(pick(near, 0), [CORE]), swap(pick(near, 1), [CORE]), across_both,
               swap(across_both, [CORE])]
    none, one, same, other = (0, 0), (1, 0), (0, 1), (1, 1)
    flips = [(none, none, 0), (none, none, 1), (other, same, 0), (other, same, 1),
             (same, other, 1), (same, other, 0), (one, one, 0), (one, one, 1)]
    return parts, columns, ([0, 1], flips)


def on_device(wide, narrow, features, projection, targets):
    rows, proj = features.shape[0], projection.shape[1]
    halves = rows // LANES
    lines = narrow * halves
    devices = wide * narrow
    scale = -2.0 / proj * math.log2(math.e)
    depth = 6 * proj + 16
    keep = 4 * devices * rows * rows <= KEEP_BYTES

    def shape(*dims, dtype=f32):
        return jax.ShapeDtypeStruct(dims, dtype)

    def scratch(*dims, dtype=f32):
        return pltpu.VMEM(dims, dtype)

    feat = features.shape[1]
    own = call(
        project_kernel, shape(1, proj + 8, rows), features, projection.T, targets.reshape(1, rows),
        in_specs=[pl.BlockSpec(memory_space=pl.ANY)] * 3, vmem=WHOLE_VMEM_BYTES,
        scratch=[scratch(CHUNKS, rows // CHUNKS, feat, dtype=bf16), scratch(proj, feat, dtype=bf16),
                 scratch(1, rows), pltpu.SemaphoreType.DMA((CHUNKS + 2,))])
    row_parts, column_blocks, flips = first_round(own, wide, narrow)
    parts = len(row_parts)
    groups = narrow // parts
    left = shape(groups, rows, depth, dtype=bf16)
    right = shape(wide, depth, rows, dtype=bf16)
    vector = shape(wide * halves, LANES)
    kept = shape(groups, wide, rows, rows) if keep else left
    group_lines = shape(groups * halves, LANES)
    sums = scratch(groups, rows, LANES)
    work = [scratch(*left.shape, dtype=bf16), sums] if keep else [sums]
    blocks, partials = [], []
    for part, row_blocks in enumerate(row_parts):
        fresh = part == 0
        first = functools.partial(
            first_kernel, proj, scale, wide, narrow, keep, flips, len(row_blocks),
            len(column_blocks) if fresh else 0)
        tiles = groups * wide * rows * rows
        made = call(
            first, (right, vector, kept, group_lines, group_lines) if fresh else (kept, group_lines),
            *row_blocks, *(column_blocks if fresh else columns_made), scratch=work,
            cost_estimate=pl.CostEstimate(
                flops=2 * tiles * depth, bytes_accessed=4 * tiles, transcendentals=tiles))
        if fresh:
            *columns_made, block, partial, own_start = made
        else:
            block, partial = made
        blocks.append(block)
        partials.append(partial)
    out = call(
        functools.partial(message_kernel, parts, wide, narrow, halves),
        shape(devices, 1, (lines + halves) * LANES), *partials, own_start,
        scratch=[scratch(lines, LANES)])
    block = blocks if keep else [columns_made[0], *blocks]
    sums = scratch(narrow, rows, LANES)
    out, step_scalars = call(
        functools.partial(second_kernel, wide, narrow, keep, parts),
        (shape(devices, 1, (halves + 1) * LANES), shape(1 + 2 * halves, LANES)),
        to_all(out), *block,
        scratch=[scratch(devices * halves, LANES)] * 3 + [scratch(lines, LANES), sums])
    answer, residual = call(
        functools.partial(last_kernel, wide, narrow), (shape(halves, LANES), shape(halves, LANES)),
        to_all(out), step_scalars,
        out_specs=(pl.BlockSpec(memory_space=pl.ANY),) * 2,
        scratch=[scratch(2, halves, LANES), pltpu.SemaphoreType.DMA((2,))])
    return answer.reshape(rows), residual.reshape(rows)


def solution(mesh):
    wide, narrow = mesh.shape["wide"], mesh.shape["narrow"]
    line = jax.sharding.Mesh(mesh.devices.reshape(wide * narrow), (ALL,))
    in_specs = (P(ALL, None), P(), P(ALL))
    return jax.shard_map(
        functools.partial(on_device, wide, narrow), mesh=line,
        in_specs=in_specs, out_specs=(P(ALL), P(ALL)), check_vma=False,
    )
```

```python
import functools
import math

import jax
import jax.numpy as jnp
import numpy as np
from jax import lax
from jax.experimental import pallas as pl
from jax.experimental.pallas import tpu as pltpu
from jax.sharding import PartitionSpec as P

noise_var = 0.5
LANES = 128
CHUNKS = 2
TOGETHER = 2
DIRECT = 8
KEEP_BYTES = 8 * 2**20
VMEM_BYTES = 32 * 2**20
WHOLE_VMEM_BYTES = (53 * 1024 + 870) * 2**10
ALL = "all"
HIGH, LOW, Y, X, CORE = range(5)
highest = lax.Precision.HIGHEST
f32 = jnp.float32
bf16 = jnp.bfloat16


def split3(values):
    high = values.astype(bf16)
    rest = values - high.astype(f32)
    mid = rest.astype(bf16)
    low = (rest - mid.astype(f32)).astype(bf16)
    return high, mid, low


def exponent_rows(first, second):
    width = (first if not isinstance(first, float) else second).shape[1]
    row = lax.broadcasted_iota(jnp.int32, (16, width), 0)
    out = jnp.zeros((16, width), f32)
    for base, value in ((0, first), (3, second)):
        parts = (1.0, 1.0, 1.0) if isinstance(value, float) else [p.astype(f32) for p in split3(value)]
        for k, part in enumerate(parts):
            out = jnp.where(row == base + k, part, out)
    return out.astype(bf16)


def right_operand(latent, scale):
    square = jnp.sum(latent * latent, axis=0, keepdims=True) * scale
    h, m, l = split3(latent)
    return jnp.concatenate([h, m, l, h, m, h, exponent_rows(square, 1.0)], axis=0)


def left_operand(latent, scale):
    square = jnp.sum(latent * latent, axis=0, keepdims=True) * scale
    h, m, l = split3(latent * (-2.0 * scale))
    stacked = jnp.concatenate([h, h, h, m, m, l, exponent_rows(1.0, square)], axis=0)
    return stacked.T


def axis_sizes(wide, narrow):
    return 2, wide // 4, 2, narrow // 2, 2


def place(wide, narrow):
    rest, out = lax.axis_index(ALL), []
    for size in reversed(axis_sizes(wide, narrow)):
        out.append(rest % size)
        rest = rest // size
    return tuple(reversed(out))


def device_at(high, low, y, x, core, wide, narrow):
    return (((high * (wide // 4) + low) * 2 + y) * (narrow // 2) + x) * 2 + core


def slot(device, wide, narrow):
    return wide * narrow - 1 - device


def part_base(part, parts, wide, narrow):
    return 0 if parts == 1 else jnp.bitwise_xor(place(wide, narrow)[X], part) * 2


def row_sources(blocks, flips, wide, narrow):
    spots = [(b, i) for b in blocks for i in range(b.shape[0])]
    if flips is None:
        return [(b, i, i) for b, i in spots]
    high = place(wide, narrow)[HIGH]
    return [(b, i, jnp.bitwise_xor(high, flip)) for (b, i), flip in zip(spots, flips)]


def column_sources(blocks, flips, wide, narrow):
    spots = [(b, i) for b in blocks for i in range(b.shape[0])]
    if flips is None:
        return [(b, i, i) for b, i in spots]
    _, low, y, _, core = place(wide, narrow)
    return [(b, i, (jnp.bitwise_xor(low, f) * 2 + jnp.bitwise_xor(y, g)) * 2 + jnp.bitwise_xor(core, h))
            for (b, i), (f, g, h) in zip(spots, flips)]


def total_sum(values):
    return jnp.sum(jnp.sum(values, axis=0, keepdims=True), axis=1, keepdims=True)


def lane_sums(values):
    parts = jnp.concatenate(split3(values), axis=1)
    ones = jnp.ones((16, parts.shape[1]), bf16)
    return lax.dot_general(ones, parts, (((1,), (1,)), ((), ())),
                           preferred_element_type=f32)[0:1, :]


def make_rows(left, right, kept, read_vector, sums):
    groups, rows, _ = left.shape
    columns = right.shape[0]
    halves = rows // LANES

    def one_group(g, _):
        left_group = left[g]

        def some_columns(step, acc):
            first = step * TOGETHER
            both = jnp.concatenate([right[first + k] for k in range(TOGETHER)], axis=1)
            exponent = jnp.dot(left_group, both, preferred_element_type=f32)
            tile = jnp.exp2(exponent)
            for k in range(TOGETHER):
                if kept is not None:
                    kept[g, first + k] = tile[:, k * rows:(k + 1) * rows]
                for half in range(halves):
                    start = k * rows + half * LANES
                    acc = acc + tile[:, start:start + LANES] * read_vector(first + k, half)
            return acc

        sums[g] = lax.fori_loop(0, columns // TOGETHER, some_columns, jnp.zeros((rows, LANES), f32),
                                unroll=8 // TOGETHER)
        return 0

    lax.fori_loop(0, groups, one_group, 0, unroll=groups <= 2)


def use_rows(kept, read_vector, sums):
    groups, columns, rows, _ = kept.shape
    halves = rows // LANES

    def one_group(g, _):
        def one_column(c, acc):
            for half in range(halves):
                acc = acc + kept[g, c, :, half * LANES:(half + 1) * LANES] * read_vector(c, half)
            return acc

        sums[g] = lax.fori_loop(0, columns, one_column, jnp.zeros((rows, LANES), f32), unroll=8)
        return 0

    lax.fori_loop(0, groups, one_group, 0, unroll=groups <= 2)


def write_rows(sums, out, bases):
    groups, rows, _ = sums.shape
    halves = rows // LANES
    total = lane_sums(sums[...].reshape(groups * rows, LANES))
    for g in range(groups):
        base = bases[g * len(bases) // groups]
        for half in range(halves):
            line = (base + g % (groups // len(bases))) * halves + half
            start = (g * halves + half) * LANES
            out[pl.ds(line, 1), :] = total[:, start:start + LANES]


def project_kernel(features, projection_t, targets, out, feature_buf, projection_buf, target_buf, sems):
    proj = projection_t.shape[0]
    chunks, height, _ = feature_buf.shape
    copies = [
        pltpu.make_async_copy(features.at[pl.ds(i * height, height)], feature_buf.at[i], sems.at[i])
        for i in range(chunks)]
    copies.insert(1, pltpu.make_async_copy(projection_t, projection_buf, sems.at[chunks]))
    copies.append(pltpu.make_async_copy(targets, target_buf, sems.at[chunks + 1]))
    for copy in copies:
        copy.start()
    copies.pop(1).wait()
    for i in range(chunks):
        copies[i].wait()
        out[0, 0:proj, i * height:(i + 1) * height] = lax.dot_general(
            projection_buf[...], feature_buf[i], (((1,), (1,)), ((), ())), preferred_element_type=f32)
    copies[-1].wait()
    out[0, proj:proj + 8, :] = jnp.broadcast_to(target_buf[...], (8, out.shape[2]))


def first_kernel(proj, scale, wide, narrow, keep, flips, row_count, column_count, *refs):
    row_blocks, column_blocks = refs[:row_count], refs[row_count:row_count + column_count]
    refs = refs[row_count + column_count:]
    right, column_vector = refs[:2]
    kept, left = (refs[2], refs[-2]) if keep else (None, refs[2])
    partial, starts, sums = refs[3], refs[4] if column_count else None, refs[-1]
    rows = left.shape[1]
    halves = rows // LANES
    for block, i, source in column_sources(column_blocks, flips[1], wide, narrow) if column_count else ():
        right[source] = right_operand(block[i, 0:proj, :], scale)
        for half in range(halves):
            column_vector[pl.ds(source * halves + half, 1), :] = block[
                i, proj:proj + 1, half * LANES:(half + 1) * LANES]
    for block, i, source in row_sources(row_blocks, flips[0], wide, narrow):
        left[source] = left_operand(block[i, 0:proj, :], scale)
        for half in range(halves) if column_count else ():
            starts[pl.ds(source * halves + half, 1), :] = block[
                i, proj:proj + 1, half * LANES:(half + 1) * LANES]
    make_rows(left, right, kept, lambda c, half: column_vector[pl.ds(c * halves + half, 1), :], sums)
    write_rows(sums, partial, [0])


def message_kernel(parts, wide, narrow, halves, *refs):
    partials, start, out, held = refs[:parts], refs[parts], refs[-2], refs[-1]
    for part, lines in enumerate(partials):
        base = part_base(part, parts, wide, narrow) * halves
        for line in range(lines.shape[0]):
            held[pl.ds(base + line, 1), :] = lines[line:line + 1, :]
    here = place(wide, narrow)
    mine = here[HIGH] * halves
    if parts == 1:
        mine = mine + here[X] * 2 * halves
    pieces = [held[line:line + 1, :] for line in range(held.shape[0])]
    pieces += [start[pl.ds(mine + half, 1), :] for half in range(halves)]
    block = jnp.concatenate(pieces, axis=1)

    def copy(i, _):
        out[i] = block
        return 0

    lax.fori_loop(0, out.shape[0], copy, 0, unroll=8)


def second_kernel(wide, narrow, keep, parts, *refs):
    arrived, out, step_scalars, direction, images, targets, partial, sums = refs[:1] + refs[-7:]
    lines = partial.shape[0]
    halves = lines // narrow
    across = narrow // 2
    group = [(high, x) for x in range(narrow // 2) for high in range(2)]

    def unpack(low, _):
        for y, core in ((0, 0), (0, 1), (1, 0), (1, 1)):
            members = [device_at(high, low, y, x, core, wide, narrow) for high, x in group]
            slots = [slot(member, wide, narrow) for member in members]
            total = arrived[slots[0], :, 0:lines * LANES]
            for spot in slots[1:]:
                total = total + arrived[spot, :, 0:lines * LANES]
            for r, member in enumerate(members):
                for half in range(halves):
                    start = arrived[slots[r], :, (lines + half) * LANES:(lines + half + 1) * LANES]
                    line = r * halves + half
                    spot = pl.ds(member * halves + half, 1)
                    targets[spot, :] = start
                    images[spot, :] = total[:, line * LANES:(line + 1) * LANES] + noise_var * start
        return 0

    lax.fori_loop(0, wide // 4, unpack, 0, unroll=2)
    start, first = targets[...], images[...]
    norm = total_sum(start * start)
    alpha = norm / total_sum(start * first)
    residual = start - alpha * first
    norm_next = total_sum(residual * residual)
    beta = norm_next / norm
    whole = residual + beta * start
    direction[...] = whole
    high, low, y, x, core = place(wide, narrow)

    def read_vector(c, half):
        source = device_at(high, c // 4, c // 2 % 2, x, c % 2, wide, narrow)
        return direction[pl.ds(source * halves + half, 1), :]

    groups = narrow // parts
    for part in range(parts):
        part_sums = sums.at[part * groups:(part + 1) * groups]
        if keep:
            use_rows(refs[1 + part], read_vector, part_sums)
        else:
            make_rows(refs[2 + part], refs[1], None, read_vector, part_sums)
    write_rows(sums, partial, [part_base(part, parts, wide, narrow) for part in range(parts)])
    share = jnp.zeros((1, LANES), f32)
    for r, (row_high, row_x) in enumerate(group):
        for half in range(halves):
            spot = pl.ds(device_at(row_high, low, y, row_x, core, wide, narrow) * halves + half, 1)
            line = r * halves + half
            share = share + direction[spot, :] * partial[line:line + 1, :]
    blocks = [
        jnp.concatenate([partial[r * halves + half:r * halves + half + 1, :]
                         for half in range(halves)] + [share], axis=1)
        for r in range(narrow)]

    def copy(to_low, _):
        for r, (to_high, to_x) in enumerate(group):
            for to_y, to_core in ((0, 0), (0, 1), (1, 0), (1, 1)):
                to = device_at(to_high, to_low, to_y, to_x, to_core, wide, narrow)
                out[slot(to, wide, narrow)] = blocks[r]
        return 0

    lax.fori_loop(0, wide // 4, copy, 0, unroll=2)
    lane = lax.broadcasted_iota(jnp.int32, (1, LANES), 1)
    noise = noise_var * total_sum(whole * whole)
    step_scalars[0:1, :] = jnp.where(lane == 0, alpha, jnp.where(
        lane == 1, norm_next, jnp.where(lane == 2, beta, noise)))
    for half in range(halves):
        spot = pl.ds(device_at(high, low, y, x, core, wide, narrow) * halves + half, 1)
        step_scalars[1 + half:2 + half, :] = images[spot, :]
        step_scalars[1 + halves + half:2 + halves + half, :] = targets[spot, :]


def last_kernel(wide, narrow, arrived, step_scalars, solution_out, residual_out, answer, sems):
    alpha = step_scalars[0:1, 0:1]
    norm = step_scalars[0:1, 1:2]
    beta = step_scalars[0:1, 2:3]
    noise = step_scalars[0:1, 3:4]
    halves = answer.shape[1]

    def add(i, total):
        return total + arrived[i, :, halves * LANES:(halves + 1) * LANES]

    share = lax.fori_loop(0, arrived.shape[0], add, jnp.zeros((1, LANES), f32), unroll=32)
    alpha_next = norm / (total_sum(share) + noise)
    _, low, y, _, core = place(wide, narrow)
    product = jnp.zeros((1, (halves + 1) * LANES), f32)
    for high in range(2):
        for x in range(narrow // 2):
            member = device_at(high, low, y, x, core, wide, narrow)
            product = product + arrived[slot(member, wide, narrow)]
    for half in range(halves):
        begin = step_scalars[1 + halves + half:2 + halves + half, :]
        residual = begin - alpha * step_scalars[1 + half:2 + half, :]
        direction = residual + beta * begin
        image = product[:, half * LANES:(half + 1) * LANES] + noise_var * direction
        answer[0, half:half + 1, :] = alpha * begin + alpha_next * direction
        answer[1, half:half + 1, :] = residual - alpha_next * image
    copies = [pltpu.make_async_copy(answer.at[i], out, sems.at[i])
              for i, out in enumerate((solution_out, residual_out))]
    for copy in copies:
        copy.start()
    for copy in copies:
        copy.wait()


def call(kernel, out_shape, *args, scratch=(), vmem=VMEM_BYTES, **options):
    return pl.pallas_call(
        kernel,
        out_shape=out_shape,
        scratch_shapes=list(scratch),
        compiler_params=pltpu.CompilerParams(vmem_limit_bytes=vmem),
        **options,
    )(*args)


def to_all(blocks):
    group = list(range(blocks.shape[0] - 1, -1, -1))
    return lax.all_to_all(blocks, ALL, split_axis=0, concat_axis=0, axis_index_groups=[group], tiled=True)


def join_kernel(*refs):
    i = 0
    for block in refs[:-1]:
        for j in range(block.shape[0]):
            refs[-1][i] = block[j]
            i += 1


def join(*blocks):
    total = sum(b.shape[0] for b in blocks)
    return call(join_kernel, jax.ShapeDtypeStruct((total, *blocks[0].shape[1:]), f32), *blocks)


def first_round(own, wide, narrow):
    lows, across = wide // 4, narrow // 2
    if lows & (lows - 1) or across != 2 or lows > DIRECT:
        every = lax.all_gather(own, ALL, axis=0, tiled=True)
        every = every.reshape(2, lows, 2, across, 2, *own.shape[1:])
        high, low, y, x, core = place(wide, narrow)
        rows = every
        for place_in, axis in ((low, 1), (y, 1), (core, 2)):
            rows = lax.dynamic_index_in_dim(rows, place_in, axis, keepdims=False)
        columns = lax.dynamic_index_in_dim(every, high, 0, keepdims=False)
        columns = lax.dynamic_index_in_dim(columns, x, 2, keepdims=False)
        rows = jnp.swapaxes(rows, 0, 1).reshape(narrow, *own.shape[1:])
        return [[rows]], [columns.reshape(wide, *own.shape[1:])], (None, None)

    sizes = axis_sizes(wide, narrow)

    def swap(value, **flips):
        pairs = []
        for i in range(wide * narrow):
            spot = list(np.unravel_index(i, sizes))
            for name, flip in flips.items():
                axis = dict(high=HIGH, low=LOW, y=Y, x=X, core=CORE)[name]
                spot[axis] = int(spot[axis]) ^ flip
            pairs.append((i, int(np.ravel_multi_index(spot, sizes))))
        return lax.ppermute(value, ALL, pairs)

    rows = join(own, swap(own, high=1))
    columns = [own] + [swap(own, low=flip // 2, y=flip % 2) for flip in range(1, 2 * lows)]
    columns += [swap(block, core=1) for block in columns]
    parts = [[rows], [swap(rows, x=1)]]
    flips = [(flip // 2, flip % 2, core) for core in range(2) for flip in range(2 * lows)]
    return parts, columns, ([0, 1], flips)


def on_device(wide, narrow, features, projection, targets):
    rows, proj = features.shape[0], projection.shape[1]
    halves = rows // LANES
    lines = narrow * halves
    devices = wide * narrow
    scale = -2.0 / proj * math.log2(math.e)
    depth = 6 * proj + 16
    keep = 4 * devices * rows * rows <= KEEP_BYTES

    def shape(*dims, dtype=f32):
        return jax.ShapeDtypeStruct(dims, dtype)

    def scratch(*dims, dtype=f32):
        return pltpu.VMEM(dims, dtype)

    feat = features.shape[1]
    own = call(
        project_kernel, shape(1, proj + 8, rows), features, projection.T, targets.reshape(1, rows),
        in_specs=[pl.BlockSpec(memory_space=pl.ANY)] * 3, vmem=WHOLE_VMEM_BYTES,
        scratch=[scratch(CHUNKS, rows // CHUNKS, feat, dtype=bf16), scratch(proj, feat, dtype=bf16),
                 scratch(1, rows), pltpu.SemaphoreType.DMA((CHUNKS + 2,))])
    row_parts, column_blocks, flips = first_round(own, wide, narrow)
    parts = len(row_parts)
    groups = narrow // parts
    left = shape(groups, rows, depth, dtype=bf16)
    right = shape(wide, depth, rows, dtype=bf16)
    vector = shape(wide * halves, LANES)
    kept = shape(groups, wide, rows, rows) if keep else left
    group_lines = shape(groups * halves, LANES)
    sums = scratch(groups, rows, LANES)
    work = [scratch(*left.shape, dtype=bf16), sums] if keep else [sums]
    blocks, partials = [], []
    for part, row_blocks in enumerate(row_parts):
        fresh = part == 0
        first = functools.partial(
            first_kernel, proj, scale, wide, narrow, keep, flips, len(row_blocks),
            len(column_blocks) if fresh else 0)
        tiles = groups * wide * rows * rows
        made = call(
            first, (right, vector, kept, group_lines, group_lines) if fresh else (kept, group_lines),
            *row_blocks, *(column_blocks if fresh else columns_made), scratch=work,
            cost_estimate=pl.CostEstimate(
                flops=2 * tiles * depth, bytes_accessed=4 * tiles, transcendentals=tiles))
        if fresh:
            *columns_made, block, partial, own_start = made
        else:
            block, partial = made
        blocks.append(block)
        partials.append(partial)
    out = call(
        functools.partial(message_kernel, parts, wide, narrow, halves),
        shape(devices, 1, (lines + halves) * LANES), *partials, own_start,
        scratch=[scratch(lines, LANES)])
    block = blocks if keep else [columns_made[0], *blocks]
    sums = scratch(narrow, rows, LANES)
    out, step_scalars = call(
        functools.partial(second_kernel, wide, narrow, keep, parts),
        (shape(devices, 1, (halves + 1) * LANES), shape(1 + 2 * halves, LANES)),
        to_all(out), *block,
        scratch=[scratch(devices * halves, LANES)] * 3 + [scratch(lines, LANES), sums])
    answer, residual = call(
        functools.partial(last_kernel, wide, narrow), (shape(halves, LANES), shape(halves, LANES)),
        to_all(out), step_scalars,
        out_specs=(pl.BlockSpec(memory_space=pl.ANY),) * 2,
        scratch=[scratch(2, halves, LANES), pltpu.SemaphoreType.DMA((2,))])
    return answer.reshape(rows), residual.reshape(rows)


def solution(mesh):
    wide, narrow = mesh.shape["wide"], mesh.shape["narrow"]
    line = jax.sharding.Mesh(mesh.devices.reshape(wide * narrow), (ALL,))
    in_specs = (P(ALL, None), P(), P(ALL))
    return jax.shard_map(
        functools.partial(on_device, wide, narrow), mesh=line,
        in_specs=in_specs, out_specs=(P(ALL), P(ALL)), check_vma=False,
    )
```

```python
import functools
import math

import jax
import jax.numpy as jnp
import numpy as np
from jax import lax
from jax.experimental import pallas as pl
from jax.experimental.pallas import tpu as pltpu
from jax.sharding import PartitionSpec as P

noise_var = 0.5
LANES = 128
CHUNKS = 2
TOGETHER = 2
DIRECT = 8
KEEP_BYTES = 8 * 2**20
VMEM_BYTES = 32 * 2**20
WHOLE_VMEM_BYTES = (53 * 1024 + 870) * 2**10
ALL = "all"
HIGH, LOW, Y, X, CORE = range(5)
highest = lax.Precision.HIGHEST
f32 = jnp.float32
bf16 = jnp.bfloat16


def split3(values):
    high = values.astype(bf16)
    rest = values - high.astype(f32)
    mid = rest.astype(bf16)
    low = (rest - mid.astype(f32)).astype(bf16)
    return high, mid, low


def exponent_rows(first, second):
    width = (first if not isinstance(first, float) else second).shape[1]
    row = lax.broadcasted_iota(jnp.int32, (16, width), 0)
    out = jnp.zeros((16, width), f32)
    for base, value in ((0, first), (3, second)):
        parts = (1.0, 1.0, 1.0) if isinstance(value, float) else [p.astype(f32) for p in split3(value)]
        for k, part in enumerate(parts):
            out = jnp.where(row == base + k, part, out)
    return out.astype(bf16)


def right_operand(latent, scale):
    square = jnp.sum(latent * latent, axis=0, keepdims=True) * scale
    h, m, l = split3(latent)
    return jnp.concatenate([h, m, l, h, m, h, exponent_rows(square, 1.0)], axis=0)


def left_operand(latent, scale):
    square = jnp.sum(latent * latent, axis=0, keepdims=True) * scale
    h, m, l = split3(latent * (-2.0 * scale))
    stacked = jnp.concatenate([h, h, h, m, m, l, exponent_rows(1.0, square)], axis=0)
    return stacked.T


def axis_sizes(wide, narrow):
    return 2, wide // 4, 2, narrow // 2, 2


def place(wide, narrow):
    rest, out = lax.axis_index(ALL), []
    for size in reversed(axis_sizes(wide, narrow)):
        out.append(rest % size)
        rest = rest // size
    return tuple(reversed(out))


def device_at(high, low, y, x, core, wide, narrow):
    return (((high * (wide // 4) + low) * 2 + y) * (narrow // 2) + x) * 2 + core


def slot(device, wide, narrow):
    return wide * narrow - 1 - device


def part_base(part, parts, wide, narrow):
    return 0 if parts == 1 else jnp.bitwise_xor(place(wide, narrow)[X], part) * 2


def row_sources(blocks, flips, wide, narrow):
    spots = [(b, i) for b in blocks for i in range(b.shape[0])]
    if flips is None:
        return [(b, i, i) for b, i in spots]
    high = place(wide, narrow)[HIGH]
    return [(b, i, jnp.bitwise_xor(high, flip)) for (b, i), flip in zip(spots, flips)]


def column_sources(blocks, flips, wide, narrow):
    spots = [(b, i) for b in blocks for i in range(b.shape[0])]
    if flips is None:
        return [(b, i, i) for b, i in spots]
    _, low, y, _, _ = place(wide, narrow)
    return [(b, i, jnp.bitwise_xor(low * 2 + y, flip)) for (b, i), flip in zip(spots, flips)]


def total_sum(values):
    return jnp.sum(jnp.sum(values, axis=0, keepdims=True), axis=1, keepdims=True)


def lane_sums(values):
    parts = jnp.concatenate(split3(values), axis=1)
    ones = jnp.ones((16, parts.shape[1]), bf16)
    return lax.dot_general(ones, parts, (((1,), (1,)), ((), ())),
                           preferred_element_type=f32)[0:1, :]


def make_rows(left, right, kept, read_vector, sums, add):
    groups, rows, _ = left.shape
    columns = right.shape[0]
    halves = rows // LANES

    def one_group(g, _):
        left_group = left[g]

        def some_columns(step, acc):
            first = step * TOGETHER
            both = jnp.concatenate([right[first + k] for k in range(TOGETHER)], axis=1)
            exponent = jnp.dot(left_group, both, preferred_element_type=f32)
            tile = jnp.exp2(exponent)
            for k in range(TOGETHER):
                if kept is not None:
                    kept[g, first + k] = tile[:, k * rows:(k + 1) * rows]
                for half in range(halves):
                    start = k * rows + half * LANES
                    acc = acc + tile[:, start:start + LANES] * read_vector(first + k, half)
            return acc

        start_sum = sums[g] if add else jnp.zeros((rows, LANES), f32)
        sums[g] = lax.fori_loop(0, columns // TOGETHER, some_columns, start_sum,
                                unroll=4 // TOGETHER)
        return 0

    lax.fori_loop(0, groups, one_group, 0, unroll=groups <= 2)


def use_rows(kept, read_vector, sums, add):
    groups, columns, rows, _ = kept.shape
    halves = rows // LANES

    def one_group(g, _):
        def one_column(c, acc):
            for half in range(halves):
                acc = acc + kept[g, c, :, half * LANES:(half + 1) * LANES] * read_vector(c, half)
            return acc

        start_sum = sums[g] if add else jnp.zeros((rows, LANES), f32)
        sums[g] = lax.fori_loop(0, columns, one_column, start_sum, unroll=4)
        return 0

    lax.fori_loop(0, groups, one_group, 0, unroll=groups <= 2)


def write_rows(sums, out, bases):
    groups, rows, _ = sums.shape
    halves = rows // LANES
    total = lane_sums(sums[...].reshape(groups * rows, LANES))
    for g in range(groups):
        base = bases[g * len(bases) // groups]
        for half in range(halves):
            line = (base + g % (groups // len(bases))) * halves + half
            start = (g * halves + half) * LANES
            out[pl.ds(line, 1), :] = total[:, start:start + LANES]


def project_kernel(features, projection_t, targets, out, feature_buf, projection_buf, target_buf, sems):
    proj = projection_t.shape[0]
    chunks, height, _ = feature_buf.shape
    copies = [
        pltpu.make_async_copy(features.at[pl.ds(i * height, height)], feature_buf.at[i], sems.at[i])
        for i in range(chunks)]
    copies.insert(1, pltpu.make_async_copy(projection_t, projection_buf, sems.at[chunks]))
    copies.append(pltpu.make_async_copy(targets, target_buf, sems.at[chunks + 1]))
    for copy in copies:
        copy.start()
    copies.pop(1).wait()
    for i in range(chunks):
        copies[i].wait()
        out[0, 0:proj, i * height:(i + 1) * height] = lax.dot_general(
            projection_buf[...], feature_buf[i], (((1,), (1,)), ((), ())), preferred_element_type=f32)
    copies[-1].wait()
    out[0, proj:proj + 8, :] = jnp.broadcast_to(target_buf[...], (8, out.shape[2]))


def prepare_rows(blocks, flips, left, proj, scale, wide, narrow):
    for block, i, source in row_sources(blocks, flips, wide, narrow):
        left[source] = left_operand(block[i, 0:proj, :], scale)


def vector_reader(vector, halves):
    return lambda c, half: vector[pl.ds(c * halves + half, 1), :]


def side_kernel(proj, scale, wide, narrow, keep, flips, row_count, column_count, *refs):
    rows_in, columns_in = refs[:row_count], refs[row_count:row_count + column_count]
    refs = refs[row_count + column_count:]
    fresh = rows_in[0].dtype == f32
    left, refs = (refs[0], refs[1:]) if fresh else (rows_in[0], refs)
    right, vector, partial, sums = refs[0], refs[1], refs[2], refs[-1]
    kept = refs[3] if keep else None
    halves = left.shape[1] // LANES
    if fresh:
        prepare_rows(rows_in, flips[0], left, proj, scale, wide, narrow)
    for block, i, source in column_sources(columns_in, flips[1], wide, narrow):
        right[source] = right_operand(block[i, 0:proj, :], scale)
        for half in range(halves):
            vector[pl.ds(source * halves + half, 1), :] = block[
                i, proj:proj + 1, half * LANES:(half + 1) * LANES]
    make_rows(left, right, kept, vector_reader(vector, halves), sums, False)
    write_rows(sums, partial, [0])


def rest_kernel(proj, scale, wide, narrow, keep, flips, *refs):
    rows_in, columns, refs = refs[:1], refs[1:5], refs[5:]
    if keep:
        partial, *kept, sums, left = refs
    else:
        left, partial, sums = refs
        kept = (None, None)
    halves = left.shape[1] // LANES
    prepare_rows(rows_in, flips[0], left, proj, scale, wide, narrow)
    for side in range(2):
        right, vector = columns[2 * side:2 * side + 2]
        make_rows(left, right, kept[side], vector_reader(vector, halves), sums, side > 0)
    write_rows(sums, partial, [0])


def message_kernel(parts, wide, narrow, halves, *refs):
    partials, vector, out, held = refs[:parts + 1], refs[parts + 1], refs[-2], refs[-1]
    lines_of = [partials[0][...] + partials[1][...]] + [partial[...] for partial in partials[2:]]
    for part, lines in enumerate(lines_of):
        base = part_base(part, parts, wide, narrow) * halves
        for line in range(lines.shape[0]):
            held[pl.ds(base + line, 1), :] = lines[line:line + 1, :]
    _, low, y, _, _ = place(wide, narrow)
    mine = (low * 2 + y) * halves
    pieces = [held[line:line + 1, :] for line in range(held.shape[0])]
    pieces += [vector[pl.ds(mine + half, 1), :] for half in range(halves)]
    block = jnp.concatenate(pieces, axis=1)

    def copy(i, _):
        out[i] = block
        return 0

    lax.fori_loop(0, out.shape[0], copy, 0, unroll=8)


def second_kernel(wide, narrow, keep, parts, *refs):
    arrived, out, step_scalars, direction, images, targets, partial, sums = refs[:1] + refs[-7:]
    lines = partial.shape[0]
    halves = lines // narrow
    across = narrow // 2
    group = [(high, x) for x in range(narrow // 2) for high in range(2)]

    def unpack(low, _):
        for y, core in ((0, 0), (0, 1), (1, 0), (1, 1)):
            members = [device_at(high, low, y, x, core, wide, narrow) for high, x in group]
            slots = [slot(member, wide, narrow) for member in members]
            total = arrived[slots[0], :, 0:lines * LANES]
            for spot in slots[1:]:
                total = total + arrived[spot, :, 0:lines * LANES]
            for r, member in enumerate(members):
                for half in range(halves):
                    start = arrived[slots[r], :, (lines + half) * LANES:(lines + half + 1) * LANES]
                    line = r * halves + half
                    spot = pl.ds(member * halves + half, 1)
                    targets[spot, :] = start
                    images[spot, :] = total[:, line * LANES:(line + 1) * LANES] + noise_var * start
        return 0

    lax.fori_loop(0, wide // 4, unpack, 0, unroll=2)
    start, first = targets[...], images[...]
    norm = total_sum(start * start)
    alpha = norm / total_sum(start * first)
    residual = start - alpha * first
    norm_next = total_sum(residual * residual)
    beta = norm_next / norm
    whole = residual + beta * start
    direction[...] = whole
    high, low, y, x, core = place(wide, narrow)

    def side_reader(side):
        def read_vector(c, half):
            source = device_at(high, c // 2, c % 2, x, jnp.bitwise_xor(core, side), wide, narrow)
            return direction[pl.ds(source * halves + half, 1), :]
        return read_vector

    groups = narrow // parts
    for part in range(parts):
        part_sums = sums.at[part * groups:(part + 1) * groups]
        for side in range(2):
            if keep:
                use_rows(refs[1 + 2 * part + side], side_reader(side), part_sums, side > 0)
            else:
                make_rows(refs[3 + part], refs[1 + side], None, side_reader(side), part_sums, side > 0)
    write_rows(sums, partial, [part_base(part, parts, wide, narrow) for part in range(parts)])
    share = jnp.zeros((1, LANES), f32)
    for r, (row_high, row_x) in enumerate(group):
        for half in range(halves):
            spot = pl.ds(device_at(row_high, low, y, row_x, core, wide, narrow) * halves + half, 1)
            line = r * halves + half
            share = share + direction[spot, :] * partial[line:line + 1, :]
    blocks = [
        jnp.concatenate([partial[r * halves + half:r * halves + half + 1, :]
                         for half in range(halves)] + [share], axis=1)
        for r in range(narrow)]

    def copy(to_low, _):
        for r, (to_high, to_x) in enumerate(group):
            for to_y, to_core in ((0, 0), (0, 1), (1, 0), (1, 1)):
                to = device_at(to_high, to_low, to_y, to_x, to_core, wide, narrow)
                out[slot(to, wide, narrow)] = blocks[r]
        return 0

    lax.fori_loop(0, wide // 4, copy, 0, unroll=2)
    lane = lax.broadcasted_iota(jnp.int32, (1, LANES), 1)
    noise = noise_var * total_sum(whole * whole)
    step_scalars[0:1, :] = jnp.where(lane == 0, alpha, jnp.where(
        lane == 1, norm_next, jnp.where(lane == 2, beta, noise)))
    for half in range(halves):
        spot = pl.ds(device_at(high, low, y, x, core, wide, narrow) * halves + half, 1)
        step_scalars[1 + half:2 + half, :] = images[spot, :]
        step_scalars[1 + halves + half:2 + halves + half, :] = targets[spot, :]


def last_kernel(wide, narrow, arrived, step_scalars, solution_out, residual_out, answer, sems):
    alpha = step_scalars[0:1, 0:1]
    norm = step_scalars[0:1, 1:2]
    beta = step_scalars[0:1, 2:3]
    noise = step_scalars[0:1, 3:4]
    halves = answer.shape[1]

    def add(i, total):
        return total + arrived[i, :, halves * LANES:(halves + 1) * LANES]

    share = lax.fori_loop(0, arrived.shape[0], add, jnp.zeros((1, LANES), f32), unroll=32)
    alpha_next = norm / (total_sum(share) + noise)
    _, low, y, _, core = place(wide, narrow)
    product = jnp.zeros((1, (halves + 1) * LANES), f32)
    for high in range(2):
        for x in range(narrow // 2):
            member = device_at(high, low, y, x, core, wide, narrow)
            product = product + arrived[slot(member, wide, narrow)]
    for half in range(halves):
        begin = step_scalars[1 + halves + half:2 + halves + half, :]
        residual = begin - alpha * step_scalars[1 + half:2 + half, :]
        direction = residual + beta * begin
        image = product[:, half * LANES:(half + 1) * LANES] + noise_var * direction
        answer[0, half:half + 1, :] = alpha * begin + alpha_next * direction
        answer[1, half:half + 1, :] = residual - alpha_next * image
    copies = [pltpu.make_async_copy(answer.at[i], out, sems.at[i])
              for i, out in enumerate((solution_out, residual_out))]
    for copy in copies:
        copy.start()
    for copy in copies:
        copy.wait()


def call(kernel, out_shape, *args, scratch=(), vmem=VMEM_BYTES, **options):
    return pl.pallas_call(
        kernel,
        out_shape=out_shape,
        scratch_shapes=list(scratch),
        compiler_params=pltpu.CompilerParams(vmem_limit_bytes=vmem),
        **options,
    )(*args)


def to_all(blocks):
    group = list(range(blocks.shape[0] - 1, -1, -1))
    return lax.all_to_all(blocks, ALL, split_axis=0, concat_axis=0, axis_index_groups=[group], tiled=True)


def join_kernel(*refs):
    i = 0
    for block in refs[:-1]:
        for j in range(block.shape[0]):
            refs[-1][i] = block[j]
            i += 1


def join(*blocks):
    total = sum(b.shape[0] for b in blocks)
    return call(join_kernel, jax.ShapeDtypeStruct((total, *blocks[0].shape[1:]), f32), *blocks)


def first_round(own, wide, narrow):
    lows, across = wide // 4, narrow // 2
    if lows & (lows - 1) or across != 2 or lows > DIRECT:
        every = lax.all_gather(own, ALL, axis=0, tiled=True)
        every = every.reshape(2, lows, 2, across, 2, *own.shape[1:])
        high, low, y, x, core = place(wide, narrow)
        rows = every
        for place_in, axis in ((low, 1), (y, 1), (core, 2)):
            rows = lax.dynamic_index_in_dim(rows, place_in, axis, keepdims=False)
        columns = lax.dynamic_index_in_dim(every, high, 0, keepdims=False)
        columns = lax.dynamic_index_in_dim(columns, x, 2, keepdims=False)
        rows = jnp.swapaxes(rows, 0, 1).reshape(narrow, *own.shape[1:])
        sides = [lax.dynamic_index_in_dim(columns, jnp.bitwise_xor(core, side), 2, keepdims=False)
                 for side in range(2)]
        sides = [[columns.reshape(wide // 2, *own.shape[1:])] for columns in sides]
        return [[rows]], sides, (None, None)

    sizes = axis_sizes(wide, narrow)

    def swap(value, **flips):
        pairs = []
        for i in range(wide * narrow):
            spot = list(np.unravel_index(i, sizes))
            for name, flip in flips.items():
                axis = dict(high=HIGH, low=LOW, y=Y, x=X, core=CORE)[name]
                spot[axis] = int(spot[axis]) ^ flip
            pairs.append((i, int(np.ravel_multi_index(spot, sizes))))
        return lax.ppermute(value, ALL, pairs)

    rows = join(own, swap(own, high=1))
    columns = [own] + [swap(own, low=flip // 2, y=flip % 2) for flip in range(1, 2 * lows)]
    sides = [columns, [swap(block, core=1) for block in columns]]
    parts = [[rows], [swap(rows, x=1)]]
    return parts, sides, ([0, 1], list(range(2 * lows)))


def on_device(wide, narrow, features, projection, targets):
    rows, proj = features.shape[0], projection.shape[1]
    halves = rows // LANES
    lines = narrow * halves
    devices = wide * narrow
    scale = -2.0 / proj * math.log2(math.e)
    depth = 6 * proj + 16
    keep = 4 * devices * rows * rows <= KEEP_BYTES

    def shape(*dims, dtype=f32):
        return jax.ShapeDtypeStruct(dims, dtype)

    def scratch(*dims, dtype=f32):
        return pltpu.VMEM(dims, dtype)

    feat = features.shape[1]
    own = call(
        project_kernel, shape(1, proj + 8, rows), features, projection.T, targets.reshape(1, rows),
        in_specs=[pl.BlockSpec(memory_space=pl.ANY)] * 3, vmem=WHOLE_VMEM_BYTES,
        scratch=[scratch(CHUNKS, rows // CHUNKS, feat, dtype=bf16), scratch(proj, feat, dtype=bf16),
                 scratch(1, rows), pltpu.SemaphoreType.DMA((CHUNKS + 2,))])
    row_parts, sides, flips = first_round(own, wide, narrow)
    parts = len(row_parts)
    groups = narrow // parts
    left = shape(groups, rows, depth, dtype=bf16)
    right = shape(wide // 2, depth, rows, dtype=bf16)
    vector = shape(wide // 2 * halves, LANES)
    kept = (shape(groups, wide // 2, rows, rows),) if keep else ()
    group_lines = shape(groups * halves, LANES)
    sums = scratch(groups, rows, LANES)
    settings = (proj, scale, wide, narrow, keep, flips)

    def cost(columns):
        tiles = groups * columns * rows * rows
        return pl.CostEstimate(flops=2 * tiles * depth, bytes_accessed=4 * tiles, transcendentals=tiles)

    lefts, columns, blocks, partials = [], [], [], []
    for side, column_blocks in enumerate(sides):
        row_blocks = row_parts[0] if side == 0 else lefts
        made = call(
            functools.partial(side_kernel, *settings, len(row_blocks), len(column_blocks)),
            ((left,) if side == 0 else ()) + (right, vector, group_lines) + kept,
            *row_blocks, *column_blocks, scratch=[sums], cost_estimate=cost(wide // 2))
        if side == 0:
            lefts, made = [made[0]], made[1:]
        columns += made[:2]
        partials.append(made[2])
        blocks += made[3:]
    for row_blocks in row_parts[1:]:
        made = call(
            functools.partial(rest_kernel, *settings),
            (group_lines, *kept * 2) if keep else (left, group_lines), *row_blocks, *columns,
            scratch=[sums, scratch(*left.shape, dtype=bf16)] if keep else [sums],
            cost_estimate=cost(wide))
        if not keep:
            lefts.append(made[0])
        partials.append(made[0 if keep else 1])
        blocks += made[1:] if keep else []
    out = call(
        functools.partial(message_kernel, parts, wide, narrow, halves),
        shape(devices, 1, (lines + halves) * LANES), *partials, columns[1],
        scratch=[scratch(lines, LANES)])
    block = blocks if keep else [columns[0], columns[2], *lefts]
    sums = scratch(narrow, rows, LANES)
    out, step_scalars = call(
        functools.partial(second_kernel, wide, narrow, keep, parts),
        (shape(devices, 1, (halves + 1) * LANES), shape(1 + 2 * halves, LANES)),
        to_all(out), *block,
        scratch=[scratch(devices * halves, LANES)] * 3 + [scratch(lines, LANES), sums])
    answer, residual = call(
        functools.partial(last_kernel, wide, narrow), (shape(halves, LANES), shape(halves, LANES)),
        to_all(out), step_scalars,
        out_specs=(pl.BlockSpec(memory_space=pl.ANY),) * 2,
        scratch=[scratch(2, halves, LANES), pltpu.SemaphoreType.DMA((2,))])
    return answer.reshape(rows), residual.reshape(rows)


def solution(mesh):
    wide, narrow = mesh.shape["wide"], mesh.shape["narrow"]
    line = jax.sharding.Mesh(mesh.devices.reshape(wide * narrow), (ALL,))
    in_specs = (P(ALL, None), P(), P(ALL))
    return jax.shard_map(
        functools.partial(on_device, wide, narrow), mesh=line,
        in_specs=in_specs, out_specs=(P(ALL), P(ALL)), check_vma=False,
    )
```

```python
import functools
import math

import jax
import jax.numpy as jnp
import numpy as np
from jax import lax
from jax.experimental import pallas as pl
from jax.experimental.pallas import tpu as pltpu
from jax.sharding import PartitionSpec as P

noise_var = 0.5
LANES = 128
CHUNKS = 2
TOGETHER = 2
EARLY = 10**9
DIRECT = 8
KEEP_BYTES = 8 * 2**20
VMEM_BYTES = 32 * 2**20
WHOLE_VMEM_BYTES = (53 * 1024 + 835) * 2**10
ALL = "all"
HIGH, LOW, Y, X, CORE = range(5)
highest = lax.Precision.HIGHEST
f32 = jnp.float32
bf16 = jnp.bfloat16


def split3(values):
    high = values.astype(bf16)
    rest = values - high.astype(f32)
    mid = rest.astype(bf16)
    low = (rest - mid.astype(f32)).astype(bf16)
    return high, mid, low


def exponent_rows(first, second):
    width = (first if not isinstance(first, float) else second).shape[1]
    row = lax.broadcasted_iota(jnp.int32, (16, width), 0)
    out = jnp.zeros((16, width), f32)
    for base, value in ((0, first), (3, second)):
        parts = (1.0, 1.0, 1.0) if isinstance(value, float) else [p.astype(f32) for p in split3(value)]
        for k, part in enumerate(parts):
            out = jnp.where(row == base + k, part, out)
    return out.astype(bf16)


def right_operand(latent, scale):
    square = jnp.sum(latent * latent, axis=0, keepdims=True) * scale
    h, m, l = split3(latent)
    return jnp.concatenate([h, m, l, h, m, h, exponent_rows(square, 1.0)], axis=0)


def left_operand(latent, scale):
    square = jnp.sum(latent * latent, axis=0, keepdims=True) * scale
    h, m, l = split3(latent * (-2.0 * scale))
    stacked = jnp.concatenate([h, h, h, m, m, l, exponent_rows(1.0, square)], axis=0)
    return stacked.T


def axis_sizes(wide, narrow):
    return 2, wide // 4, 2, narrow // 2, 2


def place(wide, narrow):
    rest, out = lax.axis_index(ALL), []
    for size in reversed(axis_sizes(wide, narrow)):
        out.append(rest % size)
        rest = rest // size
    return tuple(reversed(out))


def device_at(high, low, y, x, core, wide, narrow):
    return (((high * (wide // 4) + low) * 2 + y) * (narrow // 2) + x) * 2 + core


def slot(device, wide, narrow):
    return wide * narrow - 1 - device


def part_base(part, parts, wide, narrow):
    return 0 if parts == 1 else jnp.bitwise_xor(place(wide, narrow)[X], part) * 2


def row_sources(blocks, flips, wide, narrow):
    spots = [(b, i) for b in blocks for i in range(b.shape[0])]
    if flips is None:
        return [(b, i, i) for b, i in spots]
    high = place(wide, narrow)[HIGH]
    return [(b, i, jnp.bitwise_xor(high, flip)) for (b, i), flip in zip(spots, flips)]


def column_sources(blocks, flips, wide, narrow):
    spots = [(b, i) for b in blocks for i in range(b.shape[0])]
    if flips is None:
        return [(b, i, i) for b, i in spots]
    _, low, y, _, _ = place(wide, narrow)
    return [(b, i, jnp.bitwise_xor(low * 2 + y, flip)) for (b, i), flip in zip(spots, flips)]


def total_sum(values):
    return jnp.sum(jnp.sum(values, axis=0, keepdims=True), axis=1, keepdims=True)


def lane_sums(values):
    parts = jnp.concatenate(split3(values), axis=1)
    ones = jnp.ones((16, parts.shape[1]), bf16)
    return lax.dot_general(ones, parts, (((1,), (1,)), ((), ())),
                           preferred_element_type=f32)[0:1, :]


def make_rows(left, right, kept, read_vector, sums, add):
    groups, rows, _ = left.shape
    columns = right.shape[0]
    halves = rows // LANES

    def one_group(g, _):
        left_group = left[g]

        def some_columns(step, acc):
            first = step * TOGETHER
            both = jnp.concatenate([right[first + k] for k in range(TOGETHER)], axis=1)
            exponent = jnp.dot(left_group, both, preferred_element_type=f32)
            tile = jnp.exp2(exponent)
            for k in range(TOGETHER):
                if kept is not None:
                    kept[g, first + k] = tile[:, k * rows:(k + 1) * rows]
                for half in range(halves):
                    start = k * rows + half * LANES
                    acc = acc + tile[:, start:start + LANES] * read_vector(first + k, half)
            return acc

        start_sum = sums[g] if add else jnp.zeros((rows, LANES), f32)
        sums[g] = lax.fori_loop(0, columns // TOGETHER, some_columns, start_sum,
                                unroll=4 // TOGETHER)
        return 0

    lax.fori_loop(0, groups, one_group, 0, unroll=groups <= 2)


def use_rows(kept, read_vector, sums, add):
    groups, columns, rows, _ = kept.shape
    halves = rows // LANES

    def one_group(g, _):
        def one_column(c, acc):
            for half in range(halves):
                acc = acc + kept[g, c, :, half * LANES:(half + 1) * LANES] * read_vector(c, half)
            return acc

        start_sum = sums[g] if add else jnp.zeros((rows, LANES), f32)
        sums[g] = lax.fori_loop(0, columns, one_column, start_sum, unroll=4)
        return 0

    lax.fori_loop(0, groups, one_group, 0, unroll=groups <= 2)


def write_rows(sums, out, bases):
    groups, rows, _ = sums.shape
    halves = rows // LANES
    total = lane_sums(sums[...].reshape(groups * rows, LANES))
    for g in range(groups):
        base = bases[g * len(bases) // groups]
        for half in range(halves):
            line = (base + g % (groups // len(bases))) * halves + half
            start = (g * halves + half) * LANES
            out[pl.ds(line, 1), :] = total[:, start:start + LANES]


def project_kernel(features, projection_t, targets, latent, out, feature_buf, projection_buf, target_buf, sems):
    proj = projection_t.shape[0]
    chunks, height, _ = feature_buf.shape
    copies = [
        pltpu.make_async_copy(features.at[pl.ds(i * height, height)], feature_buf.at[i], sems.at[i])
        for i in range(chunks)]
    copies.insert(1, pltpu.make_async_copy(projection_t, projection_buf, sems.at[chunks]))
    copies.append(pltpu.make_async_copy(targets, target_buf, sems.at[chunks + 1]))
    for copy in copies:
        copy.start()
    copies.pop(1).wait()
    for i in range(chunks):
        copies[i].wait()
        some = lax.dot_general(
            projection_buf[...], feature_buf[i], (((1,), (1,)), ((), ())), preferred_element_type=f32)
        latent[0, :, i * height:(i + 1) * height] = some
        out[0, 0:proj, i * height:(i + 1) * height] = some
    copies[-1].wait()
    out[0, proj:proj + 8, :] = jnp.broadcast_to(target_buf[...], (8, out.shape[2]))


def prepare_rows(blocks, flips, left, proj, scale, wide, narrow):
    for block, i, source in row_sources(blocks, flips, wide, narrow):
        left[source] = left_operand(block[i, 0:proj, :], scale)


def vector_reader(vector, halves):
    return lambda c, half: vector[pl.ds(c * halves + half, 1), :]


def side_kernel(proj, scale, wide, narrow, keep, flips, row_count, column_count, *refs):
    rows_in, columns_in = refs[:row_count], refs[row_count:row_count + column_count]
    refs = refs[row_count + column_count:]
    fresh = rows_in[0].dtype == f32
    left, refs = (refs[0], refs[1:]) if fresh else (rows_in[0], refs)
    right, vector, partial, sums = refs[0], refs[1], refs[2], refs[-1]
    kept = refs[3] if keep else None
    halves = left.shape[1] // LANES
    if fresh:
        prepare_rows(rows_in, flips[0], left, proj, scale, wide, narrow)
    for block, i, source in column_sources(columns_in, flips[1], wide, narrow):
        right[source] = right_operand(block[i, 0:proj, :], scale)
        for half in range(halves):
            vector[pl.ds(source * halves + half, 1), :] = block[
                i, proj:proj + 1, half * LANES:(half + 1) * LANES]
    make_rows(left, right, kept, vector_reader(vector, halves), sums, False)
    write_rows(sums, partial, [0])


def rest_kernel(proj, scale, wide, narrow, keep, flips, *refs):
    rows_in, columns, refs = refs[:1], refs[1:5], refs[5:]
    if keep:
        partial, *kept, sums, left = refs
    else:
        left, partial, sums = refs
        kept = (None, None)
    halves = left.shape[1] // LANES
    prepare_rows(rows_in, flips[0], left, proj, scale, wide, narrow)
    for side in range(2):
        right, vector = columns[2 * side:2 * side + 2]
        make_rows(left, right, kept[side], vector_reader(vector, halves), sums, side > 0)
    write_rows(sums, partial, [0])


def message_kernel(parts, wide, narrow, halves, *refs):
    partials, vector, out, held = refs[:parts + 1], refs[parts + 1], refs[-2], refs[-1]
    lines_of = [partials[0][...] + partials[1][...]] + [partial[...] for partial in partials[2:]]
    for part, lines in enumerate(lines_of):
        base = part_base(part, parts, wide, narrow) * halves
        for line in range(lines.shape[0]):
            held[pl.ds(base + line, 1), :] = lines[line:line + 1, :]
    _, low, y, _, _ = place(wide, narrow)
    mine = (low * 2 + y) * halves
    pieces = [held[line:line + 1, :] for line in range(held.shape[0])]
    pieces += [vector[pl.ds(mine + half, 1), :] for half in range(halves)]
    block = jnp.concatenate(pieces, axis=1)

    def copy(i, _):
        out[i] = block
        return 0

    lax.fori_loop(0, out.shape[0], copy, 0, unroll=8)


def second_kernel(wide, narrow, keep, parts, *refs):
    arrived, out, step_scalars, direction, images, targets, partial, sums = refs[:1] + refs[-7:]
    lines = partial.shape[0]
    halves = lines // narrow
    across = narrow // 2
    group = [(high, x) for x in range(narrow // 2) for high in range(2)]

    def unpack(low, _):
        for y, core in ((0, 0), (0, 1), (1, 0), (1, 1)):
            members = [device_at(high, low, y, x, core, wide, narrow) for high, x in group]
            slots = [slot(member, wide, narrow) for member in members]
            total = arrived[slots[0], :, 0:lines * LANES]
            for spot in slots[1:]:
                total = total + arrived[spot, :, 0:lines * LANES]
            for r, member in enumerate(members):
                for half in range(halves):
                    start = arrived[slots[r], :, (lines + half) * LANES:(lines + half + 1) * LANES]
                    line = r * halves + half
                    spot = pl.ds(member * halves + half, 1)
                    targets[spot, :] = start
                    images[spot, :] = total[:, line * LANES:(line + 1) * LANES] + noise_var * start
        return 0

    lax.fori_loop(0, wide // 4, unpack, 0, unroll=2)
    start, first = targets[...], images[...]
    norm = total_sum(start * start)
    alpha = norm / total_sum(start * first)
    residual = start - alpha * first
    norm_next = total_sum(residual * residual)
    beta = norm_next / norm
    whole = residual + beta * start
    direction[...] = whole
    high, low, y, x, core = place(wide, narrow)

    def side_reader(side):
        def read_vector(c, half):
            source = device_at(high, c // 2, c % 2, x, jnp.bitwise_xor(core, side), wide, narrow)
            return direction[pl.ds(source * halves + half, 1), :]
        return read_vector

    groups = narrow // parts
    for part in range(parts):
        part_sums = sums.at[part * groups:(part + 1) * groups]
        for side in range(2):
            if keep:
                use_rows(refs[1 + 2 * part + side], side_reader(side), part_sums, side > 0)
            else:
                make_rows(refs[3 + part], refs[1 + side], None, side_reader(side), part_sums, side > 0)
    write_rows(sums, partial, [part_base(part, parts, wide, narrow) for part in range(parts)])
    share = jnp.zeros((1, LANES), f32)
    for r, (row_high, row_x) in enumerate(group):
        for half in range(halves):
            spot = pl.ds(device_at(row_high, low, y, row_x, core, wide, narrow) * halves + half, 1)
            line = r * halves + half
            share = share + direction[spot, :] * partial[line:line + 1, :]
    blocks = [
        jnp.concatenate([partial[r * halves + half:r * halves + half + 1, :]
                         for half in range(halves)] + [share], axis=1)
        for r in range(narrow)]

    def copy(to_low, _):
        for r, (to_high, to_x) in enumerate(group):
            for to_y, to_core in ((0, 0), (0, 1), (1, 0), (1, 1)):
                to = device_at(to_high, to_low, to_y, to_x, to_core, wide, narrow)
                out[slot(to, wide, narrow)] = blocks[r]
        return 0

    lax.fori_loop(0, wide // 4, copy, 0, unroll=2)
    lane = lax.broadcasted_iota(jnp.int32, (1, LANES), 1)
    noise = noise_var * total_sum(whole * whole)
    step_scalars[0:1, :] = jnp.where(lane == 0, alpha, jnp.where(
        lane == 1, norm_next, jnp.where(lane == 2, beta, noise)))
    for half in range(halves):
        spot = pl.ds(device_at(high, low, y, x, core, wide, narrow) * halves + half, 1)
        step_scalars[1 + half:2 + half, :] = images[spot, :]
        step_scalars[1 + halves + half:2 + halves + half, :] = targets[spot, :]


def last_kernel(wide, narrow, arrived, step_scalars, solution_out, residual_out, answer, sems):
    alpha = step_scalars[0:1, 0:1]
    norm = step_scalars[0:1, 1:2]
    beta = step_scalars[0:1, 2:3]
    noise = step_scalars[0:1, 3:4]
    halves = answer.shape[1]

    def add(i, total):
        return total + arrived[i, :, halves * LANES:(halves + 1) * LANES]

    share = lax.fori_loop(0, arrived.shape[0], add, jnp.zeros((1, LANES), f32), unroll=32)
    alpha_next = norm / (total_sum(share) + noise)
    _, low, y, _, core = place(wide, narrow)
    product = jnp.zeros((1, (halves + 1) * LANES), f32)
    for high in range(2):
        for x in range(narrow // 2):
            member = device_at(high, low, y, x, core, wide, narrow)
            product = product + arrived[slot(member, wide, narrow)]
    for half in range(halves):
        begin = step_scalars[1 + halves + half:2 + halves + half, :]
        residual = begin - alpha * step_scalars[1 + half:2 + half, :]
        direction = residual + beta * begin
        image = product[:, half * LANES:(half + 1) * LANES] + noise_var * direction
        answer[0, half:half + 1, :] = alpha * begin + alpha_next * direction
        answer[1, half:half + 1, :] = residual - alpha_next * image
    copies = [pltpu.make_async_copy(answer.at[i], out, sems.at[i])
              for i, out in enumerate((solution_out, residual_out))]
    for copy in copies:
        copy.start()
    for copy in copies:
        copy.wait()


def call(kernel, out_shape, *args, scratch=(), vmem=VMEM_BYTES, **options):
    return pl.pallas_call(
        kernel,
        out_shape=out_shape,
        scratch_shapes=list(scratch),
        compiler_params=pltpu.CompilerParams(vmem_limit_bytes=vmem),
        **options,
    )(*args)


def to_all(blocks):
    group = list(range(blocks.shape[0] - 1, -1, -1))
    return lax.all_to_all(blocks, ALL, split_axis=0, concat_axis=0, axis_index_groups=[group], tiled=True)


def join_kernel(*refs):
    i = 0
    for block in refs[:-1]:
        for j in range(block.shape[0]):
            refs[-1][i] = block[j]
            i += 1


def join(*blocks, flops=0):
    total = sum(b.shape[0] for b in blocks)
    return call(join_kernel, jax.ShapeDtypeStruct((total, *blocks[0].shape[1:]), f32), *blocks,
                cost_estimate=pl.CostEstimate(flops=flops, bytes_accessed=0, transcendentals=0))


def first_round(latent, own, wide, narrow):
    lows, across = wide // 4, narrow // 2
    if lows & (lows - 1) or across != 2 or lows > DIRECT:
        every = lax.all_gather(own, ALL, axis=0, tiled=True)
        every = every.reshape(2, lows, 2, across, 2, *own.shape[1:])
        high, low, y, x, core = place(wide, narrow)
        rows = every
        for place_in, axis in ((low, 1), (y, 1), (core, 2)):
            rows = lax.dynamic_index_in_dim(rows, place_in, axis, keepdims=False)
        columns = lax.dynamic_index_in_dim(every, high, 0, keepdims=False)
        columns = lax.dynamic_index_in_dim(columns, x, 2, keepdims=False)
        rows = jnp.swapaxes(rows, 0, 1).reshape(narrow, *own.shape[1:])
        sides = [lax.dynamic_index_in_dim(columns, jnp.bitwise_xor(core, side), 2, keepdims=False)
                 for side in range(2)]
        sides = [[columns.reshape(wide // 2, *own.shape[1:])] for columns in sides]
        return [[rows]], sides, (None, None)

    sizes = axis_sizes(wide, narrow)

    def swap(value, **flips):
        pairs = []
        for i in range(wide * narrow):
            spot = list(np.unravel_index(i, sizes))
            for name, flip in flips.items():
                axis = dict(high=HIGH, low=LOW, y=Y, x=X, core=CORE)[name]
                spot[axis] = int(spot[axis]) ^ flip
            pairs.append((i, int(np.ravel_multi_index(spot, sizes))))
        return lax.ppermute(value, ALL, pairs)

    rows = join(latent, swap(latent, high=1), flops=EARLY)
    columns = [own] + [swap(own, low=flip // 2, y=flip % 2) for flip in range(1, 2 * lows)]
    sides = [columns, [swap(block, core=1) for block in columns]]
    parts = [[rows], [swap(rows, x=1)]]
    return parts, sides, ([0, 1], list(range(2 * lows)))


def on_device(wide, narrow, features, projection, targets):
    rows, proj = features.shape[0], projection.shape[1]
    halves = rows // LANES
    lines = narrow * halves
    devices = wide * narrow
    scale = -2.0 / proj * math.log2(math.e)
    depth = 6 * proj + 16
    keep = 4 * devices * rows * rows <= KEEP_BYTES

    def shape(*dims, dtype=f32):
        return jax.ShapeDtypeStruct(dims, dtype)

    def scratch(*dims, dtype=f32):
        return pltpu.VMEM(dims, dtype)

    feat = features.shape[1]
    latent, own = call(
        project_kernel, (shape(1, proj, rows), shape(1, proj + 8, rows)), features, projection.T, targets.reshape(1, rows),
        in_specs=[pl.BlockSpec(memory_space=pl.ANY)] * 3, vmem=WHOLE_VMEM_BYTES,
        scratch=[scratch(CHUNKS, rows // CHUNKS, feat, dtype=bf16), scratch(proj, feat, dtype=bf16),
                 scratch(1, rows), pltpu.SemaphoreType.DMA((CHUNKS + 2,))])
    row_parts, sides, flips = first_round(latent, own, wide, narrow)
    parts = len(row_parts)
    groups = narrow // parts
    left = shape(groups, rows, depth, dtype=bf16)
    right = shape(wide // 2, depth, rows, dtype=bf16)
    vector = shape(wide // 2 * halves, LANES)
    kept = (shape(groups, wide // 2, rows, rows),) if keep else ()
    group_lines = shape(groups * halves, LANES)
    sums = scratch(groups, rows, LANES)
    settings = (proj, scale, wide, narrow, keep, flips)

    def cost(columns):
        tiles = groups * columns * rows * rows
        return pl.CostEstimate(flops=2 * tiles * depth, bytes_accessed=4 * tiles, transcendentals=tiles)

    lefts, columns, blocks, partials = [], [], [], []
    for side, column_blocks in enumerate(sides):
        row_blocks = row_parts[0] if side == 0 else lefts
        made = call(
            functools.partial(side_kernel, *settings, len(row_blocks), len(column_blocks)),
            ((left,) if side == 0 else ()) + (right, vector, group_lines) + kept,
            *row_blocks, *column_blocks, scratch=[sums], cost_estimate=cost(wide // 2))
        if side == 0:
            lefts, made = [made[0]], made[1:]
        columns += made[:2]
        partials.append(made[2])
        blocks += made[3:]
    for row_blocks in row_parts[1:]:
        made = call(
            functools.partial(rest_kernel, *settings),
            (group_lines, *kept * 2) if keep else (left, group_lines), *row_blocks, *columns,
            scratch=[sums, scratch(*left.shape, dtype=bf16)] if keep else [sums],
            cost_estimate=cost(wide))
        if not keep:
            lefts.append(made[0])
        partials.append(made[0 if keep else 1])
        blocks += made[1:] if keep else []
    out = call(
        functools.partial(message_kernel, parts, wide, narrow, halves),
        shape(devices, 1, (lines + halves) * LANES), *partials, columns[1],
        scratch=[scratch(lines, LANES)])
    block = blocks if keep else [columns[0], columns[2], *lefts]
    sums = scratch(narrow, rows, LANES)
    out, step_scalars = call(
        functools.partial(second_kernel, wide, narrow, keep, parts),
        (shape(devices, 1, (halves + 1) * LANES), shape(1 + 2 * halves, LANES)),
        to_all(out), *block,
        scratch=[scratch(devices * halves, LANES)] * 3 + [scratch(lines, LANES), sums])
    answer, residual = call(
        functools.partial(last_kernel, wide, narrow), (shape(halves, LANES), shape(halves, LANES)),
        to_all(out), step_scalars,
        out_specs=(pl.BlockSpec(memory_space=pl.ANY),) * 2,
        scratch=[scratch(2, halves, LANES), pltpu.SemaphoreType.DMA((2,))])
    return answer.reshape(rows), residual.reshape(rows)


def solution(mesh):
    wide, narrow = mesh.shape["wide"], mesh.shape["narrow"]
    line = jax.sharding.Mesh(mesh.devices.reshape(wide * narrow), (ALL,))
    in_specs = (P(ALL, None), P(), P(ALL))
    return jax.shard_map(
        functools.partial(on_device, wide, narrow), mesh=line,
        in_specs=in_specs, out_specs=(P(ALL), P(ALL)), check_vma=False,
    )
```

```python
import functools
import math

import jax
import jax.numpy as jnp
import numpy as np
from jax import lax
from jax.experimental import pallas as pl
from jax.experimental.pallas import tpu as pltpu
from jax.sharding import PartitionSpec as P

noise_var = 0.5
LANES = 128
TOGETHER = 2
EARLY = 10**9
DIRECT = 8
KEEP_BYTES = 8 * 2**20
VMEM_BYTES = 32 * 2**20
WHOLE_VMEM_BYTES = (53 * 1024 + 835) * 2**10
ALL = "all"
HIGH, LOW, Y, X, CORE = range(5)
highest = lax.Precision.HIGHEST
f32 = jnp.float32
bf16 = jnp.bfloat16


def split3(values):
    high = values.astype(bf16)
    rest = values - high.astype(f32)
    mid = rest.astype(bf16)
    low = (rest - mid.astype(f32)).astype(bf16)
    return high, mid, low


def exponent_rows(first, second):
    width = (first if not isinstance(first, float) else second).shape[1]
    row = lax.broadcasted_iota(jnp.int32, (16, width), 0)
    out = jnp.zeros((16, width), f32)
    for base, value in ((0, first), (3, second)):
        parts = (1.0, 1.0, 1.0) if isinstance(value, float) else [p.astype(f32) for p in split3(value)]
        for k, part in enumerate(parts):
            out = jnp.where(row == base + k, part, out)
    return out.astype(bf16)


def right_operand(latent, scale):
    square = jnp.sum(latent * latent, axis=0, keepdims=True) * scale
    h, m, l = split3(latent)
    return jnp.concatenate([h, m, l, h, m, h, exponent_rows(square, 1.0)], axis=0)


def left_operand(latent, scale):
    square = jnp.sum(latent * latent, axis=0, keepdims=True) * scale
    h, m, l = split3(latent * (-2.0 * scale))
    stacked = jnp.concatenate([h, h, h, m, m, l, exponent_rows(1.0, square)], axis=0)
    return stacked.T


def axis_sizes(wide, narrow):
    return 2, wide // 4, 2, narrow // 2, 2


def place(wide, narrow):
    rest, out = lax.axis_index(ALL), []
    for size in reversed(axis_sizes(wide, narrow)):
        out.append(rest % size)
        rest = rest // size
    return tuple(reversed(out))


def device_at(high, low, y, x, core, wide, narrow):
    return (((high * (wide // 4) + low) * 2 + y) * (narrow // 2) + x) * 2 + core


def slot(device, wide, narrow):
    return wide * narrow - 1 - device


def part_base(part, parts, wide, narrow):
    return 0 if parts == 1 else jnp.bitwise_xor(place(wide, narrow)[X], part) * 2


def row_sources(blocks, flips, wide, narrow):
    spots = [(b, i) for b in blocks for i in range(b.shape[0])]
    if flips is None:
        return [(b, i, i) for b, i in spots]
    high = place(wide, narrow)[HIGH]
    return [(b, i, jnp.bitwise_xor(high, flip)) for (b, i), flip in zip(spots, flips)]


def column_sources(blocks, flips, wide, narrow):
    spots = [(b, i) for b in blocks for i in range(b.shape[0])]
    if flips is None:
        return [(b, i, i) for b, i in spots]
    _, low, y, _, _ = place(wide, narrow)
    return [(b, i, jnp.bitwise_xor(low * 2 + y, flip)) for (b, i), flip in zip(spots, flips)]


def total_sum(values):
    return jnp.sum(jnp.sum(values, axis=0, keepdims=True), axis=1, keepdims=True)


def lane_sums(values):
    parts = jnp.concatenate(split3(values), axis=1)
    ones = jnp.ones((16, parts.shape[1]), bf16)
    return lax.dot_general(ones, parts, (((1,), (1,)), ((), ())),
                           preferred_element_type=f32)[0:1, :]


def make_rows(left, right, kept, read_vector, sums, add):
    groups, rows, _ = left.shape
    columns = right.shape[0]
    halves = rows // LANES

    def one_group(g, _):
        left_group = left[g]

        def some_columns(step, acc):
            first = step * TOGETHER
            both = jnp.concatenate([right[first + k] for k in range(TOGETHER)], axis=1)
            exponent = jnp.dot(left_group, both, preferred_element_type=f32)
            tile = jnp.exp2(exponent)
            for k in range(TOGETHER):
                if kept is not None:
                    kept[g, first + k] = tile[:, k * rows:(k + 1) * rows]
                for half in range(halves):
                    start = k * rows + half * LANES
                    acc = acc + tile[:, start:start + LANES] * read_vector(first + k, half)
            return acc

        start_sum = sums[g] if add else jnp.zeros((rows, LANES), f32)
        sums[g] = lax.fori_loop(0, columns // TOGETHER, some_columns, start_sum,
                                unroll=4 // TOGETHER)
        return 0

    lax.fori_loop(0, groups, one_group, 0, unroll=groups <= 2)


def use_rows(kept, read_vector, sums, add):
    groups, columns, rows, _ = kept.shape
    halves = rows // LANES

    def one_group(g, _):
        def one_column(c, acc):
            for half in range(halves):
                acc = acc + kept[g, c, :, half * LANES:(half + 1) * LANES] * read_vector(c, half)
            return acc

        start_sum = sums[g] if add else jnp.zeros((rows, LANES), f32)
        sums[g] = lax.fori_loop(0, columns, one_column, start_sum, unroll=4)
        return 0

    lax.fori_loop(0, groups, one_group, 0, unroll=groups <= 2)


def write_rows(sums, out, bases):
    groups, rows, _ = sums.shape
    halves = rows // LANES
    total = lane_sums(sums[...].reshape(groups * rows, LANES))
    for g in range(groups):
        base = bases[g * len(bases) // groups]
        for half in range(halves):
            line = (base + g % (groups // len(bases))) * halves + half
            start = (g * halves + half) * LANES
            out[pl.ds(line, 1), :] = total[:, start:start + LANES]


def project_kernel(features, projection_t, targets, latent, out, feature_buf, projection_buf, target_buf, sems):
    proj = projection_t.shape[0]
    chunks, height, _ = feature_buf.shape
    copies = [
        pltpu.make_async_copy(features.at[pl.ds(i * height, height)], feature_buf.at[i], sems.at[i])
        for i in range(chunks)]
    copies.insert(1, pltpu.make_async_copy(projection_t, projection_buf, sems.at[chunks]))
    copies.append(pltpu.make_async_copy(targets, target_buf, sems.at[chunks + 1]))
    for copy in copies:
        copy.start()
    copies.pop(1).wait()
    for i in range(chunks):
        copies[i].wait()
        some = lax.dot_general(
            projection_buf[...], feature_buf[i], (((1,), (1,)), ((), ())), preferred_element_type=f32)
        latent[0, i * proj:(i + 1) * proj, :] = some
        out[0, i * proj:(i + 1) * proj, :] = some
    copies[-1].wait()
    line = lax.broadcasted_iota(jnp.int32, (8, LANES), 0)
    tail = jnp.zeros((8, LANES), f32)
    for i in range(chunks):
        tail = jnp.where(line == i, target_buf[:, i * LANES:(i + 1) * LANES], tail)
    out[0, chunks * proj:, :] = tail


def block_latent(block, i, proj, halves):
    return jnp.concatenate([block[i, half * proj:(half + 1) * proj, :] for half in range(halves)], axis=1)


def prepare_rows(blocks, flips, left, proj, scale, wide, narrow):
    for block, i, source in row_sources(blocks, flips, wide, narrow):
        left[source] = left_operand(block_latent(block, i, proj, left.shape[1] // LANES), scale)


def vector_reader(vector, halves):
    return lambda c, half: vector[pl.ds(c * halves + half, 1), :]


def side_kernel(proj, scale, wide, narrow, keep, flips, row_count, column_count, *refs):
    rows_in, columns_in = refs[:row_count], refs[row_count:row_count + column_count]
    refs = refs[row_count + column_count:]
    fresh = rows_in[0].dtype == f32
    left, refs = (refs[0], refs[1:]) if fresh else (rows_in[0], refs)
    right, vector, partial, sums = refs[0], refs[1], refs[2], refs[-1]
    kept = refs[3] if keep else None
    halves = left.shape[1] // LANES
    if fresh:
        prepare_rows(rows_in, flips[0], left, proj, scale, wide, narrow)
    for block, i, source in column_sources(columns_in, flips[1], wide, narrow):
        right[source] = right_operand(block_latent(block, i, proj, halves), scale)
        for half in range(halves):
            line = halves * proj + half
            vector[pl.ds(source * halves + half, 1), :] = block[i, line:line + 1, :]
    make_rows(left, right, kept, vector_reader(vector, halves), sums, False)
    write_rows(sums, partial, [0])


def rest_kernel(proj, scale, wide, narrow, keep, flips, *refs):
    rows_in, columns, refs = refs[:1], refs[1:5], refs[5:]
    if keep:
        partial, *kept, sums, left = refs
    else:
        left, partial, sums = refs
        kept = (None, None)
    halves = left.shape[1] // LANES
    prepare_rows(rows_in, flips[0], left, proj, scale, wide, narrow)
    for side in range(2):
        right, vector = columns[2 * side:2 * side + 2]
        make_rows(left, right, kept[side], vector_reader(vector, halves), sums, side > 0)
    write_rows(sums, partial, [0])


def message_kernel(parts, wide, narrow, halves, *refs):
    partials, vector, out, held = refs[:parts + 1], refs[parts + 1], refs[-2], refs[-1]
    lines_of = [partials[0][...] + partials[1][...]] + [partial[...] for partial in partials[2:]]
    for part, lines in enumerate(lines_of):
        base = part_base(part, parts, wide, narrow) * halves
        for line in range(lines.shape[0]):
            held[pl.ds(base + line, 1), :] = lines[line:line + 1, :]
    _, low, y, _, _ = place(wide, narrow)
    mine = (low * 2 + y) * halves
    pieces = [held[line:line + 1, :] for line in range(held.shape[0])]
    pieces += [vector[pl.ds(mine + half, 1), :] for half in range(halves)]
    block = jnp.concatenate(pieces, axis=1)

    def copy(i, _):
        out[i] = block
        return 0

    lax.fori_loop(0, out.shape[0], copy, 0, unroll=8)


def second_kernel(wide, narrow, keep, parts, *refs):
    arrived, out, step_scalars, direction, images, targets, partial, sums = refs[:1] + refs[-7:]
    lines = partial.shape[0]
    halves = lines // narrow
    across = narrow // 2
    group = [(high, x) for x in range(narrow // 2) for high in range(2)]

    def unpack(low, _):
        for y, core in ((0, 0), (0, 1), (1, 0), (1, 1)):
            members = [device_at(high, low, y, x, core, wide, narrow) for high, x in group]
            slots = [slot(member, wide, narrow) for member in members]
            total = arrived[slots[0], :, 0:lines * LANES]
            for spot in slots[1:]:
                total = total + arrived[spot, :, 0:lines * LANES]
            for r, member in enumerate(members):
                for half in range(halves):
                    start = arrived[slots[r], :, (lines + half) * LANES:(lines + half + 1) * LANES]
                    line = r * halves + half
                    spot = pl.ds(member * halves + half, 1)
                    targets[spot, :] = start
                    images[spot, :] = total[:, line * LANES:(line + 1) * LANES] + noise_var * start
        return 0

    lax.fori_loop(0, wide // 4, unpack, 0, unroll=2)
    start, first = targets[...], images[...]
    norm = total_sum(start * start)
    alpha = norm / total_sum(start * first)
    residual = start - alpha * first
    norm_next = total_sum(residual * residual)
    beta = norm_next / norm
    whole = residual + beta * start
    direction[...] = whole
    high, low, y, x, core = place(wide, narrow)

    def side_reader(side):
        def read_vector(c, half):
            source = device_at(high, c // 2, c % 2, x, jnp.bitwise_xor(core, side), wide, narrow)
            return direction[pl.ds(source * halves + half, 1), :]
        return read_vector

    groups = narrow // parts
    for part in range(parts):
        part_sums = sums.at[part * groups:(part + 1) * groups]
        for side in range(2):
            if keep:
                use_rows(refs[1 + 2 * part + side], side_reader(side), part_sums, side > 0)
            else:
                make_rows(refs[3 + part], refs[1 + side], None, side_reader(side), part_sums, side > 0)
    write_rows(sums, partial, [part_base(part, parts, wide, narrow) for part in range(parts)])
    share = jnp.zeros((1, LANES), f32)
    for r, (row_high, row_x) in enumerate(group):
        for half in range(halves):
            spot = pl.ds(device_at(row_high, low, y, row_x, core, wide, narrow) * halves + half, 1)
            line = r * halves + half
            share = share + direction[spot, :] * partial[line:line + 1, :]
    blocks = [
        jnp.concatenate([partial[r * halves + half:r * halves + half + 1, :]
                         for half in range(halves)] + [share], axis=1)
        for r in range(narrow)]

    def copy(to_low, _):
        for r, (to_high, to_x) in enumerate(group):
            for to_y, to_core in ((0, 0), (0, 1), (1, 0), (1, 1)):
                to = device_at(to_high, to_low, to_y, to_x, to_core, wide, narrow)
                out[slot(to, wide, narrow)] = blocks[r]
        return 0

    lax.fori_loop(0, wide // 4, copy, 0, unroll=2)
    lane = lax.broadcasted_iota(jnp.int32, (1, LANES), 1)
    noise = noise_var * total_sum(whole * whole)
    step_scalars[0:1, :] = jnp.where(lane == 0, alpha, jnp.where(
        lane == 1, norm_next, jnp.where(lane == 2, beta, noise)))
    for half in range(halves):
        spot = pl.ds(device_at(high, low, y, x, core, wide, narrow) * halves + half, 1)
        step_scalars[1 + half:2 + half, :] = images[spot, :]
        step_scalars[1 + halves + half:2 + halves + half, :] = targets[spot, :]


def last_kernel(wide, narrow, arrived, step_scalars, solution_out, residual_out, answer, sems):
    alpha = step_scalars[0:1, 0:1]
    norm = step_scalars[0:1, 1:2]
    beta = step_scalars[0:1, 2:3]
    noise = step_scalars[0:1, 3:4]
    halves = answer.shape[1]

    def add(i, total):
        return total + arrived[i, :, halves * LANES:(halves + 1) * LANES]

    share = lax.fori_loop(0, arrived.shape[0], add, jnp.zeros((1, LANES), f32), unroll=32)
    alpha_next = norm / (total_sum(share) + noise)
    _, low, y, _, core = place(wide, narrow)
    product = jnp.zeros((1, (halves + 1) * LANES), f32)
    for high in range(2):
        for x in range(narrow // 2):
            member = device_at(high, low, y, x, core, wide, narrow)
            product = product + arrived[slot(member, wide, narrow)]
    for half in range(halves):
        begin = step_scalars[1 + halves + half:2 + halves + half, :]
        residual = begin - alpha * step_scalars[1 + half:2 + half, :]
        direction = residual + beta * begin
        image = product[:, half * LANES:(half + 1) * LANES] + noise_var * direction
        answer[0, half:half + 1, :] = alpha * begin + alpha_next * direction
        answer[1, half:half + 1, :] = residual - alpha_next * image
    copies = [pltpu.make_async_copy(answer.at[i], out, sems.at[i])
              for i, out in enumerate((solution_out, residual_out))]
    for copy in copies:
        copy.start()
    for copy in copies:
        copy.wait()


def call(kernel, out_shape, *args, scratch=(), vmem=VMEM_BYTES, **options):
    return pl.pallas_call(
        kernel,
        out_shape=out_shape,
        scratch_shapes=list(scratch),
        compiler_params=pltpu.CompilerParams(vmem_limit_bytes=vmem),
        **options,
    )(*args)


def to_all(blocks):
    group = list(range(blocks.shape[0] - 1, -1, -1))
    return lax.all_to_all(blocks, ALL, split_axis=0, concat_axis=0, axis_index_groups=[group], tiled=True)


def join_kernel(*refs):
    i = 0
    for block in refs[:-1]:
        for j in range(block.shape[0]):
            refs[-1][i] = block[j]
            i += 1


def join(*blocks, flops=0):
    total = sum(b.shape[0] for b in blocks)
    return call(join_kernel, jax.ShapeDtypeStruct((total, *blocks[0].shape[1:]), f32), *blocks,
                cost_estimate=pl.CostEstimate(flops=flops, bytes_accessed=0, transcendentals=0))


def first_round(latent, own, wide, narrow):
    lows, across = wide // 4, narrow // 2
    if lows & (lows - 1) or across != 2 or lows > DIRECT:
        every = lax.all_gather(own, ALL, axis=0, tiled=True)
        every = every.reshape(2, lows, 2, across, 2, *own.shape[1:])
        high, low, y, x, core = place(wide, narrow)
        rows = every
        for place_in, axis in ((low, 1), (y, 1), (core, 2)):
            rows = lax.dynamic_index_in_dim(rows, place_in, axis, keepdims=False)
        columns = lax.dynamic_index_in_dim(every, high, 0, keepdims=False)
        columns = lax.dynamic_index_in_dim(columns, x, 2, keepdims=False)
        rows = jnp.swapaxes(rows, 0, 1).reshape(narrow, *own.shape[1:])
        sides = [lax.dynamic_index_in_dim(columns, jnp.bitwise_xor(core, side), 2, keepdims=False)
                 for side in range(2)]
        sides = [[columns.reshape(wide // 2, *own.shape[1:])] for columns in sides]
        return [[rows]], sides, (None, None)

    sizes = axis_sizes(wide, narrow)

    def swap(value, **flips):
        pairs = []
        for i in range(wide * narrow):
            spot = list(np.unravel_index(i, sizes))
            for name, flip in flips.items():
                axis = dict(high=HIGH, low=LOW, y=Y, x=X, core=CORE)[name]
                spot[axis] = int(spot[axis]) ^ flip
            pairs.append((i, int(np.ravel_multi_index(spot, sizes))))
        return lax.ppermute(value, ALL, pairs)

    rows = join(latent, swap(latent, high=1), flops=EARLY)
    columns = [own] + [swap(own, low=flip // 2, y=flip % 2) for flip in range(1, 2 * lows)]
    sides = [columns, [swap(block, core=1) for block in columns]]
    parts = [[rows], [swap(rows, x=1)]]
    return parts, sides, ([0, 1], list(range(2 * lows)))


def on_device(wide, narrow, features, projection, targets):
    rows, proj = features.shape[0], projection.shape[1]
    halves = rows // LANES
    lines = narrow * halves
    devices = wide * narrow
    scale = -2.0 / proj * math.log2(math.e)
    depth = 6 * proj + 16
    keep = 4 * devices * rows * rows <= KEEP_BYTES

    def shape(*dims, dtype=f32):
        return jax.ShapeDtypeStruct(dims, dtype)

    def scratch(*dims, dtype=f32):
        return pltpu.VMEM(dims, dtype)

    feat = features.shape[1]
    latent, own = call(
        project_kernel, (shape(1, halves * proj, LANES), shape(1, halves * proj + 8, LANES)), features, projection.T, targets.reshape(1, rows),
        in_specs=[pl.BlockSpec(memory_space=pl.ANY)] * 3, vmem=WHOLE_VMEM_BYTES,
        scratch=[scratch(halves, LANES, feat, dtype=bf16), scratch(proj, feat, dtype=bf16),
                 scratch(1, rows), pltpu.SemaphoreType.DMA((halves + 2,))])
    row_parts, sides, flips = first_round(latent, own, wide, narrow)
    parts = len(row_parts)
    groups = narrow // parts
    left = shape(groups, rows, depth, dtype=bf16)
    right = shape(wide // 2, depth, rows, dtype=bf16)
    vector = shape(wide // 2 * halves, LANES)
    kept = (shape(groups, wide // 2, rows, rows),) if keep else ()
    group_lines = shape(groups * halves, LANES)
    sums = scratch(groups, rows, LANES)
    settings = (proj, scale, wide, narrow, keep, flips)

    def cost(columns):
        tiles = groups * columns * rows * rows
        return pl.CostEstimate(flops=2 * tiles * depth, bytes_accessed=4 * tiles, transcendentals=tiles)

    lefts, columns, blocks, partials = [], [], [], []
    for side, column_blocks in enumerate(sides):
        row_blocks = row_parts[0] if side == 0 else lefts
        made = call(
            functools.partial(side_kernel, *settings, len(row_blocks), len(column_blocks)),
            ((left,) if side == 0 else ()) + (right, vector, group_lines) + kept,
            *row_blocks, *column_blocks, scratch=[sums], cost_estimate=cost(wide // 2))
        if side == 0:
            lefts, made = [made[0]], made[1:]
        columns += made[:2]
        partials.append(made[2])
        blocks += made[3:]
    for row_blocks in row_parts[1:]:
        made = call(
            functools.partial(rest_kernel, *settings),
            (group_lines, *kept * 2) if keep else (left, group_lines), *row_blocks, *columns,
            scratch=[sums, scratch(*left.shape, dtype=bf16)] if keep else [sums],
            cost_estimate=cost(wide))
        if not keep:
            lefts.append(made[0])
        partials.append(made[0 if keep else 1])
        blocks += made[1:] if keep else []
    out = call(
        functools.partial(message_kernel, parts, wide, narrow, halves),
        shape(devices, 1, (lines + halves) * LANES), *partials, columns[1],
        scratch=[scratch(lines, LANES)])
    block = blocks if keep else [columns[0], columns[2], *lefts]
    sums = scratch(narrow, rows, LANES)
    out, step_scalars = call(
        functools.partial(second_kernel, wide, narrow, keep, parts),
        (shape(devices, 1, (halves + 1) * LANES), shape(1 + 2 * halves, LANES)),
        to_all(out), *block,
        scratch=[scratch(devices * halves, LANES)] * 3 + [scratch(lines, LANES), sums])
    answer, residual = call(
        functools.partial(last_kernel, wide, narrow), (shape(halves, LANES), shape(halves, LANES)),
        to_all(out), step_scalars,
        out_specs=(pl.BlockSpec(memory_space=pl.ANY),) * 2,
        scratch=[scratch(2, halves, LANES), pltpu.SemaphoreType.DMA((2,))])
    return answer.reshape(rows), residual.reshape(rows)


def solution(mesh):
    wide, narrow = mesh.shape["wide"], mesh.shape["narrow"]
    line = jax.sharding.Mesh(mesh.devices.reshape(wide * narrow), (ALL,))
    in_specs = (P(ALL, None), P(), P(ALL))
    return jax.shard_map(
        functools.partial(on_device, wide, narrow), mesh=line,
        in_specs=in_specs, out_specs=(P(ALL), P(ALL)), check_vma=False,
    )
```

```python
import functools
import math

import jax
import jax.numpy as jnp
import numpy as np
from jax import lax
from jax.experimental import pallas as pl
from jax.experimental.pallas import tpu as pltpu
from jax.sharding import PartitionSpec as P

noise_var = 0.5
LANES = 128
TOGETHER = 2
EARLY = 10**9
DIRECT = 8
KEEP_BYTES = 8 * 2**20
VMEM_BYTES = 32 * 2**20
WHOLE_VMEM_BYTES = (53 * 1024 + 835) * 2**10
ALL = "all"
HIGH, LOW, Y, X, CORE = range(5)
highest = lax.Precision.HIGHEST
f32 = jnp.float32
bf16 = jnp.bfloat16


def split3(values):
    high = values.astype(bf16)
    rest = values - high.astype(f32)
    mid = rest.astype(bf16)
    low = (rest - mid.astype(f32)).astype(bf16)
    return high, mid, low


def exponent_rows(first, second):
    width = (first if not isinstance(first, float) else second).shape[1]
    row = lax.broadcasted_iota(jnp.int32, (16, width), 0)
    out = jnp.zeros((16, width), f32)
    for base, value in ((0, first), (3, second)):
        parts = (1.0, 1.0, 1.0) if isinstance(value, float) else [p.astype(f32) for p in split3(value)]
        for k, part in enumerate(parts):
            out = jnp.where(row == base + k, part, out)
    return out.astype(bf16)


def right_operand(latent, scale):
    square = jnp.sum(latent * latent, axis=0, keepdims=True) * scale
    h, m, l = split3(latent)
    return jnp.concatenate([h, m, l, h, m, h, exponent_rows(square, 1.0)], axis=0)


def left_operand(latent, scale):
    square = jnp.sum(latent * latent, axis=0, keepdims=True) * scale
    h, m, l = split3(latent * (-2.0 * scale))
    stacked = jnp.concatenate([h, h, h, m, m, l, exponent_rows(1.0, square)], axis=0)
    return stacked.T


def axis_sizes(wide, narrow):
    return 2, wide // 4, 2, narrow // 2, 2


def place(wide, narrow):
    rest, out = lax.axis_index(ALL), []
    for size in reversed(axis_sizes(wide, narrow)):
        out.append(rest % size)
        rest = rest // size
    return tuple(reversed(out))


def device_at(high, low, y, x, core, wide, narrow):
    return (((high * (wide // 4) + low) * 2 + y) * (narrow // 2) + x) * 2 + core


def slot(device, wide, narrow):
    return wide * narrow - 1 - device


def part_base(part, parts, wide, narrow):
    return 0 if parts == 1 else jnp.bitwise_xor(place(wide, narrow)[X], part) * 2


def row_sources(blocks, flips, wide, narrow):
    spots = [(b, i) for b in blocks for i in range(b.shape[0])]
    if flips is None:
        return [(b, i, i) for b, i in spots]
    high = place(wide, narrow)[HIGH]
    return [(b, i, jnp.bitwise_xor(high, flip)) for (b, i), flip in zip(spots, flips)]


def column_sources(blocks, flips, wide, narrow):
    spots = [(b, i) for b in blocks for i in range(b.shape[0])]
    if flips is None:
        return [(b, i, i) for b, i in spots]
    _, low, y, _, _ = place(wide, narrow)
    return [(b, i, jnp.bitwise_xor(low * 2 + y, flip)) for (b, i), flip in zip(spots, flips)]


def total_sum(values):
    return jnp.sum(jnp.sum(values, axis=0, keepdims=True), axis=1, keepdims=True)


def lane_sums(values):
    parts = jnp.concatenate(split3(values), axis=1)
    ones = jnp.ones((16, parts.shape[1]), bf16)
    return lax.dot_general(ones, parts, (((1,), (1,)), ((), ())),
                           preferred_element_type=f32)[0:1, :]


def make_rows(left, sides, sums):
    groups, rows, _ = left.shape
    halves = rows // LANES

    def one_group(g, _):
        left_group = left[g]
        acc = jnp.zeros((rows, LANES), f32)
        for right, kept, read_vector in sides:

            def some_columns(step, acc):
                first = step * TOGETHER
                both = jnp.concatenate([right[first + k] for k in range(TOGETHER)], axis=1)
                exponent = jnp.dot(left_group, both, preferred_element_type=f32)
                tile = jnp.exp2(exponent)
                for k in range(TOGETHER):
                    if kept is not None:
                        kept[g, first + k] = tile[:, k * rows:(k + 1) * rows]
                    for half in range(halves):
                        start = k * rows + half * LANES
                        acc = acc + tile[:, start:start + LANES] * read_vector(first + k, half)
                return acc

            acc = lax.fori_loop(0, right.shape[0] // TOGETHER, some_columns, acc, unroll=4 // TOGETHER)
        sums[g] = acc
        return 0

    lax.fori_loop(0, groups, one_group, 0, unroll=groups <= 2)


def use_rows(sides, sums):
    groups, rows, _ = sums.shape
    halves = rows // LANES

    def one_group(g, _):
        acc = jnp.zeros((rows, LANES), f32)
        for kept, read_vector in sides:

            def one_column(c, acc):
                for half in range(halves):
                    acc = acc + kept[g, c, :, half * LANES:(half + 1) * LANES] * read_vector(c, half)
                return acc

            acc = lax.fori_loop(0, kept.shape[1], one_column, acc, unroll=4)
        sums[g] = acc
        return 0

    lax.fori_loop(0, groups, one_group, 0, unroll=groups <= 2)


def write_rows(sums, out, bases):
    groups, rows, _ = sums.shape
    halves = rows // LANES
    total = lane_sums(sums[...].reshape(groups * rows, LANES))
    for g in range(groups):
        base = bases[g * len(bases) // groups]
        for half in range(halves):
            line = (base + g % (groups // len(bases))) * halves + half
            start = (g * halves + half) * LANES
            out[pl.ds(line, 1), :] = total[:, start:start + LANES]


def project_kernel(features, projection_t, targets, latent, out, feature_buf, projection_buf, target_buf, sems):
    proj = projection_t.shape[0]
    chunks, height, _ = feature_buf.shape
    copies = [
        pltpu.make_async_copy(features.at[pl.ds(i * height, height)], feature_buf.at[i], sems.at[i])
        for i in range(chunks)]
    copies.insert(1, pltpu.make_async_copy(projection_t, projection_buf, sems.at[chunks]))
    copies.append(pltpu.make_async_copy(targets, target_buf, sems.at[chunks + 1]))
    for copy in copies:
        copy.start()
    copies.pop(1).wait()
    for i in range(chunks):
        copies[i].wait()
        some = lax.dot_general(
            projection_buf[...], feature_buf[i], (((1,), (1,)), ((), ())), preferred_element_type=f32)
        latent[0, i * proj:(i + 1) * proj, :] = some
        out[0, i * proj:(i + 1) * proj, :] = some
    copies[-1].wait()
    line = lax.broadcasted_iota(jnp.int32, (8, LANES), 0)
    tail = jnp.zeros((8, LANES), f32)
    for i in range(chunks):
        tail = jnp.where(line == i, target_buf[:, i * LANES:(i + 1) * LANES], tail)
    out[0, chunks * proj:, :] = tail


def block_latent(block, i, proj, halves):
    return jnp.concatenate([block[i, half * proj:(half + 1) * proj, :] for half in range(halves)], axis=1)


def prepare_rows(blocks, flips, left, proj, scale, wide, narrow):
    for block, i, source in row_sources(blocks, flips, wide, narrow):
        left[source] = left_operand(block_latent(block, i, proj, left.shape[1] // LANES), scale)


def vector_reader(vector, halves):
    return lambda c, half: vector[pl.ds(c * halves + half, 1), :]


def side_kernel(proj, scale, wide, narrow, keep, flips, row_count, column_count, *refs):
    rows_in, columns_in = refs[:row_count], refs[row_count:row_count + column_count]
    refs = refs[row_count + column_count:]
    fresh = rows_in[0].dtype == f32
    left, refs = (refs[0], refs[1:]) if fresh else (rows_in[0], refs)
    right, vector, partial, sums = refs[0], refs[1], refs[2], refs[-1]
    kept = refs[3] if keep else None
    halves = left.shape[1] // LANES
    if fresh:
        prepare_rows(rows_in, flips[0], left, proj, scale, wide, narrow)
    for block, i, source in column_sources(columns_in, flips[1], wide, narrow):
        right[source] = right_operand(block_latent(block, i, proj, halves), scale)
        for half in range(halves):
            line = halves * proj + half
            vector[pl.ds(source * halves + half, 1), :] = block[i, line:line + 1, :]
    make_rows(left, [(right, kept, vector_reader(vector, halves))], sums)
    write_rows(sums, partial, [0])


def rest_kernel(proj, scale, wide, narrow, keep, flips, *refs):
    rows_in, columns, refs = refs[:1], refs[1:5], refs[5:]
    if keep:
        partial, *kept, sums, left = refs
    else:
        left, partial, sums = refs
        kept = (None, None)
    halves = left.shape[1] // LANES
    prepare_rows(rows_in, flips[0], left, proj, scale, wide, narrow)
    make_rows(left, [
        (columns[2 * side], kept[side], vector_reader(columns[2 * side + 1], halves))
        for side in range(2)], sums)
    write_rows(sums, partial, [0])


def message_kernel(parts, wide, narrow, halves, *refs):
    partials, vector, out, held = refs[:parts + 1], refs[parts + 1], refs[-2], refs[-1]
    lines_of = [partials[0][...] + partials[1][...]] + [partial[...] for partial in partials[2:]]
    for part, lines in enumerate(lines_of):
        base = part_base(part, parts, wide, narrow) * halves
        for line in range(lines.shape[0]):
            held[pl.ds(base + line, 1), :] = lines[line:line + 1, :]
    _, low, y, _, _ = place(wide, narrow)
    mine = (low * 2 + y) * halves
    pieces = [held[line:line + 1, :] for line in range(held.shape[0])]
    pieces += [vector[pl.ds(mine + half, 1), :] for half in range(halves)]
    block = jnp.concatenate(pieces, axis=1)

    def copy(i, _):
        out[i] = block
        return 0

    lax.fori_loop(0, out.shape[0], copy, 0, unroll=8)


def second_kernel(wide, narrow, keep, parts, *refs):
    arrived, out, step_scalars, direction, images, targets, partial, sums = refs[:1] + refs[-7:]
    lines = partial.shape[0]
    halves = lines // narrow
    across = narrow // 2
    group = [(high, x) for x in range(narrow // 2) for high in range(2)]

    def unpack(low, _):
        for y, core in ((0, 0), (0, 1), (1, 0), (1, 1)):
            members = [device_at(high, low, y, x, core, wide, narrow) for high, x in group]
            slots = [slot(member, wide, narrow) for member in members]
            total = arrived[slots[0], :, 0:lines * LANES]
            for spot in slots[1:]:
                total = total + arrived[spot, :, 0:lines * LANES]
            for r, member in enumerate(members):
                for half in range(halves):
                    start = arrived[slots[r], :, (lines + half) * LANES:(lines + half + 1) * LANES]
                    line = r * halves + half
                    spot = pl.ds(member * halves + half, 1)
                    targets[spot, :] = start
                    images[spot, :] = total[:, line * LANES:(line + 1) * LANES] + noise_var * start
        return 0

    lax.fori_loop(0, wide // 4, unpack, 0, unroll=2)
    start, first = targets[...], images[...]
    norm = total_sum(start * start)
    alpha = norm / total_sum(start * first)
    residual = start - alpha * first
    norm_next = total_sum(residual * residual)
    beta = norm_next / norm
    whole = residual + beta * start
    direction[...] = whole
    high, low, y, x, core = place(wide, narrow)

    def side_reader(side):
        def read_vector(c, half):
            source = device_at(high, c // 2, c % 2, x, jnp.bitwise_xor(core, side), wide, narrow)
            return direction[pl.ds(source * halves + half, 1), :]
        return read_vector

    groups = narrow // parts
    for part in range(parts):
        part_sums = sums.at[part * groups:(part + 1) * groups]
        if keep:
            use_rows([(refs[1 + 2 * part + side], side_reader(side)) for side in range(2)], part_sums)
        else:
            make_rows(refs[3 + part], [(refs[1 + side], None, side_reader(side)) for side in range(2)], part_sums)
    write_rows(sums, partial, [part_base(part, parts, wide, narrow) for part in range(parts)])
    share = jnp.zeros((1, LANES), f32)
    for r, (row_high, row_x) in enumerate(group):
        for half in range(halves):
            spot = pl.ds(device_at(row_high, low, y, row_x, core, wide, narrow) * halves + half, 1)
            line = r * halves + half
            share = share + direction[spot, :] * partial[line:line + 1, :]
    blocks = [
        jnp.concatenate([partial[r * halves + half:r * halves + half + 1, :]
                         for half in range(halves)] + [share], axis=1)
        for r in range(narrow)]

    def copy(to_low, _):
        for r, (to_high, to_x) in enumerate(group):
            for to_y, to_core in ((0, 0), (0, 1), (1, 0), (1, 1)):
                to = device_at(to_high, to_low, to_y, to_x, to_core, wide, narrow)
                out[slot(to, wide, narrow)] = blocks[r]
        return 0

    lax.fori_loop(0, wide // 4, copy, 0, unroll=2)
    lane = lax.broadcasted_iota(jnp.int32, (1, LANES), 1)
    noise = noise_var * total_sum(whole * whole)
    step_scalars[0:1, :] = jnp.where(lane == 0, alpha, jnp.where(
        lane == 1, norm_next, jnp.where(lane == 2, beta, noise)))
    for half in range(halves):
        spot = pl.ds(device_at(high, low, y, x, core, wide, narrow) * halves + half, 1)
        step_scalars[1 + half:2 + half, :] = images[spot, :]
        step_scalars[1 + halves + half:2 + halves + half, :] = targets[spot, :]


def last_kernel(wide, narrow, arrived, step_scalars, solution_out, residual_out, answer, sems):
    alpha = step_scalars[0:1, 0:1]
    norm = step_scalars[0:1, 1:2]
    beta = step_scalars[0:1, 2:3]
    noise = step_scalars[0:1, 3:4]
    halves = answer.shape[1]

    def add(i, total):
        return total + arrived[i, :, halves * LANES:(halves + 1) * LANES]

    share = lax.fori_loop(0, arrived.shape[0], add, jnp.zeros((1, LANES), f32), unroll=32)
    alpha_next = norm / (total_sum(share) + noise)
    _, low, y, _, core = place(wide, narrow)
    product = jnp.zeros((1, (halves + 1) * LANES), f32)
    for high in range(2):
        for x in range(narrow // 2):
            member = device_at(high, low, y, x, core, wide, narrow)
            product = product + arrived[slot(member, wide, narrow)]
    for half in range(halves):
        begin = step_scalars[1 + halves + half:2 + halves + half, :]
        residual = begin - alpha * step_scalars[1 + half:2 + half, :]
        direction = residual + beta * begin
        image = product[:, half * LANES:(half + 1) * LANES] + noise_var * direction
        answer[0, half:half + 1, :] = alpha * begin + alpha_next * direction
        answer[1, half:half + 1, :] = residual - alpha_next * image
    copies = [pltpu.make_async_copy(answer.at[i], out, sems.at[i])
              for i, out in enumerate((solution_out, residual_out))]
    for copy in copies:
        copy.start()
    for copy in copies:
        copy.wait()


def call(kernel, out_shape, *args, scratch=(), vmem=VMEM_BYTES, **options):
    return pl.pallas_call(
        kernel,
        out_shape=out_shape,
        scratch_shapes=list(scratch),
        compiler_params=pltpu.CompilerParams(vmem_limit_bytes=vmem),
        **options,
    )(*args)


def to_all(blocks):
    group = list(range(blocks.shape[0] - 1, -1, -1))
    return lax.all_to_all(blocks, ALL, split_axis=0, concat_axis=0, axis_index_groups=[group], tiled=True)


def join_kernel(*refs):
    i = 0
    for block in refs[:-1]:
        for j in range(block.shape[0]):
            refs[-1][i] = block[j]
            i += 1


def join(*blocks, flops=0):
    total = sum(b.shape[0] for b in blocks)
    return call(join_kernel, jax.ShapeDtypeStruct((total, *blocks[0].shape[1:]), f32), *blocks,
                cost_estimate=pl.CostEstimate(flops=flops, bytes_accessed=0, transcendentals=0))


def first_round(latent, own, wide, narrow):
    lows, across = wide // 4, narrow // 2
    if lows & (lows - 1) or across != 2 or lows > DIRECT:
        every = lax.all_gather(own, ALL, axis=0, tiled=True)
        every = every.reshape(2, lows, 2, across, 2, *own.shape[1:])
        high, low, y, x, core = place(wide, narrow)
        rows = every
        for place_in, axis in ((low, 1), (y, 1), (core, 2)):
            rows = lax.dynamic_index_in_dim(rows, place_in, axis, keepdims=False)
        columns = lax.dynamic_index_in_dim(every, high, 0, keepdims=False)
        columns = lax.dynamic_index_in_dim(columns, x, 2, keepdims=False)
        rows = jnp.swapaxes(rows, 0, 1).reshape(narrow, *own.shape[1:])
        sides = [lax.dynamic_index_in_dim(columns, jnp.bitwise_xor(core, side), 2, keepdims=False)
                 for side in range(2)]
        sides = [[columns.reshape(wide // 2, *own.shape[1:])] for columns in sides]
        return [[rows]], sides, (None, None)

    sizes = axis_sizes(wide, narrow)

    def swap(value, **flips):
        pairs = []
        for i in range(wide * narrow):
            spot = list(np.unravel_index(i, sizes))
            for name, flip in flips.items():
                axis = dict(high=HIGH, low=LOW, y=Y, x=X, core=CORE)[name]
                spot[axis] = int(spot[axis]) ^ flip
            pairs.append((i, int(np.ravel_multi_index(spot, sizes))))
        return lax.ppermute(value, ALL, pairs)

    rows = join(latent, swap(latent, high=1), flops=EARLY)
    columns = [own] + [swap(own, low=flip // 2, y=flip % 2) for flip in range(1, 2 * lows)]
    sides = [columns, [swap(block, core=1) for block in columns]]
    parts = [[rows], [swap(rows, x=1)]]
    return parts, sides, ([0, 1], list(range(2 * lows)))


def on_device(wide, narrow, features, projection, targets):
    rows, proj = features.shape[0], projection.shape[1]
    halves = rows // LANES
    lines = narrow * halves
    devices = wide * narrow
    scale = -2.0 / proj * math.log2(math.e)
    depth = 6 * proj + 16
    keep = 4 * devices * rows * rows <= KEEP_BYTES

    def shape(*dims, dtype=f32):
        return jax.ShapeDtypeStruct(dims, dtype)

    def scratch(*dims, dtype=f32):
        return pltpu.VMEM(dims, dtype)

    feat = features.shape[1]
    latent, own = call(
        project_kernel, (shape(1, halves * proj, LANES), shape(1, halves * proj + 8, LANES)), features, projection.T, targets.reshape(1, rows),
        in_specs=[pl.BlockSpec(memory_space=pl.ANY)] * 3, vmem=WHOLE_VMEM_BYTES,
        scratch=[scratch(halves, LANES, feat, dtype=bf16), scratch(proj, feat, dtype=bf16),
                 scratch(1, rows), pltpu.SemaphoreType.DMA((halves + 2,))])
    row_parts, sides, flips = first_round(latent, own, wide, narrow)
    parts = len(row_parts)
    groups = narrow // parts
    left = shape(groups, rows, depth, dtype=bf16)
    right = shape(wide // 2, depth, rows, dtype=bf16)
    vector = shape(wide // 2 * halves, LANES)
    kept = (shape(groups, wide // 2, rows, rows),) if keep else ()
    group_lines = shape(groups * halves, LANES)
    sums = scratch(groups, rows, LANES)
    settings = (proj, scale, wide, narrow, keep, flips)

    def cost(columns):
        tiles = groups * columns * rows * rows
        return pl.CostEstimate(flops=2 * tiles * depth, bytes_accessed=4 * tiles, transcendentals=tiles)

    lefts, columns, blocks, partials = [], [], [], []
    for side, column_blocks in enumerate(sides):
        row_blocks = row_parts[0] if side == 0 else lefts
        made = call(
            functools.partial(side_kernel, *settings, len(row_blocks), len(column_blocks)),
            ((left,) if side == 0 else ()) + (right, vector, group_lines) + kept,
            *row_blocks, *column_blocks, scratch=[sums], cost_estimate=cost(wide // 2))
        if side == 0:
            lefts, made = [made[0]], made[1:]
        columns += made[:2]
        partials.append(made[2])
        blocks += made[3:]
    for row_blocks in row_parts[1:]:
        made = call(
            functools.partial(rest_kernel, *settings),
            (group_lines, *kept * 2) if keep else (left, group_lines), *row_blocks, *columns,
            scratch=[sums, scratch(*left.shape, dtype=bf16)] if keep else [sums],
            cost_estimate=cost(wide))
        if not keep:
            lefts.append(made[0])
        partials.append(made[0 if keep else 1])
        blocks += made[1:] if keep else []
    out = call(
        functools.partial(message_kernel, parts, wide, narrow, halves),
        shape(devices, 1, (lines + halves) * LANES), *partials, columns[1],
        scratch=[scratch(lines, LANES)])
    block = blocks if keep else [columns[0], columns[2], *lefts]
    sums = scratch(narrow, rows, LANES)
    out, step_scalars = call(
        functools.partial(second_kernel, wide, narrow, keep, parts),
        (shape(devices, 1, (halves + 1) * LANES), shape(1 + 2 * halves, LANES)),
        to_all(out), *block,
        scratch=[scratch(devices * halves, LANES)] * 3 + [scratch(lines, LANES), sums])
    answer, residual = call(
        functools.partial(last_kernel, wide, narrow), (shape(halves, LANES), shape(halves, LANES)),
        to_all(out), step_scalars,
        out_specs=(pl.BlockSpec(memory_space=pl.ANY),) * 2,
        scratch=[scratch(2, halves, LANES), pltpu.SemaphoreType.DMA((2,))])
    return answer.reshape(rows), residual.reshape(rows)


def solution(mesh):
    wide, narrow = mesh.shape["wide"], mesh.shape["narrow"]
    line = jax.sharding.Mesh(mesh.devices.reshape(wide * narrow), (ALL,))
    in_specs = (P(ALL, None), P(), P(ALL))
    return jax.shard_map(
        functools.partial(on_device, wide, narrow), mesh=line,
        in_specs=in_specs, out_specs=(P(ALL), P(ALL)), check_vma=False,
    )
```

```python
import functools
import math

import jax
import jax.numpy as jnp
import numpy as np
from jax import lax
from jax.experimental import pallas as pl
from jax.experimental.pallas import tpu as pltpu
from jax.sharding import PartitionSpec as P

noise_var = 0.5
LANES = 128
TOGETHER = 2
EARLY = 10**9
DIRECT = 8
KEEP_BYTES = 8 * 2**20
VMEM_BYTES = 32 * 2**20
ALL = "all"
HIGH, LOW, Y, X, CORE = range(5)
highest = lax.Precision.HIGHEST
f32 = jnp.float32
bf16 = jnp.bfloat16


def split3(values):
    high = values.astype(bf16)
    rest = values - high.astype(f32)
    mid = rest.astype(bf16)
    low = (rest - mid.astype(f32)).astype(bf16)
    return high, mid, low


def exponent_rows(first, second):
    width = (first if not isinstance(first, float) else second).shape[1]
    row = lax.broadcasted_iota(jnp.int32, (16, width), 0)
    out = jnp.zeros((16, width), f32)
    for base, value in ((0, first), (3, second)):
        parts = (1.0, 1.0, 1.0) if isinstance(value, float) else [p.astype(f32) for p in split3(value)]
        for k, part in enumerate(parts):
            out = jnp.where(row == base + k, part, out)
    return out.astype(bf16)


def right_operand(latent, scale):
    square = jnp.sum(latent * latent, axis=0, keepdims=True) * scale
    h, m, l = split3(latent)
    return jnp.concatenate([h, m, l, h, m, h, exponent_rows(square, 1.0)], axis=0)


def left_operand(latent, scale):
    square = jnp.sum(latent * latent, axis=0, keepdims=True) * scale
    h, m, l = split3(latent * (-2.0 * scale))
    stacked = jnp.concatenate([h, h, h, m, m, l, exponent_rows(1.0, square)], axis=0)
    return stacked.T


def axis_sizes(wide, narrow):
    return 2, wide // 4, 2, narrow // 2, 2


def place(wide, narrow):
    rest, out = lax.axis_index(ALL), []
    for size in reversed(axis_sizes(wide, narrow)):
        out.append(rest % size)
        rest = rest // size
    return tuple(reversed(out))


def device_at(high, low, y, x, core, wide, narrow):
    return (((high * (wide // 4) + low) * 2 + y) * (narrow // 2) + x) * 2 + core


def slot(device, wide, narrow):
    return wide * narrow - 1 - device


def part_base(part, parts, wide, narrow):
    return 0 if parts == 1 else jnp.bitwise_xor(place(wide, narrow)[X], part) * 2


def row_sources(blocks, flips, wide, narrow):
    spots = [(b, i) for b in blocks for i in range(b.shape[0])]
    if flips is None:
        return [(b, i, i) for b, i in spots]
    high = place(wide, narrow)[HIGH]
    return [(b, i, jnp.bitwise_xor(high, flip)) for (b, i), flip in zip(spots, flips)]


def column_sources(blocks, flips, wide, narrow):
    spots = [(b, i) for b in blocks for i in range(b.shape[0])]
    if flips is None:
        return [(b, i, i) for b, i in spots]
    _, low, y, _, _ = place(wide, narrow)
    return [(b, i, jnp.bitwise_xor(low * 2 + y, flip)) for (b, i), flip in zip(spots, flips)]


def total_sum(values):
    return jnp.sum(jnp.sum(values, axis=0, keepdims=True), axis=1, keepdims=True)


def lane_sums(values):
    parts = jnp.concatenate(split3(values), axis=1)
    ones = jnp.ones((16, parts.shape[1]), bf16)
    return lax.dot_general(ones, parts, (((1,), (1,)), ((), ())),
                           preferred_element_type=f32)[0:1, :]


def make_rows(left, right, kept, read_vector, sums, add):
    groups, rows, _ = left.shape
    columns = right.shape[0]
    halves = rows // LANES

    def one_group(g, _):
        left_group = left[g]

        def some_columns(step, acc):
            first = step * TOGETHER
            both = jnp.concatenate([right[first + k] for k in range(TOGETHER)], axis=1)
            exponent = jnp.dot(left_group, both, preferred_element_type=f32)
            tile = jnp.exp2(exponent)
            for k in range(TOGETHER):
                if kept is not None:
                    kept[g, first + k] = tile[:, k * rows:(k + 1) * rows]
                for half in range(halves):
                    start = k * rows + half * LANES
                    acc = acc + tile[:, start:start + LANES] * read_vector(first + k, half)
            return acc

        start_sum = sums[g] if add else jnp.zeros((rows, LANES), f32)
        sums[g] = lax.fori_loop(0, columns // TOGETHER, some_columns, start_sum,
                                unroll=4 // TOGETHER)
        return 0

    lax.fori_loop(0, groups, one_group, 0, unroll=groups <= 2)


def use_rows(kept, read_vector, sums, add):
    groups, columns, rows, _ = kept.shape
    halves = rows // LANES

    def one_group(g, _):
        def one_column(c, acc):
            for half in range(halves):
                acc = acc + kept[g, c, :, half * LANES:(half + 1) * LANES] * read_vector(c, half)
            return acc

        start_sum = sums[g] if add else jnp.zeros((rows, LANES), f32)
        sums[g] = lax.fori_loop(0, columns, one_column, start_sum, unroll=4)
        return 0

    lax.fori_loop(0, groups, one_group, 0, unroll=groups <= 2)


def write_rows(sums, out, bases):
    groups, rows, _ = sums.shape
    halves = rows // LANES
    total = lane_sums(sums[...].reshape(groups * rows, LANES))
    for g in range(groups):
        base = bases[g * len(bases) // groups]
        for half in range(halves):
            line = (base + g % (groups // len(bases))) * halves + half
            start = (g * halves + half) * LANES
            out[pl.ds(line, 1), :] = total[:, start:start + LANES]


def project_kernel(features, projection_t, targets, latent, out, feature_buf, projection_buf, target_buf, sems):
    proj = projection_t.shape[0]
    chunks, height, _ = feature_buf.shape
    copies = [
        pltpu.make_async_copy(features.at[pl.ds(i * height, height)], feature_buf.at[i], sems.at[i])
        for i in range(chunks)]
    copies.insert(1, pltpu.make_async_copy(projection_t, projection_buf, sems.at[chunks]))
    copies.append(pltpu.make_async_copy(targets, target_buf, sems.at[chunks + 1]))
    for copy in copies:
        copy.start()
    copies.pop(1).wait()
    for i in range(chunks):
        copies[i].wait()
        some = lax.dot_general(
            projection_buf[...], feature_buf[i], (((1,), (1,)), ((), ())), preferred_element_type=f32)
        latent[0, i * proj:(i + 1) * proj, :] = some
        out[0, i * proj:(i + 1) * proj, :] = some
    copies[-1].wait()
    line = lax.broadcasted_iota(jnp.int32, (8, LANES), 0)
    tail = jnp.zeros((8, LANES), f32)
    for i in range(chunks):
        tail = jnp.where(line == i, target_buf[:, i * LANES:(i + 1) * LANES], tail)
    out[0, chunks * proj:, :] = tail


def block_latent(block, i, proj, halves):
    return jnp.concatenate([block[i, half * proj:(half + 1) * proj, :] for half in range(halves)], axis=1)


def prepare_rows(blocks, flips, left, proj, scale, wide, narrow):
    for block, i, source in row_sources(blocks, flips, wide, narrow):
        left[source] = left_operand(block_latent(block, i, proj, left.shape[1] // LANES), scale)


def vector_reader(vector, halves):
    return lambda c, half: vector[pl.ds(c * halves + half, 1), :]


def side_kernel(proj, scale, wide, narrow, keep, flips, row_count, column_count, *refs):
    rows_in, columns_in = refs[:row_count], refs[row_count:row_count + column_count]
    refs = refs[row_count + column_count:]
    fresh = rows_in[0].dtype == f32
    left, refs = (refs[0], refs[1:]) if fresh else (rows_in[0], refs)
    right, vector, partial, sums = refs[0], refs[1], refs[2], refs[-1]
    kept = refs[3] if keep else None
    halves = left.shape[1] // LANES
    if fresh:
        prepare_rows(rows_in, flips[0], left, proj, scale, wide, narrow)
    for block, i, source in column_sources(columns_in, flips[1], wide, narrow):
        right[source] = right_operand(block_latent(block, i, proj, halves), scale)
        for half in range(halves):
            line = halves * proj + half
            vector[pl.ds(source * halves + half, 1), :] = block[i, line:line + 1, :]
    make_rows(left, right, kept, vector_reader(vector, halves), sums, False)
    write_rows(sums, partial, [0])


def rest_kernel(proj, scale, wide, narrow, keep, flips, *refs):
    rows_in, columns, refs = refs[:1], refs[1:5], refs[5:]
    if keep:
        partial, *kept, sums, left = refs
    else:
        left, partial, sums = refs
        kept = (None, None)
    halves = left.shape[1] // LANES
    prepare_rows(rows_in, flips[0], left, proj, scale, wide, narrow)
    for side in range(2):
        right, vector = columns[2 * side:2 * side + 2]
        make_rows(left, right, kept[side], vector_reader(vector, halves), sums, side > 0)
    write_rows(sums, partial, [0])


def message_kernel(parts, wide, narrow, halves, *refs):
    partials, vector, out, held = refs[:parts + 1], refs[parts + 1], refs[-2], refs[-1]
    lines_of = [partials[0][...] + partials[1][...]] + [partial[...] for partial in partials[2:]]
    for part, lines in enumerate(lines_of):
        base = part_base(part, parts, wide, narrow) * halves
        for line in range(lines.shape[0]):
            held[pl.ds(base + line, 1), :] = lines[line:line + 1, :]
    _, low, y, _, _ = place(wide, narrow)
    mine = (low * 2 + y) * halves
    pieces = [held[line:line + 1, :] for line in range(held.shape[0])]
    pieces += [vector[pl.ds(mine + half, 1), :] for half in range(halves)]
    block = jnp.concatenate(pieces, axis=1)

    def copy(i, _):
        out[i] = block
        return 0

    lax.fori_loop(0, out.shape[0], copy, 0, unroll=8)


def second_kernel(wide, narrow, keep, parts, *refs):
    arrived, out, step_scalars, direction, images, targets, partial, sums = refs[:1] + refs[-7:]
    lines = partial.shape[0]
    halves = lines // narrow
    across = narrow // 2
    group = [(high, x) for x in range(narrow // 2) for high in range(2)]

    def unpack(low, _):
        for y, core in ((0, 0), (0, 1), (1, 0), (1, 1)):
            members = [device_at(high, low, y, x, core, wide, narrow) for high, x in group]
            slots = [slot(member, wide, narrow) for member in members]
            total = arrived[slots[0], :, 0:lines * LANES]
            for spot in slots[1:]:
                total = total + arrived[spot, :, 0:lines * LANES]
            for r, member in enumerate(members):
                for half in range(halves):
                    start = arrived[slots[r], :, (lines + half) * LANES:(lines + half + 1) * LANES]
                    line = r * halves + half
                    spot = pl.ds(member * halves + half, 1)
                    targets[spot, :] = start
                    images[spot, :] = total[:, line * LANES:(line + 1) * LANES] + noise_var * start
        return 0

    lax.fori_loop(0, wide // 4, unpack, 0, unroll=2)
    start, first = targets[...], images[...]
    norm = total_sum(start * start)
    alpha = norm / total_sum(start * first)
    residual = start - alpha * first
    norm_next = total_sum(residual * residual)
    beta = norm_next / norm
    whole = residual + beta * start
    direction[...] = whole
    high, low, y, x, core = place(wide, narrow)

    def side_reader(side):
        def read_vector(c, half):
            source = device_at(high, c // 2, c % 2, x, jnp.bitwise_xor(core, side), wide, narrow)
            return direction[pl.ds(source * halves + half, 1), :]
        return read_vector

    groups = narrow // parts
    for part in range(parts):
        part_sums = sums.at[part * groups:(part + 1) * groups]
        for side in range(2):
            if keep:
                use_rows(refs[1 + 2 * part + side], side_reader(side), part_sums, side > 0)
            else:
                make_rows(refs[3 + part], refs[1 + side], None, side_reader(side), part_sums, side > 0)
    write_rows(sums, partial, [part_base(part, parts, wide, narrow) for part in range(parts)])
    share = jnp.zeros((1, LANES), f32)
    for r, (row_high, row_x) in enumerate(group):
        for half in range(halves):
            spot = pl.ds(device_at(row_high, low, y, row_x, core, wide, narrow) * halves + half, 1)
            line = r * halves + half
            share = share + direction[spot, :] * partial[line:line + 1, :]
    blocks = [
        jnp.concatenate([partial[r * halves + half:r * halves + half + 1, :]
                         for half in range(halves)] + [share], axis=1)
        for r in range(narrow)]

    def copy(to_low, _):
        for r, (to_high, to_x) in enumerate(group):
            for to_y, to_core in ((0, 0), (0, 1), (1, 0), (1, 1)):
                to = device_at(to_high, to_low, to_y, to_x, to_core, wide, narrow)
                out[slot(to, wide, narrow)] = blocks[r]
        return 0

    lax.fori_loop(0, wide // 4, copy, 0, unroll=2)
    lane = lax.broadcasted_iota(jnp.int32, (1, LANES), 1)
    noise = noise_var * total_sum(whole * whole)
    step_scalars[0:1, :] = jnp.where(lane == 0, alpha, jnp.where(
        lane == 1, norm_next, jnp.where(lane == 2, beta, noise)))
    for half in range(halves):
        spot = pl.ds(device_at(high, low, y, x, core, wide, narrow) * halves + half, 1)
        step_scalars[1 + half:2 + half, :] = images[spot, :]
        step_scalars[1 + halves + half:2 + halves + half, :] = targets[spot, :]


def last_kernel(wide, narrow, arrived, step_scalars, solution_out, residual_out, answer, sems):
    alpha = step_scalars[0:1, 0:1]
    norm = step_scalars[0:1, 1:2]
    beta = step_scalars[0:1, 2:3]
    noise = step_scalars[0:1, 3:4]
    halves = answer.shape[1]

    def add(i, total):
        return total + arrived[i, :, halves * LANES:(halves + 1) * LANES]

    share = lax.fori_loop(0, arrived.shape[0], add, jnp.zeros((1, LANES), f32), unroll=32)
    alpha_next = norm / (total_sum(share) + noise)
    _, low, y, _, core = place(wide, narrow)
    product = jnp.zeros((1, (halves + 1) * LANES), f32)
    for high in range(2):
        for x in range(narrow // 2):
            member = device_at(high, low, y, x, core, wide, narrow)
            product = product + arrived[slot(member, wide, narrow)]
    for half in range(halves):
        begin = step_scalars[1 + halves + half:2 + halves + half, :]
        residual = begin - alpha * step_scalars[1 + half:2 + half, :]
        direction = residual + beta * begin
        image = product[:, half * LANES:(half + 1) * LANES] + noise_var * direction
        answer[0, half:half + 1, :] = alpha * begin + alpha_next * direction
        answer[1, half:half + 1, :] = residual - alpha_next * image
    copies = [pltpu.make_async_copy(answer.at[i], out, sems.at[i])
              for i, out in enumerate((solution_out, residual_out))]
    for copy in copies:
        copy.start()
    for copy in copies:
        copy.wait()


def call(kernel, out_shape, *args, scratch=(), **options):
    return pl.pallas_call(
        kernel,
        out_shape=out_shape,
        scratch_shapes=list(scratch),
        compiler_params=pltpu.CompilerParams(vmem_limit_bytes=VMEM_BYTES),
        **options,
    )(*args)


def to_all(blocks):
    group = list(range(blocks.shape[0] - 1, -1, -1))
    return lax.all_to_all(blocks, ALL, split_axis=0, concat_axis=0, axis_index_groups=[group], tiled=True)


def join_kernel(*refs):
    i = 0
    for block in refs[:-1]:
        for j in range(block.shape[0]):
            refs[-1][i] = block[j]
            i += 1


def join(*blocks, flops=0):
    total = sum(b.shape[0] for b in blocks)
    return call(join_kernel, jax.ShapeDtypeStruct((total, *blocks[0].shape[1:]), f32), *blocks,
                cost_estimate=pl.CostEstimate(flops=flops, bytes_accessed=0, transcendentals=0))


def first_round(latent, own, wide, narrow):
    lows, across = wide // 4, narrow // 2
    if lows & (lows - 1) or across != 2 or lows > DIRECT:
        every = lax.all_gather(own, ALL, axis=0, tiled=True)
        every = every.reshape(2, lows, 2, across, 2, *own.shape[1:])
        high, low, y, x, core = place(wide, narrow)
        rows = every
        for place_in, axis in ((low, 1), (y, 1), (core, 2)):
            rows = lax.dynamic_index_in_dim(rows, place_in, axis, keepdims=False)
        columns = lax.dynamic_index_in_dim(every, high, 0, keepdims=False)
        columns = lax.dynamic_index_in_dim(columns, x, 2, keepdims=False)
        rows = jnp.swapaxes(rows, 0, 1).reshape(narrow, *own.shape[1:])
        sides = [lax.dynamic_index_in_dim(columns, jnp.bitwise_xor(core, side), 2, keepdims=False)
                 for side in range(2)]
        sides = [[columns.reshape(wide // 2, *own.shape[1:])] for columns in sides]
        return [[rows]], sides, (None, None)

    sizes = axis_sizes(wide, narrow)

    def swap(value, **flips):
        pairs = []
        for i in range(wide * narrow):
            spot = list(np.unravel_index(i, sizes))
            for name, flip in flips.items():
                axis = dict(high=HIGH, low=LOW, y=Y, x=X, core=CORE)[name]
                spot[axis] = int(spot[axis]) ^ flip
            pairs.append((i, int(np.ravel_multi_index(spot, sizes))))
        return lax.ppermute(value, ALL, pairs)

    rows = join(latent, swap(latent, high=1), flops=EARLY)
    columns = [own] + [swap(own, low=flip // 2, y=flip % 2) for flip in range(1, 2 * lows)]
    sides = [columns, [swap(block, core=1) for block in columns]]
    parts = [[rows], [swap(rows, x=1)]]
    return parts, sides, ([0, 1], list(range(2 * lows)))


def on_device(wide, narrow, features, projection, targets):
    rows, proj = features.shape[0], projection.shape[1]
    halves = rows // LANES
    lines = narrow * halves
    devices = wide * narrow
    scale = -2.0 / proj * math.log2(math.e)
    depth = 6 * proj + 16
    keep = 4 * devices * rows * rows <= KEEP_BYTES

    def shape(*dims, dtype=f32):
        return jax.ShapeDtypeStruct(dims, dtype)

    def scratch(*dims, dtype=f32):
        return pltpu.VMEM(dims, dtype)

    feat = features.shape[1]
    inputs = [pltpu.with_memory_space_constraint(value, pltpu.HBM)
              for value in (features, projection.T, targets.reshape(1, rows))]
    latent, own = call(
        project_kernel, (shape(1, halves * proj, LANES), shape(1, halves * proj + 8, LANES)), *inputs,
        in_specs=[pl.BlockSpec(memory_space=pltpu.HBM)] * 3,
        scratch=[scratch(halves, LANES, feat, dtype=bf16), scratch(proj, feat, dtype=bf16),
                 scratch(1, rows), pltpu.SemaphoreType.DMA((halves + 2,))])
    row_parts, sides, flips = first_round(latent, own, wide, narrow)
    parts = len(row_parts)
    groups = narrow // parts
    left = shape(groups, rows, depth, dtype=bf16)
    right = shape(wide // 2, depth, rows, dtype=bf16)
    vector = shape(wide // 2 * halves, LANES)
    kept = (shape(groups, wide // 2, rows, rows),) if keep else ()
    group_lines = shape(groups * halves, LANES)
    sums = scratch(groups, rows, LANES)
    settings = (proj, scale, wide, narrow, keep, flips)

    def cost(columns):
        tiles = groups * columns * rows * rows
        return pl.CostEstimate(flops=2 * tiles * depth, bytes_accessed=4 * tiles, transcendentals=tiles)

    lefts, columns, blocks, partials = [], [], [], []
    for side, column_blocks in enumerate(sides):
        row_blocks = row_parts[0] if side == 0 else lefts
        made = call(
            functools.partial(side_kernel, *settings, len(row_blocks), len(column_blocks)),
            ((left,) if side == 0 else ()) + (right, vector, group_lines) + kept,
            *row_blocks, *column_blocks, scratch=[sums], cost_estimate=cost(wide // 2))
        if side == 0:
            lefts, made = [made[0]], made[1:]
        columns += made[:2]
        partials.append(made[2])
        blocks += made[3:]
    for row_blocks in row_parts[1:]:
        made = call(
            functools.partial(rest_kernel, *settings),
            (group_lines, *kept * 2) if keep else (left, group_lines), *row_blocks, *columns,
            scratch=[sums, scratch(*left.shape, dtype=bf16)] if keep else [sums],
            cost_estimate=cost(wide))
        if not keep:
            lefts.append(made[0])
        partials.append(made[0 if keep else 1])
        blocks += made[1:] if keep else []
    out = call(
        functools.partial(message_kernel, parts, wide, narrow, halves),
        shape(devices, 1, (lines + halves) * LANES), *partials, columns[1],
        scratch=[scratch(lines, LANES)])
    block = blocks if keep else [columns[0], columns[2], *lefts]
    sums = scratch(narrow, rows, LANES)
    out, step_scalars = call(
        functools.partial(second_kernel, wide, narrow, keep, parts),
        (shape(devices, 1, (halves + 1) * LANES), shape(1 + 2 * halves, LANES)),
        to_all(out), *block,
        scratch=[scratch(devices * halves, LANES)] * 3 + [scratch(lines, LANES), sums])
    answer, residual = call(
        functools.partial(last_kernel, wide, narrow), (shape(halves, LANES), shape(halves, LANES)),
        to_all(out), step_scalars,
        out_specs=(pl.BlockSpec(memory_space=pl.ANY),) * 2,
        scratch=[scratch(2, halves, LANES), pltpu.SemaphoreType.DMA((2,))])
    return answer.reshape(rows), residual.reshape(rows)


def solution(mesh):
    wide, narrow = mesh.shape["wide"], mesh.shape["narrow"]
    line = jax.sharding.Mesh(mesh.devices.reshape(wide * narrow), (ALL,))
    in_specs = (P(ALL, None), P(), P(ALL))
    return jax.shard_map(
        functools.partial(on_device, wide, narrow), mesh=line,
        in_specs=in_specs, out_specs=(P(ALL), P(ALL)), check_vma=False,
    )
```

```python
import functools
import math

import jax
import jax.numpy as jnp
import numpy as np
from jax import lax
from jax.experimental import pallas as pl
from jax.experimental.pallas import tpu as pltpu
from jax.sharding import PartitionSpec as P

noise_var = 0.5
LANES = 128
TOGETHER = 2
EARLY = 10**9
DIRECT = 8
KEEP_BYTES = 8 * 2**20
VMEM_BYTES = 32 * 2**20
ALL = "all"
HIGH, LOW, Y, X, CORE = range(5)
highest = lax.Precision.HIGHEST
f32 = jnp.float32
bf16 = jnp.bfloat16


def split3(values):
    high = values.astype(bf16)
    rest = values - high.astype(f32)
    mid = rest.astype(bf16)
    low = (rest - mid.astype(f32)).astype(bf16)
    return high, mid, low


def exponent_rows(first, second):
    width = (first if not isinstance(first, float) else second).shape[1]
    row = lax.broadcasted_iota(jnp.int32, (16, width), 0)
    out = jnp.zeros((16, width), f32)
    for base, value in ((0, first), (3, second)):
        parts = (1.0, 1.0, 1.0) if isinstance(value, float) else [p.astype(f32) for p in split3(value)]
        for k, part in enumerate(parts):
            out = jnp.where(row == base + k, part, out)
    return out.astype(bf16)


def right_operand(latent, scale):
    square = jnp.sum(latent * latent, axis=0, keepdims=True) * scale
    h, m, l = split3(latent)
    return jnp.concatenate([h, m, l, h, m, h, exponent_rows(square, 1.0)], axis=0)


def left_operand(latent, scale):
    square = jnp.sum(latent * latent, axis=0, keepdims=True) * scale
    h, m, l = split3(latent * (-2.0 * scale))
    stacked = jnp.concatenate([h, h, h, m, m, l, exponent_rows(1.0, square)], axis=0)
    return stacked.T


def axis_sizes(wide, narrow):
    return 2, wide // 4, 2, narrow // 2, 2


def place(wide, narrow):
    rest, out = lax.axis_index(ALL), []
    for size in reversed(axis_sizes(wide, narrow)):
        out.append(rest % size)
        rest = rest // size
    return tuple(reversed(out))


def device_at(high, low, y, x, core, wide, narrow):
    return (((high * (wide // 4) + low) * 2 + y) * (narrow // 2) + x) * 2 + core


def slot(device, wide, narrow):
    return wide * narrow - 1 - device


def part_base(part, parts, wide, narrow):
    return 0 if parts == 1 else jnp.bitwise_xor(place(wide, narrow)[X], part) * 2


def row_sources(blocks, flips, wide, narrow):
    spots = [(b, i) for b in blocks for i in range(b.shape[0])]
    if flips is None:
        return [(b, i, i) for b, i in spots]
    high = place(wide, narrow)[HIGH]
    return [(b, i, jnp.bitwise_xor(high, flip)) for (b, i), flip in zip(spots, flips)]


def column_sources(blocks, flips, wide, narrow):
    spots = [(b, i) for b in blocks for i in range(b.shape[0])]
    if flips is None:
        return [(b, i, i) for b, i in spots]
    _, low, y, _, _ = place(wide, narrow)
    return [(b, i, jnp.bitwise_xor(low * 2 + y, flip)) for (b, i), flip in zip(spots, flips)]


def total_sum(values):
    return jnp.sum(jnp.sum(values, axis=0, keepdims=True), axis=1, keepdims=True)


def lane_sums(values):
    parts = jnp.concatenate(split3(values), axis=1)
    ones = jnp.ones((16, parts.shape[1]), bf16)
    return lax.dot_general(ones, parts, (((1,), (1,)), ((), ())),
                           preferred_element_type=f32)[0:1, :]


def make_rows(left, sides, sums):
    groups, rows, _ = left.shape
    halves = rows // LANES

    def one_group(g, _):
        left_group = left[g]
        acc = jnp.zeros((rows, LANES), f32)
        for right, kept, read_vector in sides:

            def some_columns(step, acc):
                first = step * TOGETHER
                both = jnp.concatenate([right[first + k] for k in range(TOGETHER)], axis=1)
                exponent = jnp.dot(left_group, both, preferred_element_type=f32)
                tile = jnp.exp2(exponent)
                for k in range(TOGETHER):
                    if kept is not None:
                        kept[g, first + k] = tile[:, k * rows:(k + 1) * rows]
                    for half in range(halves):
                        start = k * rows + half * LANES
                        acc = acc + tile[:, start:start + LANES] * read_vector(first + k, half)
                return acc

            acc = lax.fori_loop(0, right.shape[0] // TOGETHER, some_columns, acc, unroll=4 // TOGETHER)
        sums[g] = acc
        return 0

    lax.fori_loop(0, groups, one_group, 0, unroll=groups <= 2)


def use_rows(sides, sums):
    groups, rows, _ = sums.shape
    halves = rows // LANES

    def one_group(g, _):
        acc = jnp.zeros((rows, LANES), f32)
        for kept, read_vector in sides:

            def one_column(c, acc):
                for half in range(halves):
                    acc = acc + kept[g, c, :, half * LANES:(half + 1) * LANES] * read_vector(c, half)
                return acc

            acc = lax.fori_loop(0, kept.shape[1], one_column, acc, unroll=4)
        sums[g] = acc
        return 0

    lax.fori_loop(0, groups, one_group, 0, unroll=groups <= 2)


def write_rows(sums, out, bases):
    groups, rows, _ = sums.shape
    halves = rows // LANES
    total = lane_sums(sums[...].reshape(groups * rows, LANES))
    for g in range(groups):
        base = bases[g * len(bases) // groups]
        for half in range(halves):
            line = (base + g % (groups // len(bases))) * halves + half
            start = (g * halves + half) * LANES
            out[pl.ds(line, 1), :] = total[:, start:start + LANES]


def project_kernel(features, projection_t, targets, latent, out, feature_buf, projection_buf, target_buf, sems):
    proj = projection_t.shape[0]
    chunks, height, _ = feature_buf.shape
    copies = [
        pltpu.make_async_copy(features.at[pl.ds(i * height, height)], feature_buf.at[i], sems.at[i])
        for i in range(chunks)]
    copies.insert(0, pltpu.make_async_copy(projection_t, projection_buf, sems.at[chunks]))
    copies.append(pltpu.make_async_copy(targets, target_buf, sems.at[chunks + 1]))
    for copy in copies:
        copy.start()
    copies.pop(0).wait()
    for i in range(chunks):
        copies[i].wait()
        some = lax.dot_general(
            projection_buf[...], feature_buf[i], (((1,), (1,)), ((), ())), preferred_element_type=f32)
        latent[0, i * proj:(i + 1) * proj, :] = some
        out[0, i * proj:(i + 1) * proj, :] = some
    copies[-1].wait()
    line = lax.broadcasted_iota(jnp.int32, (8, LANES), 0)
    tail = jnp.zeros((8, LANES), f32)
    for i in range(chunks):
        tail = jnp.where(line == i, target_buf[:, i * LANES:(i + 1) * LANES], tail)
    out[0, chunks * proj:, :] = tail


def block_latent(block, i, proj, halves):
    return jnp.concatenate([block[i, half * proj:(half + 1) * proj, :] for half in range(halves)], axis=1)


def prepare_rows(blocks, flips, left, proj, scale, wide, narrow):
    for block, i, source in row_sources(blocks, flips, wide, narrow):
        left[source] = left_operand(block_latent(block, i, proj, left.shape[1] // LANES), scale)


def vector_reader(vector, halves):
    return lambda c, half: vector[pl.ds(c * halves + half, 1), :]


def side_kernel(proj, scale, wide, narrow, keep, flips, row_count, column_count, *refs):
    rows_in, columns_in = refs[:row_count], refs[row_count:row_count + column_count]
    refs = refs[row_count + column_count:]
    fresh = rows_in[0].dtype == f32
    left, refs = (refs[0], refs[1:]) if fresh else (rows_in[0], refs)
    right, vector, partial, sums = refs[0], refs[1], refs[2], refs[-1]
    kept = refs[3] if keep else None
    halves = left.shape[1] // LANES
    if fresh:
        prepare_rows(rows_in, flips[0], left, proj, scale, wide, narrow)
    for block, i, source in column_sources(columns_in, flips[1], wide, narrow):
        right[source] = right_operand(block_latent(block, i, proj, halves), scale)
        for half in range(halves):
            line = halves * proj + half
            vector[pl.ds(source * halves + half, 1), :] = block[i, line:line + 1, :]
    make_rows(left, [(right, kept, vector_reader(vector, halves))], sums)
    write_rows(sums, partial, [0])


def rest_kernel(proj, scale, wide, narrow, keep, flips, *refs):
    rows_in, columns, earlier, refs = refs[:1], refs[1:5], refs[5:7], refs[7:]
    if keep:
        out, *kept, sums, partial, held, left = refs
    else:
        left, out, sums, partial, held = refs
        kept = (None, None)
    halves = left.shape[1] // LANES
    prepare_rows(rows_in, flips[0], left, proj, scale, wide, narrow)
    make_rows(left, [
        (columns[2 * side], kept[side], vector_reader(columns[2 * side + 1], halves))
        for side in range(2)], sums)
    write_rows(sums, partial, [0])
    message_kernel(2, wide, narrow, halves, *earlier, partial, columns[1], out, held)


def message_kernel(parts, wide, narrow, halves, *refs):
    partials, vector, out, held = refs[:parts + 1], refs[parts + 1], refs[-2], refs[-1]
    lines_of = [partials[0][...] + partials[1][...]] + [partial[...] for partial in partials[2:]]
    for part, lines in enumerate(lines_of):
        base = part_base(part, parts, wide, narrow) * halves
        for line in range(lines.shape[0]):
            held[pl.ds(base + line, 1), :] = lines[line:line + 1, :]
    _, low, y, _, _ = place(wide, narrow)
    mine = (low * 2 + y) * halves
    pieces = [held[line:line + 1, :] for line in range(held.shape[0])]
    pieces += [vector[pl.ds(mine + half, 1), :] for half in range(halves)]
    block = jnp.concatenate(pieces, axis=1)

    def copy(i, _):
        out[i] = block
        return 0

    lax.fori_loop(0, out.shape[0], copy, 0, unroll=8)


def second_kernel(wide, narrow, keep, parts, *refs):
    arrived, out, step_scalars, direction, images, targets, partial, sums = refs[:1] + refs[-7:]
    lines = partial.shape[0]
    halves = lines // narrow
    across = narrow // 2
    group = [(high, x) for x in range(narrow // 2) for high in range(2)]

    def unpack(low, _):
        for y, core in ((0, 0), (0, 1), (1, 0), (1, 1)):
            members = [device_at(high, low, y, x, core, wide, narrow) for high, x in group]
            slots = [slot(member, wide, narrow) for member in members]
            total = arrived[slots[0], :, 0:lines * LANES]
            for spot in slots[1:]:
                total = total + arrived[spot, :, 0:lines * LANES]
            for r, member in enumerate(members):
                for half in range(halves):
                    start = arrived[slots[r], :, (lines + half) * LANES:(lines + half + 1) * LANES]
                    line = r * halves + half
                    spot = pl.ds(member * halves + half, 1)
                    targets[spot, :] = start
                    images[spot, :] = total[:, line * LANES:(line + 1) * LANES] + noise_var * start
        return 0

    lax.fori_loop(0, wide // 4, unpack, 0, unroll=2)
    start, first = targets[...], images[...]
    norm = total_sum(start * start)
    alpha = norm / total_sum(start * first)
    residual = start - alpha * first
    norm_next = total_sum(residual * residual)
    beta = norm_next / norm
    whole = residual + beta * start
    direction[...] = whole
    high, low, y, x, core = place(wide, narrow)

    def side_reader(side):
        def read_vector(c, half):
            source = device_at(high, c // 2, c % 2, x, jnp.bitwise_xor(core, side), wide, narrow)
            return direction[pl.ds(source * halves + half, 1), :]
        return read_vector

    groups = narrow // parts
    for part in range(parts):
        part_sums = sums.at[part * groups:(part + 1) * groups]
        if keep:
            use_rows([(refs[1 + 2 * part + side], side_reader(side)) for side in range(2)], part_sums)
        else:
            make_rows(refs[3 + part], [(refs[1 + side], None, side_reader(side)) for side in range(2)], part_sums)
    write_rows(sums, partial, [part_base(part, parts, wide, narrow) for part in range(parts)])
    share = jnp.zeros((1, LANES), f32)
    for r, (row_high, row_x) in enumerate(group):
        for half in range(halves):
            spot = pl.ds(device_at(row_high, low, y, row_x, core, wide, narrow) * halves + half, 1)
            line = r * halves + half
            share = share + direction[spot, :] * partial[line:line + 1, :]
    blocks = [
        jnp.concatenate([partial[r * halves + half:r * halves + half + 1, :]
                         for half in range(halves)] + [share], axis=1)
        for r in range(narrow)]

    def copy(to_low, _):
        for r, (to_high, to_x) in enumerate(group):
            for to_y, to_core in ((0, 0), (0, 1), (1, 0), (1, 1)):
                to = device_at(to_high, to_low, to_y, to_x, to_core, wide, narrow)
                out[slot(to, wide, narrow)] = blocks[r]
        return 0

    lax.fori_loop(0, wide // 4, copy, 0, unroll=2)
    lane = lax.broadcasted_iota(jnp.int32, (1, LANES), 1)
    noise = noise_var * total_sum(whole * whole)
    step_scalars[0:1, :] = jnp.where(lane == 0, alpha, jnp.where(
        lane == 1, norm_next, jnp.where(lane == 2, beta, noise)))
    for half in range(halves):
        spot = pl.ds(device_at(high, low, y, x, core, wide, narrow) * halves + half, 1)
        step_scalars[1 + half:2 + half, :] = images[spot, :]
        step_scalars[1 + halves + half:2 + halves + half, :] = targets[spot, :]


def last_kernel(wide, narrow, arrived, step_scalars, solution_out, residual_out, answer, sems):
    alpha = step_scalars[0:1, 0:1]
    norm = step_scalars[0:1, 1:2]
    beta = step_scalars[0:1, 2:3]
    noise = step_scalars[0:1, 3:4]
    halves = answer.shape[1]

    def add(i, total):
        return total + arrived[i, :, halves * LANES:(halves + 1) * LANES]

    share = lax.fori_loop(0, arrived.shape[0], add, jnp.zeros((1, LANES), f32), unroll=32)
    alpha_next = norm / (total_sum(share) + noise)
    _, low, y, _, core = place(wide, narrow)
    product = jnp.zeros((1, (halves + 1) * LANES), f32)
    for high in range(2):
        for x in range(narrow // 2):
            member = device_at(high, low, y, x, core, wide, narrow)
            product = product + arrived[slot(member, wide, narrow)]
    for half in range(halves):
        begin = step_scalars[1 + halves + half:2 + halves + half, :]
        residual = begin - alpha * step_scalars[1 + half:2 + half, :]
        direction = residual + beta * begin
        image = product[:, half * LANES:(half + 1) * LANES] + noise_var * direction
        answer[0, half:half + 1, :] = alpha * begin + alpha_next * direction
        answer[1, half:half + 1, :] = residual - alpha_next * image
    copies = [pltpu.make_async_copy(answer.at[i], out, sems.at[i])
              for i, out in enumerate((solution_out, residual_out))]
    for copy in copies:
        copy.start()
    for copy in copies:
        copy.wait()


def call(kernel, out_shape, *args, scratch=(), **options):
    return pl.pallas_call(
        kernel,
        out_shape=out_shape,
        scratch_shapes=list(scratch),
        compiler_params=pltpu.CompilerParams(vmem_limit_bytes=VMEM_BYTES),
        **options,
    )(*args)


def to_all(blocks):
    group = list(range(blocks.shape[0] - 1, -1, -1))
    return lax.all_to_all(blocks, ALL, split_axis=0, concat_axis=0, axis_index_groups=[group], tiled=True)


def join_kernel(*refs):
    i = 0
    for block in refs[:-1]:
        for j in range(block.shape[0]):
            refs[-1][i] = block[j]
            i += 1


def join(*blocks, flops=0):
    total = sum(b.shape[0] for b in blocks)
    return call(join_kernel, jax.ShapeDtypeStruct((total, *blocks[0].shape[1:]), f32), *blocks,
                cost_estimate=pl.CostEstimate(flops=flops, bytes_accessed=0, transcendentals=0))


def first_round(latent, own, wide, narrow):
    lows, across = wide // 4, narrow // 2
    if lows & (lows - 1) or across != 2 or lows > DIRECT:
        every = lax.all_gather(own, ALL, axis=0, tiled=True)
        every = every.reshape(2, lows, 2, across, 2, *own.shape[1:])
        high, low, y, x, core = place(wide, narrow)
        rows = every
        for place_in, axis in ((low, 1), (y, 1), (core, 2)):
            rows = lax.dynamic_index_in_dim(rows, place_in, axis, keepdims=False)
        columns = lax.dynamic_index_in_dim(every, high, 0, keepdims=False)
        columns = lax.dynamic_index_in_dim(columns, x, 2, keepdims=False)
        rows = jnp.swapaxes(rows, 0, 1).reshape(narrow, *own.shape[1:])
        sides = [lax.dynamic_index_in_dim(columns, jnp.bitwise_xor(core, side), 2, keepdims=False)
                 for side in range(2)]
        sides = [[columns.reshape(wide // 2, *own.shape[1:])] for columns in sides]
        return [[rows]], sides, (None, None)

    sizes = axis_sizes(wide, narrow)

    def swap(value, **flips):
        pairs = []
        for i in range(wide * narrow):
            spot = list(np.unravel_index(i, sizes))
            for name, flip in flips.items():
                axis = dict(high=HIGH, low=LOW, y=Y, x=X, core=CORE)[name]
                spot[axis] = int(spot[axis]) ^ flip
            pairs.append((i, int(np.ravel_multi_index(spot, sizes))))
        return lax.ppermute(value, ALL, pairs)

    rows = join(latent, swap(latent, high=1), flops=EARLY)
    columns = [own] + [swap(own, low=flip // 2, y=flip % 2) for flip in range(1, 2 * lows)]
    sides = [columns, [swap(block, core=1) for block in columns]]
    parts = [[rows], [swap(rows, x=1)]]
    return parts, sides, ([0, 1], list(range(2 * lows)))


def on_device(wide, narrow, features, projection, targets):
    rows, proj = features.shape[0], projection.shape[1]
    halves = rows // LANES
    lines = narrow * halves
    devices = wide * narrow
    scale = -2.0 / proj * math.log2(math.e)
    depth = 6 * proj + 16
    keep = 4 * devices * rows * rows <= KEEP_BYTES

    def shape(*dims, dtype=f32):
        return jax.ShapeDtypeStruct(dims, dtype)

    def scratch(*dims, dtype=f32):
        return pltpu.VMEM(dims, dtype)

    feat = features.shape[1]
    inputs = [pltpu.with_memory_space_constraint(value, pltpu.HBM)
              for value in (features, projection.T, targets.reshape(1, rows))]
    latent, own = call(
        project_kernel, (shape(1, halves * proj, LANES), shape(1, halves * proj + 8, LANES)), *inputs,
        in_specs=[pl.BlockSpec(memory_space=pltpu.HBM)] * 3,
        scratch=[scratch(halves, LANES, feat, dtype=bf16), scratch(proj, feat, dtype=bf16),
                 scratch(1, rows), pltpu.SemaphoreType.DMA((halves + 2,))])
    row_parts, sides, flips = first_round(latent, own, wide, narrow)
    parts = len(row_parts)
    groups = narrow // parts
    left = shape(groups, rows, depth, dtype=bf16)
    right = shape(wide // 2, depth, rows, dtype=bf16)
    vector = shape(wide // 2 * halves, LANES)
    kept = (shape(groups, wide // 2, rows, rows),) if keep else ()
    group_lines = shape(groups * halves, LANES)
    sums = scratch(groups, rows, LANES)
    settings = (proj, scale, wide, narrow, keep, flips)

    def cost(columns):
        tiles = groups * columns * rows * rows
        return pl.CostEstimate(flops=2 * tiles * depth, bytes_accessed=4 * tiles, transcendentals=tiles)

    lefts, columns, blocks, partials = [], [], [], []
    for side, column_blocks in enumerate(sides):
        row_blocks = row_parts[0] if side == 0 else lefts
        made = call(
            functools.partial(side_kernel, *settings, len(row_blocks), len(column_blocks)),
            ((left,) if side == 0 else ()) + (right, vector, group_lines) + kept,
            *row_blocks, *column_blocks, scratch=[sums], cost_estimate=cost(wide // 2))
        if side == 0:
            lefts, made = [made[0]], made[1:]
        columns += made[:2]
        partials.append(made[2])
        blocks += made[3:]
    message = shape(devices, 1, (lines + halves) * LANES)
    if parts == 2:
        made = call(
            functools.partial(rest_kernel, *settings),
            (message, *kept * 2) if keep else (left, message), *row_parts[1], *columns, *partials,
            scratch=[sums, scratch(groups * halves, LANES), scratch(lines, LANES)]
            + ([scratch(*left.shape, dtype=bf16)] if keep else []),
            cost_estimate=cost(wide))
        out = made[0 if keep else 1]
        blocks += made[1:] if keep else []
        lefts += [] if keep else made[:1]
    else:
        out = call(
            functools.partial(message_kernel, parts, wide, narrow, halves), message,
            *partials, columns[1], scratch=[scratch(lines, LANES)])
    block = blocks if keep else [columns[0], columns[2], *lefts]
    sums = scratch(narrow, rows, LANES)
    out, step_scalars = call(
        functools.partial(second_kernel, wide, narrow, keep, parts),
        (shape(devices, 1, (halves + 1) * LANES), shape(1 + 2 * halves, LANES)),
        to_all(out), *block,
        scratch=[scratch(devices * halves, LANES)] * 3 + [scratch(lines, LANES), sums])
    answer, residual = call(
        functools.partial(last_kernel, wide, narrow), (shape(halves, LANES), shape(halves, LANES)),
        to_all(out), step_scalars,
        out_specs=(pl.BlockSpec(memory_space=pl.ANY),) * 2,
        scratch=[scratch(2, halves, LANES), pltpu.SemaphoreType.DMA((2,))])
    return answer.reshape(rows), residual.reshape(rows)


def solution(mesh):
    wide, narrow = mesh.shape["wide"], mesh.shape["narrow"]
    line = jax.sharding.Mesh(mesh.devices.reshape(wide * narrow), (ALL,))
    in_specs = (P(ALL, None), P(), P(ALL))
    return jax.shard_map(
        functools.partial(on_device, wide, narrow), mesh=line,
        in_specs=in_specs, out_specs=(P(ALL), P(ALL)), check_vma=False,
    )
```

```python
import functools
import math

import jax
import jax.numpy as jnp
import numpy as np
from jax import lax
from jax.experimental import pallas as pl
from jax.experimental.pallas import tpu as pltpu
from jax.sharding import PartitionSpec as P

noise_var = 0.5
LANES = 128
TOGETHER = 2
EARLY = 10**9
DIRECT = 8
KEEP_BYTES = 8 * 2**20
VMEM_BYTES = 32 * 2**20
ALL = "all"
HIGH, LOW, Y, X, CORE = range(5)
highest = lax.Precision.HIGHEST
f32 = jnp.float32
bf16 = jnp.bfloat16


def split3(values):
    high = values.astype(bf16)
    rest = values - high.astype(f32)
    mid = rest.astype(bf16)
    low = (rest - mid.astype(f32)).astype(bf16)
    return high, mid, low


def exponent_rows(first, second):
    width = (first if not isinstance(first, float) else second).shape[1]
    row = lax.broadcasted_iota(jnp.int32, (16, width), 0)
    out = jnp.zeros((16, width), f32)
    for base, value in ((0, first), (3, second)):
        parts = (1.0, 1.0, 1.0) if isinstance(value, float) else [p.astype(f32) for p in split3(value)]
        for k, part in enumerate(parts):
            out = jnp.where(row == base + k, part, out)
    return out.astype(bf16)


def right_operand(latent, scale):
    square = jnp.sum(latent * latent, axis=0, keepdims=True) * scale
    h, m, l = split3(latent)
    return jnp.concatenate([h, m, l, h, m, h, exponent_rows(square, 1.0)], axis=0)


def left_operand(latent, scale):
    square = jnp.sum(latent * latent, axis=0, keepdims=True) * scale
    h, m, l = split3(latent * (-2.0 * scale))
    stacked = jnp.concatenate([h, h, h, m, m, l, exponent_rows(1.0, square)], axis=0)
    return stacked.T


def axis_sizes(wide, narrow):
    return 2, wide // 4, 2, narrow // 2, 2


def place(wide, narrow):
    rest, out = lax.axis_index(ALL), []
    for size in reversed(axis_sizes(wide, narrow)):
        out.append(rest % size)
        rest = rest // size
    return tuple(reversed(out))


def device_at(high, low, y, x, core, wide, narrow):
    return (((high * (wide // 4) + low) * 2 + y) * (narrow // 2) + x) * 2 + core


def slot(device, wide, narrow):
    return wide * narrow - 1 - device


def part_base(part, parts, wide, narrow):
    return 0 if parts == 1 else jnp.bitwise_xor(place(wide, narrow)[X], part) * 2


def row_sources(blocks, flips, wide, narrow):
    spots = [(b, i) for b in blocks for i in range(b.shape[0])]
    if flips is None:
        return [(b, i, i) for b, i in spots]
    high = place(wide, narrow)[HIGH]
    return [(b, i, jnp.bitwise_xor(high, flip)) for (b, i), flip in zip(spots, flips)]


def column_sources(blocks, flips, wide, narrow):
    spots = [(b, i) for b in blocks for i in range(b.shape[0])]
    if flips is None:
        return [(b, i, i) for b, i in spots]
    _, low, y, _, _ = place(wide, narrow)
    return [(b, i, jnp.bitwise_xor(low * 2 + y, flip)) for (b, i), flip in zip(spots, flips)]


def total_sum(values):
    return jnp.sum(jnp.sum(values, axis=0, keepdims=True), axis=1, keepdims=True)


def lane_sums(values):
    parts = jnp.concatenate(split3(values), axis=1)
    ones = jnp.ones((16, parts.shape[1]), bf16)
    return lax.dot_general(ones, parts, (((1,), (1,)), ((), ())),
                           preferred_element_type=f32)[0:1, :]


def make_rows(left, sides, sums):
    groups, rows, _ = left.shape
    halves = rows // LANES

    def one_group(g, _):
        left_group = left[g]
        acc = jnp.zeros((rows, LANES), f32)
        for right, kept, read_vector in sides:

            def some_columns(step, acc):
                first = step * TOGETHER
                both = jnp.concatenate([right[first + k] for k in range(TOGETHER)], axis=1)
                exponent = jnp.dot(left_group, both, preferred_element_type=f32)
                tile = jnp.exp2(exponent)
                for k in range(TOGETHER):
                    if kept is not None:
                        kept[g, first + k] = tile[:, k * rows:(k + 1) * rows]
                    for half in range(halves):
                        start = k * rows + half * LANES
                        acc = acc + tile[:, start:start + LANES] * read_vector(first + k, half)
                return acc

            acc = lax.fori_loop(0, right.shape[0] // TOGETHER, some_columns, acc, unroll=4 // TOGETHER)
        sums[g] = acc
        return 0

    lax.fori_loop(0, groups, one_group, 0, unroll=groups <= 2)


def use_rows(sides, sums):
    groups, rows, _ = sums.shape
    halves = rows // LANES

    def one_group(g, _):
        acc = jnp.zeros((rows, LANES), f32)
        for kept, read_vector in sides:

            def one_column(c, acc):
                for half in range(halves):
                    acc = acc + kept[g, c, :, half * LANES:(half + 1) * LANES] * read_vector(c, half)
                return acc

            acc = lax.fori_loop(0, kept.shape[1], one_column, acc, unroll=4)
        sums[g] = acc
        return 0

    lax.fori_loop(0, groups, one_group, 0, unroll=groups <= 2)


def write_rows(sums, out, bases):
    groups, rows, _ = sums.shape
    halves = rows // LANES
    total = lane_sums(sums[...].reshape(groups * rows, LANES))
    for g in range(groups):
        base = bases[g * len(bases) // groups]
        for half in range(halves):
            line = (base + g % (groups // len(bases))) * halves + half
            start = (g * halves + half) * LANES
            out[pl.ds(line, 1), :] = total[:, start:start + LANES]


def project_kernel(features, projection_t, targets, latent, out, feature_buf, projection_buf, target_buf, sems):
    proj = projection_t.shape[0]
    chunks, height, _ = feature_buf.shape
    copies = [
        pltpu.make_async_copy(features.at[pl.ds(i * height, height)], feature_buf.at[i], sems.at[i])
        for i in range(chunks)]
    copies.insert(1, pltpu.make_async_copy(projection_t, projection_buf, sems.at[chunks]))
    copies.append(pltpu.make_async_copy(targets, target_buf, sems.at[chunks + 1]))
    for copy in copies:
        copy.start()
    copies.pop(1).wait()
    for i in range(chunks):
        copies[i].wait()
        some = lax.dot_general(
            projection_buf[...], feature_buf[i], (((1,), (1,)), ((), ())), preferred_element_type=f32)
        latent[0, i * proj:(i + 1) * proj, :] = some
        out[0, i * proj:(i + 1) * proj, :] = some
    copies[-1].wait()
    line = lax.broadcasted_iota(jnp.int32, (8, LANES), 0)
    tail = jnp.zeros((8, LANES), f32)
    for i in range(chunks):
        tail = jnp.where(line == i, target_buf[:, i * LANES:(i + 1) * LANES], tail)
    out[0, chunks * proj:, :] = tail


def block_latent(block, i, proj, halves):
    return jnp.concatenate([block[i, half * proj:(half + 1) * proj, :] for half in range(halves)], axis=1)


def prepare_rows(blocks, flips, left, proj, scale, wide, narrow):
    for block, i, source in row_sources(blocks, flips, wide, narrow):
        left[source] = left_operand(block_latent(block, i, proj, left.shape[1] // LANES), scale)


def vector_reader(vector, halves):
    return lambda c, half: vector[pl.ds(c * halves + half, 1), :]


def side_kernel(proj, scale, wide, narrow, keep, flips, row_count, column_count, *refs):
    rows_in, columns_in = refs[:row_count], refs[row_count:row_count + column_count]
    refs = refs[row_count + column_count:]
    fresh = rows_in[0].dtype == f32
    left, refs = (refs[0], refs[1:]) if fresh else (rows_in[0], refs)
    right, vector, partial, sums = refs[0], refs[1], refs[2], refs[-1]
    kept = refs[3] if keep else None
    halves = left.shape[1] // LANES
    if fresh:
        prepare_rows(rows_in, flips[0], left, proj, scale, wide, narrow)
    for block, i, source in column_sources(columns_in, flips[1], wide, narrow):
        right[source] = right_operand(block_latent(block, i, proj, halves), scale)
        for half in range(halves):
            line = halves * proj + half
            vector[pl.ds(source * halves + half, 1), :] = block[i, line:line + 1, :]
    make_rows(left, [(right, kept, vector_reader(vector, halves))], sums)
    write_rows(sums, partial, [0])


def rest_kernel(proj, scale, wide, narrow, keep, flips, *refs):
    rows_in, columns, earlier, refs = refs[:1], refs[1:5], refs[5:7], refs[7:]
    if keep:
        out, *kept, sums, partial, held, left = refs
    else:
        left, out, sums, partial, held = refs
        kept = (None, None)
    halves = left.shape[1] // LANES
    prepare_rows(rows_in, flips[0], left, proj, scale, wide, narrow)
    make_rows(left, [
        (columns[2 * side], kept[side], vector_reader(columns[2 * side + 1], halves))
        for side in range(2)], sums)
    write_rows(sums, partial, [0])
    message_kernel(2, wide, narrow, halves, *earlier, partial, columns[1], out, held)


def message_kernel(parts, wide, narrow, halves, *refs):
    partials, vector, out, held = refs[:parts + 1], refs[parts + 1], refs[-2], refs[-1]
    lines_of = [partials[0][...] + partials[1][...]] + [partial[...] for partial in partials[2:]]
    for part, lines in enumerate(lines_of):
        base = part_base(part, parts, wide, narrow) * halves
        for line in range(lines.shape[0]):
            held[pl.ds(base + line, 1), :] = lines[line:line + 1, :]
    _, low, y, _, _ = place(wide, narrow)
    mine = (low * 2 + y) * halves
    pieces = [held[line:line + 1, :] for line in range(held.shape[0])]
    pieces += [vector[pl.ds(mine + half, 1), :] for half in range(halves)]
    block = jnp.concatenate(pieces, axis=1)

    def copy(i, _):
        out[i] = block
        return 0

    lax.fori_loop(0, out.shape[0], copy, 0, unroll=8)


def second_kernel(wide, narrow, keep, parts, *refs):
    arrived, out, step_scalars, direction, images, targets, partial, sums = refs[:1] + refs[-7:]
    lines = partial.shape[0]
    halves = lines // narrow
    across = narrow // 2
    group = [(high, x) for x in range(narrow // 2) for high in range(2)]

    def unpack(low, _):
        for y, core in ((0, 0), (0, 1), (1, 0), (1, 1)):
            members = [device_at(high, low, y, x, core, wide, narrow) for high, x in group]
            slots = [slot(member, wide, narrow) for member in members]
            total = arrived[slots[0], :, 0:lines * LANES]
            for spot in slots[1:]:
                total = total + arrived[spot, :, 0:lines * LANES]
            for r, member in enumerate(members):
                for half in range(halves):
                    start = arrived[slots[r], :, (lines + half) * LANES:(lines + half + 1) * LANES]
                    line = r * halves + half
                    spot = pl.ds(member * halves + half, 1)
                    targets[spot, :] = start
                    images[spot, :] = total[:, line * LANES:(line + 1) * LANES] + noise_var * start
        return 0

    lax.fori_loop(0, wide // 4, unpack, 0, unroll=2)
    start, first = targets[...], images[...]
    norm = total_sum(start * start)
    alpha = norm / total_sum(start * first)
    residual = start - alpha * first
    norm_next = total_sum(residual * residual)
    beta = norm_next / norm
    whole = residual + beta * start
    direction[...] = whole
    high, low, y, x, core = place(wide, narrow)

    def side_reader(side):
        def read_vector(c, half):
            source = device_at(high, c // 2, c % 2, x, jnp.bitwise_xor(core, side), wide, narrow)
            return direction[pl.ds(source * halves + half, 1), :]
        return read_vector

    groups = narrow // parts
    for part in range(parts):
        part_sums = sums.at[part * groups:(part + 1) * groups]
        if keep:
            use_rows([(refs[1 + 2 * part + side], side_reader(side)) for side in range(2)], part_sums)
        else:
            make_rows(refs[3 + part], [(refs[1 + side], None, side_reader(side)) for side in range(2)], part_sums)
    write_rows(sums, partial, [part_base(part, parts, wide, narrow) for part in range(parts)])
    share = jnp.zeros((1, LANES), f32)
    for r, (row_high, row_x) in enumerate(group):
        for half in range(halves):
            spot = pl.ds(device_at(row_high, low, y, row_x, core, wide, narrow) * halves + half, 1)
            line = r * halves + half
            share = share + direction[spot, :] * partial[line:line + 1, :]
    blocks = [
        jnp.concatenate([partial[r * halves + half:r * halves + half + 1, :]
                         for half in range(halves)] + [share], axis=1)
        for r in range(narrow)]

    def copy(to_low, _):
        for r, (to_high, to_x) in enumerate(group):
            for to_y, to_core in ((0, 0), (0, 1), (1, 0), (1, 1)):
                to = device_at(to_high, to_low, to_y, to_x, to_core, wide, narrow)
                out[slot(to, wide, narrow)] = blocks[r]
        return 0

    lax.fori_loop(0, wide // 4, copy, 0, unroll=2)
    lane = lax.broadcasted_iota(jnp.int32, (1, LANES), 1)
    noise = noise_var * total_sum(whole * whole)
    step_scalars[0:1, :] = jnp.where(lane == 0, alpha, jnp.where(
        lane == 1, norm_next, jnp.where(lane == 2, beta, noise)))
    for half in range(halves):
        spot = pl.ds(device_at(high, low, y, x, core, wide, narrow) * halves + half, 1)
        step_scalars[1 + half:2 + half, :] = images[spot, :]
        step_scalars[1 + halves + half:2 + halves + half, :] = targets[spot, :]


def last_kernel(wide, narrow, arrived, step_scalars, solution_out, residual_out, answer, sems):
    alpha = step_scalars[0:1, 0:1]
    norm = step_scalars[0:1, 1:2]
    beta = step_scalars[0:1, 2:3]
    noise = step_scalars[0:1, 3:4]
    halves = answer.shape[1]

    def add(i, total):
        return total + arrived[i, :, halves * LANES:(halves + 1) * LANES]

    share = lax.fori_loop(0, arrived.shape[0], add, jnp.zeros((1, LANES), f32), unroll=32)
    alpha_next = norm / (total_sum(share) + noise)
    _, low, y, _, core = place(wide, narrow)
    product = jnp.zeros((1, (halves + 1) * LANES), f32)
    for high in range(2):
        for x in range(narrow // 2):
            member = device_at(high, low, y, x, core, wide, narrow)
            product = product + arrived[slot(member, wide, narrow)]
    for half in range(halves):
        begin = step_scalars[1 + halves + half:2 + halves + half, :]
        residual = begin - alpha * step_scalars[1 + half:2 + half, :]
        direction = residual + beta * begin
        image = product[:, half * LANES:(half + 1) * LANES] + noise_var * direction
        answer[0, half:half + 1, :] = alpha * begin + alpha_next * direction
        answer[1, half:half + 1, :] = residual - alpha_next * image
    copies = [pltpu.make_async_copy(answer.at[i], out, sems.at[i])
              for i, out in enumerate((solution_out, residual_out))]
    for copy in copies:
        copy.start()
    for copy in copies:
        copy.wait()


def call(kernel, out_shape, *args, scratch=(), **options):
    return pl.pallas_call(
        kernel,
        out_shape=out_shape,
        scratch_shapes=list(scratch),
        compiler_params=pltpu.CompilerParams(vmem_limit_bytes=VMEM_BYTES),
        **options,
    )(*args)


def to_all(blocks):
    group = list(range(blocks.shape[0] - 1, -1, -1))
    return lax.all_to_all(blocks, ALL, split_axis=0, concat_axis=0, axis_index_groups=[group], tiled=True)


def join_kernel(*refs):
    i = 0
    for block in refs[:-1]:
        for j in range(block.shape[0]):
            refs[-1][i] = block[j]
            i += 1


def join(*blocks, flops=0):
    total = sum(b.shape[0] for b in blocks)
    return call(join_kernel, jax.ShapeDtypeStruct((total, *blocks[0].shape[1:]), f32), *blocks,
                cost_estimate=pl.CostEstimate(flops=flops, bytes_accessed=0, transcendentals=0))


def first_round(latent, own, wide, narrow):
    lows, across = wide // 4, narrow // 2
    if lows & (lows - 1) or across != 2 or lows > DIRECT:
        every = lax.all_gather(own, ALL, axis=0, tiled=True)
        every = every.reshape(2, lows, 2, across, 2, *own.shape[1:])
        high, low, y, x, core = place(wide, narrow)
        rows = every
        for place_in, axis in ((low, 1), (y, 1), (core, 2)):
            rows = lax.dynamic_index_in_dim(rows, place_in, axis, keepdims=False)
        columns = lax.dynamic_index_in_dim(every, high, 0, keepdims=False)
        columns = lax.dynamic_index_in_dim(columns, x, 2, keepdims=False)
        rows = jnp.swapaxes(rows, 0, 1).reshape(narrow, *own.shape[1:])
        sides = [lax.dynamic_index_in_dim(columns, jnp.bitwise_xor(core, side), 2, keepdims=False)
                 for side in range(2)]
        sides = [[columns.reshape(wide // 2, *own.shape[1:])] for columns in sides]
        return [[rows]], sides, (None, None)

    sizes = axis_sizes(wide, narrow)

    def swap(value, **flips):
        pairs = []
        for i in range(wide * narrow):
            spot = list(np.unravel_index(i, sizes))
            for name, flip in flips.items():
                axis = dict(high=HIGH, low=LOW, y=Y, x=X, core=CORE)[name]
                spot[axis] = int(spot[axis]) ^ flip
            pairs.append((i, int(np.ravel_multi_index(spot, sizes))))
        return lax.ppermute(value, ALL, pairs)

    rows = join(latent, swap(latent, high=1), flops=EARLY)
    columns = [own] + [swap(own, low=flip // 2, y=flip % 2) for flip in range(1, 2 * lows)]
    sides = [columns, [swap(block, core=1) for block in columns]]
    parts = [[rows], [swap(rows, x=1)]]
    return parts, sides, ([0, 1], list(range(2 * lows)))


def on_device(wide, narrow, features, projection, targets):
    rows, proj = features.shape[0], projection.shape[1]
    halves = rows // LANES
    lines = narrow * halves
    devices = wide * narrow
    scale = -2.0 / proj * math.log2(math.e)
    depth = 6 * proj + 16
    keep = 4 * devices * rows * rows <= KEEP_BYTES

    def shape(*dims, dtype=f32):
        return jax.ShapeDtypeStruct(dims, dtype)

    def scratch(*dims, dtype=f32):
        return pltpu.VMEM(dims, dtype)

    feat = features.shape[1]
    inputs = [pltpu.with_memory_space_constraint(value, pltpu.HBM)
              for value in (features, projection.T, targets.reshape(1, rows))]
    latent, own = call(
        project_kernel, (shape(1, halves * proj, LANES), shape(1, halves * proj + 8, LANES)), *inputs,
        in_specs=[pl.BlockSpec(memory_space=pltpu.HBM)] * 3,
        scratch=[scratch(halves, LANES, feat, dtype=bf16), scratch(proj, feat, dtype=bf16),
                 scratch(1, rows), pltpu.SemaphoreType.DMA((halves + 2,))])
    row_parts, sides, flips = first_round(latent, own, wide, narrow)
    parts = len(row_parts)
    groups = narrow // parts
    left = shape(groups, rows, depth, dtype=bf16)
    right = shape(wide // 2, depth, rows, dtype=bf16)
    vector = shape(wide // 2 * halves, LANES)
    kept = (shape(groups, wide // 2, rows, rows),) if keep else ()
    group_lines = shape(groups * halves, LANES)
    sums = scratch(groups, rows, LANES)
    settings = (proj, scale, wide, narrow, keep, flips)

    def cost(columns):
        tiles = groups * columns * rows * rows
        return pl.CostEstimate(flops=2 * tiles * depth, bytes_accessed=4 * tiles, transcendentals=tiles)

    lefts, columns, blocks, partials = [], [], [], []
    for side, column_blocks in enumerate(sides):
        row_blocks = row_parts[0] if side == 0 else lefts
        made = call(
            functools.partial(side_kernel, *settings, len(row_blocks), len(column_blocks)),
            ((left,) if side == 0 else ()) + (right, vector, group_lines) + kept,
            *row_blocks, *column_blocks, scratch=[sums], cost_estimate=cost(wide // 2))
        if side == 0:
            lefts, made = [made[0]], made[1:]
        columns += made[:2]
        partials.append(made[2])
        blocks += made[3:]
    message = shape(devices, 1, (lines + halves) * LANES)
    if parts == 2:
        made = call(
            functools.partial(rest_kernel, *settings),
            (message, *kept * 2) if keep else (left, message), *row_parts[1], *columns, *partials,
            scratch=[sums, scratch(groups * halves, LANES), scratch(lines, LANES)]
            + ([scratch(*left.shape, dtype=bf16)] if keep else []),
            cost_estimate=cost(wide))
        out = made[0 if keep else 1]
        blocks += made[1:] if keep else []
        lefts += [] if keep else made[:1]
    else:
        out = call(
            functools.partial(message_kernel, parts, wide, narrow, halves), message,
            *partials, columns[1], scratch=[scratch(lines, LANES)])
    block = blocks if keep else [columns[0], columns[2], *lefts]
    sums = scratch(narrow, rows, LANES)
    out, step_scalars = call(
        functools.partial(second_kernel, wide, narrow, keep, parts),
        (shape(devices, 1, (halves + 1) * LANES), shape(1 + 2 * halves, LANES)),
        to_all(out), *block,
        scratch=[scratch(devices * halves, LANES)] * 3 + [scratch(lines, LANES), sums])
    answer, residual = call(
        functools.partial(last_kernel, wide, narrow), (shape(halves, LANES), shape(halves, LANES)),
        to_all(out), step_scalars,
        out_specs=(pl.BlockSpec(memory_space=pl.ANY),) * 2,
        scratch=[scratch(2, halves, LANES), pltpu.SemaphoreType.DMA((2,))])
    return answer.reshape(rows), residual.reshape(rows)


def solution(mesh):
    wide, narrow = mesh.shape["wide"], mesh.shape["narrow"]
    line = jax.sharding.Mesh(mesh.devices.reshape(wide * narrow), (ALL,))
    in_specs = (P(ALL, None), P(), P(ALL))
    return jax.shard_map(
        functools.partial(on_device, wide, narrow), mesh=line,
        in_specs=in_specs, out_specs=(P(ALL), P(ALL)), check_vma=False,
    )
```

```python
import functools
import math

import jax
import jax.numpy as jnp
import numpy as np
from jax import lax
from jax.experimental import pallas as pl
from jax.experimental.pallas import tpu as pltpu
from jax.sharding import PartitionSpec as P

noise_var = 0.5
LANES = 128
TOGETHER = 4
EARLY = 10**9
DIRECT = 8
KEEP_BYTES = 8 * 2**20
VMEM_BYTES = 32 * 2**20
ALL = "all"
HIGH, LOW, Y, X, CORE = range(5)
highest = lax.Precision.HIGHEST
f32 = jnp.float32
bf16 = jnp.bfloat16


def split3(values):
    high = values.astype(bf16)
    rest = values - high.astype(f32)
    mid = rest.astype(bf16)
    low = (rest - mid.astype(f32)).astype(bf16)
    return high, mid, low


def exponent_rows(first, second):
    width = (first if not isinstance(first, float) else second).shape[1]
    row = lax.broadcasted_iota(jnp.int32, (16, width), 0)
    out = jnp.zeros((16, width), f32)
    for base, value in ((0, first), (3, second)):
        parts = (1.0, 1.0, 1.0) if isinstance(value, float) else [p.astype(f32) for p in split3(value)]
        for k, part in enumerate(parts):
            out = jnp.where(row == base + k, part, out)
    return out.astype(bf16)


def right_operand(latent, scale):
    square = jnp.sum(latent * latent, axis=0, keepdims=True) * scale
    h, m, l = split3(latent)
    return jnp.concatenate([h, m, l, h, m, h, exponent_rows(square, 1.0)], axis=0)


def left_operand(latent, scale):
    square = jnp.sum(latent * latent, axis=0, keepdims=True) * scale
    h, m, l = split3(latent * (-2.0 * scale))
    stacked = jnp.concatenate([h, h, h, m, m, l, exponent_rows(1.0, square)], axis=0)
    return stacked.T


def axis_sizes(wide, narrow):
    return 2, wide // 4, 2, narrow // 2, 2


def place(wide, narrow):
    rest, out = lax.axis_index(ALL), []
    for size in reversed(axis_sizes(wide, narrow)):
        out.append(rest % size)
        rest = rest // size
    return tuple(reversed(out))


def device_at(high, low, y, x, core, wide, narrow):
    return (((high * (wide // 4) + low) * 2 + y) * (narrow // 2) + x) * 2 + core


def slot(device, wide, narrow):
    return wide * narrow - 1 - device


def part_base(part, parts, wide, narrow):
    return 0 if parts == 1 else jnp.bitwise_xor(place(wide, narrow)[X], part) * 2


def row_sources(blocks, flips, wide, narrow):
    spots = [(b, i) for b in blocks for i in range(b.shape[0])]
    if flips is None:
        return [(b, i, i) for b, i in spots]
    high = place(wide, narrow)[HIGH]
    return [(b, i, jnp.bitwise_xor(high, flip)) for (b, i), flip in zip(spots, flips)]


def column_sources(blocks, flips, wide, narrow):
    spots = [(b, i) for b in blocks for i in range(b.shape[0])]
    if flips is None:
        return [(b, i, i) for b, i in spots]
    _, low, y, _, _ = place(wide, narrow)
    return [(b, i, jnp.bitwise_xor(low * 2 + y, flip)) for (b, i), flip in zip(spots, flips)]


def total_sum(values):
    return jnp.sum(jnp.sum(values, axis=0, keepdims=True), axis=1, keepdims=True)


def lane_sums(values):
    parts = jnp.concatenate(split3(values), axis=1)
    ones = jnp.ones((16, parts.shape[1]), bf16)
    return lax.dot_general(ones, parts, (((1,), (1,)), ((), ())),
                           preferred_element_type=f32)[0:1, :]


def make_rows(left, sides, sums):
    groups, rows, _ = left.shape
    halves = rows // LANES

    def one_group(g, _):
        left_group = left[g]
        acc = jnp.zeros((rows, LANES), f32)
        for right, kept, read_vector in sides:

            def some_columns(step, acc):
                first = step * TOGETHER
                both = jnp.concatenate([right[first + k] for k in range(TOGETHER)], axis=1)
                exponent = jnp.dot(left_group, both, preferred_element_type=f32)
                tile = jnp.exp2(exponent)
                for k in range(TOGETHER):
                    if kept is not None:
                        kept[g, first + k] = tile[:, k * rows:(k + 1) * rows]
                    for half in range(halves):
                        start = k * rows + half * LANES
                        acc = acc + tile[:, start:start + LANES] * read_vector(first + k, half)
                return acc

            acc = lax.fori_loop(0, right.shape[0] // TOGETHER, some_columns, acc, unroll=4 // TOGETHER)
        sums[g] = acc
        return 0

    lax.fori_loop(0, groups, one_group, 0, unroll=groups <= 2)


def use_rows(sides, sums):
    groups, rows, _ = sums.shape
    halves = rows // LANES

    def one_group(g, _):
        acc = jnp.zeros((rows, LANES), f32)
        for kept, read_vector in sides:

            def one_column(c, acc):
                for half in range(halves):
                    acc = acc + kept[g, c, :, half * LANES:(half + 1) * LANES] * read_vector(c, half)
                return acc

            acc = lax.fori_loop(0, kept.shape[1], one_column, acc, unroll=4)
        sums[g] = acc
        return 0

    lax.fori_loop(0, groups, one_group, 0, unroll=groups <= 2)


def write_rows(sums, out, bases):
    groups, rows, _ = sums.shape
    halves = rows // LANES
    total = lane_sums(sums[...].reshape(groups * rows, LANES))
    for g in range(groups):
        base = bases[g * len(bases) // groups]
        for half in range(halves):
            line = (base + g % (groups // len(bases))) * halves + half
            start = (g * halves + half) * LANES
            out[pl.ds(line, 1), :] = total[:, start:start + LANES]


def project_kernel(features, projection_t, targets, latent, out, feature_buf, projection_buf, target_buf, sems):
    proj = projection_t.shape[0]
    chunks, height, _ = feature_buf.shape
    copies = [
        pltpu.make_async_copy(features.at[pl.ds(i * height, height)], feature_buf.at[i], sems.at[i])
        for i in range(chunks)]
    copies.insert(1, pltpu.make_async_copy(projection_t, projection_buf, sems.at[chunks]))
    copies.append(pltpu.make_async_copy(targets, target_buf, sems.at[chunks + 1]))
    for copy in copies:
        copy.start()
    copies.pop(1).wait()
    for i in range(chunks):
        copies[i].wait()
        some = lax.dot_general(
            projection_buf[...], feature_buf[i], (((1,), (1,)), ((), ())), preferred_element_type=f32)
        latent[0, i * proj:(i + 1) * proj, :] = some
        out[0, i * proj:(i + 1) * proj, :] = some
    copies[-1].wait()
    line = lax.broadcasted_iota(jnp.int32, (8, LANES), 0)
    tail = jnp.zeros((8, LANES), f32)
    for i in range(chunks):
        tail = jnp.where(line == i, target_buf[:, i * LANES:(i + 1) * LANES], tail)
    out[0, chunks * proj:, :] = tail


def block_latent(block, i, proj, halves):
    return jnp.concatenate([block[i, half * proj:(half + 1) * proj, :] for half in range(halves)], axis=1)


def prepare_rows(blocks, flips, left, proj, scale, wide, narrow):
    for block, i, source in row_sources(blocks, flips, wide, narrow):
        left[source] = left_operand(block_latent(block, i, proj, left.shape[1] // LANES), scale)


def vector_reader(vector, halves):
    return lambda c, half: vector[pl.ds(c * halves + half, 1), :]


def side_kernel(proj, scale, wide, narrow, keep, flips, row_count, column_count, *refs):
    rows_in, columns_in = refs[:row_count], refs[row_count:row_count + column_count]
    refs = refs[row_count + column_count:]
    fresh = rows_in[0].dtype == f32
    left, refs = (refs[0], refs[1:]) if fresh else (rows_in[0], refs)
    right, vector, partial, sums = refs[0], refs[1], refs[2], refs[-1]
    kept = refs[3] if keep else None
    halves = left.shape[1] // LANES
    if fresh:
        prepare_rows(rows_in, flips[0], left, proj, scale, wide, narrow)
    for block, i, source in column_sources(columns_in, flips[1], wide, narrow):
        right[source] = right_operand(block_latent(block, i, proj, halves), scale)
        for half in range(halves):
            line = halves * proj + half
            vector[pl.ds(source * halves + half, 1), :] = block[i, line:line + 1, :]
    make_rows(left, [(right, kept, vector_reader(vector, halves))], sums)
    write_rows(sums, partial, [0])


def rest_kernel(proj, scale, wide, narrow, keep, flips, *refs):
    rows_in, columns, earlier, refs = refs[:1], refs[1:5], refs[5:7], refs[7:]
    if keep:
        out, *kept, sums, partial, held, left = refs
    else:
        left, out, sums, partial, held = refs
        kept = (None, None)
    halves = left.shape[1] // LANES
    prepare_rows(rows_in, flips[0], left, proj, scale, wide, narrow)
    make_rows(left, [
        (columns[2 * side], kept[side], vector_reader(columns[2 * side + 1], halves))
        for side in range(2)], sums)
    write_rows(sums, partial, [0])
    message_kernel(2, wide, narrow, halves, *earlier, partial, columns[1], out, held)


def message_kernel(parts, wide, narrow, halves, *refs):
    partials, vector, out, held = refs[:parts + 1], refs[parts + 1], refs[-2], refs[-1]
    lines_of = [partials[0][...] + partials[1][...]] + [partial[...] for partial in partials[2:]]
    for part, lines in enumerate(lines_of):
        base = part_base(part, parts, wide, narrow) * halves
        for line in range(lines.shape[0]):
            held[pl.ds(base + line, 1), :] = lines[line:line + 1, :]
    _, low, y, _, _ = place(wide, narrow)
    mine = (low * 2 + y) * halves
    pieces = [held[line:line + 1, :] for line in range(held.shape[0])]
    pieces += [vector[pl.ds(mine + half, 1), :] for half in range(halves)]
    block = jnp.concatenate(pieces, axis=1)

    def copy(i, _):
        out[i] = block
        return 0

    lax.fori_loop(0, out.shape[0], copy, 0, unroll=8)


def second_kernel(wide, narrow, keep, parts, *refs):
    arrived, out, step_scalars, direction, images, targets, partial, sums = refs[:1] + refs[-7:]
    lines = partial.shape[0]
    halves = lines // narrow
    across = narrow // 2
    group = [(high, x) for x in range(narrow // 2) for high in range(2)]

    def unpack(low, _):
        for y, core in ((0, 0), (0, 1), (1, 0), (1, 1)):
            members = [device_at(high, low, y, x, core, wide, narrow) for high, x in group]
            slots = [slot(member, wide, narrow) for member in members]
            total = arrived[slots[0], :, 0:lines * LANES]
            for spot in slots[1:]:
                total = total + arrived[spot, :, 0:lines * LANES]
            for r, member in enumerate(members):
                for half in range(halves):
                    start = arrived[slots[r], :, (lines + half) * LANES:(lines + half + 1) * LANES]
                    line = r * halves + half
                    spot = pl.ds(member * halves + half, 1)
                    targets[spot, :] = start
                    images[spot, :] = total[:, line * LANES:(line + 1) * LANES] + noise_var * start
        return 0

    lax.fori_loop(0, wide // 4, unpack, 0, unroll=2)
    start, first = targets[...], images[...]
    norm = total_sum(start * start)
    alpha = norm / total_sum(start * first)
    residual = start - alpha * first
    norm_next = total_sum(residual * residual)
    beta = norm_next / norm
    whole = residual + beta * start
    direction[...] = whole
    high, low, y, x, core = place(wide, narrow)

    def side_reader(side):
        def read_vector(c, half):
            source = device_at(high, c // 2, c % 2, x, jnp.bitwise_xor(core, side), wide, narrow)
            return direction[pl.ds(source * halves + half, 1), :]
        return read_vector

    groups = narrow // parts
    for part in range(parts):
        part_sums = sums.at[part * groups:(part + 1) * groups]
        if keep:
            use_rows([(refs[1 + 2 * part + side], side_reader(side)) for side in range(2)], part_sums)
        else:
            make_rows(refs[3 + part], [(refs[1 + side], None, side_reader(side)) for side in range(2)], part_sums)
    write_rows(sums, partial, [part_base(part, parts, wide, narrow) for part in range(parts)])
    share = jnp.zeros((1, LANES), f32)
    for r, (row_high, row_x) in enumerate(group):
        for half in range(halves):
            spot = pl.ds(device_at(row_high, low, y, row_x, core, wide, narrow) * halves + half, 1)
            line = r * halves + half
            share = share + direction[spot, :] * partial[line:line + 1, :]
    blocks = [
        jnp.concatenate([partial[r * halves + half:r * halves + half + 1, :]
                         for half in range(halves)] + [share], axis=1)
        for r in range(narrow)]

    def copy(to_low, _):
        for r, (to_high, to_x) in enumerate(group):
            for to_y, to_core in ((0, 0), (0, 1), (1, 0), (1, 1)):
                to = device_at(to_high, to_low, to_y, to_x, to_core, wide, narrow)
                out[slot(to, wide, narrow)] = blocks[r]
        return 0

    lax.fori_loop(0, wide // 4, copy, 0, unroll=2)
    lane = lax.broadcasted_iota(jnp.int32, (1, LANES), 1)
    noise = noise_var * total_sum(whole * whole)
    step_scalars[0:1, :] = jnp.where(lane == 0, alpha, jnp.where(
        lane == 1, norm_next, jnp.where(lane == 2, beta, noise)))
    for half in range(halves):
        spot = pl.ds(device_at(high, low, y, x, core, wide, narrow) * halves + half, 1)
        step_scalars[1 + half:2 + half, :] = images[spot, :]
        step_scalars[1 + halves + half:2 + halves + half, :] = targets[spot, :]


def last_kernel(wide, narrow, arrived, step_scalars, solution_out, residual_out, answer, sems):
    alpha = step_scalars[0:1, 0:1]
    norm = step_scalars[0:1, 1:2]
    beta = step_scalars[0:1, 2:3]
    noise = step_scalars[0:1, 3:4]
    halves = answer.shape[1]

    def add(i, total):
        return total + arrived[i, :, halves * LANES:(halves + 1) * LANES]

    share = lax.fori_loop(0, arrived.shape[0], add, jnp.zeros((1, LANES), f32), unroll=32)
    alpha_next = norm / (total_sum(share) + noise)
    _, low, y, _, core = place(wide, narrow)
    product = jnp.zeros((1, (halves + 1) * LANES), f32)
    for high in range(2):
        for x in range(narrow // 2):
            member = device_at(high, low, y, x, core, wide, narrow)
            product = product + arrived[slot(member, wide, narrow)]
    for half in range(halves):
        begin = step_scalars[1 + halves + half:2 + halves + half, :]
        residual = begin - alpha * step_scalars[1 + half:2 + half, :]
        direction = residual + beta * begin
        image = product[:, half * LANES:(half + 1) * LANES] + noise_var * direction
        answer[0, half:half + 1, :] = alpha * begin + alpha_next * direction
        answer[1, half:half + 1, :] = residual - alpha_next * image
    copies = [pltpu.make_async_copy(answer.at[i], out, sems.at[i])
              for i, out in enumerate((solution_out, residual_out))]
    for copy in copies:
        copy.start()
    for copy in copies:
        copy.wait()


def call(kernel, out_shape, *args, scratch=(), **options):
    return pl.pallas_call(
        kernel,
        out_shape=out_shape,
        scratch_shapes=list(scratch),
        compiler_params=pltpu.CompilerParams(vmem_limit_bytes=VMEM_BYTES),
        **options,
    )(*args)


def to_all(blocks):
    group = list(range(blocks.shape[0] - 1, -1, -1))
    return lax.all_to_all(blocks, ALL, split_axis=0, concat_axis=0, axis_index_groups=[group], tiled=True)


def join_kernel(*refs):
    i = 0
    for block in refs[:-1]:
        for j in range(block.shape[0]):
            refs[-1][i] = block[j]
            i += 1


def join(*blocks, flops=0):
    total = sum(b.shape[0] for b in blocks)
    return call(join_kernel, jax.ShapeDtypeStruct((total, *blocks[0].shape[1:]), f32), *blocks,
                cost_estimate=pl.CostEstimate(flops=flops, bytes_accessed=0, transcendentals=0))


def first_round(latent, own, wide, narrow):
    lows, across = wide // 4, narrow // 2
    if lows & (lows - 1) or across != 2 or lows > DIRECT:
        every = lax.all_gather(own, ALL, axis=0, tiled=True)
        every = every.reshape(2, lows, 2, across, 2, *own.shape[1:])
        high, low, y, x, core = place(wide, narrow)
        rows = every
        for place_in, axis in ((low, 1), (y, 1), (core, 2)):
            rows = lax.dynamic_index_in_dim(rows, place_in, axis, keepdims=False)
        columns = lax.dynamic_index_in_dim(every, high, 0, keepdims=False)
        columns = lax.dynamic_index_in_dim(columns, x, 2, keepdims=False)
        rows = jnp.swapaxes(rows, 0, 1).reshape(narrow, *own.shape[1:])
        sides = [lax.dynamic_index_in_dim(columns, jnp.bitwise_xor(core, side), 2, keepdims=False)
                 for side in range(2)]
        sides = [[columns.reshape(wide // 2, *own.shape[1:])] for columns in sides]
        return [[rows]], sides, (None, None)

    sizes = axis_sizes(wide, narrow)

    def swap(value, **flips):
        pairs = []
        for i in range(wide * narrow):
            spot = list(np.unravel_index(i, sizes))
            for name, flip in flips.items():
                axis = dict(high=HIGH, low=LOW, y=Y, x=X, core=CORE)[name]
                spot[axis] = int(spot[axis]) ^ flip
            pairs.append((i, int(np.ravel_multi_index(spot, sizes))))
        return lax.ppermute(value, ALL, pairs)

    rows = join(latent, swap(latent, high=1), flops=EARLY)
    columns = [own] + [swap(own, low=flip // 2, y=flip % 2) for flip in range(1, 2 * lows)]
    sides = [columns, [swap(block, core=1) for block in columns]]
    parts = [[rows], [swap(rows, x=1)]]
    return parts, sides, ([0, 1], list(range(2 * lows)))


def on_device(wide, narrow, features, projection, targets):
    rows, proj = features.shape[0], projection.shape[1]
    halves = rows // LANES
    lines = narrow * halves
    devices = wide * narrow
    scale = -2.0 / proj * math.log2(math.e)
    depth = 6 * proj + 16
    keep = 4 * devices * rows * rows <= KEEP_BYTES

    def shape(*dims, dtype=f32):
        return jax.ShapeDtypeStruct(dims, dtype)

    def scratch(*dims, dtype=f32):
        return pltpu.VMEM(dims, dtype)

    feat = features.shape[1]
    inputs = [pltpu.with_memory_space_constraint(value, pltpu.HBM)
              for value in (features, projection.T, targets.reshape(1, rows))]
    latent, own = call(
        project_kernel, (shape(1, halves * proj, LANES), shape(1, halves * proj + 8, LANES)), *inputs,
        in_specs=[pl.BlockSpec(memory_space=pltpu.HBM)] * 3,
        scratch=[scratch(halves, LANES, feat, dtype=bf16), scratch(proj, feat, dtype=bf16),
                 scratch(1, rows), pltpu.SemaphoreType.DMA((halves + 2,))])
    row_parts, sides, flips = first_round(latent, own, wide, narrow)
    parts = len(row_parts)
    groups = narrow // parts
    left = shape(groups, rows, depth, dtype=bf16)
    right = shape(wide // 2, depth, rows, dtype=bf16)
    vector = shape(wide // 2 * halves, LANES)
    kept = (shape(groups, wide // 2, rows, rows),) if keep else ()
    group_lines = shape(groups * halves, LANES)
    sums = scratch(groups, rows, LANES)
    settings = (proj, scale, wide, narrow, keep, flips)

    def cost(columns):
        tiles = groups * columns * rows * rows
        return pl.CostEstimate(flops=2 * tiles * depth, bytes_accessed=4 * tiles, transcendentals=tiles)

    lefts, columns, blocks, partials = [], [], [], []
    for side, column_blocks in enumerate(sides):
        row_blocks = row_parts[0] if side == 0 else lefts
        made = call(
            functools.partial(side_kernel, *settings, len(row_blocks), len(column_blocks)),
            ((left,) if side == 0 else ()) + (right, vector, group_lines) + kept,
            *row_blocks, *column_blocks, scratch=[sums], cost_estimate=cost(wide // 2))
        if side == 0:
            lefts, made = [made[0]], made[1:]
        columns += made[:2]
        partials.append(made[2])
        blocks += made[3:]
    message = shape(devices, 1, (lines + halves) * LANES)
    if parts == 2:
        made = call(
            functools.partial(rest_kernel, *settings),
            (message, *kept * 2) if keep else (left, message), *row_parts[1], *columns, *partials,
            scratch=[sums, scratch(groups * halves, LANES), scratch(lines, LANES)]
            + ([scratch(*left.shape, dtype=bf16)] if keep else []),
            cost_estimate=cost(wide))
        out = made[0 if keep else 1]
        blocks += made[1:] if keep else []
        lefts += [] if keep else made[:1]
    else:
        out = call(
            functools.partial(message_kernel, parts, wide, narrow, halves), message,
            *partials, columns[1], scratch=[scratch(lines, LANES)])
    block = blocks if keep else [columns[0], columns[2], *lefts]
    sums = scratch(narrow, rows, LANES)
    out, step_scalars = call(
        functools.partial(second_kernel, wide, narrow, keep, parts),
        (shape(devices, 1, (halves + 1) * LANES), shape(1 + 2 * halves, LANES)),
        to_all(out), *block,
        scratch=[scratch(devices * halves, LANES)] * 3 + [scratch(lines, LANES), sums])
    answer, residual = call(
        functools.partial(last_kernel, wide, narrow), (shape(halves, LANES), shape(halves, LANES)),
        to_all(out), step_scalars,
        out_specs=(pl.BlockSpec(memory_space=pl.ANY),) * 2,
        scratch=[scratch(2, halves, LANES), pltpu.SemaphoreType.DMA((2,))])
    return answer.reshape(rows), residual.reshape(rows)


def solution(mesh):
    wide, narrow = mesh.shape["wide"], mesh.shape["narrow"]
    line = jax.sharding.Mesh(mesh.devices.reshape(wide * narrow), (ALL,))
    in_specs = (P(ALL, None), P(), P(ALL))
    return jax.shard_map(
        functools.partial(on_device, wide, narrow), mesh=line,
        in_specs=in_specs, out_specs=(P(ALL), P(ALL)), check_vma=False,
    )
```

```python
import functools
import math

import jax
import jax.numpy as jnp
import numpy as np
from jax import lax
from jax.experimental import pallas as pl
from jax.experimental.pallas import tpu as pltpu
from jax.sharding import PartitionSpec as P

noise_var = 0.5
LANES = 128
TOGETHER = 4
EARLY = 10**9
DIRECT = 8
KEEP_BYTES = 8 * 2**20
VMEM_BYTES = 32 * 2**20
ALL = "all"
HIGH, LOW, Y, X, CORE = range(5)
highest = lax.Precision.HIGHEST
f32 = jnp.float32
bf16 = jnp.bfloat16


def split3(values):
    high = values.astype(bf16)
    rest = values - high.astype(f32)
    mid = rest.astype(bf16)
    low = (rest - mid.astype(f32)).astype(bf16)
    return high, mid, low


def exponent_rows(first, second):
    width = (first if not isinstance(first, float) else second).shape[1]
    row = lax.broadcasted_iota(jnp.int32, (16, width), 0)
    out = jnp.zeros((16, width), f32)
    for base, value in ((0, first), (3, second)):
        parts = (1.0, 1.0, 1.0) if isinstance(value, float) else [p.astype(f32) for p in split3(value)]
        for k, part in enumerate(parts):
            out = jnp.where(row == base + k, part, out)
    return out.astype(bf16)


def right_operand(latent, scale):
    square = jnp.sum(latent * latent, axis=0, keepdims=True) * scale
    h, m, l = split3(latent)
    return jnp.concatenate([h, m, l, h, m, h, exponent_rows(square, 1.0)], axis=0)


def left_operand(latent, scale):
    square = jnp.sum(latent * latent, axis=0, keepdims=True) * scale
    h, m, l = split3(latent * (-2.0 * scale))
    stacked = jnp.concatenate([h, h, h, m, m, l, exponent_rows(1.0, square)], axis=0)
    return stacked.T


def axis_sizes(wide, narrow):
    return 2, wide // 4, 2, narrow // 2, 2


def place(wide, narrow):
    rest, out = lax.axis_index(ALL), []
    for size in reversed(axis_sizes(wide, narrow)):
        out.append(rest % size)
        rest = rest // size
    return tuple(reversed(out))


def device_at(high, low, y, x, core, wide, narrow):
    return (((high * (wide // 4) + low) * 2 + y) * (narrow // 2) + x) * 2 + core


def slot(device, wide, narrow):
    return wide * narrow - 1 - device


def part_base(part, parts, wide, narrow):
    return 0 if parts == 1 else jnp.bitwise_xor(place(wide, narrow)[X], part) * 2


def row_sources(blocks, flips, wide, narrow):
    spots = [(b, i) for b in blocks for i in range(b.shape[0])]
    if flips is None:
        return [(b, i, i) for b, i in spots]
    high = place(wide, narrow)[HIGH]
    return [(b, i, jnp.bitwise_xor(high, flip)) for (b, i), flip in zip(spots, flips)]


def column_sources(blocks, flips, wide, narrow):
    spots = [(b, i) for b in blocks for i in range(b.shape[0])]
    if flips is None:
        return [(b, i, i) for b, i in spots]
    _, low, y, _, _ = place(wide, narrow)
    return [(b, i, jnp.bitwise_xor(low * 2 + y, flip)) for (b, i), flip in zip(spots, flips)]


def total_sum(values):
    return jnp.sum(jnp.sum(values, axis=0, keepdims=True), axis=1, keepdims=True)


def lane_sums(values):
    parts = jnp.concatenate(split3(values), axis=1)
    ones = jnp.ones((16, parts.shape[1]), bf16)
    return lax.dot_general(ones, parts, (((1,), (1,)), ((), ())),
                           preferred_element_type=f32)[0:1, :]


def make_rows(left, sides, sums):
    groups, rows, _ = left.shape
    halves = rows // LANES

    def one_group(g, _):
        left_group = left[g]
        acc = jnp.zeros((rows, LANES), f32)
        for right, kept, read_vector in sides:

            def some_columns(step, acc):
                first = step * TOGETHER
                both = jnp.concatenate([right[first + k] for k in range(TOGETHER)], axis=1)
                exponent = jnp.dot(left_group, both, preferred_element_type=f32)
                tile = jnp.exp2(exponent)
                for k in range(TOGETHER):
                    if kept is not None:
                        kept[g, first + k] = tile[:, k * rows:(k + 1) * rows]
                    for half in range(halves):
                        start = k * rows + half * LANES
                        acc = acc + tile[:, start:start + LANES] * read_vector(first + k, half)
                return acc

            acc = lax.fori_loop(0, right.shape[0] // TOGETHER, some_columns, acc, unroll=4 // TOGETHER)
        sums[g] = acc
        return 0

    lax.fori_loop(0, groups, one_group, 0, unroll=groups <= 2)


def use_rows(sides, sums):
    groups, rows, _ = sums.shape
    halves = rows // LANES

    def one_group(g, _):
        acc = jnp.zeros((rows, LANES), f32)
        for kept, read_vector in sides:

            def one_column(c, acc):
                for half in range(halves):
                    acc = acc + kept[g, c, :, half * LANES:(half + 1) * LANES] * read_vector(c, half)
                return acc

            acc = lax.fori_loop(0, kept.shape[1], one_column, acc, unroll=4)
        sums[g] = acc
        return 0

    lax.fori_loop(0, groups, one_group, 0, unroll=groups <= 2)


def write_rows(sums, out, bases):
    groups, rows, _ = sums.shape
    halves = rows // LANES
    total = lane_sums(sums[...].reshape(groups * rows, LANES))
    for g in range(groups):
        base = bases[g * len(bases) // groups]
        for half in range(halves):
            line = (base + g % (groups // len(bases))) * halves + half
            start = (g * halves + half) * LANES
            out[pl.ds(line, 1), :] = total[:, start:start + LANES]


def project_kernel(features, projection_t, targets, latent, out, feature_buf, projection_buf, target_buf, sems):
    proj = projection_t.shape[0]
    chunks, height, _ = feature_buf.shape
    some_rows = height // 2
    streams = [[
        pltpu.make_async_copy(
            features.at[pl.ds(i * height + k * some_rows, some_rows)],
            feature_buf.at[i, pl.ds(k * some_rows, some_rows)], sems.at[2 * i + k])
        for k in range(2)] for i in range(chunks)]
    matrix = pltpu.make_async_copy(projection_t, projection_buf, sems.at[2 * chunks])
    last = pltpu.make_async_copy(targets, target_buf, sems.at[2 * chunks + 1])
    for copy in (*streams[0], matrix, *[c for stream in streams[1:] for c in stream], last):
        copy.start()
    matrix.wait()
    for i in range(chunks):
        for copy in streams[i]:
            copy.wait()
        some = lax.dot_general(
            projection_buf[...], feature_buf[i], (((1,), (1,)), ((), ())), preferred_element_type=f32)
        latent[0, i * proj:(i + 1) * proj, :] = some
        out[0, i * proj:(i + 1) * proj, :] = some
    last.wait()
    line = lax.broadcasted_iota(jnp.int32, (8, LANES), 0)
    tail = jnp.zeros((8, LANES), f32)
    for i in range(chunks):
        tail = jnp.where(line == i, target_buf[:, i * LANES:(i + 1) * LANES], tail)
    out[0, chunks * proj:, :] = tail


def block_latent(block, i, proj, halves):
    return jnp.concatenate([block[i, half * proj:(half + 1) * proj, :] for half in range(halves)], axis=1)


def prepare_rows(blocks, flips, left, proj, scale, wide, narrow):
    for block, i, source in row_sources(blocks, flips, wide, narrow):
        left[source] = left_operand(block_latent(block, i, proj, left.shape[1] // LANES), scale)


def vector_reader(vector, halves):
    return lambda c, half: vector[pl.ds(c * halves + half, 1), :]


def side_kernel(proj, scale, wide, narrow, keep, flips, row_count, column_count, *refs):
    rows_in, columns_in = refs[:row_count], refs[row_count:row_count + column_count]
    refs = refs[row_count + column_count:]
    fresh = rows_in[0].dtype == f32
    left, refs = (refs[0], refs[1:]) if fresh else (rows_in[0], refs)
    right, vector, partial, sums = refs[0], refs[1], refs[2], refs[-1]
    kept = refs[3] if keep else None
    halves = left.shape[1] // LANES
    if fresh:
        prepare_rows(rows_in, flips[0], left, proj, scale, wide, narrow)
    for block, i, source in column_sources(columns_in, flips[1], wide, narrow):
        right[source] = right_operand(block_latent(block, i, proj, halves), scale)
        for half in range(halves):
            line = halves * proj + half
            vector[pl.ds(source * halves + half, 1), :] = block[i, line:line + 1, :]
    make_rows(left, [(right, kept, vector_reader(vector, halves))], sums)
    write_rows(sums, partial, [0])


def rest_kernel(proj, scale, wide, narrow, keep, flips, *refs):
    rows_in, columns, earlier, refs = refs[:1], refs[1:5], refs[5:7], refs[7:]
    if keep:
        out, *kept, sums, partial, held, left = refs
    else:
        left, out, sums, partial, held = refs
        kept = (None, None)
    halves = left.shape[1] // LANES
    prepare_rows(rows_in, flips[0], left, proj, scale, wide, narrow)
    make_rows(left, [
        (columns[2 * side], kept[side], vector_reader(columns[2 * side + 1], halves))
        for side in range(2)], sums)
    write_rows(sums, partial, [0])
    message_kernel(2, wide, narrow, halves, *earlier, partial, columns[1], out, held)


def message_kernel(parts, wide, narrow, halves, *refs):
    partials, vector, out, held = refs[:parts + 1], refs[parts + 1], refs[-2], refs[-1]
    lines_of = [partials[0][...] + partials[1][...]] + [partial[...] for partial in partials[2:]]
    for part, lines in enumerate(lines_of):
        base = part_base(part, parts, wide, narrow) * halves
        for line in range(lines.shape[0]):
            held[pl.ds(base + line, 1), :] = lines[line:line + 1, :]
    _, low, y, _, _ = place(wide, narrow)
    mine = (low * 2 + y) * halves
    pieces = [held[line:line + 1, :] for line in range(held.shape[0])]
    pieces += [vector[pl.ds(mine + half, 1), :] for half in range(halves)]
    block = jnp.concatenate(pieces, axis=1)

    def copy(i, _):
        out[i] = block
        return 0

    lax.fori_loop(0, out.shape[0], copy, 0, unroll=8)


def second_kernel(wide, narrow, keep, parts, *refs):
    arrived, out, step_scalars, direction, images, targets, partial, sums = refs[:1] + refs[-7:]
    lines = partial.shape[0]
    halves = lines // narrow
    across = narrow // 2
    group = [(high, x) for x in range(narrow // 2) for high in range(2)]

    def unpack(low, _):
        for y, core in ((0, 0), (0, 1), (1, 0), (1, 1)):
            members = [device_at(high, low, y, x, core, wide, narrow) for high, x in group]
            slots = [slot(member, wide, narrow) for member in members]
            total = arrived[slots[0], :, 0:lines * LANES]
            for spot in slots[1:]:
                total = total + arrived[spot, :, 0:lines * LANES]
            for r, member in enumerate(members):
                for half in range(halves):
                    start = arrived[slots[r], :, (lines + half) * LANES:(lines + half + 1) * LANES]
                    line = r * halves + half
                    spot = pl.ds(member * halves + half, 1)
                    targets[spot, :] = start
                    images[spot, :] = total[:, line * LANES:(line + 1) * LANES] + noise_var * start
        return 0

    lax.fori_loop(0, wide // 4, unpack, 0, unroll=2)
    start, first = targets[...], images[...]
    norm = total_sum(start * start)
    alpha = norm / total_sum(start * first)
    residual = start - alpha * first
    norm_next = total_sum(residual * residual)
    beta = norm_next / norm
    whole = residual + beta * start
    direction[...] = whole
    high, low, y, x, core = place(wide, narrow)

    def side_reader(side):
        def read_vector(c, half):
            source = device_at(high, c // 2, c % 2, x, jnp.bitwise_xor(core, side), wide, narrow)
            return direction[pl.ds(source * halves + half, 1), :]
        return read_vector

    groups = narrow // parts
    for part in range(parts):
        part_sums = sums.at[part * groups:(part + 1) * groups]
        if keep:
            use_rows([(refs[1 + 2 * part + side], side_reader(side)) for side in range(2)], part_sums)
        else:
            make_rows(refs[3 + part], [(refs[1 + side], None, side_reader(side)) for side in range(2)], part_sums)
    write_rows(sums, partial, [part_base(part, parts, wide, narrow) for part in range(parts)])
    share = jnp.zeros((1, LANES), f32)
    for r, (row_high, row_x) in enumerate(group):
        for half in range(halves):
            spot = pl.ds(device_at(row_high, low, y, row_x, core, wide, narrow) * halves + half, 1)
            line = r * halves + half
            share = share + direction[spot, :] * partial[line:line + 1, :]
    blocks = [
        jnp.concatenate([partial[r * halves + half:r * halves + half + 1, :]
                         for half in range(halves)] + [share], axis=1)
        for r in range(narrow)]

    def copy(to_low, _):
        for r, (to_high, to_x) in enumerate(group):
            for to_y, to_core in ((0, 0), (0, 1), (1, 0), (1, 1)):
                to = device_at(to_high, to_low, to_y, to_x, to_core, wide, narrow)
                out[slot(to, wide, narrow)] = blocks[r]
        return 0

    lax.fori_loop(0, wide // 4, copy, 0, unroll=2)
    lane = lax.broadcasted_iota(jnp.int32, (1, LANES), 1)
    noise = noise_var * total_sum(whole * whole)
    step_scalars[0:1, :] = jnp.where(lane == 0, alpha, jnp.where(
        lane == 1, norm_next, jnp.where(lane == 2, beta, noise)))
    for half in range(halves):
        spot = pl.ds(device_at(high, low, y, x, core, wide, narrow) * halves + half, 1)
        step_scalars[1 + half:2 + half, :] = images[spot, :]
        step_scalars[1 + halves + half:2 + halves + half, :] = targets[spot, :]


def last_kernel(wide, narrow, arrived, step_scalars, solution_out, residual_out, answer, sems):
    alpha = step_scalars[0:1, 0:1]
    norm = step_scalars[0:1, 1:2]
    beta = step_scalars[0:1, 2:3]
    noise = step_scalars[0:1, 3:4]
    halves = answer.shape[1]

    def add(i, total):
        return total + arrived[i, :, halves * LANES:(halves + 1) * LANES]

    share = lax.fori_loop(0, arrived.shape[0], add, jnp.zeros((1, LANES), f32), unroll=32)
    alpha_next = norm / (total_sum(share) + noise)
    _, low, y, _, core = place(wide, narrow)
    product = jnp.zeros((1, (halves + 1) * LANES), f32)
    for high in range(2):
        for x in range(narrow // 2):
            member = device_at(high, low, y, x, core, wide, narrow)
            product = product + arrived[slot(member, wide, narrow)]
    for half in range(halves):
        begin = step_scalars[1 + halves + half:2 + halves + half, :]
        residual = begin - alpha * step_scalars[1 + half:2 + half, :]
        direction = residual + beta * begin
        image = product[:, half * LANES:(half + 1) * LANES] + noise_var * direction
        answer[0, half:half + 1, :] = alpha * begin + alpha_next * direction
        answer[1, half:half + 1, :] = residual - alpha_next * image
    copies = [pltpu.make_async_copy(answer.at[i], out, sems.at[i])
              for i, out in enumerate((solution_out, residual_out))]
    for copy in copies:
        copy.start()
    for copy in copies:
        copy.wait()


def call(kernel, out_shape, *args, scratch=(), **options):
    return pl.pallas_call(
        kernel,
        out_shape=out_shape,
        scratch_shapes=list(scratch),
        compiler_params=pltpu.CompilerParams(vmem_limit_bytes=VMEM_BYTES),
        **options,
    )(*args)


def to_all(blocks):
    group = list(range(blocks.shape[0] - 1, -1, -1))
    return lax.all_to_all(blocks, ALL, split_axis=0, concat_axis=0, axis_index_groups=[group], tiled=True)


def join_kernel(*refs):
    i = 0
    for block in refs[:-1]:
        for j in range(block.shape[0]):
            refs[-1][i] = block[j]
            i += 1


def join(*blocks, flops=0):
    total = sum(b.shape[0] for b in blocks)
    return call(join_kernel, jax.ShapeDtypeStruct((total, *blocks[0].shape[1:]), f32), *blocks,
                cost_estimate=pl.CostEstimate(flops=flops, bytes_accessed=0, transcendentals=0))


def first_round(latent, own, wide, narrow):
    lows, across = wide // 4, narrow // 2
    if lows & (lows - 1) or across != 2 or lows > DIRECT:
        every = lax.all_gather(own, ALL, axis=0, tiled=True)
        every = every.reshape(2, lows, 2, across, 2, *own.shape[1:])
        high, low, y, x, core = place(wide, narrow)
        rows = every
        for place_in, axis in ((low, 1), (y, 1), (core, 2)):
            rows = lax.dynamic_index_in_dim(rows, place_in, axis, keepdims=False)
        columns = lax.dynamic_index_in_dim(every, high, 0, keepdims=False)
        columns = lax.dynamic_index_in_dim(columns, x, 2, keepdims=False)
        rows = jnp.swapaxes(rows, 0, 1).reshape(narrow, *own.shape[1:])
        sides = [lax.dynamic_index_in_dim(columns, jnp.bitwise_xor(core, side), 2, keepdims=False)
                 for side in range(2)]
        sides = [[columns.reshape(wide // 2, *own.shape[1:])] for columns in sides]
        return [[rows]], sides, (None, None)

    sizes = axis_sizes(wide, narrow)

    def swap(value, **flips):
        pairs = []
        for i in range(wide * narrow):
            spot = list(np.unravel_index(i, sizes))
            for name, flip in flips.items():
                axis = dict(high=HIGH, low=LOW, y=Y, x=X, core=CORE)[name]
                spot[axis] = int(spot[axis]) ^ flip
            pairs.append((i, int(np.ravel_multi_index(spot, sizes))))
        return lax.ppermute(value, ALL, pairs)

    rows = join(latent, swap(latent, high=1), flops=EARLY)
    columns = [own] + [swap(own, low=flip // 2, y=flip % 2) for flip in range(1, 2 * lows)]
    sides = [columns, [swap(block, core=1) for block in columns]]
    parts = [[rows], [swap(rows, x=1)]]
    return parts, sides, ([0, 1], list(range(2 * lows)))


def on_device(wide, narrow, features, projection, targets):
    rows, proj = features.shape[0], projection.shape[1]
    halves = rows // LANES
    lines = narrow * halves
    devices = wide * narrow
    scale = -2.0 / proj * math.log2(math.e)
    depth = 6 * proj + 16
    keep = 4 * devices * rows * rows <= KEEP_BYTES

    def shape(*dims, dtype=f32):
        return jax.ShapeDtypeStruct(dims, dtype)

    def scratch(*dims, dtype=f32):
        return pltpu.VMEM(dims, dtype)

    feat = features.shape[1]
    inputs = [pltpu.with_memory_space_constraint(value, pltpu.HBM)
              for value in (features, projection.T, targets.reshape(1, rows))]
    latent, own = call(
        project_kernel, (shape(1, halves * proj, LANES), shape(1, halves * proj + 8, LANES)), *inputs,
        in_specs=[pl.BlockSpec(memory_space=pltpu.HBM)] * 3,
        scratch=[scratch(halves, LANES, feat, dtype=bf16), scratch(proj, feat, dtype=bf16),
                 scratch(1, rows), pltpu.SemaphoreType.DMA((2 * halves + 2,))])
    row_parts, sides, flips = first_round(latent, own, wide, narrow)
    parts = len(row_parts)
    groups = narrow // parts
    left = shape(groups, rows, depth, dtype=bf16)
    right = shape(wide // 2, depth, rows, dtype=bf16)
    vector = shape(wide // 2 * halves, LANES)
    kept = (shape(groups, wide // 2, rows, rows),) if keep else ()
    group_lines = shape(groups * halves, LANES)
    sums = scratch(groups, rows, LANES)
    settings = (proj, scale, wide, narrow, keep, flips)

    def cost(columns):
        tiles = groups * columns * rows * rows
        return pl.CostEstimate(flops=2 * tiles * depth, bytes_accessed=4 * tiles, transcendentals=tiles)

    lefts, columns, blocks, partials = [], [], [], []
    for side, column_blocks in enumerate(sides):
        row_blocks = row_parts[0] if side == 0 else lefts
        made = call(
            functools.partial(side_kernel, *settings, len(row_blocks), len(column_blocks)),
            ((left,) if side == 0 else ()) + (right, vector, group_lines) + kept,
            *row_blocks, *column_blocks, scratch=[sums], cost_estimate=cost(wide // 2))
        if side == 0:
            lefts, made = [made[0]], made[1:]
        columns += made[:2]
        partials.append(made[2])
        blocks += made[3:]
    message = shape(devices, 1, (lines + halves) * LANES)
    if parts == 2:
        made = call(
            functools.partial(rest_kernel, *settings),
            (message, *kept * 2) if keep else (left, message), *row_parts[1], *columns, *partials,
            scratch=[sums, scratch(groups * halves, LANES), scratch(lines, LANES)]
            + ([scratch(*left.shape, dtype=bf16)] if keep else []),
            cost_estimate=cost(wide))
        out = made[0 if keep else 1]
        blocks += made[1:] if keep else []
        lefts += [] if keep else made[:1]
    else:
        out = call(
            functools.partial(message_kernel, parts, wide, narrow, halves), message,
            *partials, columns[1], scratch=[scratch(lines, LANES)])
    block = blocks if keep else [columns[0], columns[2], *lefts]
    sums = scratch(narrow, rows, LANES)
    out, step_scalars = call(
        functools.partial(second_kernel, wide, narrow, keep, parts),
        (shape(devices, 1, (halves + 1) * LANES), shape(1 + 2 * halves, LANES)),
        to_all(out), *block,
        scratch=[scratch(devices * halves, LANES)] * 3 + [scratch(lines, LANES), sums])
    answer, residual = call(
        functools.partial(last_kernel, wide, narrow), (shape(halves, LANES), shape(halves, LANES)),
        to_all(out), step_scalars,
        out_specs=(pl.BlockSpec(memory_space=pl.ANY),) * 2,
        scratch=[scratch(2, halves, LANES), pltpu.SemaphoreType.DMA((2,))])
    return answer.reshape(rows), residual.reshape(rows)


def solution(mesh):
    wide, narrow = mesh.shape["wide"], mesh.shape["narrow"]
    line = jax.sharding.Mesh(mesh.devices.reshape(wide * narrow), (ALL,))
    in_specs = (P(ALL, None), P(), P(ALL))
    return jax.shard_map(
        functools.partial(on_device, wide, narrow), mesh=line,
        in_specs=in_specs, out_specs=(P(ALL), P(ALL)), check_vma=False,
    )
```
